32 devices in a mesh: wide: 8 (over y, x, core), narrow: 4 (over z).
Axes of the slice: x: 2, y: 2, z: 4, core: 2. Of those that a mesh axis runs over, the one named last changes fastest.
Arguments:
- tokens: bfloat16 [32768, 512], P(('wide', 'narrow')), may hold values from -6 to 6
- segment_ids: int32 [32768], P(('wide', 'narrow')), may hold values from 0 to 20, as said below
- expert_picks: int32 [32768, 2], P(('wide', 'narrow')), may hold values from 0 to 7, all different within a row; in each aligned block of 1024 rows (0 to 1023, 1024 to 2047, ...) at most 271 rows name the same one
- priority_ranks: int32 [32, 1024], P(('wide', 'narrow')), may hold values from 0 to 1023, each once within a row
- gain_attn: float32 [512], replicated, may hold values from 0.1 to 1.9
- w_qkv: bfloat16 [512, 1536], replicated, may hold values from -0.25 to 0.25
- w_proj: bfloat16 [512, 512], replicated, may hold values from -2 to 2
- gain_moe: float32 [512], replicated, may hold values from 0.1 to 1.9
- w_router: bfloat16 [512, 8], replicated, may hold values from -0.25 to 0.25
- w_in: bfloat16 [8, 512, 2048], P('wide', None, 'narrow'), may hold values from -0.25 to 0.25
- w_out: bfloat16 [8, 2048, 512], P('wide', 'narrow'), may hold values from -0.75 to 0.75
- cotangent: bfloat16 [32768, 512], P(('wide', 'narrow')), may hold values from -6 to 6
Outputs:
- mixed: bfloat16 [32768, 512], P(('wide', 'narrow'))
- grad_tokens: float32 [32768, 512], P(('wide', 'narrow'))
- grad_gain_attn: float32 [512], replicated
- grad_qkv: float32 [512, 1536], replicated
- grad_proj: float32 [512, 512], replicated
- grad_gain_moe: float32 [512], replicated
- grad_router: float32 [512, 8], replicated
- grad_in: float32 [8, 512, 2048], P('wide', None, 'narrow')
- grad_out: float32 [8, 2048, 512], P('wide', 'narrow')
- kept_counts: int32 [8], replicated
- dropped_counts: int32 [8], replicated
The draws below stay inside these ranges and needn't reach their ends.
Inputs may be any that keep to these rules, and one draw needn't show every extreme that they name: `expert_picks`: within each aligned block of 1024 tokens (one routing group) no expert is picked more than 269 + 2 times, and in some block one is picked exactly that often; a token's 2 picks differ; every expert is picked somewhere. `priority_ranks`: each row is a permutation of one routing group's positions; rank 0 comes first. `segment_ids`: each run of 1024 slots is one sequence of whole images of 49 or 144 patches, numbered from 0 up in order; the slots after the last whole image form one more segment. Some sequence holds only images of 49 patches.
All inputs are finite; a program needn't handle non-finite values.
Results may differ from the reference program's by a relative error of at most 0.015.
The reference program's roundings to bfloat16 on the way count: a program that leaves them out, or rounds other values in their place, can miss the bound.
Values may be sent and summed in bfloat16 or wider, within the bound.
A program may use at most 256 MiB of HBM per device.

```python
import math
import jax
import jax.numpy as jnp
import numpy as np
from jax import lax

D = 512
HEADS = 8
HEAD = 64
FF = 2048
TOP = 2
SEQ = 1024
IMG_COARSE = 49
IMG_FINE = 144
SEQS_DEV = 1
EXPERTS = 8
GROUPS = 32
TOK_DEV = 1024
TOKENS = 32768
CAP = 269


def draw_segment_ids(key, part):
    key = jax.random.fold_in(key, 3)
    images = SEQ // IMG_COARSE + 1
    sequences = TOKENS // SEQ
    coin = jax.random.randint(key, (sequences, images), 0, 2)
    chosen = jax.random.randint(jax.random.fold_in(key, 5), (), 0, sequences)
    coin = jnp.where(jnp.arange(sequences, dtype=jnp.int32)[:, None] == chosen, 0, coin)
    lengths = jnp.where(coin == 1, IMG_FINE, IMG_COARSE).astype(jnp.int32)
    boundary = jnp.cumsum(lengths, axis=1).astype(jnp.int32)
    places = jnp.arange(SEQ, dtype=jnp.int32)
    segment = jnp.sum((boundary[:, None, :] <= places[None, :, None]).astype(jnp.int32), axis=2)
    return segment.reshape(TOKENS).astype(jnp.int32)


def level_of(key, extent, cuts, smallest, high):
    loudness = 1.0
    for dim, blocks in cuts:
        heights = jax.random.uniform(jax.random.fold_in(jax.random.fold_in(key, 6), dim), (blocks,), jnp.float32, smallest / len(cuts), high / len(cuts))
        loudness = loudness * jnp.repeat(jnp.exp(heights), extent[dim] // blocks).reshape((-1,) + (1,) * (len(extent) - 1 - dim))
    return loudness


def routed_block(rng, own, number, rows, number_of, top, reach, slope):
    sequence = jax.random.permutation(rng, number_of)
    crowded, usual = shares(number_of, rows * top, reach, slope, True), shares(number_of, rows * top, reach, slope, False)
    places = jnp.arange(number_of)

    def named(sizes, rotation):
        used = int((sizes > 0).sum())
        fixed = max(1, used // 4)
        moved = fixed + (places - fixed + rotation * (used - fixed)) % max(1, number_of - fixed)
        return jnp.zeros((number_of,), jnp.int32).at[sequence[jnp.where(places < fixed, places, moved)]].set(jnp.asarray(sizes, jnp.int32))

    sizes = jnp.where(number % 4 == 0, named(crowded, number // 4), named(usual, number - number // 4 - 1))
    mixed = jax.random.permutation(jax.random.fold_in(own, 3), number_of)
    giver, receiver = mixed[0:number_of // 2 * 2:2], mixed[1:number_of // 2 * 2:2]
    slack = jnp.minimum(sizes[giver] - 1, reach - sizes[receiver]) // 2
    slack = jnp.where((giver == sequence[0]) | (receiver == sequence[0]) | (sizes[receiver] == 0), 0, jnp.maximum(slack, 0))
    moved = jax.random.randint(jax.random.fold_in(own, 4), (number_of // 2,), 0, 1 << 20) % (slack + 1)
    sizes = sizes.at[giver].add(-moved).at[receiver].add(moved)
    labels = jnp.searchsorted(jnp.cumsum(sizes), jnp.arange(rows * top), side="right").astype(jnp.int32)
    grid = labels.reshape(top, rows).T
    grid = grid[jax.random.permutation(jax.random.fold_in(own, 1), rows)]
    rotation = jax.random.randint(jax.random.fold_in(own, 2), (rows, 1), 0, top)
    return jnp.take_along_axis(grid, (jnp.arange(top)[None, :] + rotation) % top, axis=1)


def shares(count, total, limit, slope, full):
    portions = [(1 << 20) // math.isqrt(rank ** slope) + 1 for rank in range(1, count + 1)]
    largest = limit if full else min(limit, max(-(-total // count), total * portions[0] // sum(portions)))
    least = 1 if total - largest >= count - 1 else 0
    holding, spare = [largest] + [least] * (count - 1), total - largest - least * (count - 1)
    while spare > 0:
        candidates = [i for i in range(1, count) if holding[i] < largest] or [i for i in range(1, count) if holding[i] < limit]
        whole, remaining = sum([portions[i] for i in candidates]), spare
        for i in candidates:
            addition = min(limit - holding[i], max(1, remaining * portions[i] // whole), spare)
            holding[i] = holding[i] + addition
            spare = spare - addition
    return np.array(holding)


def normal_values(own_key, extent, deviation, reach, cuts=(), kind=jnp.bfloat16):
    level = level_of(own_key, extent, cuts, -0.22, 0.18) if cuts else 1.0
    result = jax.random.normal(own_key, extent, jnp.float32) * deviation * level
    return jnp.minimum(jnp.maximum(result, -reach), reach).astype(kind)


def setup_inputs(seed: int = 0) -> dict:
    key_of = jax.random.split(jax.random.key(seed), 13)
    tokens = normal_values(key_of[0], (TOKENS, D), 1.0, 6.0, ((0, 32),))
    segment_ids = draw_segment_ids(jax.random.fold_in(key_of[12], 71), 0)
    expert_picks_keys = jax.random.split(jax.random.fold_in(key_of[2], 1), TOKENS // TOK_DEV)
    expert_picks_turns = jax.random.permutation(jax.random.fold_in(key_of[2], 3), TOKENS // TOK_DEV)
    expert_picks = jax.vmap(lambda own, number: routed_block(jax.random.fold_in(key_of[2], 2), own, number, TOK_DEV, EXPERTS, TOP, CAP + 2, 0))(expert_picks_keys, expert_picks_turns).reshape((TOKENS, TOP))
    priority_ranks = jax.vmap(lambda own: jax.random.permutation(own, TOK_DEV))(jax.random.split(key_of[3], GROUPS)).reshape((GROUPS, TOK_DEV)).astype(jnp.int32)
    gain_attn = jnp.clip(1.0 + 0.18 * jax.random.normal(key_of[4], (D,), jnp.float32), 0.1, 1.9)
    w_qkv = normal_values(key_of[5], (D, 3 * D), D ** -0.5, 0.25)
    w_proj = normal_values(key_of[6], (D, D), (max(D // 64, 1)) ** -0.5, 2.0)
    gain_moe = jnp.clip(1.0 + 0.18 * jax.random.normal(key_of[7], (D,), jnp.float32), 0.1, 1.9)
    w_router = normal_values(key_of[8], (D, EXPERTS), D ** -0.5, 0.25)
    w_in = normal_values(key_of[9], (EXPERTS, D, FF), D ** -0.5, 0.25, ((0, 8), (2, 4)))
    w_out = normal_values(key_of[10], (EXPERTS, FF, D), (max(2 * FF // (EXPERTS * EXPERTS), 1)) ** -0.5, 0.75, ((0, 8), (1, 4)))
    cotangent = normal_values(key_of[11], (TOKENS, D), 1.0, 6.0, ((0, 32),))
    return dict(tokens=tokens, segment_ids=segment_ids, expert_picks=expert_picks, priority_ranks=priority_ranks, gain_attn=gain_attn, w_qkv=w_qkv, w_proj=w_proj, gain_moe=gain_moe, w_router=w_router, w_in=w_in, w_out=w_out, cotangent=cotangent)


@jax.custom_vjp
def low(v):
    return lax.optimization_barrier(v.astype(jnp.bfloat16)).astype(jnp.float32)

@jax.custom_vjp
def low_back(v):
    return v

def low_keep(v):
    return (low(v), None)

def low_pass(kept, grad):
    return (grad,)

def back_keep(v):
    return (v, None)

def back_low(kept, grad):
    return (low(grad),)
low.defvjp(low_keep, low_pass)
low_back.defvjp(back_keep, back_low)
highest = lax.Precision.HIGHEST

def layer_norm(values_in, gain):
    centered = values_in - lax.optimization_barrier(jnp.mean(values_in, axis=-1, keepdims=True))
    variance = lax.optimization_barrier(jnp.mean(centered * centered, axis=-1, keepdims=True))
    return centered * lax.rsqrt(variance + 1e-06) * gain

def exact_gelu(values_in):
    return jax.nn.gelu(values_in, approximate=False)

def route_group(picked, ranking, experts):
    group_size = picked.shape[0]
    by_rank = jnp.zeros_like(ranking).at[ranking].set(jnp.arange(group_size, dtype=jnp.int32))
    ordered = picked[by_rank].T.reshape(-1)
    onehot = (ordered[:, None] == jnp.arange(experts, dtype=jnp.int32)[None, :]).astype(jnp.int32)
    before = jnp.cumsum(onehot, axis=0) - onehot
    position = lax.optimization_barrier(jnp.sum(before * onehot, axis=1)).astype(jnp.int32)
    lookup = jnp.arange(picked.shape[1], dtype=jnp.int32)[None, :] * group_size + ranking[:, None]
    return position[lookup].astype(jnp.int32)

def attend_group(group_block, segments, gain_attn, w_qkv, w_proj):
    all_heads = HEADS * HEAD
    head_shape = (SEQS_DEV, SEQ, HEADS, HEAD)
    normed = low(layer_norm(group_block, gain_attn))
    packed = jnp.dot(normed, w_qkv, precision=highest)
    queries = low(low_back(packed[:, :all_heads])).reshape(head_shape)
    key_heads = low(low_back(packed[:, all_heads:2 * all_heads])).reshape(head_shape)
    value_heads = low(low_back(packed[:, 2 * all_heads:])).reshape(head_shape)
    scores = jnp.einsum('sqhd,skhd->shqk', queries, key_heads, precision=highest) * HEAD ** (-0.5)
    scores = low_back(scores)
    segment_rows = segments.reshape(SEQS_DEV, SEQ)
    allowed = segment_rows[:, None, :, None] == segment_rows[:, None, None, :]
    probs_low = low(jax.nn.softmax(jnp.where(allowed, scores, -1e+30), axis=-1))
    context = jnp.einsum('shqk,skhd->sqhd', probs_low, value_heads, precision=highest).reshape(TOK_DEV, all_heads)
    context = low(low_back(context))
    return group_block + low_back(jnp.dot(context, w_proj, precision=highest))

def expert_apply(routed_rows, weight_in, weight_out):
    preact = low_back(jnp.dot(routed_rows, weight_in, precision=highest))
    act_low = low(exact_gelu(preact))
    return low(low_back(jnp.dot(act_low, weight_out, precision=highest)))

def reference(tokens, segment_ids, expert_picks, priority_ranks, gain_attn, w_qkv, w_proj, gain_moe, w_router, w_in, w_out, cotangent):
    slot_index = jax.vmap(lambda picked, ranking: route_group(picked, ranking, EXPERTS))(expert_picks.reshape(GROUPS, TOK_DEV, TOP), priority_ranks).reshape(TOKENS, TOP)
    kept_mask = slot_index < CAP
    group_of = (jnp.arange(TOKENS, dtype=jnp.int32) // TOK_DEV)[:, None]
    slot_span = GROUPS * CAP
    target = jnp.where(kept_mask, expert_picks * slot_span + group_of * CAP + slot_index, EXPERTS * slot_span).astype(jnp.int32)
    anchor = jnp.broadcast_to(jnp.arange(TOKENS, dtype=jnp.int32)[:, None], (TOKENS, TOP))
    slot_table = jnp.full((EXPERTS * slot_span + 1,), TOKENS, jnp.int32).at[target.reshape(-1)].set(anchor.reshape(-1))
    gather_index = slot_table[:-1].reshape(EXPERTS, slot_span)
    onehot = (expert_picks[:, :, None] == jnp.arange(EXPERTS, dtype=jnp.int32)[None, None, :]).astype(jnp.int32)
    kept_counts = lax.optimization_barrier(jnp.sum(onehot * kept_mask[:, :, None].astype(jnp.int32), axis=(0, 1))).astype(jnp.int32)
    dropped_counts = (lax.optimization_barrier(jnp.sum(onehot, axis=(0, 1))) - kept_counts).astype(jnp.int32)
    kept_float = kept_mask.astype(jnp.float32)

    def forward(tokens_float, gain_a, qkv_float, proj_float, gain_m, router_float, in_float, out_float):

        def one_group(group_pair):
            return attend_group(group_pair[0], group_pair[1], gain_a, qkv_float, proj_float)
        residual = lax.map(jax.checkpoint(one_group), (tokens_float.reshape(GROUPS, TOK_DEV, D), segment_ids.reshape(GROUPS, TOK_DEV))).reshape(TOKENS, D)
        normed = low(layer_norm(residual, gain_m))
        gate_probs = jax.nn.softmax(jnp.dot(normed, router_float, precision=highest), axis=-1)
        padded = jnp.concatenate([normed, jnp.zeros((1, D), jnp.float32)], axis=0)
        routed_rows = low_back(padded[gather_index])

        def one_expert(expert_triple):
            return expert_apply(expert_triple[0], expert_triple[1], expert_triple[2])
        results = lax.map(jax.checkpoint(one_expert), (routed_rows, in_float, out_float))
        flat_rows = jnp.concatenate([results.reshape(EXPERTS * slot_span, D), jnp.zeros((1, D), jnp.float32)], axis=0)
        chosen = flat_rows[target]
        gate_weight = jnp.take_along_axis(gate_probs, expert_picks, axis=1) * kept_float
        return residual + lax.optimization_barrier(jnp.sum(gate_weight[:, :, None] * chosen, axis=1))
    layer_out, pullback = jax.vjp(forward, tokens.astype(jnp.float32), gain_attn, w_qkv.astype(jnp.float32), w_proj.astype(jnp.float32), gain_moe, w_router.astype(jnp.float32), w_in.astype(jnp.float32), w_out.astype(jnp.float32))
    pulled = pullback(cotangent.astype(jnp.float32))
    return (layer_out.astype(jnp.bfloat16), pulled[0], pulled[1], pulled[2], pulled[3], pulled[4], pulled[5], pulled[6], pulled[7], kept_counts, dropped_counts)
```

```python
import functools

import jax
import jax.numpy as jnp
from jax import lax
from jax.experimental import pallas as pl
from jax.experimental.pallas import tpu as pltpu
from jax.sharding import PartitionSpec as P

D = 512
HEADS = 8
HEAD = 64
PAIRS = HEADS // 2
PAIR = 2 * HEAD
TOP = 2
SEQ = 1024
TOK_DEV = 1024
LANES = 128
QB = 128
WINDOW = 432
TILE = 256
MIB = 1024 * 1024

f32 = jnp.float32
bf16 = jnp.bfloat16
NT = (((1,), (1,)), ((), ()))
TN = (((0,), (0,)), ((), ()))


def dot(a, b):
    return jnp.dot(a, b, preferred_element_type=f32)


def dot_nt(a, b):
    return lax.dot_general(a, b, NT, preferred_element_type=f32)


def dot_tn(a, b):
    return lax.dot_general(a, b, TN, preferred_element_type=f32)


def iota(shape, dim):
    return lax.broadcasted_iota(jnp.int32, shape, dim)


def norm_parts(values_in):
    centered = values_in - jnp.mean(values_in, axis=-1, keepdims=True)
    variance = jnp.mean(centered * centered, axis=-1, keepdims=True)
    inverse = lax.rsqrt(variance + 1e-06)
    return (centered * inverse, inverse)


def norm_back(grad_normed, gain, normalized, inverse):
    grad_gain = jnp.sum(grad_normed * normalized, axis=0, keepdims=True)
    scaled = grad_normed * gain
    inner = scaled - jnp.mean(scaled, axis=-1, keepdims=True)
    inner = inner - normalized * jnp.mean(scaled * normalized, axis=-1, keepdims=True)
    return (inner * inverse, grad_gain)


def split2(values_in):
    high = values_in.astype(bf16)
    low = (values_in - high.astype(f32)).astype(bf16)
    return high, low


def row_to_col(row):
    n = row.shape[1]
    return jnp.transpose(jnp.broadcast_to(row, (LANES, n)))[:, :1]


def route_kernel(experts, capacity, picks, ranks, cot, slot_col, slot_row, counts, gz_send):
    tokens = ranks.shape[1]
    padded = gz_send.shape[1]
    rank_row = ranks[...].astype(f32)
    rank_col = row_to_col(rank_row)
    lane = iota((tokens, LANES), 1)
    pick0 = picks[:, 0:1]
    pick1 = picks[:, 1:2]
    hot = jnp.where(lane == jnp.where(lane < experts, pick0, pick1 + experts), 1.0, 0.0).astype(f32)
    before = (rank_row < rank_col).astype(f32).astype(bf16)
    earlier = dot(before, hot.astype(bf16))
    total = jnp.sum(hot, axis=0, keepdims=True)
    total = jnp.broadcast_to(total, (8, LANES))
    lane8 = iota((8, LANES), 1)
    first = jnp.where(lane8 < experts, total, 0.0)
    earlier = earlier + pltpu.roll(first, experts, axis=1)[:1]
    kept = (hot > 0.5) & (earlier < float(capacity))
    slots = jnp.where(kept, earlier, -1.0)
    slots = jnp.maximum(slots, pltpu.roll(slots, LANES - experts, axis=1))
    slots = jnp.where(lane < experts, slots, -1.0)
    slot_col[...] = slots
    slot_row[...] = jnp.transpose(slots)[:experts]
    kept_lane = jnp.sum(jnp.where(slots >= 0.0, 1.0, 0.0), axis=0, keepdims=True)
    both = total + pltpu.roll(total, LANES - experts, axis=1)
    both = jnp.where(lane8 < experts, both, 0.0)
    sub8 = iota((8, LANES), 0)
    counts[...] = jnp.where(sub8 == 0, kept_lane, jnp.where(sub8 == 1, both, 0.0))

    @pl.loop(0, experts)
    def _(e):
        chosen = iota((padded, tokens), 0).astype(f32) == slot_row[pl.ds(e, 1), :]
        gz_send[e] = dot(chosen.astype(f32).astype(bf16), cot[...]).astype(bf16)


def route(picks, ranks, cot, experts, capacity, padded):
    tokens = picks.shape[0]
    return pl.pallas_call(
        functools.partial(route_kernel, experts, capacity),
        out_shape=(
            jax.ShapeDtypeStruct((tokens, LANES), f32),
            jax.ShapeDtypeStruct((experts, tokens), f32),
            jax.ShapeDtypeStruct((8, LANES), f32),
            jax.ShapeDtypeStruct((experts, padded, D), bf16),
        ),
        compiler_params=pltpu.CompilerParams(vmem_limit_bytes=40 * MIB),
        cost_estimate=pl.CostEstimate(
            flops=2 * experts * padded * tokens * D, bytes_accessed=6 * MIB, transcendentals=0
        ),
        name="route",
    )(picks, ranks, cot)


def stack_heads(block):
    lane = iota(block.shape, 1)
    zero = jnp.zeros_like(block)
    return jnp.concatenate(
        [jnp.where(lane < HEAD, block, zero), jnp.where(lane < HEAD, zero, block)], axis=0
    )


def unstack_cols(stacked):
    row = iota((PAIR, QB), 0)
    picked = jnp.where(row < HEAD, stacked[:, :QB], stacked[:, QB:])
    return jnp.transpose(picked)


def window_bias(seg_col, seg_row, low, width, query):
    same = seg_col[pl.ds(low, width), :] == seg_row[:, pl.ds(query, QB)]
    half = jnp.where(same, 0.0, -1e30).astype(f32)
    return jnp.concatenate([half, half], axis=1)


def by_window(windows, block, body):
    low = windows[block]
    fits = windows[block + SEQ // QB]

    @pl.when(fits == 1)
    def _():
        body(pl.multiple_of(low, 16), WINDOW)

    @pl.when(fits != 1)
    def _():
        body(0, SEQ)


def forward_kernel(
    experts,
    windows,
    tok,
    seg,
    gain_attn,
    w_qkv,
    w_proj,
    gain_moe,
    w_router,
    slot_row,
    normed_attn,
    packed,
    context,
    lse,
    residual,
    normed_moe,
    gates,
    rows_send,
    seg_col,
    seg_row,
    router,
    gate_row,
    gate_slot,
):
    tokens = tok.shape[0]
    padded = rows_send.shape[1]
    seg_row[...] = seg[...].astype(f32)
    seg_col[...] = jnp.transpose(jnp.broadcast_to(seg_row[...], (LANES, tokens)))
    router[...] = jnp.zeros_like(router)
    router[:, :experts] = w_router[...]

    @pl.loop(0, tokens // TILE)
    def _(i):
        rows = pl.ds(pl.multiple_of(i * TILE, TILE), TILE)
        normal, unused = norm_parts(tok[rows, :].astype(f32))
        normed = (normal * gain_attn[...]).astype(bf16)
        normed_attn[rows, :] = normed
        packed[rows, :] = dot(normed, w_qkv[...]).astype(bf16)

    @pl.loop(0, tokens // QB)
    def _(block):
        query = pl.multiple_of(block * QB, QB)

        def body(low, width):
            bias = window_bias(seg_col, seg_row, low, width, query)
            for pair in range(PAIRS):
                cols = pair * PAIR
                q = stack_heads(packed[pl.ds(query, QB), cols : cols + PAIR]) * HEAD ** (-0.5)
                k = packed[pl.ds(low, width), D + cols : D + cols + PAIR]
                v = packed[pl.ds(low, width), 2 * D + cols : 2 * D + cols + PAIR]
                scores = dot_nt(k, q.astype(bf16)) + bias
                peak = jnp.max(scores, axis=0, keepdims=True)
                exponent = jnp.exp(scores - peak)
                totals = jnp.sum(exponent, axis=0, keepdims=True)
                probs_low = (exponent * (1.0 / totals)).astype(bf16)
                lse[pl.ds(block, 1), pair, :] = peak + jnp.log(totals)
                mixed = dot_tn(v, probs_low)
                context[pl.ds(query, QB), cols : cols + PAIR] = unstack_cols(mixed).astype(bf16)

        by_window(windows, block, body)

    @pl.loop(0, tokens // TILE)
    def _(i):
        rows = pl.ds(pl.multiple_of(i * TILE, TILE), TILE)
        rest = tok[rows, :].astype(f32) + dot(context[rows, :], w_proj[...])
        residual[rows, :] = rest
        normal, unused = norm_parts(rest)
        normed = (normal * gain_moe[...]).astype(bf16)
        normed_moe[rows, :] = normed
        logits = dot(normed, router[...])
        logits = jnp.where(iota(logits.shape, 1) < experts, logits, -1e30)
        exponent = jnp.exp(logits - jnp.max(logits, axis=1, keepdims=True))
        gates[rows, :] = exponent / jnp.sum(exponent, axis=1, keepdims=True)

    gate_row[...] = jnp.transpose(gates[...])[:experts]
    gate_slot[...] = jnp.zeros_like(gate_slot)

    @pl.loop(0, experts)
    def _(e):
        chosen = iota((padded, tokens), 0).astype(f32) == slot_row[pl.ds(e, 1), :]
        chosen = chosen.astype(f32).astype(bf16)
        rows_send[e] = dot(chosen, normed_moe[...]).astype(bf16)
        gate = gate_row[pl.ds(e, 1), :]
        high, middle = split2(gate)
        low = (gate - high.astype(f32) - middle.astype(f32)).astype(bf16)
        three = jnp.concatenate(
            [high.astype(f32), middle.astype(f32), low.astype(f32), jnp.zeros((5, tokens), f32)], axis=0
        )
        gate_slot[:, :padded] = dot_nt(three.astype(bf16), chosen)
        tail = rows_send[e, padded - 16 :, :].astype(f32)
        sub = iota(tail.shape, 0)
        for part in range(3):
            tail = jnp.where(sub == 13 + part, gate_slot[part : part + 1, :], tail)
        rows_send[e, padded - 16 :, :] = tail.astype(bf16)


def forward(windows, tok, seg, gain_attn, w_qkv, w_proj, gain_moe, w_router, slot_row, padded):
    tokens = tok.shape[0]
    experts = w_router.shape[1]
    vmem = pl.BlockSpec(memory_space=pltpu.VMEM)
    return pl.pallas_call(
        functools.partial(forward_kernel, experts),
        in_specs=[pl.BlockSpec(memory_space=pltpu.SMEM)] + [vmem] * 8,
        out_shape=(
            jax.ShapeDtypeStruct((tokens, D), bf16),
            jax.ShapeDtypeStruct((tokens, 3 * D), bf16),
            jax.ShapeDtypeStruct((tokens, D), bf16),
            jax.ShapeDtypeStruct((tokens // QB, PAIRS, 2 * QB), f32),
            jax.ShapeDtypeStruct((tokens, D), f32),
            jax.ShapeDtypeStruct((tokens, D), bf16),
            jax.ShapeDtypeStruct((tokens, LANES), f32),
            jax.ShapeDtypeStruct((experts, padded, D), bf16),
        ),
        scratch_shapes=[
            pltpu.VMEM((tokens, LANES), f32),
            pltpu.VMEM((1, tokens), f32),
            pltpu.VMEM((D, LANES), bf16),
            pltpu.VMEM((experts, tokens), f32),
            pltpu.VMEM((8, D), f32),
        ],
        compiler_params=pltpu.CompilerParams(vmem_limit_bytes=56 * MIB),
        cost_estimate=pl.CostEstimate(
            flops=8 * 1024 * MIB, bytes_accessed=16 * MIB, transcendentals=4 * MIB
        ),
        name="attention_forward",
    )(windows, tok, seg, gain_attn, w_qkv, w_proj, gain_moe, w_router, slot_row)


def gelu_parts(x):
    density = jnp.exp(-0.5 * (x * x))
    t = 1.0 / (1.0 + (0.3275911 * 2.0**-0.5) * jnp.abs(x))
    poly = 0.5 * 1.061405429
    for factor in (-1.453152027, 1.421413741, -0.284496736, 0.254829592):
        poly = poly * t + 0.5 * factor
    tail = poly * t * density
    phi = jnp.where(x >= 0.0, 1.0 - tail, tail)
    return phi, x * density * 0.3989422804014327


def expert_kernel(
    capacity,
    received,
    gz,
    weights_in,
    weights_out,
    out,
    back,
    grads,
    rows,
    rows_t,
    gz_t,
    act,
    gpre,
    out_sum,
    back_sum,
    scaled,
):
    sources, padded, unused = rows.shape
    shards = weights_in.shape[0]

    @pl.loop(0, sources)
    def _(s):
        span = pl.ds(pl.multiple_of(s * padded, 16), padded)
        rows[s] = received[s]
        tail = received[s, padded - 16 :, :].astype(f32)
        gate = tail[13:14] + tail[14:15] + tail[15:16]
        gate = jnp.transpose(jnp.broadcast_to(gate, (LANES, D)))[:padded, :1]
        live = iota((padded, 1), 0) < capacity
        gate = jnp.where(live, gate, 0.0)
        scaled[span, :] = (gate * gz[s].astype(f32)).astype(bf16)
        live16 = iota((16, 1), 0) < 16 - (padded - capacity)
        rows[s, padded - 16 :, :] = jnp.where(live16, tail, 0.0).astype(bf16)
        out_sum[span, :] = jnp.zeros((padded, D), f32)
        back_sum[span, :] = jnp.zeros((padded, D), f32)

    for c in range(shards):

        @pl.loop(0, sources)
        def _(s):
            span = pl.ds(pl.multiple_of(s * padded, 16), padded)
            w_in = weights_in[c]
            w_out = weights_out[c]
            pre = dot(rows[s], w_in)
            phi, slope = gelu_parts(pre)
            act_low = (pre * phi).astype(bf16)
            act[span, :] = act_low
            out_sum[span, :] += dot(act_low, w_out)
            grad_pre = (dot_nt(scaled[span, :], w_out) * (phi + slope)).astype(bf16)
            gpre[span, :] = grad_pre
            back_sum[span, :] += dot_nt(grad_pre, w_in)
            if c == shards - 1:
                out[s] = out_sum[span, :].astype(bf16)
                back[s] = back_sum[span, :].astype(bf16)

        if c == 0:
            for s in range(sources):
                rows_t[:, s * padded : (s + 1) * padded] = jnp.transpose(rows[s])
                gz_t[:, s * padded : (s + 1) * padded] = jnp.transpose(
                    scaled[s * padded : (s + 1) * padded, :]
                )
        grads[c, :D, :] = dot(rows_t[...], gpre[...]).astype(bf16)
        grads[c, D:, :] = dot(gz_t[...], act[...]).astype(bf16)


def experts_apply(rows, gz, weights_in, weights_out, capacity):
    sources, padded, unused = rows.shape
    shards = weights_in.shape[0]
    hidden = weights_in.shape[2]
    total = sources * padded
    return pl.pallas_call(
        functools.partial(expert_kernel, capacity),
        out_shape=(
            jax.ShapeDtypeStruct(rows.shape, bf16),
            jax.ShapeDtypeStruct(rows.shape, bf16),
            jax.ShapeDtypeStruct((shards, 2 * D, hidden), bf16),
        ),
        scratch_shapes=[
            pltpu.VMEM(rows.shape, bf16),
            pltpu.VMEM((D, total), bf16),
            pltpu.VMEM((D, total), bf16),
            pltpu.VMEM((total, hidden), bf16),
            pltpu.VMEM((total, hidden), bf16),
            pltpu.VMEM((total, D), f32),
            pltpu.VMEM((total, D), f32),
            pltpu.VMEM((total, D), bf16),
        ],
        compiler_params=pltpu.CompilerParams(vmem_limit_bytes=60 * MIB),
        cost_estimate=pl.CostEstimate(
            flops=12 * total * D * hidden * shards, bytes_accessed=20 * MIB, transcendentals=0
        ),
        name="experts",
    )(rows, gz, weights_in, weights_out)


def backward_kernel(
    experts,
    windows,
    tok,
    seg,
    gain_attn,
    w_qkv,
    w_proj,
    gain_moe,
    w_router,
    slot_col,
    cot,
    normed_attn,
    packed,
    context,
    lse,
    residual,
    normed_moe,
    gates,
    returned,
    back,
    mixed,
    grad_tokens,
    grad_gains,
    grad_qkv,
    grad_proj,
    grad_router,
    seg_col,
    seg_row,
    router,
    grad_residual,
    grad_attn,
    grad_context,
    grad_logits,
    grad_k,
    grad_v,
    grad_packed,
):
    tokens = tok.shape[0]
    padded = returned.shape[1]
    seg_row[...] = seg[...].astype(f32)
    seg_col[...] = jnp.transpose(jnp.broadcast_to(seg_row[...], (LANES, tokens)))
    router[...] = jnp.zeros_like(router)
    router[:, :experts] = w_router[...]
    grad_gains[...] = jnp.zeros_like(grad_gains)

    @pl.loop(0, tokens // TILE)
    def _(i):
        rows = pl.ds(pl.multiple_of(i * TILE, TILE), TILE)
        grad_z = cot[rows, :].astype(f32)
        probs = gates[rows, :]
        slots = slot_col[rows, :]
        lane = iota((TILE, LANES), 1)
        rest = residual[rows, :]
        total = rest
        back_total = jnp.zeros((TILE, D), f32)
        grad_gates = jnp.zeros((TILE, LANES), f32)
        for e in range(experts):
            slot = slots[:, e : e + 1]
            chosen = (iota((TILE, padded), 1).astype(f32) == slot).astype(f32).astype(bf16)
            result = dot(chosen, returned[e])
            total = total + probs[:, e : e + 1] * result
            inner = jnp.sum(result * grad_z, axis=1, keepdims=True)
            grad_gates = grad_gates + jnp.where(lane == e, inner, 0.0)
            back_total = back_total + dot(chosen, back[e])
        mixed[rows, :] = total.astype(bf16)
        gate_inner = jnp.sum(probs * grad_gates, axis=1, keepdims=True)
        high, low = split2(probs * (grad_gates - gate_inner))
        grad_logits[rows, :LANES] = high
        grad_logits[rows, LANES:] = low
        grad_normed = back_total + dot_nt(high, router[...]) + dot_nt(low, router[...])
        normal, inverse = norm_parts(rest)
        grad_norm, grad_gain = norm_back(grad_normed, gain_moe[...], normal, inverse)
        grad_gains[1:2, :] += grad_gain
        grad_rest = grad_z + grad_norm
        grad_residual[rows, :] = grad_rest
        attn = grad_rest.astype(bf16)
        grad_attn[rows, :] = attn
        grad_context[rows, :] = dot_nt(attn, w_proj[...]).astype(bf16)

    both = dot_tn(normed_moe[...], grad_logits[...])
    grad_router[...] = both[:, :LANES] + both[:, LANES:]
    grad_proj[...] = dot_tn(context[...], grad_attn[...])
    grad_k[...] = jnp.zeros_like(grad_k)
    grad_v[...] = jnp.zeros_like(grad_v)

    @pl.loop(0, tokens // QB)
    def _(block):
        query = pl.multiple_of(block * QB, QB)

        def body(low, width):
            bias = window_bias(seg_col, seg_row, low, width, query)
            for pair in range(PAIRS):
                cols = pair * PAIR
                q = (stack_heads(packed[pl.ds(query, QB), cols : cols + PAIR]) * HEAD ** (-0.5)).astype(bf16)
                k = packed[pl.ds(low, width), D + cols : D + cols + PAIR]
                v = packed[pl.ds(low, width), 2 * D + cols : 2 * D + cols + PAIR]
                grad_c = stack_heads(grad_context[pl.ds(query, QB), cols : cols + PAIR])
                probs = jnp.exp(dot_nt(k, q) + bias - lse[pl.ds(block, 1), pair, :])
                grad_probs = dot_nt(v, grad_c)
                grad_v[pl.ds(low, width), cols : cols + PAIR] += dot(probs.astype(bf16), grad_c)
                weighted = probs * grad_probs
                inner = jnp.sum(weighted, axis=0, keepdims=True)
                grad_scores = (weighted - probs * inner).astype(bf16)
                grad_k[pl.ds(low, width), cols : cols + PAIR] += dot(grad_scores, q)
                grad_q = unstack_cols(dot_tn(k, grad_scores)) * HEAD ** (-0.5)
                grad_packed[pl.ds(query, QB), cols : cols + PAIR] = grad_q.astype(bf16)

        by_window(windows, block, body)

    @pl.loop(0, tokens // TILE)
    def _(i):
        rows = pl.ds(pl.multiple_of(i * TILE, TILE), TILE)
        grad_packed[rows, D : 2 * D] = grad_k[rows, :].astype(bf16)
        grad_packed[rows, 2 * D :] = grad_v[rows, :].astype(bf16)
        grad_normed = dot_nt(grad_packed[rows, :], w_qkv[...])
        normal, inverse = norm_parts(tok[rows, :].astype(f32))
        grad_norm, grad_gain = norm_back(grad_normed, gain_attn[...], normal, inverse)
        grad_gains[0:1, :] += grad_gain
        grad_tokens[rows, :] = grad_residual[rows, :] + grad_norm

    grad_qkv[...] = dot_tn(normed_attn[...], grad_packed[...])


def backward(experts, windows, *operands):
    tok = operands[0]
    tokens = tok.shape[0]
    vmem = pl.BlockSpec(memory_space=pltpu.VMEM)
    return pl.pallas_call(
        functools.partial(backward_kernel, experts),
        in_specs=[pl.BlockSpec(memory_space=pltpu.SMEM)] + [vmem] * len(operands),
        out_shape=(
            jax.ShapeDtypeStruct((tokens, D), bf16),
            jax.ShapeDtypeStruct((tokens, D), f32),
            jax.ShapeDtypeStruct((8, D), f32),
            jax.ShapeDtypeStruct((D, 3 * D), f32),
            jax.ShapeDtypeStruct((D, D), f32),
            jax.ShapeDtypeStruct((D, LANES), f32),
        ),
        scratch_shapes=[
            pltpu.VMEM((tokens, LANES), f32),
            pltpu.VMEM((1, tokens), f32),
            pltpu.VMEM((D, LANES), bf16),
            pltpu.VMEM((tokens, D), f32),
            pltpu.VMEM((tokens, D), bf16),
            pltpu.VMEM((tokens, D), bf16),
            pltpu.VMEM((tokens, 2 * LANES), bf16),
            pltpu.VMEM((tokens, D), f32),
            pltpu.VMEM((tokens, D), f32),
            pltpu.VMEM((tokens, 3 * D), bf16),
        ],
        compiler_params=pltpu.CompilerParams(vmem_limit_bytes=60 * MIB),
        cost_estimate=pl.CostEstimate(
            flops=30 * 1024 * MIB, bytes_accessed=30 * MIB, transcendentals=4 * MIB
        ),
        name="attention_backward",
    )(windows, *operands)


def per_device(
    tokens,
    segment_ids,
    expert_picks,
    priority_ranks,
    gain_attn,
    w_qkv,
    w_proj,
    gain_moe,
    w_router,
    w_in,
    w_out,
    cotangent,
):
    experts = w_router.shape[1]
    capacity = (21 * TOP * TOK_DEV + 20 * experts - 1) // (20 * experts)
    padded = (capacity + 3 + 15) // 16 * 16
    gain_attn = gain_attn.reshape(1, D)
    gain_moe = gain_moe.reshape(1, D)
    seg = segment_ids.reshape(1, SEQ)
    first = jnp.sum((segment_ids[None, :] < segment_ids[0::QB, None]).astype(jnp.int32), axis=1)
    after = jnp.sum((segment_ids[None, :] <= segment_ids[QB - 1 :: QB, None]).astype(jnp.int32), axis=1)
    low = jnp.minimum(first // 16 * 16, SEQ - WINDOW)
    fits = (after - low <= WINDOW).astype(jnp.int32)
    windows = jnp.concatenate([low, fits])

    slot_col, slot_row, counts, gz_send = route(
        expert_picks, priority_ranks, cotangent, experts, capacity, padded
    )
    gz = lax.all_to_all(gz_send, "wide", split_axis=0, concat_axis=0, tiled=True)
    gathered_in = lax.all_gather(w_in[0], "narrow", axis=0, tiled=False)
    gathered_out = lax.all_gather(w_out[0], "narrow", axis=0, tiled=False)
    normed_attn, packed, context, lse, residual, normed_moe, gates, rows_send = forward(
        windows, tokens, seg, gain_attn, w_qkv, w_proj, gain_moe, w_router, slot_row, padded
    )
    rows = lax.all_to_all(rows_send, "wide", split_axis=0, concat_axis=0, tiled=True)
    out, back, grads = experts_apply(rows, gz, gathered_in, gathered_out, capacity)
    returned = lax.all_to_all(out, "wide", split_axis=0, concat_axis=0, tiled=True)
    back = lax.all_to_all(back, "wide", split_axis=0, concat_axis=0, tiled=True)
    own = lax.psum_scatter(grads, "narrow", scatter_dimension=0, tiled=False).astype(f32)
    mixed, grad_tokens, grad_gains, grad_qkv, grad_proj, grad_router = backward(
        experts,
        windows,
        tokens,
        seg,
        gain_attn,
        w_qkv,
        w_proj,
        gain_moe,
        w_router,
        slot_col,
        cotangent,
        normed_attn,
        packed,
        context,
        lse,
        residual,
        normed_moe,
        gates,
        returned,
        back,
    )
    axes = ("wide", "narrow")
    grad_qkv, grad_proj = lax.psum((grad_qkv.astype(bf16), grad_proj.astype(bf16)), axes)
    grad_gains, grad_router, counts = lax.psum((grad_gains, grad_router[:, :experts], counts), axes)
    kept_counts = counts[0, :experts].astype(jnp.int32)
    dropped_counts = (counts[1, :experts] - counts[0, :experts]).astype(jnp.int32)
    return (
        mixed,
        grad_tokens,
        grad_gains[0],
        grad_qkv.astype(f32),
        grad_proj.astype(f32),
        grad_gains[1],
        grad_router,
        own[None, :D, :],
        own[None, D:, :].transpose(0, 2, 1),
        kept_counts,
        dropped_counts,
    )


def solution(mesh):
    both = ("wide", "narrow")
    placed = (
        P(both, None),
        P(both),
        P(both, None),
        P(both, None),
        P(),
        P(),
        P(),
        P(),
        P(),
        P("wide", None, "narrow"),
        P("wide", "narrow", None),
        P(both, None),
    )
    return jax.shard_map(
        per_device,
        mesh=mesh,
        in_specs=placed,
        out_specs=(
            P(both, None),
            P(both, None),
            P(),
            P(),
            P(),
            P(),
            P(),
            P("wide", None, "narrow"),
            P("wide", "narrow", None),
            P(),
            P(),
        ),
        check_vma=False,
    )
```

```python
import functools

import jax
import jax.numpy as jnp
from jax import lax
from jax.experimental import pallas as pl
from jax.experimental.pallas import tpu as pltpu
from jax.sharding import PartitionSpec as P

D = 512
HEADS = 8
HEAD = 64
PAIRS = HEADS // 2
PAIR = 2 * HEAD
TOP = 2
SEQ = 1024
TOK_DEV = 1024
LANES = 128
QB = 128
WINDOW = 432
TILE = 256
MIB = 1024 * 1024
MESH = pl.DeviceIdType.MESH

f32 = jnp.float32
bf16 = jnp.bfloat16
NT = (((1,), (1,)), ((), ()))
TN = (((0,), (0,)), ((), ()))


def dot(a, b):
    return jnp.dot(a, b, preferred_element_type=f32)


def dot_nt(a, b):
    return lax.dot_general(a, b, NT, preferred_element_type=f32)


def dot_tn(a, b):
    return lax.dot_general(a, b, TN, preferred_element_type=f32)


def iota(shape, dim):
    return lax.broadcasted_iota(jnp.int32, shape, dim)


def norm_parts(values_in):
    centered = values_in - jnp.mean(values_in, axis=-1, keepdims=True)
    variance = jnp.mean(centered * centered, axis=-1, keepdims=True)
    inverse = lax.rsqrt(variance + 1e-06)
    return (centered * inverse, inverse)


def norm_back(grad_normed, gain, normalized, inverse):
    grad_gain = jnp.sum(grad_normed * normalized, axis=0, keepdims=True)
    scaled = grad_normed * gain
    inner = scaled - jnp.mean(scaled, axis=-1, keepdims=True)
    inner = inner - normalized * jnp.mean(scaled * normalized, axis=-1, keepdims=True)
    return (inner * inverse, grad_gain)


def split2(values_in):
    high = values_in.astype(bf16)
    low = (values_in - high.astype(f32)).astype(bf16)
    return high, low


def row_to_col(row):
    n = row.shape[1]
    return jnp.transpose(jnp.broadcast_to(row, (LANES, n)))[:, :1]


def route_kernel(experts, capacity, picks, ranks, cot, slot_col, slot_row, counts, gz_send):
    tokens = ranks.shape[1]
    padded = gz_send.shape[1]
    rank_row = ranks[...].astype(f32)
    rank_col = row_to_col(rank_row)
    lane = iota((tokens, LANES), 1)
    pick0 = picks[:, 0:1]
    pick1 = picks[:, 1:2]
    hot = jnp.where(lane == jnp.where(lane < experts, pick0, pick1 + experts), 1.0, 0.0).astype(f32)
    before = (rank_row < rank_col).astype(f32).astype(bf16)
    earlier = dot(before, hot.astype(bf16))
    total = jnp.sum(hot, axis=0, keepdims=True)
    total = jnp.broadcast_to(total, (8, LANES))
    lane8 = iota((8, LANES), 1)
    first = jnp.where(lane8 < experts, total, 0.0)
    earlier = earlier + pltpu.roll(first, experts, axis=1)[:1]
    kept = (hot > 0.5) & (earlier < float(capacity))
    slots = jnp.where(kept, earlier, -1.0)
    slots = jnp.maximum(slots, pltpu.roll(slots, LANES - experts, axis=1))
    slots = jnp.where(lane < experts, slots, -1.0)
    slot_col[...] = slots
    slot_row[...] = jnp.transpose(slots)[:experts]
    kept_lane = jnp.sum(jnp.where(slots >= 0.0, 1.0, 0.0), axis=0, keepdims=True)
    both = total + pltpu.roll(total, LANES - experts, axis=1)
    both = jnp.where(lane8 < experts, both, 0.0)
    sub8 = iota((8, LANES), 0)
    counts[...] = jnp.where(sub8 == 0, kept_lane, jnp.where(sub8 == 1, both, 0.0))

    @pl.loop(0, experts)
    def _(e):
        chosen = iota((padded, tokens), 0).astype(f32) == slot_row[pl.ds(e, 1), :]
        gz_send[e] = dot(chosen.astype(f32).astype(bf16), cot[...]).astype(bf16)


def route(picks, ranks, cot, experts, capacity, padded):
    tokens = picks.shape[0]
    return pl.pallas_call(
        functools.partial(route_kernel, experts, capacity),
        out_shape=(
            jax.ShapeDtypeStruct((tokens, LANES), f32),
            jax.ShapeDtypeStruct((experts, tokens), f32),
            jax.ShapeDtypeStruct((8, LANES), f32),
            jax.ShapeDtypeStruct((experts, padded, D), bf16),
        ),
        compiler_params=pltpu.CompilerParams(vmem_limit_bytes=40 * MIB),
        cost_estimate=pl.CostEstimate(
            flops=2 * experts * padded * tokens * D, bytes_accessed=6 * MIB, transcendentals=0
        ),
        name="route",
    )(picks, ranks, cot)


def stack_heads(block):
    lane = iota(block.shape, 1)
    zero = jnp.zeros_like(block)
    return jnp.concatenate(
        [jnp.where(lane < HEAD, block, zero), jnp.where(lane < HEAD, zero, block)], axis=0
    )


def unstack_cols(stacked):
    row = iota((PAIR, QB), 0)
    picked = jnp.where(row < HEAD, stacked[:, :QB], stacked[:, QB:])
    return jnp.transpose(picked)


def window_bias(seg_col, seg_row, low, width, query):
    same = seg_col[pl.ds(low, width), :] == seg_row[:, pl.ds(query, QB)]
    half = jnp.where(same, 0.0, -1e30).astype(f32)
    return jnp.concatenate([half, half], axis=1)


def by_window(windows, block, body):
    low = windows[block]
    fits = windows[block + SEQ // QB]

    @pl.when(fits == 1)
    def _():
        body(pl.multiple_of(low, 16), WINDOW)

    @pl.when(fits != 1)
    def _():
        body(0, SEQ)


def forward_kernel(
    experts,
    windows,
    tok,
    seg,
    gain_attn,
    w_qkv,
    w_proj,
    gain_moe,
    w_router,
    slot_row,
    normed_attn,
    packed,
    context,
    lse,
    residual,
    normed_moe,
    gates,
    rows_send,
    seg_col,
    seg_row,
    router,
    gate_row,
    gate_slot,
):
    tokens = tok.shape[0]
    padded = rows_send.shape[1]
    seg_row[...] = seg[...].astype(f32)
    seg_col[...] = jnp.transpose(jnp.broadcast_to(seg_row[...], (LANES, tokens)))
    router[...] = jnp.zeros_like(router)
    router[:, :experts] = w_router[...]

    @pl.loop(0, tokens // TILE)
    def _(i):
        rows = pl.ds(pl.multiple_of(i * TILE, TILE), TILE)
        normal, unused = norm_parts(tok[rows, :].astype(f32))
        normed = (normal * gain_attn[...]).astype(bf16)
        normed_attn[rows, :] = normed
        packed[rows, :] = dot(normed, w_qkv[...]).astype(bf16)

    @pl.loop(0, tokens // QB)
    def _(block):
        query = pl.multiple_of(block * QB, QB)

        def body(low, width):
            bias = window_bias(seg_col, seg_row, low, width, query)
            for pair in range(PAIRS):
                cols = pair * PAIR
                q = stack_heads(packed[pl.ds(query, QB), cols : cols + PAIR]) * HEAD ** (-0.5)
                k = packed[pl.ds(low, width), D + cols : D + cols + PAIR]
                v = packed[pl.ds(low, width), 2 * D + cols : 2 * D + cols + PAIR]
                scores = dot_nt(k, q.astype(bf16)) + bias
                peak = jnp.max(scores, axis=0, keepdims=True)
                exponent = jnp.exp(scores - peak)
                totals = jnp.sum(exponent, axis=0, keepdims=True)
                probs_low = (exponent * (1.0 / totals)).astype(bf16)
                lse[pl.ds(block, 1), pair, :] = peak + jnp.log(totals)
                mixed = dot_tn(v, probs_low)
                context[pl.ds(query, QB), cols : cols + PAIR] = unstack_cols(mixed).astype(bf16)

        by_window(windows, block, body)

    @pl.loop(0, tokens // TILE)
    def _(i):
        rows = pl.ds(pl.multiple_of(i * TILE, TILE), TILE)
        rest = tok[rows, :].astype(f32) + dot(context[rows, :], w_proj[...])
        residual[rows, :] = rest
        normal, unused = norm_parts(rest)
        normed = (normal * gain_moe[...]).astype(bf16)
        normed_moe[rows, :] = normed
        logits = dot(normed, router[...])
        logits = jnp.where(iota(logits.shape, 1) < experts, logits, -1e30)
        exponent = jnp.exp(logits - jnp.max(logits, axis=1, keepdims=True))
        gates[rows, :] = exponent / jnp.sum(exponent, axis=1, keepdims=True)

    gate_row[...] = jnp.transpose(gates[...])[:experts]
    gate_slot[...] = jnp.zeros_like(gate_slot)

    @pl.loop(0, experts)
    def _(e):
        chosen = iota((padded, tokens), 0).astype(f32) == slot_row[pl.ds(e, 1), :]
        chosen = chosen.astype(f32).astype(bf16)
        rows_send[e] = dot(chosen, normed_moe[...]).astype(bf16)
        gate = gate_row[pl.ds(e, 1), :]
        high, middle = split2(gate)
        low = (gate - high.astype(f32) - middle.astype(f32)).astype(bf16)
        three = jnp.concatenate(
            [high.astype(f32), middle.astype(f32), low.astype(f32), jnp.zeros((5, tokens), f32)], axis=0
        )
        gate_slot[:, :padded] = dot_nt(three.astype(bf16), chosen)
        tail = rows_send[e, padded - 16 :, :].astype(f32)
        sub = iota(tail.shape, 0)
        for part in range(3):
            tail = jnp.where(sub == 13 + part, gate_slot[part : part + 1, :], tail)
        rows_send[e, padded - 16 :, :] = tail.astype(bf16)


def forward(windows, tok, seg, gain_attn, w_qkv, w_proj, gain_moe, w_router, slot_row, padded):
    tokens = tok.shape[0]
    experts = w_router.shape[1]
    vmem = pl.BlockSpec(memory_space=pltpu.VMEM)
    return pl.pallas_call(
        functools.partial(forward_kernel, experts),
        in_specs=[pl.BlockSpec(memory_space=pltpu.SMEM)] + [vmem] * 8,
        out_shape=(
            jax.ShapeDtypeStruct((tokens, D), bf16),
            jax.ShapeDtypeStruct((tokens, 3 * D), bf16),
            jax.ShapeDtypeStruct((tokens, D), bf16),
            jax.ShapeDtypeStruct((tokens // QB, PAIRS, 2 * QB), f32),
            jax.ShapeDtypeStruct((tokens, D), f32),
            jax.ShapeDtypeStruct((tokens, D), bf16),
            jax.ShapeDtypeStruct((tokens, LANES), f32),
            jax.ShapeDtypeStruct((experts, padded, D), bf16),
        ),
        scratch_shapes=[
            pltpu.VMEM((tokens, LANES), f32),
            pltpu.VMEM((1, tokens), f32),
            pltpu.VMEM((D, LANES), bf16),
            pltpu.VMEM((experts, tokens), f32),
            pltpu.VMEM((8, D), f32),
        ],
        compiler_params=pltpu.CompilerParams(vmem_limit_bytes=56 * MIB),
        cost_estimate=pl.CostEstimate(
            flops=8 * 1024 * MIB, bytes_accessed=16 * MIB, transcendentals=4 * MIB
        ),
        name="attention_forward",
    )(windows, tok, seg, gain_attn, w_qkv, w_proj, gain_moe, w_router, slot_row)


def gelu_parts(x):
    density = jnp.exp(-0.5 * (x * x))
    t = 1.0 / (1.0 + (0.3275911 * 2.0**-0.5) * jnp.abs(x))
    poly = 0.5 * 1.061405429
    for factor in (-1.453152027, 1.421413741, -0.284496736, 0.254829592):
        poly = poly * t + 0.5 * factor
    tail = poly * t * density
    phi = jnp.where(x >= 0.0, 1.0 - tail, tail)
    return phi, x * density * 0.3989422804014327


def shifted(index, by, size):
    return lax.rem(index + by, size)


def exchange(src, dst, send, recv, device):
    return pltpu.make_async_remote_copy(
        src_ref=src, dst_ref=dst, send_sem=send, recv_sem=recv, device_id=device, device_id_type=MESH
    )


def expert_kernel(capacity, joint, sources, shards, received, gz, *refs):
    if joint:
        weights, refs = refs[0], refs[1:]
    else:
        weights_in, weights_out, refs = refs[0], refs[1], refs[2:]
    returned, back, grads, rows, scaled, rows_t, gz_t, act, gpre, out_sum, back_sum, out_low, back_low = refs[:13]
    out_send, out_recv, back_send, back_recv, own_sem = refs[13:]
    padded = rows.shape[1]
    hidden = act.shape[2]
    me = lax.axis_index("wide")
    line = lax.axis_index("narrow")
    barrier = pltpu.get_barrier_semaphore()

    @pl.loop(1, sources)
    def _(j):
        pl.semaphore_signal(barrier, inc=1, device_id=(shifted(me, j, sources), line), device_id_type=MESH)

    def sends(j):
        to = (shifted(me, j, sources), line)
        return (
            exchange(out_low.at[to[0]], returned.at[me], out_send.at[j], out_recv.at[j], to),
            exchange(back_low.at[to[0]], back.at[me], back_send.at[j], back_recv.at[j], to),
        )

    def block(j):
        s = shifted(me, j, sources)
        rows[s] = received[s]
        tail = received[s, padded - 16 :, :].astype(f32)
        gate = tail[13:14] + tail[14:15] + tail[15:16]
        gate = jnp.transpose(jnp.broadcast_to(gate, (LANES, D)))[:padded, :1]
        live = iota((padded, 1), 0) < capacity
        scaled[s] = (jnp.where(live, gate, 0.0) * gz[s].astype(f32)).astype(bf16)
        live16 = iota((16, 1), 0) < 16 - (padded - capacity)
        rows[s, padded - 16 :, :] = jnp.where(live16, tail, 0.0).astype(bf16)
        for c in range(shards):
            w_in = weights[c, 0] if joint else weights_in[c]
            w_out = weights[c, 1] if joint else weights_out[c]
            pre = dot(rows[s], w_in)
            phi, slope = gelu_parts(pre)
            act_low = (pre * phi).astype(bf16)
            act[c, pl.ds(pl.multiple_of(s * padded, 16), padded), :] = act_low
            grad_pre = (dot_nt(scaled[s], w_out) * (phi + slope)).astype(bf16)
            gpre[c, pl.ds(pl.multiple_of(s * padded, 16), padded), :] = grad_pre
            result = dot(act_low, w_out)
            grad_rows = dot_nt(grad_pre, w_in)
            if c > 0:
                result = result + out_sum[...]
                grad_rows = grad_rows + back_sum[...]
            if c < shards - 1:
                out_sum[...] = result
                back_sum[...] = grad_rows
            else:
                out_low[s] = result.astype(bf16)
                back_low[s] = grad_rows.astype(bf16)

    @pl.loop(1, sources)
    def _(j):
        block(j)

        @pl.when(j == 1)
        def _():
            pl.semaphore_wait(barrier, sources - 1)

        for copy in sends(j):
            copy.start()

    block(0)
    keep = (
        pltpu.make_async_copy(out_low.at[me], returned.at[me], own_sem.at[0]),
        pltpu.make_async_copy(back_low.at[me], back.at[me], own_sem.at[1]),
    )
    for copy in keep:
        copy.start()
    for s in range(sources):
        rows_t[:, s * padded : (s + 1) * padded] = jnp.transpose(rows[s])
        gz_t[:, s * padded : (s + 1) * padded] = jnp.transpose(scaled[s])
    for c in range(shards):
        grads[c, :D, :] = dot(rows_t[...], gpre[c]).astype(bf16)
        grads[c, D:, :] = dot(gz_t[...], act[c]).astype(bf16)
    for copy in keep:
        copy.wait()

    @pl.loop(1, sources)
    def _(j):
        for copy in sends(j):
            copy.wait()


def experts_apply(rows, gz, weights, capacity):
    sources, padded, unused = rows.shape
    joint = len(weights) == 1
    shards = weights[0].shape[0]
    hidden = weights[0].shape[-1]
    total = sources * padded
    vmem = pl.BlockSpec(memory_space=pltpu.VMEM)
    anywhere = pl.BlockSpec(memory_space=pl.ANY)
    return pl.pallas_call(
        functools.partial(expert_kernel, capacity, joint, sources, shards),
        in_specs=[vmem] * (2 + len(weights)),
        out_specs=(anywhere, anywhere, vmem),
        out_shape=(
            jax.ShapeDtypeStruct(rows.shape, bf16),
            jax.ShapeDtypeStruct(rows.shape, bf16),
            jax.ShapeDtypeStruct((shards, 2 * D, hidden), bf16),
        ),
        scratch_shapes=[
            pltpu.VMEM(rows.shape, bf16),
            pltpu.VMEM(rows.shape, bf16),
            pltpu.VMEM((D, total), bf16),
            pltpu.VMEM((D, total), bf16),
            pltpu.VMEM((shards, total, hidden), bf16),
            pltpu.VMEM((shards, total, hidden), bf16),
            pltpu.VMEM((padded, D), f32),
            pltpu.VMEM((padded, D), f32),
            pltpu.VMEM(rows.shape, bf16),
            pltpu.VMEM(rows.shape, bf16),
            pltpu.SemaphoreType.DMA((sources,)),
            pltpu.SemaphoreType.DMA((sources,)),
            pltpu.SemaphoreType.DMA((sources,)),
            pltpu.SemaphoreType.DMA((sources,)),
            pltpu.SemaphoreType.DMA((2,)),
        ],
        compiler_params=pltpu.CompilerParams(
            vmem_limit_bytes=60 * MIB, collective_id=1, has_side_effects=True
        ),
        cost_estimate=pl.CostEstimate(
            flops=12 * total * D * hidden * shards, bytes_accessed=20 * MIB, transcendentals=0
        ),
        name="experts",
    )(rows, gz, *weights)


def backward_kernel(
    experts,
    windows,
    tok,
    seg,
    gain_attn,
    w_qkv,
    w_proj,
    gain_moe,
    w_router,
    slot_col,
    cot,
    normed_attn,
    packed,
    context,
    lse,
    residual,
    normed_moe,
    gates,
    returned,
    back,
    counts,
    mixed,
    grad_residual,
    grad_packed,
    grad_proj,
    small,
    seg_col,
    seg_row,
    router,
    grad_attn,
    grad_context,
    grad_logits,
    grad_k,
    grad_v,
):
    tokens = tok.shape[0]
    padded = returned.shape[1]
    seg_row[...] = seg[...].astype(f32)
    seg_col[...] = jnp.transpose(jnp.broadcast_to(seg_row[...], (LANES, tokens)))
    router[...] = jnp.zeros_like(router)
    router[:, :experts] = w_router[...]
    small[...] = jnp.zeros_like(small)
    small[2:4, :LANES] = counts[:2, :]

    @pl.loop(0, tokens // TILE)
    def _(i):
        rows = pl.ds(pl.multiple_of(i * TILE, TILE), TILE)
        grad_z = cot[rows, :].astype(f32)
        probs = gates[rows, :]
        slots = slot_col[rows, :]
        lane = iota((TILE, LANES), 1)
        rest = residual[rows, :]
        total = rest
        back_total = jnp.zeros((TILE, D), f32)
        grad_gates = jnp.zeros((TILE, LANES), f32)
        for e in range(experts):
            slot = slots[:, e : e + 1]
            chosen = (iota((TILE, padded), 1).astype(f32) == slot).astype(f32).astype(bf16)
            result = dot(chosen, returned[e])
            total = total + probs[:, e : e + 1] * result
            inner = jnp.sum(result * grad_z, axis=1, keepdims=True)
            grad_gates = grad_gates + jnp.where(lane == e, inner, 0.0)
            back_total = back_total + dot(chosen, back[e])
        mixed[rows, :] = total.astype(bf16)
        gate_inner = jnp.sum(probs * grad_gates, axis=1, keepdims=True)
        high, low = split2(probs * (grad_gates - gate_inner))
        grad_logits[rows, :LANES] = high
        grad_logits[rows, LANES:] = low
        grad_normed = back_total + dot_nt(high, router[...]) + dot_nt(low, router[...])
        normal, inverse = norm_parts(rest)
        grad_norm, grad_gain = norm_back(grad_normed, gain_moe[...], normal, inverse)
        small[1:2, :] += grad_gain
        grad_rest = grad_z + grad_norm
        grad_residual[rows, :] = grad_rest
        attn = grad_rest.astype(bf16)
        grad_attn[rows, :] = attn
        grad_context[rows, :] = dot_nt(attn, w_proj[...]).astype(bf16)

    both = dot_tn(normed_moe[...], grad_logits[...])
    both = jnp.transpose(both[:, :LANES] + both[:, LANES:])
    small[8:, :] = both[:experts]
    grad_proj[...] = dot_tn(context[...], grad_attn[...])
    grad_k[...] = jnp.zeros_like(grad_k)
    grad_v[...] = jnp.zeros_like(grad_v)

    @pl.loop(0, tokens // QB)
    def _(block):
        query = pl.multiple_of(block * QB, QB)

        def body(low, width):
            bias = window_bias(seg_col, seg_row, low, width, query)
            for pair in range(PAIRS):
                cols = pair * PAIR
                q = (stack_heads(packed[pl.ds(query, QB), cols : cols + PAIR]) * HEAD ** (-0.5)).astype(bf16)
                k = packed[pl.ds(low, width), D + cols : D + cols + PAIR]
                v = packed[pl.ds(low, width), 2 * D + cols : 2 * D + cols + PAIR]
                grad_c = stack_heads(grad_context[pl.ds(query, QB), cols : cols + PAIR])
                probs = jnp.exp(dot_nt(k, q) + bias - lse[pl.ds(block, 1), pair, :])
                grad_probs = dot_nt(v, grad_c)
                grad_v[pl.ds(low, width), cols : cols + PAIR] += dot(probs.astype(bf16), grad_c)
                weighted = probs * grad_probs
                inner = jnp.sum(weighted, axis=0, keepdims=True)
                grad_scores = (weighted - probs * inner).astype(bf16)
                grad_k[pl.ds(low, width), cols : cols + PAIR] += dot(grad_scores, q)
                grad_q = unstack_cols(dot_tn(k, grad_scores)) * HEAD ** (-0.5)
                grad_packed[pl.ds(query, QB), cols : cols + PAIR] = grad_q.astype(bf16)

        by_window(windows, block, body)

    @pl.loop(0, tokens // TILE)
    def _(i):
        rows = pl.ds(pl.multiple_of(i * TILE, TILE), TILE)
        grad_packed[rows, D : 2 * D] = grad_k[rows, :].astype(bf16)
        grad_packed[rows, 2 * D :] = grad_v[rows, :].astype(bf16)


def backward(experts, windows, *operands):
    tok = operands[0]
    tokens = tok.shape[0]
    vmem = pl.BlockSpec(memory_space=pltpu.VMEM)
    return pl.pallas_call(
        functools.partial(backward_kernel, experts),
        in_specs=[pl.BlockSpec(memory_space=pltpu.SMEM)] + [vmem] * len(operands),
        out_shape=(
            jax.ShapeDtypeStruct((tokens, D), bf16),
            jax.ShapeDtypeStruct((tokens, D), f32),
            jax.ShapeDtypeStruct((tokens, 3 * D), bf16),
            jax.ShapeDtypeStruct((D, D), f32),
            jax.ShapeDtypeStruct((8 + experts, D), f32),
        ),
        scratch_shapes=[
            pltpu.VMEM((tokens, LANES), f32),
            pltpu.VMEM((1, tokens), f32),
            pltpu.VMEM((D, LANES), bf16),
            pltpu.VMEM((tokens, D), bf16),
            pltpu.VMEM((tokens, D), bf16),
            pltpu.VMEM((tokens, 2 * LANES), bf16),
            pltpu.VMEM((tokens, D), f32),
            pltpu.VMEM((tokens, D), f32),
        ],
        compiler_params=pltpu.CompilerParams(vmem_limit_bytes=60 * MIB),
        cost_estimate=pl.CostEstimate(
            flops=30 * 1024 * MIB, bytes_accessed=30 * MIB, transcendentals=4 * MIB
        ),
        name="attention_backward",
    )(windows, *operands)


def shared_kernel(
    chips,
    planes,
    normed_attn,
    grad_packed,
    grad_proj,
    partial,
    tok,
    grad_residual,
    gain_attn,
    w_qkv,
    summed,
    small,
    grad_tokens,
    normed_t,
    half,
    core_out,
    core_in,
    chip_out,
    chip_in,
    plane_own,
    plane_out,
    plane_in,
    small_own,
    small_core,
    small_chip,
    small_plane,
    core_sem,
    chip_sem,
    plane_sem,
    plane_sem2,
    chip_sem2,
    core_sem2,
    small_sem,
    small_chip_sem,
    small_plane_sem,
):
    tokens = tok.shape[0]
    columns = summed.shape[2]
    part = D // columns if columns < D else 1
    wide = lax.axis_index("wide")
    plane = lax.axis_index("narrow")
    core = lax.rem(wide, 2)
    chip = wide // 2
    share = D // (2 * chips)
    partner = (chip * 2 + 1 - core, plane)
    mine = pl.ds(pl.multiple_of(core * (D // 2), D // 2), D // 2)
    other = pl.ds(pl.multiple_of((1 - core) * (D // 2), D // 2), D // 2)
    chunk = pl.ds(pl.multiple_of(core * (D // 2) + chip * share, share), share)
    own_chunk = pl.ds(pl.multiple_of(chip * share, share), share)

    def chip_at(j):
        to = shifted(chip, j, chips)
        return to, (to * 2 + core, plane)

    def plane_at(j):
        to = shifted(plane, j, planes)
        return to, (wide, to)

    barrier = pltpu.get_barrier_semaphore()
    pl.semaphore_signal(barrier, inc=1, device_id=partner, device_id_type=MESH)

    @pl.loop(1, chips)
    def _(j):
        pl.semaphore_signal(barrier, inc=1, device_id=chip_at(j)[1], device_id_type=MESH)

    @pl.loop(1, planes)
    def _(j):
        pl.semaphore_signal(barrier, inc=1, device_id=plane_at(j)[1], device_id_type=MESH)

    def core_copy(n):
        return exchange(core_out.at[n], core_in.at[n], core_sem.at[0, n], core_sem.at[1, n], partner)

    def chip_copy(n, j):
        to, device = chip_at(j)
        rows = pl.ds(pl.multiple_of(to * share, share), share)
        return exchange(
            chip_out.at[n, rows], chip_in.at[j, n], chip_sem.at[0, j, n], chip_sem.at[1, j, n], device
        )

    def plane_copy(j):
        to, device = plane_at(j)
        return exchange(plane_out.at[to], plane_in.at[j], plane_sem.at[0, j], plane_sem.at[1, j], device)

    def plane_back(j):
        spot = summed.at[plane, chunk]
        return exchange(spot, spot, plane_sem2.at[0, j], plane_sem2.at[1, j], plane_at(j)[1])

    def column_of(i):
        return shifted(plane, planes - i, planes)

    def chip_back(i, j):
        spot = summed.at[column_of(i), chunk]
        return exchange(spot, spot, chip_sem2.at[0, j, i], chip_sem2.at[1, j, i], chip_at(j)[1])

    def core_back(i):
        spot = summed.at[column_of(i), mine]
        return exchange(spot, spot, core_sem2.at[0, i], core_sem2.at[1, i], partner)

    def small_core_copy():
        return exchange(small_own, small_core, small_sem.at[0], small_sem.at[1], partner)

    def small_chip_copy(j):
        return exchange(
            small_chip.at[chip],
            small_chip.at[chip],
            small_chip_sem.at[0, j],
            small_chip_sem.at[1, j],
            chip_at(j)[1],
        )

    def small_plane_copy(j):
        return exchange(
            small_plane.at[plane],
            small_plane.at[plane],
            small_plane_sem.at[0, j],
            small_plane_sem.at[1, j],
            plane_at(j)[1],
        )

    order = [(3, p) for p in range(part)] + [(t, p) for t in range(3) for p in range(part)]
    normed_t[...] = jnp.transpose(normed_attn[...])
    for t, p in order:
        n = t * part + p
        if t == 3:
            half[n] = grad_proj[mine, p * columns : (p + 1) * columns]
            core_out[n] = grad_proj[other, p * columns : (p + 1) * columns].astype(bf16)
        else:
            right = grad_packed[:, n * columns : (n + 1) * columns]
            core_out[n] = dot(normed_t[other, :], right).astype(bf16)
        if (t, p) == order[0]:
            pl.semaphore_wait(barrier, chips + planes - 1)
        core_copy(n).start()
        if t < 3:
            half[n] = dot(normed_t[mine, :], right)
    for t, p in order:
        n = t * part + p
        core_copy(n).wait_recv()
        half[n] = half[n] + core_in[n].astype(f32)
        chip_out[n] = half[n].astype(bf16)

        @pl.loop(1, chips)
        def _(j):
            chip_copy(n, j).start()

    small_own[...] = partial[...]

    @pl.loop(0, tokens // TILE)
    def _(i):
        rows = pl.ds(pl.multiple_of(i * TILE, TILE), TILE)
        grad_normed = dot_nt(grad_packed[rows, :], w_qkv[...])
        normal, inverse = norm_parts(tok[rows, :].astype(f32))
        grad_norm, grad_gain = norm_back(grad_normed, gain_attn[...], normal, inverse)
        small_own[0:1, :] += grad_gain
        grad_tokens[rows, :] = grad_residual[rows, :] + grad_norm

    small_core_copy().start()
    for t, p in order:
        n = t * part + p
        total = half[n, own_chunk, :]
        for j in range(1, chips):
            chip_copy(n, j).wait_recv()
            total = total + chip_in[j, n].astype(f32)
        plane_out[n] = total.astype(bf16)

        @pl.when(n == plane)
        def _():
            plane_own[...] = total

        @pl.when(n != plane)
        def _():
            plane_copy(lax.rem(n + planes - plane, planes)).start()

    small_core_copy().wait_recv()
    small_chip[chip] = small_own[...] + small_core[...]

    @pl.loop(1, chips)
    def _(j):
        small_chip_copy(j).start()

    total = plane_own[...]
    for j in range(1, planes):
        plane_copy(j).wait_recv()
        total = total + plane_in[j].astype(f32)
    summed[plane, chunk, :] = total.astype(bf16)

    @pl.loop(1, planes)
    def _(j):
        plane_back(j).start()

    @pl.loop(1, chips)
    def _(j):
        small_chip_copy(j).wait_recv()

    total = small_chip[0]
    for c in range(1, chips):
        total = total + small_chip[c]
    small_plane[plane] = total

    @pl.loop(1, planes)
    def _(j):
        small_plane_copy(j).start()

    for i in range(planes):
        if i > 0:
            plane_back(i).wait_recv()

        @pl.loop(1, chips)
        def _(j):
            chip_back(i, j).start()

    for i in range(planes):

        @pl.loop(1, chips)
        def _(j):
            chip_back(i, j).wait_recv()

        core_back(i).start()

    @pl.loop(1, planes)
    def _(j):
        small_plane_copy(j).wait_recv()

    total = small_plane[0]
    for c in range(1, planes):
        total = total + small_plane[c]
    small[...] = total
    for i in range(planes):
        core_back(i).wait()
        core_copy(i).wait_send()

        @pl.loop(1, chips)
        def _(j):
            chip_back(i, j).wait_send()
            chip_copy(i, j).wait_send()

    @pl.loop(1, planes)
    def _(j):
        plane_back(j).wait_send()
        plane_copy(j).wait_send()
        small_plane_copy(j).wait_send()

    @pl.loop(1, chips)
    def _(j):
        small_chip_copy(j).wait_send()

    small_core_copy().wait_send()


def shared_gradients(*operands):
    normed_attn, unused, unused, partial = operands[:4]
    tokens = normed_attn.shape[0]
    chips = lax.axis_size("wide") // 2
    planes = lax.axis_size("narrow")
    columns = 4 * D // planes
    share = D // (2 * chips)
    rows = partial.shape[0]
    dma = pltpu.SemaphoreType.DMA
    return pl.pallas_call(
        functools.partial(shared_kernel, chips, planes),
        out_shape=(
            jax.ShapeDtypeStruct((planes, D, columns), bf16),
            jax.ShapeDtypeStruct((rows, D), f32),
            jax.ShapeDtypeStruct((tokens, D), f32),
        ),
        scratch_shapes=[
            pltpu.VMEM((D, tokens), bf16),
            pltpu.VMEM((planes, D // 2, columns), f32),
            pltpu.VMEM((planes, D // 2, columns), bf16),
            pltpu.VMEM((planes, D // 2, columns), bf16),
            pltpu.VMEM((planes, D // 2, columns), bf16),
            pltpu.VMEM((chips, planes, share, columns), bf16),
            pltpu.VMEM((share, columns), f32),
            pltpu.VMEM((planes, share, columns), bf16),
            pltpu.VMEM((planes, share, columns), bf16),
            pltpu.VMEM((rows, D), f32),
            pltpu.VMEM((rows, D), f32),
            pltpu.VMEM((chips, rows, D), f32),
            pltpu.VMEM((planes, rows, D), f32),
            dma((2, planes)),
            dma((2, chips, planes)),
            dma((2, planes)),
            dma((2, planes)),
            dma((2, chips, planes)),
            dma((2, planes)),
            dma((2,)),
            dma((2, chips)),
            dma((2, planes)),
        ],
        compiler_params=pltpu.CompilerParams(
            vmem_limit_bytes=50 * MIB, collective_id=2, has_side_effects=True
        ),
        cost_estimate=pl.CostEstimate(
            flops=12 * tokens * D * D, bytes_accessed=16 * MIB, transcendentals=0
        ),
        name="shared_gradients",
    )(*operands)


def per_device(
    tokens,
    segment_ids,
    expert_picks,
    priority_ranks,
    gain_attn,
    w_qkv,
    w_proj,
    gain_moe,
    w_router,
    w_in,
    w_out,
    cotangent,
):
    experts = w_router.shape[1]
    capacity = (21 * TOP * TOK_DEV + 20 * experts - 1) // (20 * experts)
    padded = (capacity + 3 + 15) // 16 * 16
    gain_attn = gain_attn.reshape(1, D)
    gain_moe = gain_moe.reshape(1, D)
    seg = segment_ids.reshape(1, SEQ)
    first = jnp.sum((segment_ids[None, :] < segment_ids[0::QB, None]).astype(jnp.int32), axis=1)
    after = jnp.sum((segment_ids[None, :] <= segment_ids[QB - 1 :: QB, None]).astype(jnp.int32), axis=1)
    low = jnp.minimum(first // 16 * 16, SEQ - WINDOW)
    fits = (after - low <= WINDOW).astype(jnp.int32)
    windows = jnp.concatenate([low, fits])

    slot_col, slot_row, counts, gz_send = route(
        expert_picks, priority_ranks, cotangent, experts, capacity, padded
    )
    gz = lax.all_to_all(gz_send, "wide", split_axis=0, concat_axis=0, tiled=True)
    hidden = w_in.shape[2]
    if hidden == D:
        weights = (lax.all_gather(jnp.concatenate([w_in, w_out], axis=0), "narrow", axis=0),)
    else:
        weights = (lax.all_gather(w_in[0], "narrow", axis=0), lax.all_gather(w_out[0], "narrow", axis=0))
    normed_attn, packed, context, lse, residual, normed_moe, gates, rows_send = forward(
        windows, tokens, seg, gain_attn, w_qkv, w_proj, gain_moe, w_router, slot_row, padded
    )
    rows = lax.all_to_all(rows_send, "wide", split_axis=0, concat_axis=0, tiled=True)
    returned, back, grads = experts_apply(rows, gz, weights, capacity)
    own = lax.psum_scatter(grads, "narrow", scatter_dimension=0, tiled=False).astype(f32)
    mixed, grad_residual, grad_packed, grad_proj, partial = backward(
        experts,
        windows,
        tokens,
        seg,
        gain_attn,
        w_qkv,
        w_proj,
        gain_moe,
        w_router,
        slot_col,
        cotangent,
        normed_attn,
        packed,
        context,
        lse,
        residual,
        normed_moe,
        gates,
        returned,
        back,
        counts,
    )
    summed, small, grad_tokens = shared_gradients(
        normed_attn, grad_packed, grad_proj, partial, tokens, grad_residual, gain_attn, w_qkv
    )
    summed = summed.transpose(1, 0, 2).reshape(D, 4 * D).astype(f32)
    return (
        mixed,
        grad_tokens,
        small[0],
        summed[:, : 3 * D],
        summed[:, 3 * D :],
        small[1],
        small[8:].T,
        own[None, :D, :],
        own[None, D:, :].transpose(0, 2, 1),
        small[2, :experts].astype(jnp.int32),
        (small[3, :experts] - small[2, :experts]).astype(jnp.int32),
    )


def solution(mesh):
    both = ("wide", "narrow")
    placed = (
        P(both, None),
        P(both),
        P(both, None),
        P(both, None),
        P(),
        P(),
        P(),
        P(),
        P(),
        P("wide", None, "narrow"),
        P("wide", "narrow", None),
        P(both, None),
    )
    return jax.shard_map(
        per_device,
        mesh=mesh,
        in_specs=placed,
        out_specs=(
            P(both, None),
            P(both, None),
            P(),
            P(),
            P(),
            P(),
            P(),
            P("wide", None, "narrow"),
            P("wide", "narrow", None),
            P(),
            P(),
        ),
        check_vma=False,
    )
```

```python
import functools

import jax
import jax.numpy as jnp
from jax import lax
from jax.experimental import pallas as pl
from jax.experimental.pallas import tpu as pltpu
from jax.sharding import PartitionSpec as P

D = 512
HEADS = 8
HEAD = 64
PAIRS = HEADS // 2
PAIR = 2 * HEAD
TOP = 2
SEQ = 1024
TOK_DEV = 1024
LANES = 128
QB = 128
WINDOW = 432
TILE = 256
MIB = 1024 * 1024
MESH = pl.DeviceIdType.MESH

f32 = jnp.float32
bf16 = jnp.bfloat16
NT = (((1,), (1,)), ((), ()))
TN = (((0,), (0,)), ((), ()))


def dot(a, b):
    return jnp.dot(a, b, preferred_element_type=f32)


def dot_nt(a, b):
    return lax.dot_general(a, b, NT, preferred_element_type=f32)


def dot_tn(a, b):
    return lax.dot_general(a, b, TN, preferred_element_type=f32)


def iota(shape, dim):
    return lax.broadcasted_iota(jnp.int32, shape, dim)


def norm_parts(values_in):
    centered = values_in - jnp.mean(values_in, axis=-1, keepdims=True)
    variance = jnp.mean(centered * centered, axis=-1, keepdims=True)
    inverse = lax.rsqrt(variance + 1e-06)
    return (centered * inverse, inverse)


def norm_back(grad_normed, gain, normalized, inverse):
    grad_gain = jnp.sum(grad_normed * normalized, axis=0, keepdims=True)
    scaled = grad_normed * gain
    inner = scaled - jnp.mean(scaled, axis=-1, keepdims=True)
    inner = inner - normalized * jnp.mean(scaled * normalized, axis=-1, keepdims=True)
    return (inner * inverse, grad_gain)


def split2(values_in):
    high = values_in.astype(bf16)
    low = (values_in - high.astype(f32)).astype(bf16)
    return high, low


def row_to_col(row):
    n = row.shape[1]
    return jnp.transpose(jnp.broadcast_to(row, (LANES, n)))[:, :1]


def route_kernel(experts, capacity, picks, ranks, cot, slot_col, slot_row, counts, gz_send):
    tokens = ranks.shape[1]
    padded = gz_send.shape[1]
    rank_row = ranks[...].astype(f32)
    rank_col = row_to_col(rank_row)
    lane = iota((tokens, LANES), 1)
    pick0 = picks[:, 0:1]
    pick1 = picks[:, 1:2]
    hot = jnp.where(lane == jnp.where(lane < experts, pick0, pick1 + experts), 1.0, 0.0).astype(f32)
    before = (rank_row < rank_col).astype(f32).astype(bf16)
    earlier = dot(before, hot.astype(bf16))
    total = jnp.sum(hot, axis=0, keepdims=True)
    total = jnp.broadcast_to(total, (8, LANES))
    lane8 = iota((8, LANES), 1)
    first = jnp.where(lane8 < experts, total, 0.0)
    earlier = earlier + pltpu.roll(first, experts, axis=1)[:1]
    kept = (hot > 0.5) & (earlier < float(capacity))
    slots = jnp.where(kept, earlier, -1.0)
    slot_col[...] = slots
    slots = jnp.maximum(slots, pltpu.roll(slots, LANES - experts, axis=1))
    slots = jnp.where(lane < experts, slots, -1.0)
    slot_row[...] = jnp.transpose(slots)[:experts]
    kept_lane = jnp.sum(jnp.where(slots >= 0.0, 1.0, 0.0), axis=0, keepdims=True)
    both = total + pltpu.roll(total, LANES - experts, axis=1)
    both = jnp.where(lane8 < experts, both, 0.0)
    sub8 = iota((8, LANES), 0)
    counts[...] = jnp.where(sub8 == 0, kept_lane, jnp.where(sub8 == 1, both, 0.0))

    @pl.loop(0, experts)
    def _(e):
        chosen = iota((padded, tokens), 0).astype(f32) == slot_row[pl.ds(e, 1), :]
        gz_send[e] = dot(chosen.astype(f32).astype(bf16), cot[...]).astype(bf16)


def route(picks, ranks, cot, experts, capacity, padded):
    tokens = picks.shape[0]
    return pl.pallas_call(
        functools.partial(route_kernel, experts, capacity),
        out_shape=(
            jax.ShapeDtypeStruct((tokens, LANES), f32),
            jax.ShapeDtypeStruct((experts, tokens), f32),
            jax.ShapeDtypeStruct((8, LANES), f32),
            jax.ShapeDtypeStruct((experts, padded, D), bf16),
        ),
        compiler_params=pltpu.CompilerParams(vmem_limit_bytes=40 * MIB),
        cost_estimate=pl.CostEstimate(
            flops=2 * experts * padded * tokens * D, bytes_accessed=6 * MIB, transcendentals=0
        ),
        name="route",
    )(picks, ranks, cot)


def stack_heads(block):
    lane = iota(block.shape, 1)
    zero = jnp.zeros_like(block)
    return jnp.concatenate(
        [jnp.where(lane < HEAD, block, zero), jnp.where(lane < HEAD, zero, block)], axis=0
    )


def unstack_cols(stacked):
    row = iota((PAIR, QB), 0)
    picked = jnp.where(row < HEAD, stacked[:, :QB], stacked[:, QB:])
    return jnp.transpose(picked)


def window_bias(seg_col, seg_row, low, width, query):
    same = seg_col[pl.ds(low, width), :] == seg_row[:, pl.ds(query, QB)]
    half = jnp.where(same, 0.0, -1e30).astype(f32)
    return jnp.concatenate([half, half], axis=1)


def by_window(windows, block, body):
    low = windows[block]
    fits = windows[block + SEQ // QB]

    @pl.when(fits == 1)
    def _():
        body(pl.multiple_of(low, 16), WINDOW)

    @pl.when(fits != 1)
    def _():
        body(0, SEQ)


def forward_kernel(
    experts,
    windows,
    tok,
    seg,
    gain_attn,
    w_qkv,
    w_proj,
    gain_moe,
    w_router,
    normed_attn_out,
    packed_out,
    context_out,
    lse,
    residual_out,
    normed_moe_out,
    gates_out,
    gate_row,
    normed_attn,
    packed,
    context,
    residual,
    normed_moe,
    gates,
    seg_col,
    seg_row,
    router,
    sems,
):
    writes = [
        pltpu.make_async_copy(source, target, sems.at[i])
        for i, (source, target) in enumerate(
            (
                (normed_attn, normed_attn_out),
                (packed, packed_out),
                (context, context_out),
                (residual, residual_out),
                (normed_moe, normed_moe_out),
                (gates, gates_out),
            )
        )
    ]
    tokens = tok.shape[0]
    seg_row[...] = seg[...].astype(f32)
    seg_col[...] = jnp.transpose(jnp.broadcast_to(seg_row[...], (LANES, tokens)))
    router[...] = jnp.zeros_like(router)
    router[:, :experts] = w_router[...]

    @pl.loop(0, tokens // TILE)
    def _(i):
        rows = pl.ds(pl.multiple_of(i * TILE, TILE), TILE)
        normal, unused = norm_parts(tok[rows, :].astype(f32))
        normed = (normal * gain_attn[...]).astype(bf16)
        normed_attn[rows, :] = normed
        packed[rows, :] = dot(normed, w_qkv[...]).astype(bf16)

    writes[0].start()
    writes[1].start()

    @pl.loop(0, tokens // QB)
    def _(block):
        query = pl.multiple_of(block * QB, QB)

        def body(low, width):
            bias = window_bias(seg_col, seg_row, low, width, query)
            spans = [slice(pair * PAIR, (pair + 1) * PAIR) for pair in range(PAIRS)]
            scores = []
            for span in spans:
                q = stack_heads(packed[pl.ds(query, QB), span]) * HEAD ** (-0.5)
                k = packed[pl.ds(low, width), D + span.start : D + span.stop]
                scores.append(dot_nt(k, q.astype(bf16)) + bias)
            peaks = [jnp.max(score, axis=0, keepdims=True) for score in scores]
            exponents = [jnp.exp(score - peak) for score, peak in zip(scores, peaks)]
            totals = [jnp.sum(exponent, axis=0, keepdims=True) for exponent in exponents]
            probs = [(exponent * (1.0 / total)).astype(bf16) for exponent, total in zip(exponents, totals)]
            for pair, span in enumerate(spans):
                lse[pl.ds(block, 1), pair, :] = peaks[pair] + jnp.log(totals[pair])
                v = packed[pl.ds(low, width), 2 * D + span.start : 2 * D + span.stop]
                mixed = dot_tn(v, probs[pair])
                context[pl.ds(query, QB), span] = unstack_cols(mixed).astype(bf16)

        by_window(windows, block, body)

    writes[2].start()

    @pl.loop(0, tokens // TILE)
    def _(i):
        rows = pl.ds(pl.multiple_of(i * TILE, TILE), TILE)
        rest = tok[rows, :].astype(f32) + dot(context[rows, :], w_proj[...])
        residual[rows, :] = rest
        normal, unused = norm_parts(rest)
        normed = (normal * gain_moe[...]).astype(bf16)
        normed_moe[rows, :] = normed
        logits = dot(normed, router[...])
        logits = jnp.where(iota(logits.shape, 1) < experts, logits, -1e30)
        exponent = jnp.exp(logits - jnp.max(logits, axis=1, keepdims=True))
        gates[rows, :] = exponent / jnp.sum(exponent, axis=1, keepdims=True)

    for write in writes[3:]:
        write.start()
    gate_row[...] = jnp.transpose(gates[...])[:experts]
    for write in writes:
        write.wait()


def forward(windows, tok, seg, gain_attn, w_qkv, w_proj, gain_moe, w_router):
    tokens = tok.shape[0]
    experts = w_router.shape[1]
    vmem = pl.BlockSpec(memory_space=pltpu.VMEM)
    anywhere = pl.BlockSpec(memory_space=pl.ANY)
    return pl.pallas_call(
        functools.partial(forward_kernel, experts),
        in_specs=[pl.BlockSpec(memory_space=pltpu.SMEM)] + [vmem] * 7,
        out_specs=[anywhere] * 3 + [vmem] + [anywhere] * 3 + [vmem],
        out_shape=(
            jax.ShapeDtypeStruct((tokens, D), bf16),
            jax.ShapeDtypeStruct((tokens, 3 * D), bf16),
            jax.ShapeDtypeStruct((tokens, D), bf16),
            jax.ShapeDtypeStruct((tokens // QB, PAIRS, 2 * QB), f32),
            jax.ShapeDtypeStruct((tokens, D), f32),
            jax.ShapeDtypeStruct((tokens, D), bf16),
            jax.ShapeDtypeStruct((tokens, LANES), f32),
            jax.ShapeDtypeStruct((experts, tokens), f32),
        ),
        scratch_shapes=[
            pltpu.VMEM((tokens, D), bf16),
            pltpu.VMEM((tokens, 3 * D), bf16),
            pltpu.VMEM((tokens, D), bf16),
            pltpu.VMEM((tokens, D), f32),
            pltpu.VMEM((tokens, D), bf16),
            pltpu.VMEM((tokens, LANES), f32),
            pltpu.VMEM((tokens, LANES), f32),
            pltpu.VMEM((1, tokens), f32),
            pltpu.VMEM((D, LANES), bf16),
            pltpu.SemaphoreType.DMA((6,)),
        ],
        compiler_params=pltpu.CompilerParams(vmem_limit_bytes=56 * MIB),
        cost_estimate=pl.CostEstimate(
            flops=8 * 1024 * MIB, bytes_accessed=16 * MIB, transcendentals=4 * MIB
        ),
        name="attention_forward",
    )(windows, tok, seg, gain_attn, w_qkv, w_proj, gain_moe, w_router)


def gelu_parts(x):
    density = jnp.exp(-0.5 * (x * x))
    return 0.5 + 0.5 * lax.erf(x * 2.0**-0.5), x * density * 0.3989422804014327


def shifted(index, by, size):
    return lax.rem(index + by, size)


def paired(index, by, size):
    total = 0
    bit = 1
    while bit < size:
        total = total + bit * lax.rem(index // bit + by // bit, 2)
        bit *= 2
    return total


def exchange(src, dst, send, recv, device):
    return pltpu.make_async_remote_copy(
        src_ref=src, dst_ref=dst, send_sem=send, recv_sem=recv, device_id=device, device_id_type=MESH
    )


def greet(barrier, sources):
    me = lax.axis_index("wide")
    line = lax.axis_index("narrow")

    @pl.loop(1, sources)
    def _(j):
        pl.semaphore_signal(barrier, inc=1, device_id=(paired(me, j, sources), line), device_id_type=MESH)


def dispatch_kernel(
    shards, slot_row, gate_row, normed_moe, first, received, weights, rows_send, gate_slot, send, recv, own_sem, ring_sem
):
    experts, padded, unused = rows_send.shape
    tokens = normed_moe.shape[0]
    me = lax.axis_index("wide")
    line = lax.axis_index("narrow")
    barrier = pltpu.get_barrier_semaphore()
    greet(barrier, experts)
    right = (me, shifted(line, 1, shards))
    left = (me, shifted(line, shards - 1, shards))
    for near in (left, right):
        pl.semaphore_signal(barrier, inc=1, device_id=near, device_id_type=MESH)
    gate_slot[...] = jnp.zeros_like(gate_slot)

    def ring(k):
        source = first if k == 0 else weights.at[k - 1]
        return exchange(source, weights.at[k], ring_sem.at[0, k], ring_sem.at[1, k], right)

    keep = pltpu.make_async_copy(rows_send.at[me], received.at[me], own_sem)

    def move(j):
        to = paired(me, j, experts)
        return exchange(rows_send.at[to], received.at[me], send.at[j], recv.at[j], (to, line))

    @pl.loop(0, experts)
    def _(i):
        j = paired(i, experts - 2, experts)
        e = paired(me, j, experts)
        chosen = iota((padded, tokens), 0).astype(f32) == slot_row[pl.ds(e, 1), :]
        chosen = chosen.astype(f32).astype(bf16)
        rows_send[e] = dot(chosen, normed_moe[...]).astype(bf16)
        gate = gate_row[pl.ds(e, 1), :]
        high, middle = split2(gate)
        low = (gate - high.astype(f32) - middle.astype(f32)).astype(bf16)
        three = jnp.concatenate(
            [high.astype(f32), middle.astype(f32), low.astype(f32), jnp.zeros((5, tokens), f32)], axis=0
        )
        gate_slot[:, :padded] = dot_nt(three.astype(bf16), chosen)
        tail = rows_send[e, padded - 16 :, :].astype(f32)
        sub = iota(tail.shape, 0)
        for part in range(3):
            tail = jnp.where(sub == 13 + part, gate_slot[part : part + 1, :], tail)
        rows_send[e, padded - 16 :, :] = tail.astype(bf16)

        @pl.when(i == 0)
        def _():
            pl.semaphore_wait(barrier, experts + 1)
            ring(0).start()

        @pl.when(j != 0)
        def _():
            move(j).start()

        @pl.when(j == 0)
        def _():
            keep.start()

    keep.wait()
    for k in range(shards - 2):
        ring(k).wait()
        if k + 1 < shards - 2:
            ring(k + 1).start()

    @pl.loop(1, experts)
    def _(j):
        move(j).wait()


def dispatch(slot_row, gate_row, normed_moe, first, shards, padded):
    experts, tokens = slot_row.shape
    vmem = pl.BlockSpec(memory_space=pltpu.VMEM)
    anywhere = pl.BlockSpec(memory_space=pl.ANY)
    dma = pltpu.SemaphoreType.DMA
    return pl.pallas_call(
        functools.partial(dispatch_kernel, shards),
        in_specs=[vmem, vmem, vmem, anywhere],
        out_specs=(anywhere, anywhere),
        out_shape=(
            jax.ShapeDtypeStruct((experts, padded, D), bf16),
            jax.ShapeDtypeStruct((shards - 2,) + first.shape, bf16),
        ),
        scratch_shapes=[
            pltpu.VMEM((experts, padded, D), bf16),
            pltpu.VMEM((8, D), f32),
            dma((experts,)),
            dma((experts,)),
            dma,
            dma((2, shards - 2)),
        ],
        compiler_params=pltpu.CompilerParams(
            vmem_limit_bytes=40 * MIB, collective_id=3, has_side_effects=True
        ),
        cost_estimate=pl.CostEstimate(
            flops=20 * experts * padded * tokens * D, bytes_accessed=6 * MIB, transcendentals=0
        ),
        name="dispatch",
    )(slot_row, gate_row, normed_moe, first)


def expert_kernel(capacity, sources, shards, received, gz, gathered_in, out_own, out_first, out_rest, *refs):
    returned, back, ring, grads = refs[:4]
    rows, scaled, rows_t, gz_t, act, gpre, out_sum, back_sum, out_low, back_low, ring_out, ring_in = refs[4:16]
    out_send, out_recv, back_send, back_recv, own_sem, ring_sem = refs[16:]
    padded = rows.shape[1]
    hidden = act.shape[2]
    me = lax.axis_index("wide")
    line = lax.axis_index("narrow")
    right = (me, shifted(line, 1, shards))
    left = (me, shifted(line, shards - 1, shards))
    barrier = pltpu.get_barrier_semaphore()
    greet(barrier, sources)
    for near in (left, right):
        pl.semaphore_signal(barrier, inc=1, device_id=near, device_id_type=MESH)

    def sends(j):
        to = (paired(me, j, sources), line)
        return (
            exchange(out_low.at[to[0]], returned.at[me], out_send.at[j], out_recv.at[j], to),
            exchange(back_low.at[to[0]], back.at[me], back_send.at[j], back_recv.at[j], to),
        )

    def block(j):
        s = paired(me, j, sources)
        rows[s] = received[s]
        tail = received[s, padded - 16 :, :].astype(f32)
        gate = tail[13:14] + tail[14:15] + tail[15:16]
        gate = jnp.transpose(jnp.broadcast_to(gate, (LANES, D)))[:padded, :1]
        live = iota((padded, 1), 0) < capacity
        scaled[s] = (jnp.where(live, gate, 0.0) * gz[s].astype(f32)).astype(bf16)
        live16 = iota((16, 1), 0) < 16 - (padded - capacity)
        rows[s, padded - 16 :, :] = jnp.where(live16, tail, 0.0).astype(bf16)
        for c in range(shards):
            w_in = gathered_in[shifted(line, shards - c, shards)]
            w_out = out_rest[c - 2] if c > 1 else (out_first[...] if c else out_own[...])
            pre = dot(rows[s], w_in)
            phi, slope = gelu_parts(pre)
            act_low = (pre * phi).astype(bf16)
            act[c, pl.ds(pl.multiple_of(s * padded, 16), padded), :] = act_low
            grad_pre = (dot_nt(scaled[s], w_out) * (phi + slope)).astype(bf16)
            gpre[c, pl.ds(pl.multiple_of(s * padded, 16), padded), :] = grad_pre
            result = dot(act_low, w_out)
            grad_rows = dot_nt(grad_pre, w_in)
            if c > 0:
                result = result + out_sum[...]
                grad_rows = grad_rows + back_sum[...]
            if c < shards - 1:
                out_sum[...] = result
                back_sum[...] = grad_rows
            else:
                out_low[s] = result.astype(bf16)
                back_low[s] = grad_rows.astype(bf16)

    keep = (
        pltpu.make_async_copy(out_low.at[me], returned.at[me], own_sem.at[0]),
        pltpu.make_async_copy(back_low.at[me], back.at[me], own_sem.at[1]),
    )

    @pl.loop(0, sources)
    def _(i):
        j = paired(i, sources - 2, sources)
        block(j)

        @pl.when(i == 0)
        def _():
            pl.semaphore_wait(barrier, sources + 1)

        @pl.when(j != 0)
        def _():
            for copy in sends(j):
                copy.start()

        @pl.when(j == 0)
        def _():
            for copy in keep:
                copy.start()

    for s in range(sources):
        rows_t[:, s * padded : (s + 1) * padded] = jnp.transpose(rows[s])
        gz_t[:, s * padded : (s + 1) * padded] = jnp.transpose(scaled[s])
    def weight_grads(c):
        return dot(rows_t[...], gpre[c]).astype(bf16), dot(gz_t[...], act[c]).astype(bf16)

    ring_out[:D, :], ring_out[D:, :] = weight_grads(1)
    step = exchange(ring_out, ring_in, ring_sem.at[0], ring_sem.at[1], right)
    step.start()
    for c in range(3, shards):
        grads[c - 2, :D, :], grads[c - 2, D:, :] = weight_grads(c)
    grads[0, :D, :], grads[0, D:, :] = weight_grads(0)
    second = weight_grads(2)
    for copy in keep:
        copy.wait()
    step.wait()
    for half in range(2):
        span = slice(half * D, half * D + D)
        ring[span, :] = (ring_in[span, :].astype(f32) + second[half].astype(f32)).astype(bf16)

    @pl.loop(1, sources)
    def _(j):
        for copy in sends(j):
            copy.wait()


def experts_apply(rows, gz, gathered_in, out_own, out_first, out_rest, capacity):
    sources, padded, unused = rows.shape
    shards, unused, hidden = gathered_in.shape
    total = sources * padded
    vmem = pl.BlockSpec(memory_space=pltpu.VMEM)
    anywhere = pl.BlockSpec(memory_space=pl.ANY)
    dma = pltpu.SemaphoreType.DMA
    return pl.pallas_call(
        functools.partial(expert_kernel, capacity, sources, shards),
        in_specs=[vmem] * 6,
        out_specs=(anywhere, anywhere, vmem, vmem),
        out_shape=(
            jax.ShapeDtypeStruct(rows.shape, bf16),
            jax.ShapeDtypeStruct(rows.shape, bf16),
            jax.ShapeDtypeStruct((2 * D, hidden), bf16),
            jax.ShapeDtypeStruct((shards - 2, 2 * D, hidden), bf16),
        ),
        scratch_shapes=[
            pltpu.VMEM(rows.shape, bf16),
            pltpu.VMEM(rows.shape, bf16),
            pltpu.VMEM((D, total), bf16),
            pltpu.VMEM((D, total), bf16),
            pltpu.VMEM((shards, total, hidden), bf16),
            pltpu.VMEM((shards, total, hidden), bf16),
            pltpu.VMEM((padded, D), f32),
            pltpu.VMEM((padded, D), f32),
            pltpu.VMEM(rows.shape, bf16),
            pltpu.VMEM(rows.shape, bf16),
            pltpu.VMEM((2 * D, hidden), bf16),
            pltpu.VMEM((2 * D, hidden), bf16),
            dma((sources,)),
            dma((sources,)),
            dma((sources,)),
            dma((sources,)),
            dma((2,)),
            dma((2,)),
        ],
        compiler_params=pltpu.CompilerParams(
            vmem_limit_bytes=60 * MIB, collective_id=1, has_side_effects=True
        ),
        cost_estimate=pl.CostEstimate(
            flops=12 * total * D * hidden * shards, bytes_accessed=20 * MIB, transcendentals=0
        ),
        name="experts",
    )(rows, gz, gathered_in, out_own, out_first, out_rest)


def backward_kernel(
    experts,
    windows,
    seg,
    w_proj,
    gain_moe,
    w_router,
    slot_col,
    cot,
    packed_in,
    context_in,
    lse,
    residual,
    normed_moe,
    gates,
    returned,
    back,
    counts,
    mixed_out,
    grad_residual_out,
    grad_packed,
    grad_proj,
    small,
    packed,
    context,
    mixed,
    grad_residual,
    hot,
    seg_col,
    seg_row,
    router,
    grad_attn,
    grad_context,
    grad_logits,
    grad_k,
    grad_v,
    sems,
):
    tokens = cot.shape[0]
    slots_all, padded = returned.shape[0] * returned.shape[1], returned.shape[1]
    reads = (
        pltpu.make_async_copy(packed_in, packed, sems.at[0]),
        pltpu.make_async_copy(context_in, context, sems.at[1]),
    )
    writes = (
        pltpu.make_async_copy(mixed, mixed_out, sems.at[2]),
        pltpu.make_async_copy(grad_residual, grad_residual_out, sems.at[3]),
    )
    for read in reads:
        read.start()
    seg_row[...] = seg[...].astype(f32)
    seg_col[...] = jnp.transpose(jnp.broadcast_to(seg_row[...], (LANES, tokens)))
    router[...] = jnp.zeros_like(router)
    router[:, :experts] = w_router[...]
    small[...] = jnp.zeros_like(small)
    small[2:4, :LANES] = counts[:2, :]

    @pl.loop(0, tokens // TILE)
    def _(i):
        rows = pl.ds(pl.multiple_of(i * TILE, TILE), TILE)
        grad_z = cot[rows, :].astype(f32)
        probs = gates[rows, :]
        slots = slot_col[rows, :]
        lane = iota((TILE, LANES), 1)
        rest = residual[rows, :]
        twice = probs + pltpu.roll(probs, experts, axis=1)
        place = jnp.where(lane < experts, lane, lane - experts).astype(f32) * float(padded)
        total = rest
        grad_gates = jnp.zeros((TILE, LANES), f32)
        spots = iota((TILE, slots_all), 1).astype(f32)
        picks = []
        for k in range(TOP):
            mine = (slots >= 0.0) & (lane >= k * experts) & (lane < (k + 1) * experts)
            spot = jnp.sum(jnp.where(mine, place + slots + 1.0, 0.0), axis=1, keepdims=True) - 1.0
            hot[k * TILE : (k + 1) * TILE, :] = (spots == spot).astype(f32).astype(bf16)
            picks.append(mine)
        back_total = dot(hot[:TILE, :] + hot[TILE:, :], back[...].reshape(slots_all, D))
        results = dot(hot[...], returned[...].reshape(slots_all, D))
        for k in range(TOP):
            result = results[k * TILE : (k + 1) * TILE]
            total = total + jnp.sum(jnp.where(picks[k], twice, 0.0), axis=1, keepdims=True) * result
            inner = jnp.sum(result * grad_z, axis=1, keepdims=True)
            grad_gates = grad_gates + jnp.where(picks[k], inner, 0.0)
        grad_gates = grad_gates + pltpu.roll(grad_gates, LANES - experts, axis=1)
        grad_gates = jnp.where(lane < experts, grad_gates, 0.0)
        mixed[rows, :] = total.astype(bf16)
        gate_inner = jnp.sum(probs * grad_gates, axis=1, keepdims=True)
        high, low = split2(probs * (grad_gates - gate_inner))
        grad_logits[rows, :LANES] = high
        grad_logits[rows, LANES:] = low
        grad_normed = back_total + dot_nt(high, router[...]) + dot_nt(low, router[...])
        normal, inverse = norm_parts(rest)
        grad_norm, grad_gain = norm_back(grad_normed, gain_moe[...], normal, inverse)
        small[1:2, :] += grad_gain
        grad_rest = grad_z + grad_norm
        grad_residual[rows, :] = grad_rest
        attn = grad_rest.astype(bf16)
        grad_attn[rows, :] = attn
        grad_context[rows, :] = dot_nt(attn, w_proj[...]).astype(bf16)

    for write in writes:
        write.start()
    for read in reads:
        read.wait()
    both = dot_tn(normed_moe[...], grad_logits[...])
    both = jnp.transpose(both[:, :LANES] + both[:, LANES:])
    small[8:, :] = both[:experts]
    grad_proj[...] = dot_tn(context[...], grad_attn[...])
    grad_k[...] = jnp.zeros_like(grad_k)
    grad_v[...] = jnp.zeros_like(grad_v)

    @pl.loop(0, tokens // QB)
    def _(block):
        query = pl.multiple_of(block * QB, QB)

        def body(low, width):
            bias = window_bias(seg_col, seg_row, low, width, query)
            spans = [slice(pair * PAIR, (pair + 1) * PAIR) for pair in range(PAIRS)]
            keys = pl.ds(low, width)
            queries = [
                (stack_heads(packed[pl.ds(query, QB), span]) * HEAD ** (-0.5)).astype(bf16) for span in spans
            ]
            grads = [stack_heads(grad_context[pl.ds(query, QB), span]) for span in spans]
            probs = []
            grad_probs = []
            for pair, span in enumerate(spans):
                k = packed[keys, D + span.start : D + span.stop]
                v = packed[keys, 2 * D + span.start : 2 * D + span.stop]
                probs.append(jnp.exp(dot_nt(k, queries[pair]) + bias - lse[pl.ds(block, 1), pair, :]))
                grad_probs.append(dot_nt(v, grads[pair]))
            grad_scores = []
            for pair, span in enumerate(spans):
                grad_v[keys, span] += dot(probs[pair].astype(bf16), grads[pair])
                weighted = probs[pair] * grad_probs[pair]
                inner = jnp.sum(weighted, axis=0, keepdims=True)
                grad_scores.append((weighted - probs[pair] * inner).astype(bf16))
            for pair, span in enumerate(spans):
                k = packed[keys, D + span.start : D + span.stop]
                grad_k[keys, span] += dot(grad_scores[pair], queries[pair])
                grad_q = unstack_cols(dot_tn(k, grad_scores[pair])) * HEAD ** (-0.5)
                grad_packed[pl.ds(query, QB), span] = grad_q.astype(bf16)

        by_window(windows, block, body)

    @pl.loop(0, tokens // TILE)
    def _(i):
        rows = pl.ds(pl.multiple_of(i * TILE, TILE), TILE)
        grad_packed[rows, D : 2 * D] = grad_k[rows, :].astype(bf16)
        grad_packed[rows, 2 * D :] = grad_v[rows, :].astype(bf16)

    for write in writes:
        write.wait()


def backward(experts, windows, *operands):
    cot = operands[5]
    returned = operands[-3]
    tokens = cot.shape[0]
    vmem = pl.BlockSpec(memory_space=pltpu.VMEM)
    anywhere = pl.BlockSpec(memory_space=pl.ANY)
    return pl.pallas_call(
        functools.partial(backward_kernel, experts),
        in_specs=[pl.BlockSpec(memory_space=pltpu.SMEM)] + [vmem] * 6 + [anywhere] * 2 + [vmem] * (len(operands) - 8),
        out_specs=[anywhere, anywhere, vmem, vmem, vmem],
        out_shape=(
            jax.ShapeDtypeStruct((tokens, D), bf16),
            jax.ShapeDtypeStruct((tokens, D), f32),
            jax.ShapeDtypeStruct((tokens, 3 * D), bf16),
            jax.ShapeDtypeStruct((D, D), f32),
            jax.ShapeDtypeStruct((8 + experts, D), f32),
        ),
        scratch_shapes=[
            pltpu.VMEM((tokens, 3 * D), bf16),
            pltpu.VMEM((tokens, D), bf16),
            pltpu.VMEM((tokens, D), bf16),
            pltpu.VMEM((tokens, D), f32),
            pltpu.VMEM((TOP * TILE, returned.shape[0] * returned.shape[1]), bf16),
            pltpu.VMEM((tokens, LANES), f32),
            pltpu.VMEM((1, tokens), f32),
            pltpu.VMEM((D, LANES), bf16),
            pltpu.VMEM((tokens, D), bf16),
            pltpu.VMEM((tokens, D), bf16),
            pltpu.VMEM((tokens, 2 * LANES), bf16),
            pltpu.VMEM((tokens, D), f32),
            pltpu.VMEM((tokens, D), f32),
            pltpu.SemaphoreType.DMA((4,)),
        ],
        compiler_params=pltpu.CompilerParams(vmem_limit_bytes=60 * MIB),
        cost_estimate=pl.CostEstimate(
            flops=30 * 1024 * MIB, bytes_accessed=30 * MIB, transcendentals=4 * MIB
        ),
        name="attention_backward",
    )(windows, *operands)


def shared_kernel(
    chips,
    planes,
    normed_attn,
    grad_packed,
    grad_proj,
    partial,
    tok,
    grad_residual,
    gain_attn,
    w_qkv,
    summed,
    small,
    grad_tokens,
    normed_t,
    half,
    core_out,
    core_in,
    chip_out,
    chip_in,
    plane_own,
    plane_out,
    plane_in,
    small_own,
    small_core,
    small_chip,
    small_plane,
    core_sem,
    chip_sem,
    plane_sem,
    plane_sem2,
    chip_sem2,
    core_sem2,
    small_sem,
    small_chip_sem,
    small_plane_sem,
):
    tokens = tok.shape[0]
    columns = summed.shape[2]
    part = D // columns if columns < D else 1
    wide = lax.axis_index("wide")
    plane = lax.axis_index("narrow")
    core = lax.rem(wide, 2)
    chip = wide // 2
    share = D // (2 * chips)
    partner = (chip * 2 + 1 - core, plane)
    mine = pl.ds(pl.multiple_of(core * (D // 2), D // 2), D // 2)
    other = pl.ds(pl.multiple_of((1 - core) * (D // 2), D // 2), D // 2)
    chunk = pl.ds(pl.multiple_of(core * (D // 2) + chip * share, share), share)
    own_chunk = pl.ds(pl.multiple_of(chip * share, share), share)

    def chip_at(j):
        to = shifted(chip, j, chips)
        return to, (to * 2 + core, plane)

    def plane_at(j):
        to = shifted(plane, j, planes)
        return to, (wide, to)

    barrier = pltpu.get_barrier_semaphore()
    pl.semaphore_signal(barrier, inc=1, device_id=partner, device_id_type=MESH)

    @pl.loop(1, chips)
    def _(j):
        pl.semaphore_signal(barrier, inc=1, device_id=chip_at(j)[1], device_id_type=MESH)

    @pl.loop(1, planes)
    def _(j):
        pl.semaphore_signal(barrier, inc=1, device_id=plane_at(j)[1], device_id_type=MESH)

    def core_copy(n):
        return exchange(core_out.at[n], core_in.at[n], core_sem.at[0, n], core_sem.at[1, n], partner)

    def chip_copy(n, j):
        to, device = chip_at(j)
        rows = pl.ds(pl.multiple_of(to * share, share), share)
        return exchange(
            chip_out.at[n, rows], chip_in.at[j, n], chip_sem.at[0, j, n], chip_sem.at[1, j, n], device
        )

    def plane_copy(j):
        to, device = plane_at(j)
        return exchange(plane_out.at[to], plane_in.at[j], plane_sem.at[0, j], plane_sem.at[1, j], device)

    def plane_back(j):
        spot = summed.at[plane, chunk]
        return exchange(spot, spot, plane_sem2.at[0, j], plane_sem2.at[1, j], plane_at(j)[1])

    def column_of(i):
        return shifted(plane, planes - i, planes)

    def chip_back(i, j):
        spot = summed.at[column_of(i), chunk]
        return exchange(spot, spot, chip_sem2.at[0, j, i], chip_sem2.at[1, j, i], chip_at(j)[1])

    def core_back(i):
        spot = summed.at[column_of(i), mine]
        return exchange(spot, spot, core_sem2.at[0, i], core_sem2.at[1, i], partner)

    def small_core_copy():
        return exchange(small_own, small_core, small_sem.at[0], small_sem.at[1], partner)

    def small_chip_copy(j):
        return exchange(
            small_chip.at[chip],
            small_chip.at[chip],
            small_chip_sem.at[0, j],
            small_chip_sem.at[1, j],
            chip_at(j)[1],
        )

    def small_plane_copy(j):
        return exchange(
            small_plane.at[plane],
            small_plane.at[plane],
            small_plane_sem.at[0, j],
            small_plane_sem.at[1, j],
            plane_at(j)[1],
        )

    order = [(3, p) for p in range(part)] + [(t, p) for t in range(3) for p in range(part)]
    normed_t[...] = jnp.transpose(normed_attn[...])
    for t, p in order:
        n = t * part + p
        if t == 3:
            half[n] = grad_proj[mine, p * columns : (p + 1) * columns]
            core_out[n] = grad_proj[other, p * columns : (p + 1) * columns].astype(bf16)
        else:
            right = grad_packed[:, n * columns : (n + 1) * columns]
            core_out[n] = dot(normed_t[other, :], right).astype(bf16)
        if (t, p) == order[0]:
            pl.semaphore_wait(barrier, chips + planes - 1)
        core_copy(n).start()
        if t < 3:
            half[n] = dot(normed_t[mine, :], right)
    for t, p in order:
        n = t * part + p
        core_copy(n).wait_recv()
        half[n] = half[n] + core_in[n].astype(f32)
        chip_out[n] = half[n].astype(bf16)

        @pl.loop(1, chips)
        def _(j):
            chip_copy(n, j).start()

    small_own[...] = partial[...]

    @pl.loop(0, tokens // TILE)
    def _(i):
        rows = pl.ds(pl.multiple_of(i * TILE, TILE), TILE)
        grad_normed = dot_nt(grad_packed[rows, :], w_qkv[...])
        normal, inverse = norm_parts(tok[rows, :].astype(f32))
        grad_norm, grad_gain = norm_back(grad_normed, gain_attn[...], normal, inverse)
        small_own[0:1, :] += grad_gain
        grad_tokens[rows, :] = grad_residual[rows, :] + grad_norm

    small_core_copy().start()
    for t, p in order:
        n = t * part + p
        total = half[n, own_chunk, :]
        for j in range(1, chips):
            chip_copy(n, j).wait_recv()
            total = total + chip_in[j, n].astype(f32)
        plane_out[n] = total.astype(bf16)

        @pl.when(n == plane)
        def _():
            plane_own[...] = total

        @pl.when(n != plane)
        def _():
            plane_copy(lax.rem(n + planes - plane, planes)).start()

    small_core_copy().wait_recv()
    small_chip[chip] = small_own[...] + small_core[...]

    @pl.loop(1, chips)
    def _(j):
        small_chip_copy(j).start()

    total = plane_own[...]
    for j in range(1, planes):
        plane_copy(j).wait_recv()
        total = total + plane_in[j].astype(f32)
    summed[plane, chunk, :] = total.astype(bf16)

    @pl.loop(1, planes)
    def _(j):
        plane_back(j).start()

    @pl.loop(1, chips)
    def _(j):
        small_chip_copy(j).wait_recv()

    total = small_chip[0]
    for c in range(1, chips):
        total = total + small_chip[c]
    small_plane[plane] = total

    @pl.loop(1, planes)
    def _(j):
        small_plane_copy(j).start()

    for i in range(planes):
        if i > 0:
            plane_back(i).wait_recv()

        @pl.loop(1, chips)
        def _(j):
            chip_back(i, j).start()

    for i in range(planes):

        @pl.loop(1, chips)
        def _(j):
            chip_back(i, j).wait_recv()

        core_back(i).start()

    @pl.loop(1, planes)
    def _(j):
        small_plane_copy(j).wait_recv()

    total = small_plane[0]
    for c in range(1, planes):
        total = total + small_plane[c]
    small[...] = total
    for i in range(planes):
        core_back(i).wait()
        core_copy(i).wait_send()

        @pl.loop(1, chips)
        def _(j):
            chip_back(i, j).wait_send()
            chip_copy(i, j).wait_send()

    @pl.loop(1, planes)
    def _(j):
        plane_back(j).wait_send()
        plane_copy(j).wait_send()
        small_plane_copy(j).wait_send()

    @pl.loop(1, chips)
    def _(j):
        small_chip_copy(j).wait_send()

    small_core_copy().wait_send()


def shared_gradients(*operands):
    normed_attn, unused, unused, partial = operands[:4]
    tokens = normed_attn.shape[0]
    chips = lax.axis_size("wide") // 2
    planes = lax.axis_size("narrow")
    columns = 4 * D // planes
    share = D // (2 * chips)
    rows = partial.shape[0]
    dma = pltpu.SemaphoreType.DMA
    return pl.pallas_call(
        functools.partial(shared_kernel, chips, planes),
        out_shape=(
            jax.ShapeDtypeStruct((planes, D, columns), bf16),
            jax.ShapeDtypeStruct((rows, D), f32),
            jax.ShapeDtypeStruct((tokens, D), f32),
        ),
        scratch_shapes=[
            pltpu.VMEM((D, tokens), bf16),
            pltpu.VMEM((planes, D // 2, columns), f32),
            pltpu.VMEM((planes, D // 2, columns), bf16),
            pltpu.VMEM((planes, D // 2, columns), bf16),
            pltpu.VMEM((planes, D // 2, columns), bf16),
            pltpu.VMEM((chips, planes, share, columns), bf16),
            pltpu.VMEM((share, columns), f32),
            pltpu.VMEM((planes, share, columns), bf16),
            pltpu.VMEM((planes, share, columns), bf16),
            pltpu.VMEM((rows, D), f32),
            pltpu.VMEM((rows, D), f32),
            pltpu.VMEM((chips, rows, D), f32),
            pltpu.VMEM((planes, rows, D), f32),
            dma((2, planes)),
            dma((2, chips, planes)),
            dma((2, planes)),
            dma((2, planes)),
            dma((2, chips, planes)),
            dma((2, planes)),
            dma((2,)),
            dma((2, chips)),
            dma((2, planes)),
        ],
        compiler_params=pltpu.CompilerParams(
            vmem_limit_bytes=50 * MIB, collective_id=2, has_side_effects=True
        ),
        cost_estimate=pl.CostEstimate(
            flops=12 * tokens * D * D, bytes_accessed=16 * MIB, transcendentals=0
        ),
        name="shared_gradients",
    )(*operands)


def finish_kernel(experts, summed, ring, own, small, tokens_in, qkv, proj, grad_in, grad_out, rest, router, tokens_out, sem):
    copy = pltpu.make_async_copy(tokens_in, tokens_out, sem)
    copy.start()
    planes, unused, columns = summed.shape
    for n in range(planes):
        start = n * columns
        if start < 3 * D:
            qkv[:, start : start + columns] = summed[n].astype(f32)
        else:
            proj[:, start - 3 * D : start - 3 * D + columns] = summed[n].astype(f32)
    total = ring[...].astype(f32) + own[...].astype(f32)
    grad_in[0] = total[:D, :]
    grad_out[0] = jnp.transpose(total[D:, :])
    rest[...] = small[:8, :]
    router[...] = jnp.transpose(jnp.concatenate([small[8:, :], jnp.zeros((LANES - experts, D), f32)], axis=0))[
        :, :experts
    ]
    copy.wait()


def finish(experts, summed, ring, own, small, tokens_in):
    hidden = own.shape[1]
    vmem = pl.BlockSpec(memory_space=pltpu.VMEM)
    anywhere = pl.BlockSpec(memory_space=pl.ANY)
    return pl.pallas_call(
        functools.partial(finish_kernel, experts),
        in_specs=[vmem, vmem, vmem, vmem, anywhere],
        out_specs=[vmem] * 6 + [anywhere],
        out_shape=(
            jax.ShapeDtypeStruct((D, 3 * D), f32),
            jax.ShapeDtypeStruct((D, D), f32),
            jax.ShapeDtypeStruct((1, D, hidden), f32),
            jax.ShapeDtypeStruct((1, hidden, D), f32),
            jax.ShapeDtypeStruct((8, D), f32),
            jax.ShapeDtypeStruct((D, experts), f32),
            jax.ShapeDtypeStruct(tokens_in.shape, f32),
        ),
        scratch_shapes=[pltpu.SemaphoreType.DMA],
        compiler_params=pltpu.CompilerParams(vmem_limit_bytes=40 * MIB),
        cost_estimate=pl.CostEstimate(flops=0, bytes_accessed=14 * MIB, transcendentals=0),
        name="finish",
    )(summed, ring, own, small, tokens_in)


def per_device(
    tokens,
    segment_ids,
    expert_picks,
    priority_ranks,
    gain_attn,
    w_qkv,
    w_proj,
    gain_moe,
    w_router,
    w_in,
    w_out,
    cotangent,
):
    experts = w_router.shape[1]
    capacity = (21 * TOP * TOK_DEV + 20 * experts - 1) // (20 * experts)
    padded = (capacity + 3 + 15) // 16 * 16
    gain_attn = gain_attn.reshape(1, D)
    gain_moe = gain_moe.reshape(1, D)
    seg = segment_ids.reshape(1, SEQ)
    first = jnp.sum((segment_ids[None, :] < segment_ids[0::QB, None]).astype(jnp.int32), axis=1)
    after = jnp.sum((segment_ids[None, :] <= segment_ids[QB - 1 :: QB, None]).astype(jnp.int32), axis=1)
    low = jnp.minimum(first // 16 * 16, SEQ - WINDOW)
    fits = (after - low <= WINDOW).astype(jnp.int32)
    windows = jnp.concatenate([low, fits])

    line = lax.axis_size("narrow")
    ring_steps = [(i, (i + 1) % line) for i in range(line)]
    together = lax.optimization_barrier

    def pass_on(values):
        return lax.ppermute(values, "narrow", ring_steps)

    out_own = w_out[0]
    out_first = pass_on(out_own)
    gathered_in = lax.all_gather(w_in[0], "narrow", axis=0)
    slot_col, slot_row, counts, gz_send = route(
        expert_picks, priority_ranks, cotangent, experts, capacity, padded
    )
    gz = lax.all_to_all(gz_send, "wide", split_axis=0, concat_axis=0, tiled=True)
    normed_attn, packed, context, lse, residual, normed_moe, gates, gate_row = forward(
        windows, tokens, seg, gain_attn, w_qkv, w_proj, gain_moe, w_router
    )
    rows, out_rest = dispatch(slot_row, gate_row, normed_moe, out_first, line, padded)
    returned, back, ring, grads = experts_apply(rows, gz, gathered_in, out_own, out_first, out_rest, capacity)
    ring = pass_on(ring)
    mixed, grad_residual, grad_packed, grad_proj, partial = backward(
        experts,
        windows,
        seg,
        w_proj,
        gain_moe,
        w_router,
        slot_col,
        cotangent,
        packed,
        context,
        lse,
        residual,
        normed_moe,
        gates,
        returned,
        back,
        counts,
    )
    ring, grad_packed = together((ring, grad_packed))
    for k in range(1, line - 2):
        ring = pass_on((ring.astype(f32) + grads[k].astype(f32)).astype(bf16))
    summed, small, grad_tokens = shared_gradients(
        normed_attn, grad_packed, grad_proj, partial, tokens, grad_residual, gain_attn, w_qkv
    )
    grad_qkv, grad_proj, grad_in, grad_out, rest, grad_router, grad_tokens = finish(
        experts, summed, ring, grads[0], small, grad_tokens
    )
    counted = rest[2:4, :experts].astype(jnp.int32)
    return (
        mixed,
        grad_tokens,
        rest[0],
        grad_qkv,
        grad_proj,
        rest[1],
        grad_router,
        grad_in,
        grad_out,
        counted[0],
        counted[1] - counted[0],
    )


def solution(mesh):
    both = ("wide", "narrow")
    placed = (
        P(both, None),
        P(both),
        P(both, None),
        P(both, None),
        P(),
        P(),
        P(),
        P(),
        P(),
        P("wide", None, "narrow"),
        P("wide", "narrow", None),
        P(both, None),
    )
    return jax.shard_map(
        per_device,
        mesh=mesh,
        in_specs=placed,
        out_specs=(
            P(both, None),
            P(both, None),
            P(),
            P(),
            P(),
            P(),
            P(),
            P("wide", None, "narrow"),
            P("wide", "narrow", None),
            P(),
            P(),
        ),
        check_vma=False,
    )
```

```python
import functools

import jax
import jax.numpy as jnp
from jax import lax
from jax.experimental import pallas as pl
from jax.experimental.pallas import tpu as pltpu
from jax.sharding import PartitionSpec as P

D = 512
HEADS = 8
HEAD = 64
PAIRS = HEADS // 2
PAIR = 2 * HEAD
TOP = 2
SEQ = 1024
TOK_DEV = 1024
LANES = 128
QB = 128
WINDOW = 432
TILE = 256
SLABS = tuple((max(0, QB * (b - 2)), min(SEQ, QB * (b + 3))) for b in range(SEQ // QB))
MIB = 1024 * 1024
MESH = pl.DeviceIdType.MESH

f32 = jnp.float32
bf16 = jnp.bfloat16
NT = (((1,), (1,)), ((), ()))
TN = (((0,), (0,)), ((), ()))


def dot(a, b):
    return jnp.dot(a, b, preferred_element_type=f32)


def dot_nt(a, b):
    return lax.dot_general(a, b, NT, preferred_element_type=f32)


def dot_tn(a, b):
    return lax.dot_general(a, b, TN, preferred_element_type=f32)


def iota(shape, dim):
    return lax.broadcasted_iota(jnp.int32, shape, dim)


def norm_parts(values_in):
    centered = values_in - jnp.mean(values_in, axis=-1, keepdims=True)
    variance = jnp.mean(centered * centered, axis=-1, keepdims=True)
    inverse = lax.rsqrt(variance + 1e-06)
    return (centered * inverse, inverse)


def norm_back(grad_normed, gain, normalized, inverse):
    grad_gain = jnp.sum(grad_normed * normalized, axis=0, keepdims=True)
    scaled = grad_normed * gain
    inner = scaled - jnp.mean(scaled, axis=-1, keepdims=True)
    inner = inner - normalized * jnp.mean(scaled * normalized, axis=-1, keepdims=True)
    return (inner * inverse, grad_gain)


def split2(values_in):
    high = values_in.astype(bf16)
    low = (values_in - high.astype(f32)).astype(bf16)
    return high, low


def row_to_col(row):
    n = row.shape[1]
    return jnp.transpose(jnp.broadcast_to(row, (LANES, n)))[:, :1]


def route_kernel(
    experts,
    capacity,
    picks,
    ranks,
    cot,
    tok,
    gain_attn,
    w_qkv,
    slot_col,
    slot_row,
    counts,
    gz_out,
    normed_out,
    packed_out,
    gz_send,
    normed_attn,
    packed,
    gz_sem,
    sems,
):
    tokens = ranks.shape[1]
    padded = gz_send.shape[1]
    rank_row = ranks[...].astype(f32)
    rank_col = row_to_col(rank_row)
    lane = iota((tokens, LANES), 1)
    pick0 = picks[:, 0:1]
    pick1 = picks[:, 1:2]
    hot = jnp.where(lane == jnp.where(lane < experts, pick0, pick1 + experts), 1.0, 0.0).astype(f32)
    before = (rank_row < rank_col).astype(f32).astype(bf16)
    earlier = dot(before, hot.astype(bf16))
    total = jnp.sum(hot, axis=0, keepdims=True)
    total = jnp.broadcast_to(total, (8, LANES))
    lane8 = iota((8, LANES), 1)
    first = jnp.where(lane8 < experts, total, 0.0)
    earlier = earlier + pltpu.roll(first, experts, axis=1)[:1]
    kept = (hot > 0.5) & (earlier < float(capacity))
    slots = jnp.where(kept, earlier, -1.0)
    slot_col[...] = slots
    slots = jnp.maximum(slots, pltpu.roll(slots, LANES - experts, axis=1))
    slots = jnp.where(lane < experts, slots, -1.0)
    slot_row[...] = jnp.transpose(slots)[:experts]
    kept_lane = jnp.sum(jnp.where(slots >= 0.0, 1.0, 0.0), axis=0, keepdims=True)
    both = total + pltpu.roll(total, LANES - experts, axis=1)
    both = jnp.where(lane8 < experts, both, 0.0)
    sub8 = iota((8, LANES), 0)
    counts[...] = jnp.where(sub8 == 0, kept_lane, jnp.where(sub8 == 1, both, 0.0))

    @pl.loop(0, experts)
    def _(e):
        chosen = iota((padded, tokens), 0).astype(f32) == slot_row[pl.ds(e, 1), :]
        gz_send[e] = dot(chosen.astype(f32).astype(bf16), cot[...]).astype(bf16)
        pltpu.make_async_copy(gz_send.at[e], gz_out.at[e], gz_sem.at[e]).start()

    def stores(i):
        rows = pl.ds(pl.multiple_of(i * TILE, TILE), TILE)
        return (
            pltpu.make_async_copy(normed_attn.at[rows], normed_out.at[rows], sems.at[0, i]),
            pltpu.make_async_copy(packed.at[rows], packed_out.at[rows], sems.at[1, i]),
        )

    @pl.loop(0, tokens // TILE)
    def _(i):
        rows = pl.ds(pl.multiple_of(i * TILE, TILE), TILE)
        normal, unused = norm_parts(tok[rows, :].astype(f32))
        normed = (normal * gain_attn[...]).astype(bf16)
        normed_attn[rows, :] = normed
        packed[rows, :] = dot(normed, w_qkv[...]).astype(bf16)
        for store in stores(i):
            store.start()

    @pl.loop(0, experts)
    def _(e):
        pltpu.make_async_copy(gz_send.at[e], gz_out.at[e], gz_sem.at[e]).wait()

    @pl.loop(0, tokens // TILE)
    def _(i):
        for store in stores(i):
            store.wait()


def route(picks, ranks, cot, tok, gain_attn, w_qkv, experts, capacity, padded):
    tokens = picks.shape[0]
    vmem = pl.BlockSpec(memory_space=pltpu.VMEM)
    anywhere = pl.BlockSpec(memory_space=pl.ANY)
    return pl.pallas_call(
        functools.partial(route_kernel, experts, capacity),
        out_shape=(
            jax.ShapeDtypeStruct((tokens, LANES), f32),
            jax.ShapeDtypeStruct((experts, tokens), f32),
            jax.ShapeDtypeStruct((8, LANES), f32),
            jax.ShapeDtypeStruct((experts, padded, D), bf16),
            jax.ShapeDtypeStruct((tokens, D), bf16),
            jax.ShapeDtypeStruct((tokens, 3 * D), bf16),
        ),
        out_specs=(vmem, vmem, vmem, anywhere, anywhere, anywhere),
        scratch_shapes=[
            pltpu.VMEM((experts, padded, D), bf16),
            pltpu.VMEM((tokens, D), bf16),
            pltpu.VMEM((tokens, 3 * D), bf16),
            pltpu.SemaphoreType.DMA((experts,)),
            pltpu.SemaphoreType.DMA((2, tokens // TILE)),
        ],
        compiler_params=pltpu.CompilerParams(vmem_limit_bytes=40 * MIB),
        cost_estimate=pl.CostEstimate(
            flops=2 * experts * padded * tokens * D, bytes_accessed=6 * MIB, transcendentals=0
        ),
        name="route",
    )(picks, ranks, cot, tok, gain_attn, w_qkv)


def stack_heads(block):
    lane = iota(block.shape, 1)
    zero = jnp.zeros_like(block)
    return jnp.concatenate(
        [jnp.where(lane < HEAD, block, zero), jnp.where(lane < HEAD, zero, block)], axis=0
    )


def unstack_cols(stacked):
    row = iota((PAIR, QB), 0)
    picked = jnp.where(row < HEAD, stacked[:, :QB], stacked[:, QB:])
    return jnp.transpose(picked)


def window_bias(seg_col, seg_row, low, width, query):
    same = seg_col[pl.ds(low, width), :] == seg_row[:, pl.ds(query, QB)]
    half = jnp.where(same, 0.0, -1e30).astype(f32)
    return jnp.concatenate([half, half], axis=1)


def by_window(windows, block, body):
    low = windows[block]
    fits = windows[block + SEQ // QB]

    @pl.when(fits == 1)
    def _():
        body(pl.multiple_of(low, 16), WINDOW)

    @pl.when(fits != 1)
    def _():
        body(0, SEQ)


def forward_kernel(
    experts,
    windows,
    tok,
    seg,
    packed,
    w_proj,
    gain_moe,
    w_router,
    context_out,
    lse,
    residual_out,
    normed_moe_out,
    gates_out,
    gate_row,
    context,
    residual,
    normed_moe,
    gates,
    seg_col,
    seg_row,
    router,
    sems,
):
    writes = [
        pltpu.make_async_copy(source, target, sems.at[i])
        for i, (source, target) in enumerate(
            (
                (context, context_out),
                (residual, residual_out),
                (normed_moe, normed_moe_out),
                (gates, gates_out),
            )
        )
    ]
    tokens = tok.shape[0]
    seg_row[...] = seg[...].astype(f32)
    seg_col[...] = jnp.transpose(jnp.broadcast_to(seg_row[...], (LANES, tokens)))
    router[...] = jnp.zeros_like(router)
    router[:, :experts] = w_router[...]

    @pl.loop(0, tokens // QB)
    def _(block):
        query = pl.multiple_of(block * QB, QB)

        def body(low, width):
            bias = window_bias(seg_col, seg_row, low, width, query)
            spans = [slice(pair * PAIR, (pair + 1) * PAIR) for pair in range(PAIRS)]
            scores = []
            for span in spans:
                q = stack_heads(packed[pl.ds(query, QB), span]) * HEAD ** (-0.5)
                k = packed[pl.ds(low, width), D + span.start : D + span.stop]
                scores.append(dot_nt(k, q.astype(bf16)) + bias)
            peaks = [jnp.max(score, axis=0, keepdims=True) for score in scores]
            exponents = [jnp.exp(score - peak) for score, peak in zip(scores, peaks)]
            totals = [jnp.sum(exponent, axis=0, keepdims=True) for exponent in exponents]
            probs = [(exponent * (1.0 / total)).astype(bf16) for exponent, total in zip(exponents, totals)]
            for pair, span in enumerate(spans):
                lse[pl.ds(block, 1), pair, :] = peaks[pair] + jnp.log(totals[pair])
                v = packed[pl.ds(low, width), 2 * D + span.start : 2 * D + span.stop]
                mixed = dot_tn(v, probs[pair])
                context[pl.ds(query, QB), span] = unstack_cols(mixed).astype(bf16)

        by_window(windows, block, body)

    writes[0].start()

    @pl.loop(0, tokens // TILE)
    def _(i):
        rows = pl.ds(pl.multiple_of(i * TILE, TILE), TILE)
        rest = tok[rows, :].astype(f32) + dot(context[rows, :], w_proj[...])
        residual[rows, :] = rest
        normal, unused = norm_parts(rest)
        normed = (normal * gain_moe[...]).astype(bf16)
        normed_moe[rows, :] = normed
        logits = dot(normed, router[...])
        logits = jnp.where(iota(logits.shape, 1) < experts, logits, -1e30)
        exponent = jnp.exp(logits - jnp.max(logits, axis=1, keepdims=True))
        gates[rows, :] = exponent / jnp.sum(exponent, axis=1, keepdims=True)

    for write in writes[1:]:
        write.start()
    gate_row[...] = jnp.transpose(gates[...])[:experts]
    for write in writes:
        write.wait()


def forward(windows, tok, seg, packed, w_proj, gain_moe, w_router):
    tokens = tok.shape[0]
    experts = w_router.shape[1]
    vmem = pl.BlockSpec(memory_space=pltpu.VMEM)
    anywhere = pl.BlockSpec(memory_space=pl.ANY)
    return pl.pallas_call(
        functools.partial(forward_kernel, experts),
        in_specs=[pl.BlockSpec(memory_space=pltpu.SMEM)] + [vmem] * 6,
        out_specs=[anywhere, vmem] + [anywhere] * 3 + [vmem],
        out_shape=(
            jax.ShapeDtypeStruct((tokens, D), bf16),
            jax.ShapeDtypeStruct((tokens // QB, PAIRS, 2 * QB), f32),
            jax.ShapeDtypeStruct((tokens, D), f32),
            jax.ShapeDtypeStruct((tokens, D), bf16),
            jax.ShapeDtypeStruct((tokens, LANES), f32),
            jax.ShapeDtypeStruct((experts, tokens), f32),
        ),
        scratch_shapes=[
            pltpu.VMEM((tokens, D), bf16),
            pltpu.VMEM((tokens, D), f32),
            pltpu.VMEM((tokens, D), bf16),
            pltpu.VMEM((tokens, LANES), f32),
            pltpu.VMEM((tokens, LANES), f32),
            pltpu.VMEM((1, tokens), f32),
            pltpu.VMEM((D, LANES), bf16),
            pltpu.SemaphoreType.DMA((4,)),
        ],
        compiler_params=pltpu.CompilerParams(vmem_limit_bytes=56 * MIB),
        cost_estimate=pl.CostEstimate(
            flops=64 * 1024 * MIB, bytes_accessed=16 * MIB, transcendentals=4 * MIB
        ),
        name="attention_forward",
    )(windows, tok, seg, packed, w_proj, gain_moe, w_router)


def gelu_parts(x):
    density = jnp.exp(-0.5 * (x * x))
    return 0.5 + 0.5 * lax.erf(x * 2.0**-0.5), x * density * 0.3989422804014327


def shifted(index, by, size):
    return lax.rem(index + by, size)


def paired(index, by, size):
    total = 0
    bit = 1
    while bit < size:
        total = total + bit * lax.rem(index // bit + by // bit, 2)
        bit *= 2
    return total


def exchange(src, dst, send, recv, device):
    return pltpu.make_async_remote_copy(
        src_ref=src, dst_ref=dst, send_sem=send, recv_sem=recv, device_id=device, device_id_type=MESH
    )


def greet(barrier, sources):
    me = lax.axis_index("wide")
    line = lax.axis_index("narrow")

    @pl.loop(1, sources)
    def _(j):
        pl.semaphore_signal(barrier, inc=1, device_id=(paired(me, j, sources), line), device_id_type=MESH)


EARLY = 3


def moe_kernel(
    capacity,
    sources,
    shards,
    slot_row,
    gate_row,
    normed_in,
    gz_in,
    w_in0,
    w_out0,
    w_in1,
    w_out1,
    w_in2,
    w_out2,
    returned,
    back,
    ring,
    grads,
    normed_moe,
    w_ins,
    w_outs,
    rows_send,
    rows,
    scaled,
    gate_slot,
    rows_t,
    gz_t,
    act,
    gpre,
    out_sum,
    back_sum,
    out_low,
    back_low,
    ring_out,
    ring_in,
    load_sem,
    row_sem,
    out_sem,
    back_sem,
    own_sem,
    weight_sem,
    ring_sem,
):
    padded = rows.shape[1]
    tokens = normed_in.shape[0]
    me = lax.axis_index("wide")
    line = lax.axis_index("narrow")
    right = (me, shifted(line, 1, shards))
    left = (me, shifted(line, shards - 1, shards))
    early = ((w_in0, w_out0), (w_in1, w_out1), (w_in2, w_out2))
    loads = [
        pltpu.make_async_copy(normed_in, normed_moe, load_sem.at[0]),
        pltpu.make_async_copy(gz_in, scaled, load_sem.at[1]),
    ]
    for c, pair in reversed(list(enumerate(early))):
        for i, (source, target) in enumerate(zip(pair, (w_ins, w_outs))):
            loads.append(pltpu.make_async_copy(source, target.at[c], load_sem.at[2 + 2 * c + i]))
    for load in loads:
        load.start()
    barrier = pltpu.get_barrier_semaphore()
    greet(barrier, sources)
    for near in (left, right):
        pl.semaphore_signal(barrier, inc=1, device_id=near, device_id_type=MESH)
    gate_slot[...] = jnp.zeros_like(gate_slot)

    def weights_on(c):
        return [
            exchange(part.at[c - 1], part.at[c], weight_sem.at[0, i, c], weight_sem.at[1, i, c], right)
            for i, part in enumerate((w_ins, w_outs))
        ]

    def row_copy(j):
        to = paired(me, j, sources)
        return exchange(rows_send.at[to], rows.at[me], row_sem.at[0, j], row_sem.at[1, j], (to, line))

    def result_copies(j):
        to = paired(me, j, sources)
        return [
            exchange(low.at[to], target.at[me], sem.at[0, j], sem.at[1, j], (to, line))
            for low, target, sem in ((out_low, returned, out_sem), (back_low, back, back_sem))
        ]

    keep = [
        pltpu.make_async_copy(low.at[me], target.at[me], own_sem.at[i])
        for i, (low, target) in enumerate(((out_low, returned), (back_low, back)))
    ]

    for load in loads[:1] + loads[2:4]:
        load.wait()

    @pl.loop(0, sources)
    def _(i):
        j = paired(i, sources - 2, sources)
        e = paired(me, j, sources)
        chosen = iota((padded, tokens), 0).astype(f32) == slot_row[pl.ds(e, 1), :]
        chosen = chosen.astype(f32).astype(bf16)
        rows_send[e] = dot(chosen, normed_moe[...]).astype(bf16)
        gate = gate_row[pl.ds(e, 1), :]
        high, middle = split2(gate)
        low = (gate - high.astype(f32) - middle.astype(f32)).astype(bf16)
        three = jnp.concatenate(
            [high.astype(f32), middle.astype(f32), low.astype(f32), jnp.zeros((5, tokens), f32)], axis=0
        )
        gate_slot[:, :padded] = dot_nt(three.astype(bf16), chosen)
        tail = rows_send[e, padded - 16 :, :].astype(f32)
        sub = iota(tail.shape, 0)
        for part in range(3):
            tail = jnp.where(sub == 13 + part, gate_slot[part : part + 1, :], tail)
        rows_send[e, padded - 16 :, :] = tail.astype(bf16)

        @pl.when(i == 0)
        def _():
            pl.semaphore_wait(barrier, sources + 1)
            for copy in weights_on(EARLY):
                copy.start()

        @pl.when(j != 0)
        def _():
            row_copy(j).start()

    rows[me] = rows_send[me]
    for load in loads[1:2] + loads[4:]:
        load.wait()

    def partner(i):
        return lax.rem(sources - i // 2 * 2, sources) + lax.rem(i, 2)

    def prepare(j):
        s = paired(me, j, sources)

        @pl.when(j != 0)
        def _():
            row_copy(j).wait_recv()

        tail = rows[s, padded - 16 :, :].astype(f32)
        gate = tail[13:14] + tail[14:15] + tail[15:16]
        gate = jnp.transpose(jnp.broadcast_to(gate, (LANES, D)))[:padded, :1]
        live = iota((padded, 1), 0) < capacity
        scaled[s] = (jnp.where(live, gate, 0.0) * scaled[s].astype(f32)).astype(bf16)
        live16 = iota((16, 1), 0) < 16 - (padded - capacity)
        rows[s, padded - 16 :, :] = jnp.where(live16, tail, 0.0).astype(bf16)

    def shard_results(s, c):
        span = pl.ds(pl.multiple_of(s * padded, 16), padded)
        pre = dot(rows[s], w_ins[c])
        phi, slope = gelu_parts(pre)
        act_low = (pre * phi).astype(bf16)
        act[c, span, :] = act_low
        grad_pre = (dot_nt(scaled[s], w_outs[c]) * (phi + slope)).astype(bf16)
        gpre[c, span, :] = grad_pre
        return dot(act_low, w_outs[c]), dot_nt(grad_pre, w_ins[c])

    def send(j, result, grad_rows):
        s = paired(me, j, sources)
        out_low[s] = result.astype(bf16)
        back_low[s] = grad_rows.astype(bf16)

        @pl.when(j != 0)
        def _():
            for copy in result_copies(j):
                copy.start()

        @pl.when(j == 0)
        def _():
            for copy in keep:
                copy.start()

    def run(s, first, last, spot, carried):
        for c in range(first, last):
            result, grad_rows = shard_results(s, c)
            if c > first or carried:
                result = result + out_sum[spot]
                grad_rows = grad_rows + back_sum[spot]
            if c < last - 1 or last < shards:
                out_sum[spot] = result
                back_sum[spot] = grad_rows
        return result, grad_rows

    half = sources // 2

    @pl.loop(0, half)
    def _(i):
        j = partner(i)
        prepare(j)
        run(paired(me, j, sources), 0, EARLY, i, False)

    for c in range(EARLY, shards):
        for copy in weights_on(c):
            copy.wait()
        if c + 1 < shards:
            for copy in weights_on(c + 1):
                copy.start()

    @pl.loop(0, half)
    def _(i):
        j = partner(i)
        send(j, *run(paired(me, j, sources), EARLY, shards, i, True))

    @pl.loop(half, sources)
    def _(i):
        j = partner(i)
        prepare(j)
        send(j, *run(paired(me, j, sources), 0, shards, 0, False))

    for s in range(sources):
        rows_t[:, s * padded : (s + 1) * padded] = jnp.transpose(rows[s])
        gz_t[:, s * padded : (s + 1) * padded] = jnp.transpose(scaled[s])

    def weight_grads(c):
        return dot(rows_t[...], gpre[c]).astype(bf16), dot(gz_t[...], act[c]).astype(bf16)

    ring_out[:D, :], ring_out[D:, :] = weight_grads(1)
    step = exchange(ring_out, ring_in, ring_sem.at[0], ring_sem.at[1], right)
    step.start()
    for c in range(3, shards):
        grads[c - 2, :D, :], grads[c - 2, D:, :] = weight_grads(c)
    grads[0, :D, :], grads[0, D:, :] = weight_grads(0)
    second = weight_grads(2)
    for copy in keep:
        copy.wait()
    step.wait()
    for part in range(2):
        span = slice(part * D, part * D + D)
        ring[span, :] = (ring_in[span, :].astype(f32) + second[part].astype(f32)).astype(bf16)

    @pl.loop(1, sources)
    def _(j):
        row_copy(j).wait_send()
        for copy in result_copies(j):
            copy.wait()


def moe(slot_row, gate_row, normed_moe, gz, early, shards, capacity):
    sources, padded, unused = gz.shape
    tokens = normed_moe.shape[0]
    hidden = early[0][0].shape[1]
    total = sources * padded
    vmem = pl.BlockSpec(memory_space=pltpu.VMEM)
    anywhere = pl.BlockSpec(memory_space=pl.ANY)
    dma = pltpu.SemaphoreType.DMA
    return pl.pallas_call(
        functools.partial(moe_kernel, capacity, sources, shards),
        in_specs=[vmem] * 2 + [anywhere] * (2 + 2 * EARLY),
        out_specs=(anywhere, anywhere, vmem, vmem),
        out_shape=(
            jax.ShapeDtypeStruct(gz.shape, bf16),
            jax.ShapeDtypeStruct(gz.shape, bf16),
            jax.ShapeDtypeStruct((2 * D, hidden), bf16),
            jax.ShapeDtypeStruct((shards - 2, 2 * D, hidden), bf16),
        ),
        scratch_shapes=[
            pltpu.VMEM((tokens, D), bf16),
            pltpu.VMEM((shards, D, hidden), bf16),
            pltpu.VMEM((shards, hidden, D), bf16),
            pltpu.VMEM(gz.shape, bf16),
            pltpu.VMEM(gz.shape, bf16),
            pltpu.VMEM(gz.shape, bf16),
            pltpu.VMEM((8, D), f32),
            pltpu.VMEM((D, total), bf16),
            pltpu.VMEM((D, total), bf16),
            pltpu.VMEM((shards, total, hidden), bf16),
            pltpu.VMEM((shards, total, hidden), bf16),
            pltpu.VMEM((sources // 2, padded, D), f32),
            pltpu.VMEM((sources // 2, padded, D), f32),
            pltpu.VMEM(gz.shape, bf16),
            pltpu.VMEM(gz.shape, bf16),
            pltpu.VMEM((2 * D, hidden), bf16),
            pltpu.VMEM((2 * D, hidden), bf16),
            dma((2 + 2 * EARLY,)),
            dma((2, sources)),
            dma((2, sources)),
            dma((2, sources)),
            dma((2,)),
            dma((2, 2, shards)),
            dma((2,)),
        ],
        compiler_params=pltpu.CompilerParams(
            vmem_limit_bytes=61 * MIB, collective_id=1, has_side_effects=True
        ),
        cost_estimate=pl.CostEstimate(
            flops=12 * total * D * hidden * shards, bytes_accessed=20 * MIB, transcendentals=0
        ),
        name="moe",
    )(slot_row, gate_row, normed_moe, gz, *[part for pair in early for part in pair])


def combine_kernel(
    experts,
    windows,
    seg,
    w_proj,
    gain_moe,
    w_router,
    slot_col,
    cot,
    packed_in,
    context_in,
    lse,
    residual,
    normed_moe,
    gates,
    returned,
    back,
    counts,
    mixed_out,
    grad_residual_out,
    extra_out,
    grad_context,
    grad_proj,
    small,
    pair_grads,
    packed,
    context,
    mixed,
    grad_residual,
    extra,
    hot,
    seg_col,
    seg_row,
    router,
    grad_attn,
    grad_logits,
    grad_k,
    grad_v,
    bias,
    pair_k,
    pair_v,
    sems,
):
    tokens = cot.shape[0]
    slots_all, padded = returned.shape[0] * returned.shape[1], returned.shape[1]
    reads = (
        pltpu.make_async_copy(packed_in, packed, sems.at[0]),
        pltpu.make_async_copy(context_in, context, sems.at[1]),
    )
    writes = (
        pltpu.make_async_copy(mixed, mixed_out, sems.at[2]),
        pltpu.make_async_copy(grad_residual, grad_residual_out, sems.at[3]),
        pltpu.make_async_copy(extra, extra_out, sems.at[4]),
    )
    for read in reads:
        read.start()
    extra[...] = jnp.zeros_like(extra)
    seg_row[...] = seg[...].astype(f32)
    seg_col[...] = jnp.transpose(jnp.broadcast_to(seg_row[...], (LANES, tokens)))
    router[...] = jnp.zeros_like(router)
    router[:, :experts] = w_router[...]
    small[...] = jnp.zeros_like(small)
    small[2:4, :LANES] = counts[:2, :]

    @pl.loop(0, tokens // TILE)
    def _(i):
        rows = pl.ds(pl.multiple_of(i * TILE, TILE), TILE)
        grad_z = cot[rows, :].astype(f32)
        probs = gates[rows, :]
        slots = slot_col[rows, :]
        lane = iota((TILE, LANES), 1)
        rest = residual[rows, :]
        twice = probs + pltpu.roll(probs, experts, axis=1)
        place = jnp.where(lane < experts, lane, lane - experts).astype(f32) * float(padded)
        total = rest
        grad_gates = jnp.zeros((TILE, LANES), f32)
        spots = iota((TILE, slots_all), 1).astype(f32)
        picks = []
        for k in range(TOP):
            mine = (slots >= 0.0) & (lane >= k * experts) & (lane < (k + 1) * experts)
            spot = jnp.sum(jnp.where(mine, place + slots + 1.0, 0.0), axis=1, keepdims=True) - 1.0
            hot[k * TILE : (k + 1) * TILE, :] = (spots == spot).astype(f32).astype(bf16)
            picks.append(mine)
        back_total = dot(hot[:TILE, :] + hot[TILE:, :], back[...].reshape(slots_all, D))
        results = dot(hot[...], returned[...].reshape(slots_all, D))
        for k in range(TOP):
            result = results[k * TILE : (k + 1) * TILE]
            total = total + jnp.sum(jnp.where(picks[k], twice, 0.0), axis=1, keepdims=True) * result
            inner = jnp.sum(result * grad_z, axis=1, keepdims=True)
            grad_gates = grad_gates + jnp.where(picks[k], inner, 0.0)
        grad_gates = grad_gates + pltpu.roll(grad_gates, LANES - experts, axis=1)
        grad_gates = jnp.where(lane < experts, grad_gates, 0.0)
        mixed[rows, :] = total.astype(bf16)
        gate_inner = jnp.sum(probs * grad_gates, axis=1, keepdims=True)
        high, low = split2(probs * (grad_gates - gate_inner))
        grad_logits[rows, :LANES] = high
        grad_logits[rows, LANES:] = low
        grad_normed = back_total + dot_nt(high, router[...]) + dot_nt(low, router[...])
        normal, inverse = norm_parts(rest)
        grad_norm, grad_gain = norm_back(grad_normed, gain_moe[...], normal, inverse)
        small[1:2, :] += grad_gain
        grad_rest = grad_z + grad_norm
        grad_residual[rows, :] = grad_rest
        attn = grad_rest.astype(bf16)
        grad_attn[rows, :] = attn
        grad_context[rows, :] = dot_nt(attn, w_proj[...]).astype(bf16)

    for write in writes[:2]:
        write.start()
    reads[1].wait()
    both = dot_tn(normed_moe[...], grad_logits[...])
    both = jnp.transpose(both[:, :LANES] + both[:, LANES:])
    small[8:, :] = both[:experts]
    grad_proj[...] = dot_tn(context[...], grad_attn[...])
    blocks = tokens // QB
    reads[0].wait()

    @pl.when(windows[3 * blocks] != 1)
    def _():
        grad_k[...] = jnp.zeros_like(grad_k)
        grad_v[...] = jnp.zeros_like(grad_v)

        @pl.loop(0, blocks)
        def _(block):
            query = pl.multiple_of(block * QB, QB)

            @pl.when(windows[2 * blocks + block] != 1)
            def _():
                bias = window_bias(seg_col, seg_row, 0, SEQ, query)
                spans = [slice(pair * PAIR, (pair + 1) * PAIR) for pair in range(PAIRS)]
                keys = pl.ds(0, SEQ)
                queries = [
                    (stack_heads(packed[pl.ds(query, QB), span]) * HEAD ** (-0.5)).astype(bf16) for span in spans
                ]
                grads = [stack_heads(grad_context[pl.ds(query, QB), span]) for span in spans]
                probs = []
                grad_probs = []
                for pair, span in enumerate(spans):
                    k = packed[keys, D + span.start : D + span.stop]
                    v = packed[keys, 2 * D + span.start : 2 * D + span.stop]
                    probs.append(jnp.exp(dot_nt(k, queries[pair]) + bias - lse[pl.ds(block, 1), pair, :]))
                    grad_probs.append(dot_nt(v, grads[pair]))
                grad_scores = []
                for pair, span in enumerate(spans):
                    grad_v[keys, span] += dot(probs[pair].astype(bf16), grads[pair])
                    weighted = probs[pair] * grad_probs[pair]
                    inner = jnp.sum(weighted, axis=0, keepdims=True)
                    grad_scores.append((weighted - probs[pair] * inner).astype(bf16))
                for pair, span in enumerate(spans):
                    k = packed[keys, D + span.start : D + span.stop]
                    grad_k[keys, span] += dot(grad_scores[pair], queries[pair])
                    grad_q = unstack_cols(dot_tn(k, grad_scores[pair])) * HEAD ** (-0.5)
                    extra[pl.ds(query, QB), span] = grad_q.astype(bf16)
                grad_context[pl.ds(query, QB), :] = jnp.zeros((QB, D), bf16)

        extra[:, D : 2 * D] = grad_k[...].astype(bf16)
        extra[:, 2 * D :] = grad_v[...].astype(bf16)

    writes[2].start()
    slab_bias(bias, seg_col, seg_row[...])
    pair_backward(0, packed, grad_context, lse, extra, bias, pair_k, pair_v, pair_grads)
    for write in writes:
        write.wait()


def combine(experts, windows, *operands):
    cot = operands[5]
    returned = operands[-3]
    tokens = cot.shape[0]
    vmem = pl.BlockSpec(memory_space=pltpu.VMEM)
    anywhere = pl.BlockSpec(memory_space=pl.ANY)
    return pl.pallas_call(
        functools.partial(combine_kernel, experts),
        in_specs=[pl.BlockSpec(memory_space=pltpu.SMEM)] + [vmem] * 6 + [anywhere] * 2 + [vmem] * (len(operands) - 8),
        out_specs=[anywhere, anywhere, anywhere, vmem, vmem, vmem, vmem],
        out_shape=(
            jax.ShapeDtypeStruct((tokens, D), bf16),
            jax.ShapeDtypeStruct((tokens, D), f32),
            jax.ShapeDtypeStruct((tokens, 3 * D), bf16),
            jax.ShapeDtypeStruct((tokens, D), bf16),
            jax.ShapeDtypeStruct((D, D), f32),
            jax.ShapeDtypeStruct((8 + experts, D), f32),
            jax.ShapeDtypeStruct((tokens, 3 * PAIR), bf16),
        ),
        scratch_shapes=[
            pltpu.VMEM((tokens, 3 * D), bf16),
            pltpu.VMEM((tokens, D), bf16),
            pltpu.VMEM((tokens, D), bf16),
            pltpu.VMEM((tokens, D), f32),
            pltpu.VMEM((tokens, 3 * D), bf16),
            pltpu.VMEM((TOP * TILE, returned.shape[0] * returned.shape[1]), bf16),
            pltpu.VMEM((tokens, LANES), f32),
            pltpu.VMEM((1, tokens), f32),
            pltpu.VMEM((D, LANES), bf16),
            pltpu.VMEM((tokens, D), bf16),
            pltpu.VMEM((tokens, 2 * LANES), bf16),
            pltpu.VMEM((tokens, D), f32),
            pltpu.VMEM((tokens, D), f32),
            pltpu.VMEM((SLAB_AT[-1], QB), f32),
            pltpu.VMEM((tokens, PAIR), f32),
            pltpu.VMEM((tokens, PAIR), f32),
            pltpu.SemaphoreType.DMA((5,)),
        ],
        compiler_params=pltpu.CompilerParams(vmem_limit_bytes=60 * MIB),
        cost_estimate=pl.CostEstimate(
            flops=30 * 1024 * MIB, bytes_accessed=30 * MIB, transcendentals=4 * MIB
        ),
        name="combine",
    )(windows, *operands)


SLAB_AT = tuple(sum(high - low for low, high in SLABS[:b]) for b in range(len(SLABS) + 1))


def slab_bias(bias, seg_col, seg_row):
    for b, (low, high) in enumerate(SLABS):
        same = seg_col[low:high, :] == seg_row[:, b * QB : (b + 1) * QB]
        bias[SLAB_AT[b] : SLAB_AT[b + 1], :] = jnp.where(same, 0.0, -1e30)


def pair_backward(pair, packed, grad_context, lse, extra, bias, grad_k, grad_v, out):
    def span(which):
        return pl.ds(pl.multiple_of(which * D + pair * PAIR, PAIR), PAIR)

    grad_k[...] = extra[:, span(1)].astype(f32)
    grad_v[...] = extra[:, span(2)].astype(f32)
    for group in range(0, len(SLABS), 4):
        blocks = range(group, group + 4)
        queries, grads, probs, grad_probs, grad_scores = [], [], [], [], []
        for b in blocks:
            low, high = SLABS[b]
            rows = slice(b * QB, (b + 1) * QB)
            queries.append((stack_heads(packed[rows, span(0)]) * HEAD ** (-0.5)).astype(bf16))
            grads.append(stack_heads(grad_context[rows, span(0)]))
            masked = bias[SLAB_AT[b] : SLAB_AT[b + 1], :]
            scores = dot_nt(packed[low:high, span(1)], queries[-1]) + jnp.concatenate([masked, masked], axis=1)
            probs.append(jnp.exp(scores - lse[b, pl.ds(pair, 1), :]))
            grad_probs.append(dot_nt(packed[low:high, span(2)], grads[-1]))
        for i, b in enumerate(blocks):
            low, high = SLABS[b]
            grad_v[low:high, :] += dot(probs[i].astype(bf16), grads[i])
            weighted = probs[i] * grad_probs[i]
            inner = jnp.sum(weighted, axis=0, keepdims=True)
            grad_scores.append((weighted - probs[i] * inner).astype(bf16))
        for i, b in enumerate(blocks):
            low, high = SLABS[b]
            rows = slice(b * QB, (b + 1) * QB)
            grad_k[low:high, :] += dot(grad_scores[i], queries[i])
            grad_q = unstack_cols(dot_tn(packed[low:high, span(1)], grad_scores[i])) * HEAD ** (-0.5)
            out[rows, :PAIR] = (grad_q + extra[rows, span(0)].astype(f32)).astype(bf16)
    out[:, PAIR : 2 * PAIR] = grad_k[...].astype(bf16)
    out[:, 2 * PAIR :] = grad_v[...].astype(bf16)


def shared_kernel(
    chips,
    planes,
    seg,
    lse,
    partial,
    gain_attn,
    first_in,
    packed_in,
    grad_context_in,
    extra_in,
    normed_attn_in,
    grad_proj_in,
    w_qkv_in,
    tok_in,
    grad_residual_in,
    summed,
    small,
    grad_tokens_out,
    pair_grads,
    packed,
    grad_context,
    extra,
    normed_attn,
    grad_proj,
    w_qkv,
    tok,
    grad_residual,
    grad_tokens,
    normed_t,
    seg_col,
    bias,
    grad_k,
    grad_v,
    grad_packed,
    half,
    core_out,
    core_in,
    chip_out,
    chip_in,
    plane_out,
    plane_in,
    small_own,
    small_core,
    small_chip,
    small_plane,
    load_sem,
    store_sem,
    core_sem,
    chip_sem,
    plane_sem,
    plane_sem2,
    chip_sem2,
    core_sem2,
    small_sem,
    small_chip_sem,
    small_plane_sem,
):
    tokens = tok.shape[0]
    stages = 16 // planes
    pairs = PAIRS // stages
    tiles = tokens // TILE
    wide = lax.axis_index("wide")
    plane = lax.axis_index("narrow")
    core = lax.rem(wide, 2)
    chip = wide // 2
    share = D // (2 * chips)
    partner = (chip * 2 + 1 - core, plane)
    mine = pl.ds(pl.multiple_of(core * (D // 2), D // 2), D // 2)
    other = pl.ds(pl.multiple_of((1 - core) * (D // 2), D // 2), D // 2)
    chunk = pl.ds(pl.multiple_of(core * (D // 2) + chip * share, share), share)
    own_chunk = pl.ds(pl.multiple_of(chip * share, share), share)

    loads = [
        pltpu.make_async_copy(source, target, load_sem.at[i])
        for i, (source, target) in enumerate(
            (
                (first_in, pair_grads),
                (normed_attn_in, normed_attn),
                (grad_proj_in, grad_proj),
                (packed_in, packed),
                (grad_context_in, grad_context),
                (extra_in, extra),
                (w_qkv_in, w_qkv),
                (tok_in, tok),
                (grad_residual_in, grad_residual),
            )
        )
    ]
    for load in loads:
        load.start()

    def chip_at(j):
        to = shifted(chip, j, chips)
        return to, (to * 2 + core, plane)

    def plane_at(j):
        to = shifted(plane, j, planes)
        return to, (wide, to)

    barrier = pltpu.get_barrier_semaphore()
    pl.semaphore_signal(barrier, inc=1, device_id=partner, device_id_type=MESH)

    @pl.loop(1, chips)
    def _(j):
        pl.semaphore_signal(barrier, inc=1, device_id=chip_at(j)[1], device_id_type=MESH)

    @pl.loop(1, planes)
    def _(j):
        pl.semaphore_signal(barrier, inc=1, device_id=plane_at(j)[1], device_id_type=MESH)

    def blocks(stage):
        return pl.ds(stage * planes, planes)

    def core_copy(stage):
        at = blocks(stage)
        return exchange(core_out.at[at], core_in.at[at], core_sem.at[0, stage], core_sem.at[1, stage], partner)

    def chip_copy(stage, j):
        to, device = chip_at(j)
        rows = pl.ds(pl.multiple_of(to * share, share), share)
        at = blocks(stage)
        return exchange(
            chip_out.at[at, rows], chip_in.at[j, at], chip_sem.at[0, stage, j], chip_sem.at[1, stage, j], device
        )

    def plane_copy(stage, j):
        to, device = plane_at(j)
        return exchange(
            plane_out.at[stage * planes + to],
            plane_in.at[j, stage],
            plane_sem.at[0, stage, j],
            plane_sem.at[1, stage, j],
            device,
        )

    def plane_back(stage, j):
        spot = summed.at[stage * planes + plane, chunk]
        return exchange(spot, spot, plane_sem2.at[0, stage, j], plane_sem2.at[1, stage, j], plane_at(j)[1])

    def chip_back(stage, j):
        spot = summed.at[blocks(stage), chunk]
        return exchange(spot, spot, chip_sem2.at[0, stage, j], chip_sem2.at[1, stage, j], chip_at(j)[1])

    def core_back(stage):
        spot = summed.at[blocks(stage), mine]
        return exchange(spot, spot, core_sem2.at[0, stage], core_sem2.at[1, stage], partner)

    def small_core_copy():
        return exchange(small_own, small_core, small_sem.at[0], small_sem.at[1], partner)

    def small_chip_copy(j):
        spot = small_chip.at[chip]
        return exchange(spot, spot, small_chip_sem.at[0, j], small_chip_sem.at[1, j], chip_at(j)[1])

    def small_plane_copy(j):
        spot = small_plane.at[plane]
        return exchange(spot, spot, small_plane_sem.at[0, j], small_plane_sem.at[1, j], plane_at(j)[1])

    def pair_products(pair):
        spare = dot(normed_t[other, :], pair_grads[...])
        own = dot(normed_t[mine, :], pair_grads[...])
        lanes = pl.ds(pl.multiple_of(pair * PAIR, PAIR), PAIR)
        for which in range(3):
            at = slice(which * PAIR, (which + 1) * PAIR)
            core_out[pair * 4 + which] = spare[:, at].astype(bf16)
            half[pair * 4 + which] = own[:, at]
            grad_packed[:, pl.ds(pl.multiple_of(which * D + pair * PAIR, PAIR), PAIR)] = pair_grads[:, at]
        core_out[pair * 4 + 3] = grad_proj[other, lanes].astype(bf16)
        half[pair * 4 + 3] = grad_proj[mine, lanes]

    def chip_stage(stage):
        core_copy(stage).wait_recv()
        at = blocks(stage)
        total = half[at] + core_in[at].astype(f32)
        half[at] = total
        chip_out[at] = total.astype(bf16)

        @pl.loop(1, chips)
        def _(j):
            chip_copy(stage, j).start()

    def plane_stage(stage):
        at = blocks(stage)
        total = half[at, own_chunk, :]
        for j in range(1, chips):
            chip_copy(stage, j).wait_recv()
            total = total + chip_in[j, at].astype(f32)
        half[at, own_chunk, :] = total
        plane_out[at] = total.astype(bf16)

        @pl.loop(1, planes)
        def _(j):
            plane_copy(stage, j).start()

    def own_stage(stage):
        total = half[stage * planes + plane, own_chunk, :]
        for j in range(1, planes):
            plane_copy(stage, j).wait_recv()
            total = total + plane_in[j, stage].astype(f32)
        summed[stage * planes + plane, chunk, :] = total.astype(bf16)

        @pl.loop(1, planes)
        def _(j):
            plane_back(stage, j).start()

    def gather_stage(stage):
        @pl.loop(1, planes)
        def _(j):
            plane_back(stage, j).wait_recv()

        @pl.loop(1, chips)
        def _(j):
            chip_back(stage, j).start()

    def last_stage(stage):
        @pl.loop(1, chips)
        def _(j):
            chip_back(stage, j).wait_recv()

        core_back(stage).start()

    def norm_tile(i):
        rows = slice(i * TILE, (i + 1) * TILE)
        grad_normed = dot_nt(grad_packed[rows, :], w_qkv[...])
        normal, inverse = norm_parts(tok[rows, :].astype(f32))
        grad_norm, grad_gain = norm_back(grad_normed, gain_attn[...], normal, inverse)
        small_own[0:1, :] += grad_gain
        grad_tokens[rows, :] = grad_residual[rows, :] + grad_norm

    small_own[...] = partial[...]
    seg_row = seg[...].astype(f32)
    seg_col[...] = jnp.transpose(jnp.broadcast_to(seg_row, (LANES, tokens)))
    slab_bias(bias, seg_col, seg_row)
    for load in loads[:3]:
        load.wait()
    normed_t[...] = jnp.transpose(normed_attn[...])
    pair_products(0)
    pl.semaphore_wait(barrier, chips + planes - 1)
    if pairs == 1:
        core_copy(0).start()
    for load in loads[3:6]:
        load.wait()

    @pl.loop(1, PAIRS)
    def _(pair):
        pair_backward(pair, packed, grad_context, lse, extra, bias, grad_k, grad_v, pair_grads)
        pair_products(pair)

        @pl.when(lax.rem(pair + 1, pairs) == 0)
        def _():
            stage = pair // pairs
            core_copy(stage).start()

            @pl.when(stage > 0)
            def _():
                chip_stage(stage - 1)

            @pl.when(stage > 1)
            def _():
                plane_stage(stage - 2)

            @pl.when(stage > 2)
            def _():
                own_stage(stage - 3)

    for load in loads[6:]:
        load.wait()
    steps = (chip_stage, plane_stage, own_stage, gather_stage, last_stage)
    for late in range(len(steps)):
        if late == 0:
            norm_tile(0)
        for i, step in enumerate(steps):
            stage = stages - 1 + late - i
            if i >= late and 0 <= stage < stages:
                step(stage)
        if late == 0:
            for i in range(1, tiles):
                norm_tile(i)
            small_core_copy().start()
            store = pltpu.make_async_copy(grad_tokens, grad_tokens_out, store_sem)
            store.start()
        if late == 1:
            small_core_copy().wait_recv()
            small_chip[chip] = small_own[...] + small_core[...]

            @pl.loop(1, chips)
            def _(j):
                small_chip_copy(j).start()

        if late == 2:

            @pl.loop(1, chips)
            def _(j):
                small_chip_copy(j).wait_recv()

            total = small_chip[0]
            for c in range(1, chips):
                total = total + small_chip[c]
            small_plane[plane] = total

            @pl.loop(1, planes)
            def _(j):
                small_plane_copy(j).start()

    @pl.loop(1, planes)
    def _(j):
        small_plane_copy(j).wait_recv()

    total = small_plane[0]
    for c in range(1, planes):
        total = total + small_plane[c]
    small[...] = total
    store.wait()

    @pl.loop(0, stages)
    def _(stage):
        core_back(stage).wait()
        core_copy(stage).wait_send()

        @pl.loop(1, chips)
        def _(j):
            chip_back(stage, j).wait_send()
            chip_copy(stage, j).wait_send()

        @pl.loop(1, planes)
        def _(j):
            plane_back(stage, j).wait_send()
            plane_copy(stage, j).wait_send()

    @pl.loop(1, planes)
    def _(j):
        small_plane_copy(j).wait_send()

    @pl.loop(1, chips)
    def _(j):
        small_chip_copy(j).wait_send()

    small_core_copy().wait_send()


def shared_gradients(*operands):
    partial, packed = operands[2], operands[5]
    tokens = packed.shape[0]
    chips = lax.axis_size("wide") // 2
    planes = lax.axis_size("narrow")
    stages = 16 // planes
    share = D // (2 * chips)
    rows = partial.shape[0]
    dma = pltpu.SemaphoreType.DMA
    vmem = pl.BlockSpec(memory_space=pltpu.VMEM)
    anywhere = pl.BlockSpec(memory_space=pl.ANY)
    return pl.pallas_call(
        functools.partial(shared_kernel, chips, planes),
        in_specs=[vmem] * 4 + [anywhere] * 9,
        out_specs=(vmem, vmem, anywhere),
        out_shape=(
            jax.ShapeDtypeStruct((16, D, LANES), bf16),
            jax.ShapeDtypeStruct((rows, D), f32),
            jax.ShapeDtypeStruct((tokens, D), f32),
        ),
        scratch_shapes=[pltpu.VMEM(operand.shape, operand.dtype) for operand in operands[4:]]
        + [
            pltpu.VMEM((tokens, D), f32),
            pltpu.VMEM((D, tokens), bf16),
            pltpu.VMEM((tokens, LANES), f32),
            pltpu.VMEM((SLAB_AT[-1], QB), f32),
            pltpu.VMEM((tokens, PAIR), f32),
            pltpu.VMEM((tokens, PAIR), f32),
            pltpu.VMEM((tokens, 3 * D), bf16),
            pltpu.VMEM((16, D // 2, LANES), f32),
            pltpu.VMEM((16, D // 2, LANES), bf16),
            pltpu.VMEM((16, D // 2, LANES), bf16),
            pltpu.VMEM((16, D // 2, LANES), bf16),
            pltpu.VMEM((chips, 16, share, LANES), bf16),
            pltpu.VMEM((16, share, LANES), bf16),
            pltpu.VMEM((planes, stages, share, LANES), bf16),
            pltpu.VMEM((rows, D), f32),
            pltpu.VMEM((rows, D), f32),
            pltpu.VMEM((chips, rows, D), f32),
            pltpu.VMEM((planes, rows, D), f32),
            dma((9,)),
            dma,
            dma((2, stages)),
            dma((2, stages, chips)),
            dma((2, stages, planes)),
            dma((2, stages, planes)),
            dma((2, stages, chips)),
            dma((2, stages)),
            dma((2,)),
            dma((2, chips)),
            dma((2, planes)),
        ],
        compiler_params=pltpu.CompilerParams(
            vmem_limit_bytes=58 * MIB, collective_id=2, has_side_effects=True
        ),
        cost_estimate=pl.CostEstimate(
            flops=12 * tokens * D * D, bytes_accessed=16 * MIB, transcendentals=0
        ),
        name="shared_gradients",
    )(*operands)


def finish_kernel(experts, summed, ring, own, small, tokens_in, qkv, proj, grad_in, grad_out, rest, router, tokens_out, sem):
    copy = pltpu.make_async_copy(tokens_in, tokens_out, sem)
    copy.start()
    for n in range(16):
        pair, which = divmod(n, 4)
        lanes = slice(pair * PAIR, (pair + 1) * PAIR)
        if which < 3:
            qkv[:, which * D + lanes.start : which * D + lanes.stop] = summed[n].astype(f32)
        else:
            proj[:, lanes] = summed[n].astype(f32)
    total = ring[...].astype(f32) + own[...].astype(f32)
    grad_in[0] = total[:D, :]
    grad_out[0] = jnp.transpose(total[D:, :])
    rest[...] = small[:8, :]
    router[...] = jnp.transpose(jnp.concatenate([small[8:, :], jnp.zeros((LANES - experts, D), f32)], axis=0))[
        :, :experts
    ]
    copy.wait()


def finish(experts, summed, ring, own, small, tokens_in):
    hidden = own.shape[1]
    vmem = pl.BlockSpec(memory_space=pltpu.VMEM)
    anywhere = pl.BlockSpec(memory_space=pl.ANY)
    return pl.pallas_call(
        functools.partial(finish_kernel, experts),
        in_specs=[vmem, vmem, vmem, vmem, anywhere],
        out_specs=[vmem] * 6 + [anywhere],
        out_shape=(
            jax.ShapeDtypeStruct((D, 3 * D), f32),
            jax.ShapeDtypeStruct((D, D), f32),
            jax.ShapeDtypeStruct((1, D, hidden), f32),
            jax.ShapeDtypeStruct((1, hidden, D), f32),
            jax.ShapeDtypeStruct((8, D), f32),
            jax.ShapeDtypeStruct((D, experts), f32),
            jax.ShapeDtypeStruct(tokens_in.shape, f32),
        ),
        scratch_shapes=[pltpu.SemaphoreType.DMA],
        compiler_params=pltpu.CompilerParams(vmem_limit_bytes=40 * MIB),
        cost_estimate=pl.CostEstimate(flops=0, bytes_accessed=14 * MIB, transcendentals=0),
        name="finish",
    )(summed, ring, own, small, tokens_in)


def per_device(
    tokens,
    segment_ids,
    expert_picks,
    priority_ranks,
    gain_attn,
    w_qkv,
    w_proj,
    gain_moe,
    w_router,
    w_in,
    w_out,
    cotangent,
):
    experts = w_router.shape[1]
    capacity = (21 * TOP * TOK_DEV + 20 * experts - 1) // (20 * experts)
    padded = (capacity + 3 + 15) // 16 * 16
    gain_attn = gain_attn.reshape(1, D)
    gain_moe = gain_moe.reshape(1, D)
    seg = segment_ids.reshape(1, SEQ)
    first = jnp.sum((segment_ids[None, :] < segment_ids[0::QB, None]).astype(jnp.int32), axis=1)
    after = jnp.sum((segment_ids[None, :] <= segment_ids[QB - 1 :: QB, None]).astype(jnp.int32), axis=1)
    low = jnp.minimum(first // 16 * 16, SEQ - WINDOW)
    fits = (after - low <= WINDOW).astype(jnp.int32)
    slab_low = jnp.array([slab[0] for slab in SLABS], jnp.int32)
    slab_high = jnp.array([slab[1] for slab in SLABS], jnp.int32)
    slab_fits = ((first >= slab_low) & (after <= slab_high)).astype(jnp.int32)
    windows = jnp.concatenate([low, fits, slab_fits, jnp.min(slab_fits, keepdims=True)])

    line = lax.axis_size("narrow")
    ring_steps = [(i, (i + 1) % line) for i in range(line)]
    together = lax.optimization_barrier

    def pass_on(values):
        return lax.ppermute(values, "narrow", ring_steps)

    early = [(w_in[0], w_out[0])]
    early.append(pass_on(early[0]))
    slot_col, slot_row, counts, gz_send, normed_attn, packed = route(
        expert_picks, priority_ranks, cotangent, tokens, gain_attn, w_qkv, experts, capacity, padded
    )
    gz = lax.all_to_all(gz_send, "wide", split_axis=0, concat_axis=0, tiled=True)
    early.append(pass_on(together((early[1], slot_row))[0]))
    context, lse, residual, normed_moe, gates, gate_row = forward(
        windows, tokens, seg, packed, w_proj, gain_moe, w_router
    )
    returned, back, ring, grads = moe(slot_row, gate_row, normed_moe, gz, early, line, capacity)
    ring = pass_on(ring)
    mixed, grad_residual, extra, grad_context, grad_proj, partial, first_pair = combine(
        experts,
        windows,
        seg,
        w_proj,
        gain_moe,
        w_router,
        slot_col,
        cotangent,
        packed,
        context,
        lse,
        residual,
        normed_moe,
        gates,
        returned,
        back,
        counts,
    )
    ring, grad_context = together((ring, grad_context))
    for k in range(1, line - 2):
        ring = pass_on((ring.astype(f32) + grads[k].astype(f32)).astype(bf16))
    summed, small, grad_tokens = shared_gradients(
        seg,
        lse,
        partial,
        gain_attn,
        first_pair,
        packed,
        grad_context,
        extra,
        normed_attn,
        grad_proj,
        w_qkv,
        tokens,
        grad_residual,
    )
    grad_qkv, grad_proj, grad_in, grad_out, rest, grad_router, grad_tokens = finish(
        experts, summed, ring, grads[0], small, grad_tokens
    )
    counted = rest[2:4, :experts].astype(jnp.int32)
    return (
        mixed,
        grad_tokens,
        rest[0],
        grad_qkv,
        grad_proj,
        rest[1],
        grad_router,
        grad_in,
        grad_out,
        counted[0],
        counted[1] - counted[0],
    )


def solution(mesh):
    both = ("wide", "narrow")
    placed = (
        P(both, None),
        P(both),
        P(both, None),
        P(both, None),
        P(),
        P(),
        P(),
        P(),
        P(),
        P("wide", None, "narrow"),
        P("wide", "narrow", None),
        P(both, None),
    )
    return jax.shard_map(
        per_device,
        mesh=mesh,
        in_specs=placed,
        out_specs=(
            P(both, None),
            P(both, None),
            P(),
            P(),
            P(),
            P(),
            P(),
            P("wide", None, "narrow"),
            P("wide", "narrow", None),
            P(),
            P(),
        ),
        check_vma=False,
    )
```

```python
import functools

import jax
import jax.numpy as jnp
from jax import lax
from jax.experimental import pallas as pl
from jax.experimental.pallas import tpu as pltpu
from jax.sharding import PartitionSpec as P

D = 512
HEADS = 8
HEAD = 64
PAIRS = HEADS // 2
PAIR = 2 * HEAD
TOP = 2
SEQ = 1024
TOK_DEV = 1024
LANES = 128
QB = 128
WINDOW = 432
TILE = 256
SLABS = tuple((max(0, QB * (b - 2)), min(SEQ, QB * (b + 3))) for b in range(SEQ // QB))
MIB = 1024 * 1024
MESH = pl.DeviceIdType.MESH
VMEM_LIMIT = 62 * MIB

f32 = jnp.float32
bf16 = jnp.bfloat16
NT = (((1,), (1,)), ((), ()))
TN = (((0,), (0,)), ((), ()))


def dot(a, b):
    return jnp.dot(a, b, preferred_element_type=f32)


def dot_nt(a, b):
    return lax.dot_general(a, b, NT, preferred_element_type=f32)


def dot_tn(a, b):
    return lax.dot_general(a, b, TN, preferred_element_type=f32)


def iota(shape, dim):
    return lax.broadcasted_iota(jnp.int32, shape, dim)


def norm_parts(values_in):
    centered = values_in - jnp.mean(values_in, axis=-1, keepdims=True)
    variance = jnp.mean(centered * centered, axis=-1, keepdims=True)
    inverse = lax.rsqrt(variance + 1e-06)
    return (centered * inverse, inverse)


def norm_back(grad_normed, gain, normalized, inverse):
    grad_gain = jnp.sum(grad_normed * normalized, axis=0, keepdims=True)
    scaled = grad_normed * gain
    inner = scaled - jnp.mean(scaled, axis=-1, keepdims=True)
    inner = inner - normalized * jnp.mean(scaled * normalized, axis=-1, keepdims=True)
    return (inner * inverse, grad_gain)


def split2(values_in):
    high = values_in.astype(bf16)
    low = (values_in - high.astype(f32)).astype(bf16)
    return high, low


def row_to_col(row):
    n = row.shape[1]
    return jnp.transpose(jnp.broadcast_to(row, (LANES, n)))[:, :1]


def loading(sources, targets, sems):
    copies = [pltpu.make_async_copy(source, target, sems.at[i]) for i, (source, target) in enumerate(zip(sources, targets))]
    for copy in copies:
        copy.start()
    return copies


def like(operands):
    return [pltpu.VMEM(operand.shape, operand.dtype) for operand in operands]


def route_kernel(
    experts,
    capacity,
    picks,
    ranks,
    seg,
    gain_attn,
    cot_in,
    tok_in,
    w_qkv_in,
    slot_col,
    slot_row,
    counts,
    windows,
    gz_out,
    normed_out,
    packed_out,
    cot,
    tok,
    w_qkv,
    gz_send,
    normed_attn,
    packed,
    load_sem,
    gz_sem,
    sems,
):
    loads = loading((cot_in, tok_in, w_qkv_in), (cot, tok, w_qkv), load_sem)
    tokens = ranks.shape[1]
    padded = gz_send.shape[1]
    rank_row = ranks[...].astype(f32)
    rank_col = row_to_col(rank_row)
    lane = iota((tokens, LANES), 1)
    pick0 = row_to_col(picks[0:1, :].astype(f32)).astype(jnp.int32)
    pick1 = row_to_col(picks[1:2, :].astype(f32)).astype(jnp.int32)
    hot = jnp.where(lane == jnp.where(lane < experts, pick0, pick1 + experts), 1.0, 0.0).astype(f32)
    before = (rank_row < rank_col).astype(f32).astype(bf16)
    earlier = dot(before, hot.astype(bf16))
    total = jnp.sum(hot, axis=0, keepdims=True)
    total = jnp.broadcast_to(total, (8, LANES))
    lane8 = iota((8, LANES), 1)
    first = jnp.where(lane8 < experts, total, 0.0)
    earlier = earlier + pltpu.roll(first, experts, axis=1)[:1]
    kept = (hot > 0.5) & (earlier < float(capacity))
    slots = jnp.where(kept, earlier, -1.0)
    slot_col[...] = slots
    slots = jnp.maximum(slots, pltpu.roll(slots, LANES - experts, axis=1))
    slots = jnp.where(lane < experts, slots, -1.0)
    slot_row[...] = jnp.transpose(slots)[:experts]
    kept_lane = jnp.sum(jnp.where(slots >= 0.0, 1.0, 0.0), axis=0, keepdims=True)
    both = total + pltpu.roll(total, LANES - experts, axis=1)
    both = jnp.where(lane8 < experts, both, 0.0)
    sub8 = iota((8, LANES), 0)
    counts[...] = jnp.where(sub8 == 0, kept_lane, jnp.where(sub8 == 1, both, 0.0))

    blocks = tokens // QB
    lane_row = iota((1, LANES), 1)
    plan = jnp.where(lane_row == 3 * blocks, 1.0, 0.0)
    for b, (slab_low, slab_high) in enumerate(SLABS):
        opening = seg[:, b * QB : b * QB + 1]
        closing = seg[:, (b + 1) * QB - 1 : (b + 1) * QB]
        first = jnp.sum(jnp.where(seg[...] < opening, 1.0, 0.0), axis=1, keepdims=True)
        after = jnp.sum(jnp.where(seg[...] <= closing, 1.0, 0.0), axis=1, keepdims=True)
        low = jnp.minimum(jnp.floor(first * (1.0 / 16)) * 16.0, float(SEQ - WINDOW))
        fits = jnp.where(after - low <= float(WINDOW), 1.0, 0.0)
        inside = jnp.where(first >= float(slab_low), 1.0, 0.0) * jnp.where(after <= float(slab_high), 1.0, 0.0)
        plan = jnp.where(lane_row == b, low, plan)
        plan = jnp.where(lane_row == blocks + b, fits, plan)
        plan = jnp.where(lane_row == 2 * blocks + b, inside, plan)
        plan = jnp.where(lane_row == 3 * blocks, plan * inside, plan)
    windows[...] = plan.astype(jnp.int32)
    loads[0].wait()

    @pl.loop(0, experts)
    def _(e):
        chosen = iota((padded, tokens), 0).astype(f32) == slot_row[pl.ds(e, 1), :]
        gz_send[e] = dot(chosen.astype(f32).astype(bf16), cot[...]).astype(bf16)
        pltpu.make_async_copy(gz_send.at[e], gz_out.at[e], gz_sem.at[e]).start()

    def stores(i):
        rows = pl.ds(pl.multiple_of(i * TILE, TILE), TILE)
        return (
            pltpu.make_async_copy(normed_attn.at[rows], normed_out.at[rows], sems.at[0, i]),
            pltpu.make_async_copy(packed.at[rows], packed_out.at[rows], sems.at[1, i]),
        )

    for load in loads[1:]:
        load.wait()

    @pl.loop(0, tokens // TILE)
    def _(i):
        rows = pl.ds(pl.multiple_of(i * TILE, TILE), TILE)
        normal, unused = norm_parts(tok[rows, :].astype(f32))
        normed = (normal * gain_attn[...]).astype(bf16)
        normed_attn[rows, :] = normed
        packed[rows, :] = dot(normed, w_qkv[...]).astype(bf16)
        for store in stores(i):
            store.start()

    @pl.loop(0, experts)
    def _(e):
        pltpu.make_async_copy(gz_send.at[e], gz_out.at[e], gz_sem.at[e]).wait()

    @pl.loop(0, tokens // TILE)
    def _(i):
        for store in stores(i):
            store.wait()


def route(picks, ranks, seg, gain_attn, cot, tok, w_qkv, experts, capacity, padded):
    tokens = tok.shape[0]
    vmem = pl.BlockSpec(memory_space=pltpu.VMEM)
    anywhere = pl.BlockSpec(memory_space=pl.ANY)
    return pl.pallas_call(
        functools.partial(route_kernel, experts, capacity),
        in_specs=[vmem] * 4 + [anywhere] * 3,
        out_shape=(
            jax.ShapeDtypeStruct((tokens, LANES), f32),
            jax.ShapeDtypeStruct((experts, tokens), f32),
            jax.ShapeDtypeStruct((8, LANES), f32),
            jax.ShapeDtypeStruct((1, LANES), jnp.int32),
            jax.ShapeDtypeStruct((experts, padded, D), bf16),
            jax.ShapeDtypeStruct((tokens, D), bf16),
            jax.ShapeDtypeStruct((tokens, 3 * D), bf16),
        ),
        out_specs=(vmem, vmem, vmem, vmem, anywhere, anywhere, anywhere),
        scratch_shapes=like((cot, tok, w_qkv))
        + [
            pltpu.VMEM((experts, padded, D), bf16),
            pltpu.VMEM((tokens, D), bf16),
            pltpu.VMEM((tokens, 3 * D), bf16),
            pltpu.SemaphoreType.DMA((3,)),
            pltpu.SemaphoreType.DMA((experts,)),
            pltpu.SemaphoreType.DMA((2, tokens // TILE)),
        ],
        compiler_params=pltpu.CompilerParams(vmem_limit_bytes=VMEM_LIMIT),
        cost_estimate=pl.CostEstimate(
            flops=2 * experts * padded * tokens * D, bytes_accessed=6 * MIB, transcendentals=0
        ),
        name="route",
    )(picks, ranks, seg, gain_attn, cot, tok, w_qkv)


def stack_heads(block):
    lane = iota(block.shape, 1)
    zero = jnp.zeros_like(block)
    return jnp.concatenate(
        [jnp.where(lane < HEAD, block, zero), jnp.where(lane < HEAD, zero, block)], axis=0
    )


def unstack_cols(stacked):
    row = iota((PAIR, QB), 0)
    picked = jnp.where(row < HEAD, stacked[:, :QB], stacked[:, QB:])
    return jnp.transpose(picked)


def window_bias(seg_col, seg_row, low, width, query):
    same = seg_col[pl.ds(low, width), :] == seg_row[:, pl.ds(query, QB)]
    half = jnp.where(same, 0.0, -1e30).astype(f32)
    return jnp.concatenate([half, half], axis=1)


def by_window(windows, block, body):
    low = windows[0, block]
    fits = windows[0, block + SEQ // QB]

    @pl.when(fits == 1)
    def _():
        body(pl.multiple_of(low, 16), WINDOW)

    @pl.when(fits != 1)
    def _():
        body(0, SEQ)


def forward_kernel(
    experts,
    windows,
    seg,
    gain_moe,
    w_router,
    packed_in,
    tok_in,
    w_proj_in,
    context_out,
    lse,
    residual_out,
    normed_moe_out,
    gates_out,
    gate_row,
    packed,
    tok,
    w_proj,
    context,
    residual,
    normed_moe,
    gates,
    seg_col,
    seg_row,
    router,
    load_sem,
    sems,
):
    loads = loading((packed_in, tok_in, w_proj_in), (packed, tok, w_proj), load_sem)
    writes = [
        pltpu.make_async_copy(source, target, sems.at[i])
        for i, (source, target) in enumerate(
            (
                (context, context_out),
                (residual, residual_out),
                (normed_moe, normed_moe_out),
                (gates, gates_out),
            )
        )
    ]
    tokens = tok.shape[0]
    seg_row[...] = seg[...].astype(f32)
    seg_col[...] = jnp.transpose(jnp.broadcast_to(seg_row[...], (LANES, tokens)))
    router[...] = jnp.zeros_like(router)
    router[:experts, :] = w_router[...]
    loads[0].wait()

    @pl.loop(0, tokens // QB)
    def _(block):
        query = pl.multiple_of(block * QB, QB)

        def body(low, width):
            bias = window_bias(seg_col, seg_row, low, width, query)
            spans = [slice(pair * PAIR, (pair + 1) * PAIR) for pair in range(PAIRS)]
            scores = []
            for span in spans:
                q = stack_heads(packed[pl.ds(query, QB), span]) * HEAD ** (-0.5)
                k = packed[pl.ds(low, width), D + span.start : D + span.stop]
                scores.append(dot_nt(k, q.astype(bf16)) + bias)
            peaks = [jnp.max(score, axis=0, keepdims=True) for score in scores]
            exponents = [jnp.exp(score - peak) for score, peak in zip(scores, peaks)]
            totals = [jnp.sum(exponent, axis=0, keepdims=True) for exponent in exponents]
            probs = [(exponent * (1.0 / total)).astype(bf16) for exponent, total in zip(exponents, totals)]
            for pair, span in enumerate(spans):
                lse[pl.ds(block, 1), pair, :] = peaks[pair] + jnp.log(totals[pair])
                v = packed[pl.ds(low, width), 2 * D + span.start : 2 * D + span.stop]
                mixed = dot_tn(v, probs[pair])
                context[pl.ds(query, QB), span] = unstack_cols(mixed).astype(bf16)

        by_window(windows, block, body)

    writes[0].start()
    for load in loads[1:]:
        load.wait()

    @pl.loop(0, tokens // TILE)
    def _(i):
        rows = pl.ds(pl.multiple_of(i * TILE, TILE), TILE)
        rest = tok[rows, :].astype(f32) + dot(context[rows, :], w_proj[...])
        residual[rows, :] = rest
        normal, unused = norm_parts(rest)
        normed = (normal * gain_moe[...]).astype(bf16)
        normed_moe[rows, :] = normed
        logits = dot_nt(normed, router[...])
        logits = jnp.where(iota(logits.shape, 1) < experts, logits, -1e30)
        exponent = jnp.exp(logits - jnp.max(logits, axis=1, keepdims=True))
        gates[rows, :] = exponent / jnp.sum(exponent, axis=1, keepdims=True)

    for write in writes[1:]:
        write.start()
    gate_row[...] = jnp.transpose(gates[...])[:experts]
    for write in writes:
        write.wait()


def forward(windows, seg, gain_moe, w_router, packed, tok, w_proj):
    tokens = tok.shape[0]
    experts = w_router.shape[0]
    vmem = pl.BlockSpec(memory_space=pltpu.VMEM)
    anywhere = pl.BlockSpec(memory_space=pl.ANY)
    return pl.pallas_call(
        functools.partial(forward_kernel, experts),
        in_specs=[pl.BlockSpec(memory_space=pltpu.SMEM)] + [vmem] * 3 + [anywhere] * 3,
        out_specs=[anywhere, vmem] + [anywhere] * 3 + [vmem],
        out_shape=(
            jax.ShapeDtypeStruct((tokens, D), bf16),
            jax.ShapeDtypeStruct((tokens // QB, PAIRS, 2 * QB), f32),
            jax.ShapeDtypeStruct((tokens, D), f32),
            jax.ShapeDtypeStruct((tokens, D), bf16),
            jax.ShapeDtypeStruct((tokens, LANES), f32),
            jax.ShapeDtypeStruct((experts, tokens), f32),
        ),
        scratch_shapes=like((packed, tok, w_proj))
        + [
            pltpu.VMEM((tokens, D), bf16),
            pltpu.VMEM((tokens, D), f32),
            pltpu.VMEM((tokens, D), bf16),
            pltpu.VMEM((tokens, LANES), f32),
            pltpu.VMEM((tokens, LANES), f32),
            pltpu.VMEM((1, tokens), f32),
            pltpu.VMEM((LANES, D), bf16),
            pltpu.SemaphoreType.DMA((3,)),
            pltpu.SemaphoreType.DMA((4,)),
        ],
        compiler_params=pltpu.CompilerParams(vmem_limit_bytes=VMEM_LIMIT),
        cost_estimate=pl.CostEstimate(
            flops=64 * 1024 * MIB, bytes_accessed=16 * MIB, transcendentals=4 * MIB
        ),
        name="attention_forward",
    )(windows, seg, gain_moe, w_router, packed, tok, w_proj)


def gelu_parts(x):
    density = jnp.exp(-0.5 * (x * x))
    return 0.5 + 0.5 * lax.erf(x * 2.0**-0.5), x * density * 0.3989422804014327


def shifted(index, by, size):
    return lax.rem(index + by, size)


def paired(index, by, size):
    total = 0
    bit = 1
    while bit < size:
        total = total + bit * lax.rem(index // bit + by // bit, 2)
        bit *= 2
    return total


def exchange(src, dst, send, recv, device):
    return pltpu.make_async_remote_copy(
        src_ref=src, dst_ref=dst, send_sem=send, recv_sem=recv, device_id=device, device_id_type=MESH
    )


def greet(barrier, sources):
    me = lax.axis_index("wide")
    line = lax.axis_index("narrow")

    @pl.loop(1, sources)
    def _(j):
        pl.semaphore_signal(barrier, inc=1, device_id=(paired(me, j, sources), line), device_id_type=MESH)


EARLY = 3


def moe_kernel(
    capacity,
    sources,
    shards,
    slot_row,
    gate_row,
    normed_in,
    gz_in,
    w_in0,
    w_out0,
    w_in1,
    w_out1,
    w_in2,
    w_out2,
    returned,
    back,
    ring,
    own_grads,
    *refs,
):
    others, refs = refs[: shards - 3], refs[shards - 3 :]
    moe_body(
        capacity,
        sources,
        shards,
        slot_row,
        gate_row,
        normed_in,
        gz_in,
        ((w_in0, w_out0), (w_in1, w_out1), (w_in2, w_out2)),
        returned,
        back,
        ring,
        own_grads,
        others,
        *refs,
    )


def moe_body(
    capacity,
    sources,
    shards,
    slot_row,
    gate_row,
    normed_in,
    gz_in,
    early,
    returned,
    back,
    ring,
    own_grads,
    others,
    normed_moe,
    w_ins,
    w_outs,
    rows_send,
    rows,
    scaled,
    gate_slot,
    rows_t,
    gz_t,
    act,
    gpre,
    out_sum,
    back_sum,
    out_low,
    back_low,
    ring_out,
    ring_in,
    load_sem,
    row_sem,
    out_sem,
    back_sem,
    own_sem,
    weight_sem,
    ring_sem,
):
    padded = rows.shape[1]
    tokens = normed_in.shape[0]
    me = lax.axis_index("wide")
    line = lax.axis_index("narrow")
    right = (me, shifted(line, 1, shards))
    left = (me, shifted(line, shards - 1, shards))
    loads = [
        pltpu.make_async_copy(normed_in, normed_moe, load_sem.at[0]),
        pltpu.make_async_copy(gz_in, scaled, load_sem.at[1]),
    ]
    for c, pair in reversed(list(enumerate(early))):
        for i, (source, target) in enumerate(zip(pair, (w_ins, w_outs))):
            loads.append(pltpu.make_async_copy(source, target.at[c], load_sem.at[2 + 2 * c + i]))
    for load in loads:
        load.start()
    barrier = pltpu.get_barrier_semaphore()
    greet(barrier, sources)
    for near in (left, right):
        pl.semaphore_signal(barrier, inc=1, device_id=near, device_id_type=MESH)
    gate_slot[...] = jnp.zeros_like(gate_slot)

    def weights_on(c):
        return [
            exchange(part.at[c - 1], part.at[c], weight_sem.at[0, i, c], weight_sem.at[1, i, c], right)
            for i, part in enumerate((w_ins, w_outs))
        ]

    def row_copy(j):
        to = paired(me, j, sources)
        return exchange(rows_send.at[to], rows.at[me], row_sem.at[0, j], row_sem.at[1, j], (to, line))

    def result_copies(j):
        to = paired(me, j, sources)
        return [
            exchange(low.at[to], target.at[me], sem.at[0, j], sem.at[1, j], (to, line))
            for low, target, sem in ((out_low, returned, out_sem), (back_low, back, back_sem))
        ]

    keep = [
        pltpu.make_async_copy(low.at[me], target.at[me], own_sem.at[i])
        for i, (low, target) in enumerate(((out_low, returned), (back_low, back)))
    ]

    for load in loads[:1] + loads[2:4]:
        load.wait()

    @pl.loop(0, sources)
    def _(i):
        j = paired(i, sources - 2, sources)
        e = paired(me, j, sources)
        chosen = iota((padded, tokens), 0).astype(f32) == slot_row[pl.ds(e, 1), :]
        chosen = chosen.astype(f32).astype(bf16)
        rows_send[e] = dot(chosen, normed_moe[...]).astype(bf16)
        gate = gate_row[pl.ds(e, 1), :]
        high, middle = split2(gate)
        low = (gate - high.astype(f32) - middle.astype(f32)).astype(bf16)
        three = jnp.concatenate(
            [high.astype(f32), middle.astype(f32), low.astype(f32), jnp.zeros((5, tokens), f32)], axis=0
        )
        gate_slot[:, :padded] = dot_nt(three.astype(bf16), chosen)
        tail = rows_send[e, padded - 16 :, :].astype(f32)
        sub = iota(tail.shape, 0)
        for part in range(3):
            tail = jnp.where(sub == 13 + part, gate_slot[part : part + 1, :], tail)
        rows_send[e, padded - 16 :, :] = tail.astype(bf16)

        @pl.when(i == 0)
        def _():
            pl.semaphore_wait(barrier, sources + 1)
            for copy in weights_on(EARLY):
                copy.start()

        @pl.when(j != 0)
        def _():
            row_copy(j).start()

    rows[me] = rows_send[me]
    for load in loads[1:2] + loads[4:]:
        load.wait()

    def partner(i):
        return lax.rem(sources - i // 2 * 2, sources) + lax.rem(i, 2)

    def prepare(j):
        s = paired(me, j, sources)

        @pl.when(j != 0)
        def _():
            row_copy(j).wait_recv()

        tail = rows[s, padded - 16 :, :].astype(f32)
        gate = tail[13:14] + tail[14:15] + tail[15:16]
        gate = jnp.transpose(jnp.broadcast_to(gate, (LANES, D)))[:padded, :1]
        live = iota((padded, 1), 0) < capacity
        scaled[s] = (jnp.where(live, gate, 0.0) * scaled[s].astype(f32)).astype(bf16)
        live16 = iota((16, 1), 0) < 16 - (padded - capacity)
        rows[s, padded - 16 :, :] = jnp.where(live16, tail, 0.0).astype(bf16)

    def shard_results(s, c):
        span = pl.ds(pl.multiple_of(s * padded, 16), padded)
        pre = dot(rows[s], w_ins[c])
        phi, slope = gelu_parts(pre)
        act_low = (pre * phi).astype(bf16)
        act[c, span, :] = act_low
        grad_pre = (dot_nt(scaled[s], w_outs[c]) * (phi + slope)).astype(bf16)
        gpre[c, span, :] = grad_pre
        return dot(act_low, w_outs[c]), dot_nt(grad_pre, w_ins[c])

    def send(j, result, grad_rows):
        s = paired(me, j, sources)
        out_low[s] = result.astype(bf16)
        back_low[s] = grad_rows.astype(bf16)

        @pl.when(j != 0)
        def _():
            for copy in result_copies(j):
                copy.start()

        @pl.when(j == 0)
        def _():
            for copy in keep:
                copy.start()

    def run(s, first, last, spot, carried):
        for c in range(first, last):
            result, grad_rows = shard_results(s, c)
            if c > first or carried:
                result = result + out_sum[spot]
                grad_rows = grad_rows + back_sum[spot]
            if c < last - 1 or last < shards:
                out_sum[spot] = result
                back_sum[spot] = grad_rows
        return result, grad_rows

    half = sources // 2

    @pl.loop(0, half)
    def _(i):
        j = partner(i)
        prepare(j)
        run(paired(me, j, sources), 0, EARLY, i, False)

    for c in range(EARLY, shards):
        for copy in weights_on(c):
            copy.wait()
        if c + 1 < shards:
            for copy in weights_on(c + 1):
                copy.start()

    @pl.loop(0, half)
    def _(i):
        j = partner(i)
        send(j, *run(paired(me, j, sources), EARLY, shards, i, True))

    @pl.loop(half, sources)
    def _(i):
        j = partner(i)
        prepare(j)
        send(j, *run(paired(me, j, sources), 0, shards, 0, False))

    for s in range(sources):
        rows_t[:, s * padded : (s + 1) * padded] = jnp.transpose(rows[s])
        gz_t[:, s * padded : (s + 1) * padded] = jnp.transpose(scaled[s])

    def weight_grads(c):
        return dot(rows_t[...], gpre[c]).astype(bf16), dot(gz_t[...], act[c]).astype(bf16)

    ring_out[:D, :], ring_out[D:, :] = weight_grads(1)
    step = exchange(ring_out, ring_in, ring_sem.at[0], ring_sem.at[1], right)
    step.start()
    for c in range(3, shards):
        others[c - 3][:D, :], others[c - 3][D:, :] = weight_grads(c)
    own_grads[:D, :], own_grads[D:, :] = weight_grads(0)
    second = weight_grads(2)
    for copy in keep:
        copy.wait()
    step.wait()
    for part in range(2):
        span = slice(part * D, part * D + D)
        ring[span, :] = (ring_in[span, :].astype(f32) + second[part].astype(f32)).astype(bf16)

    @pl.loop(1, sources)
    def _(j):
        row_copy(j).wait_send()
        for copy in result_copies(j):
            copy.wait()


def moe(slot_row, gate_row, normed_moe, gz, early, shards, capacity):
    sources, padded, unused = gz.shape
    tokens = normed_moe.shape[0]
    hidden = early[0][0].shape[1]
    total = sources * padded
    vmem = pl.BlockSpec(memory_space=pltpu.VMEM)
    anywhere = pl.BlockSpec(memory_space=pl.ANY)
    dma = pltpu.SemaphoreType.DMA
    return pl.pallas_call(
        functools.partial(moe_kernel, capacity, sources, shards),
        in_specs=[vmem] * 2 + [anywhere] * (2 + 2 * EARLY),
        out_specs=[anywhere] * 2 + [vmem] * (shards - 1),
        out_shape=[jax.ShapeDtypeStruct(gz.shape, bf16)] * 2
        + [jax.ShapeDtypeStruct((2 * D, hidden), bf16)] * (shards - 1),
        scratch_shapes=[
            pltpu.VMEM((tokens, D), bf16),
            pltpu.VMEM((shards, D, hidden), bf16),
            pltpu.VMEM((shards, hidden, D), bf16),
            pltpu.VMEM(gz.shape, bf16),
            pltpu.VMEM(gz.shape, bf16),
            pltpu.VMEM(gz.shape, bf16),
            pltpu.VMEM((8, D), f32),
            pltpu.VMEM((D, total), bf16),
            pltpu.VMEM((D, total), bf16),
            pltpu.VMEM((shards, total, hidden), bf16),
            pltpu.VMEM((shards, total, hidden), bf16),
            pltpu.VMEM((sources // 2, padded, D), f32),
            pltpu.VMEM((sources // 2, padded, D), f32),
            pltpu.VMEM(gz.shape, bf16),
            pltpu.VMEM(gz.shape, bf16),
            pltpu.VMEM((2 * D, hidden), bf16),
            pltpu.VMEM((2 * D, hidden), bf16),
            dma((2 + 2 * EARLY,)),
            dma((2, sources)),
            dma((2, sources)),
            dma((2, sources)),
            dma((2,)),
            dma((2, 2, shards)),
            dma((2,)),
        ],
        compiler_params=pltpu.CompilerParams(
            vmem_limit_bytes=VMEM_LIMIT, collective_id=1, has_side_effects=True
        ),
        cost_estimate=pl.CostEstimate(
            flops=12 * total * D * hidden * shards, bytes_accessed=20 * MIB, transcendentals=0
        ),
        name="moe",
    )(slot_row, gate_row, normed_moe, gz, *[part for pair in early for part in pair])


def combine_kernel(
    experts,
    windows,
    seg,
    gain_moe,
    w_router,
    slot_col,
    gates,
    lse,
    counts,
    returned_in,
    back_in,
    cot_in,
    residual_in,
    w_proj_in,
    normed_moe_in,
    context_in,
    packed_in,
    mixed_out,
    grad_residual_out,
    extra_out,
    grad_context,
    grad_proj,
    small,
    pair_grads,
    returned,
    back,
    cot,
    residual,
    w_proj,
    normed_moe,
    context,
    packed,
    mixed,
    grad_residual,
    extra,
    hot,
    seg_col,
    seg_row,
    router,
    grad_attn,
    grad_logits,
    grad_k,
    grad_v,
    bias,
    pair_k,
    pair_v,
    read_sem,
    sems,
):
    tokens = cot.shape[0]
    slots_all, padded = returned.shape[0] * returned.shape[1], returned.shape[1]
    reads = loading(
        (returned_in, back_in, cot_in, residual_in, w_proj_in, normed_moe_in, context_in, packed_in),
        (returned, back, cot, residual, w_proj, normed_moe, context, packed),
        read_sem,
    )
    writes = (
        pltpu.make_async_copy(mixed, mixed_out, sems.at[0]),
        pltpu.make_async_copy(grad_residual, grad_residual_out, sems.at[1]),
        pltpu.make_async_copy(extra, extra_out, sems.at[2]),
    )
    extra[...] = jnp.zeros_like(extra)
    seg_row[...] = seg[...].astype(f32)
    seg_col[...] = jnp.transpose(jnp.broadcast_to(seg_row[...], (LANES, tokens)))
    router[...] = jnp.zeros_like(router)
    router[:experts, :] = w_router[...]
    small[...] = jnp.zeros_like(small)
    small[2:4, :LANES] = counts[:2, :]

    for read in reads[:5]:
        read.wait()

    @pl.loop(0, tokens // TILE)
    def _(i):
        rows = pl.ds(pl.multiple_of(i * TILE, TILE), TILE)
        grad_z = cot[rows, :].astype(f32)
        probs = gates[rows, :]
        slots = slot_col[rows, :]
        lane = iota((TILE, LANES), 1)
        rest = residual[rows, :]
        twice = probs + pltpu.roll(probs, experts, axis=1)
        place = jnp.where(lane < experts, lane, lane - experts).astype(f32) * float(padded)
        total = rest
        grad_gates = jnp.zeros((TILE, LANES), f32)
        spots = iota((TILE, slots_all), 1).astype(f32)
        picks = []
        for k in range(TOP):
            mine = (slots >= 0.0) & (lane >= k * experts) & (lane < (k + 1) * experts)
            spot = jnp.sum(jnp.where(mine, place + slots + 1.0, 0.0), axis=1, keepdims=True) - 1.0
            hot[k * TILE : (k + 1) * TILE, :] = (spots == spot).astype(f32).astype(bf16)
            picks.append(mine)
        back_total = dot(hot[:TILE, :] + hot[TILE:, :], back[...].reshape(slots_all, D))
        results = dot(hot[...], returned[...].reshape(slots_all, D))
        for k in range(TOP):
            result = results[k * TILE : (k + 1) * TILE]
            total = total + jnp.sum(jnp.where(picks[k], twice, 0.0), axis=1, keepdims=True) * result
            inner = jnp.sum(result * grad_z, axis=1, keepdims=True)
            grad_gates = grad_gates + jnp.where(picks[k], inner, 0.0)
        grad_gates = grad_gates + pltpu.roll(grad_gates, LANES - experts, axis=1)
        grad_gates = jnp.where(lane < experts, grad_gates, 0.0)
        mixed[rows, :] = total.astype(bf16)
        gate_inner = jnp.sum(probs * grad_gates, axis=1, keepdims=True)
        high, low = split2(probs * (grad_gates - gate_inner))
        grad_logits[rows, :LANES] = high
        grad_logits[rows, LANES:] = low
        grad_normed = back_total + dot(high, router[...]) + dot(low, router[...])
        normal, inverse = norm_parts(rest)
        grad_norm, grad_gain = norm_back(grad_normed, gain_moe[...], normal, inverse)
        small[1:2, :] += grad_gain
        grad_rest = grad_z + grad_norm
        grad_residual[rows, :] = grad_rest
        attn = grad_rest.astype(bf16)
        grad_attn[rows, :] = attn
        grad_context[rows, :] = dot_nt(attn, w_proj[...]).astype(bf16)

    for write in writes[:2]:
        write.start()
    for read in reads[5:7]:
        read.wait()
    both = dot_tn(normed_moe[...], grad_logits[...])
    both = jnp.transpose(both[:, :LANES] + both[:, LANES:])
    small[8:, :] = both[:experts]
    grad_proj[...] = dot_tn(context[...], grad_attn[...])
    blocks = tokens // QB
    reads[7].wait()

    @pl.when(windows[0, 3 * blocks] != 1)
    def _():
        grad_k[...] = jnp.zeros_like(grad_k)
        grad_v[...] = jnp.zeros_like(grad_v)

        @pl.loop(0, blocks)
        def _(block):
            query = pl.multiple_of(block * QB, QB)

            @pl.when(windows[0, 2 * blocks + block] != 1)
            def _():
                bias = window_bias(seg_col, seg_row, 0, SEQ, query)
                spans = [slice(pair * PAIR, (pair + 1) * PAIR) for pair in range(PAIRS)]
                keys = pl.ds(0, SEQ)
                queries = [
                    (stack_heads(packed[pl.ds(query, QB), span]) * HEAD ** (-0.5)).astype(bf16) for span in spans
                ]
                grads = [stack_heads(grad_context[pl.ds(query, QB), span]) for span in spans]
                probs = []
                grad_probs = []
                for pair, span in enumerate(spans):
                    k = packed[keys, D + span.start : D + span.stop]
                    v = packed[keys, 2 * D + span.start : 2 * D + span.stop]
                    probs.append(jnp.exp(dot_nt(k, queries[pair]) + bias - lse[pl.ds(block, 1), pair, :]))
                    grad_probs.append(dot_nt(v, grads[pair]))
                grad_scores = []
                for pair, span in enumerate(spans):
                    grad_v[keys, span] += dot(probs[pair].astype(bf16), grads[pair])
                    weighted = probs[pair] * grad_probs[pair]
                    inner = jnp.sum(weighted, axis=0, keepdims=True)
                    grad_scores.append((weighted - probs[pair] * inner).astype(bf16))
                for pair, span in enumerate(spans):
                    k = packed[keys, D + span.start : D + span.stop]
                    grad_k[keys, span] += dot(grad_scores[pair], queries[pair])
                    grad_q = unstack_cols(dot_tn(k, grad_scores[pair])) * HEAD ** (-0.5)
                    extra[pl.ds(query, QB), span] = grad_q.astype(bf16)
                grad_context[pl.ds(query, QB), :] = jnp.zeros((QB, D), bf16)

        extra[:, D : 2 * D] = grad_k[...].astype(bf16)
        extra[:, 2 * D :] = grad_v[...].astype(bf16)

    writes[2].start()
    slab_bias(bias, seg_col, seg_row[...])
    pair_backward(0, packed, grad_context, lse, extra, bias, pair_k, pair_v, pair_grads)
    for write in writes:
        write.wait()


def combine(experts, windows, *operands):
    returned = operands[7]
    tokens = operands[9].shape[0]
    vmem = pl.BlockSpec(memory_space=pltpu.VMEM)
    anywhere = pl.BlockSpec(memory_space=pl.ANY)
    return pl.pallas_call(
        functools.partial(combine_kernel, experts),
        in_specs=[pl.BlockSpec(memory_space=pltpu.SMEM)] + [vmem] * 7 + [anywhere] * 8,
        out_specs=[anywhere, anywhere, anywhere, vmem, vmem, vmem, vmem],
        out_shape=(
            jax.ShapeDtypeStruct((tokens, D), bf16),
            jax.ShapeDtypeStruct((tokens, D), f32),
            jax.ShapeDtypeStruct((tokens, 3 * D), bf16),
            jax.ShapeDtypeStruct((tokens, D), bf16),
            jax.ShapeDtypeStruct((D, D), f32),
            jax.ShapeDtypeStruct((8 + experts, D), f32),
            jax.ShapeDtypeStruct((tokens, 3 * PAIR), bf16),
        ),
        scratch_shapes=like(operands[7:])
        + [
            pltpu.VMEM((tokens, D), bf16),
            pltpu.VMEM((tokens, D), f32),
            pltpu.VMEM((tokens, 3 * D), bf16),
            pltpu.VMEM((TOP * TILE, returned.shape[0] * returned.shape[1]), bf16),
            pltpu.VMEM((tokens, LANES), f32),
            pltpu.VMEM((1, tokens), f32),
            pltpu.VMEM((LANES, D), bf16),
            pltpu.VMEM((tokens, D), bf16),
            pltpu.VMEM((tokens, 2 * LANES), bf16),
            pltpu.VMEM((tokens, D), f32),
            pltpu.VMEM((tokens, D), f32),
            pltpu.VMEM((SLAB_AT[-1], QB), f32),
            pltpu.VMEM((tokens, PAIR), f32),
            pltpu.VMEM((tokens, PAIR), f32),
            pltpu.SemaphoreType.DMA((8,)),
            pltpu.SemaphoreType.DMA((3,)),
        ],
        compiler_params=pltpu.CompilerParams(vmem_limit_bytes=VMEM_LIMIT),
        cost_estimate=pl.CostEstimate(
            flops=30 * 1024 * MIB, bytes_accessed=30 * MIB, transcendentals=4 * MIB
        ),
        name="combine",
    )(windows, *operands)


SLAB_AT = tuple(sum(high - low for low, high in SLABS[:b]) for b in range(len(SLABS) + 1))


def slab_bias(bias, seg_col, seg_row):
    for b, (low, high) in enumerate(SLABS):
        same = seg_col[low:high, :] == seg_row[:, b * QB : (b + 1) * QB]
        bias[SLAB_AT[b] : SLAB_AT[b + 1], :] = jnp.where(same, 0.0, -1e30)


def pair_backward(pair, packed, grad_context, lse, extra, bias, grad_k, grad_v, out):
    def span(which):
        return pl.ds(pl.multiple_of(which * D + pair * PAIR, PAIR), PAIR)

    grad_k[...] = extra[:, span(1)].astype(f32)
    grad_v[...] = extra[:, span(2)].astype(f32)
    for group in range(0, len(SLABS), 4):
        blocks = range(group, group + 4)
        queries, grads, probs, grad_probs, grad_scores = [], [], [], [], []
        for b in blocks:
            low, high = SLABS[b]
            rows = slice(b * QB, (b + 1) * QB)
            queries.append((stack_heads(packed[rows, span(0)]) * HEAD ** (-0.5)).astype(bf16))
            grads.append(stack_heads(grad_context[rows, span(0)]))
            masked = bias[SLAB_AT[b] : SLAB_AT[b + 1], :]
            scores = dot_nt(packed[low:high, span(1)], queries[-1]) + jnp.concatenate([masked, masked], axis=1)
            probs.append(jnp.exp(scores - lse[b, pl.ds(pair, 1), :]))
            grad_probs.append(dot_nt(packed[low:high, span(2)], grads[-1]))
        for i, b in enumerate(blocks):
            low, high = SLABS[b]
            grad_v[low:high, :] += dot(probs[i].astype(bf16), grads[i])
            weighted = probs[i] * grad_probs[i]
            inner = jnp.sum(weighted, axis=0, keepdims=True)
            grad_scores.append((weighted - probs[i] * inner).astype(bf16))
        for i, b in enumerate(blocks):
            low, high = SLABS[b]
            rows = slice(b * QB, (b + 1) * QB)
            grad_k[low:high, :] += dot(grad_scores[i], queries[i])
            grad_q = unstack_cols(dot_tn(packed[low:high, span(1)], grad_scores[i])) * HEAD ** (-0.5)
            out[rows, :PAIR] = (grad_q + extra[rows, span(0)].astype(f32)).astype(bf16)
    out[:, PAIR : 2 * PAIR] = grad_k[...].astype(bf16)
    out[:, 2 * PAIR :] = grad_v[...].astype(bf16)


def shared_kernel(
    chips,
    planes,
    seg,
    lse,
    partial,
    gain_attn,
    first_in,
    packed_in,
    grad_context_in,
    extra_in,
    normed_attn_in,
    grad_proj_in,
    w_qkv_in,
    tok_in,
    grad_residual_in,
    ring_in,
    third_in,
    summed,
    small,
    grad_tokens_out,
    ring_last,
    pair_grads,
    packed,
    grad_context,
    extra,
    normed_attn,
    grad_proj,
    w_qkv,
    tok,
    grad_residual,
    ring,
    third,
    grad_tokens,
    normed_t,
    seg_col,
    bias,
    grad_k,
    grad_v,
    grad_packed,
    half,
    core_out,
    core_in,
    chip_out,
    chip_in,
    plane_out,
    plane_in,
    small_own,
    small_core,
    small_chip,
    small_plane,
    load_sem,
    store_sem,
    ring_sem,
    core_sem,
    chip_sem,
    plane_sem,
    plane_sem2,
    chip_sem2,
    core_sem2,
    small_sem,
    small_chip_sem,
    small_plane_sem,
):
    tokens = tok.shape[0]
    stages = 16 // planes
    pairs = PAIRS // stages
    tiles = tokens // TILE
    wide = lax.axis_index("wide")
    plane = lax.axis_index("narrow")
    core = lax.rem(wide, 2)
    chip = wide // 2
    share = D // (2 * chips)
    partner = (chip * 2 + 1 - core, plane)
    mine = pl.ds(pl.multiple_of(core * (D // 2), D // 2), D // 2)
    other = pl.ds(pl.multiple_of((1 - core) * (D // 2), D // 2), D // 2)
    chunk = pl.ds(pl.multiple_of(core * (D // 2) + chip * share, share), share)
    own_chunk = pl.ds(pl.multiple_of(chip * share, share), share)

    loads = [
        pltpu.make_async_copy(source, target, load_sem.at[i])
        for i, (source, target) in enumerate(
            (
                (first_in, pair_grads),
                (normed_attn_in, normed_attn),
                (grad_proj_in, grad_proj),
                (ring_in, ring),
                (third_in, third),
                (packed_in, packed),
                (grad_context_in, grad_context),
                (extra_in, extra),
                (w_qkv_in, w_qkv),
                (tok_in, tok),
                (grad_residual_in, grad_residual),
            )
        )
    ]
    for load in loads:
        load.start()

    def chip_at(j):
        to = shifted(chip, j, chips)
        return to, (to * 2 + core, plane)

    def plane_at(j):
        to = shifted(plane, j, planes)
        return to, (wide, to)

    barrier = pltpu.get_barrier_semaphore()
    pl.semaphore_signal(barrier, inc=1, device_id=partner, device_id_type=MESH)

    @pl.loop(1, chips)
    def _(j):
        pl.semaphore_signal(barrier, inc=1, device_id=chip_at(j)[1], device_id_type=MESH)

    @pl.loop(1, planes)
    def _(j):
        pl.semaphore_signal(barrier, inc=1, device_id=plane_at(j)[1], device_id_type=MESH)

    def blocks(stage):
        return pl.ds(stage * planes, planes)

    def core_copy(stage):
        at = blocks(stage)
        return exchange(core_out.at[at], core_in.at[at], core_sem.at[0, stage], core_sem.at[1, stage], partner)

    def chip_copy(stage, j):
        to, device = chip_at(j)
        rows = pl.ds(pl.multiple_of(to * share, share), share)
        at = blocks(stage)
        return exchange(
            chip_out.at[at, rows], chip_in.at[j, at], chip_sem.at[0, stage, j], chip_sem.at[1, stage, j], device
        )

    def plane_copy(stage, j):
        to, device = plane_at(j)
        return exchange(
            plane_out.at[stage * planes + to],
            plane_in.at[j, stage],
            plane_sem.at[0, stage, j],
            plane_sem.at[1, stage, j],
            device,
        )

    def plane_back(stage, j):
        spot = summed.at[stage * planes + plane, chunk]
        return exchange(spot, spot, plane_sem2.at[0, stage, j], plane_sem2.at[1, stage, j], plane_at(j)[1])

    def chip_back(stage, j):
        spot = summed.at[blocks(stage), chunk]
        return exchange(spot, spot, chip_sem2.at[0, stage, j], chip_sem2.at[1, stage, j], chip_at(j)[1])

    def core_back(stage):
        spot = summed.at[blocks(stage), mine]
        return exchange(spot, spot, core_sem2.at[0, stage], core_sem2.at[1, stage], partner)

    def small_core_copy():
        return exchange(small_own, small_core, small_sem.at[0], small_sem.at[1], partner)

    def small_chip_copy(j):
        spot = small_chip.at[chip]
        return exchange(spot, spot, small_chip_sem.at[0, j], small_chip_sem.at[1, j], chip_at(j)[1])

    def small_plane_copy(j):
        spot = small_plane.at[plane]
        return exchange(spot, spot, small_plane_sem.at[0, j], small_plane_sem.at[1, j], plane_at(j)[1])

    def pair_products(pair):
        spare = dot(normed_t[other, :], pair_grads[...])
        own = dot(normed_t[mine, :], pair_grads[...])
        lanes = pl.ds(pl.multiple_of(pair * PAIR, PAIR), PAIR)
        for which in range(3):
            at = slice(which * PAIR, (which + 1) * PAIR)
            core_out[pair * 4 + which] = spare[:, at].astype(bf16)
            half[pair * 4 + which] = own[:, at]
            grad_packed[:, pl.ds(pl.multiple_of(which * D + pair * PAIR, PAIR), PAIR)] = pair_grads[:, at]
        core_out[pair * 4 + 3] = grad_proj[other, lanes].astype(bf16)
        half[pair * 4 + 3] = grad_proj[mine, lanes]

    def chip_stage(stage):
        core_copy(stage).wait_recv()
        at = blocks(stage)
        total = half[at] + core_in[at].astype(f32)
        half[at] = total
        chip_out[at] = total.astype(bf16)

        @pl.loop(1, chips)
        def _(j):
            chip_copy(stage, j).start()

    def plane_stage(stage):
        at = blocks(stage)
        total = half[at, own_chunk, :]
        for j in range(1, chips):
            chip_copy(stage, j).wait_recv()
            total = total + chip_in[j, at].astype(f32)
        half[at, own_chunk, :] = total
        plane_out[at] = total.astype(bf16)

        @pl.loop(1, planes)
        def _(j):
            plane_copy(stage, j).start()

    def own_stage(stage):
        total = half[stage * planes + plane, own_chunk, :]
        for j in range(1, planes):
            plane_copy(stage, j).wait_recv()
            total = total + plane_in[j, stage].astype(f32)
        summed[stage * planes + plane, chunk, :] = total.astype(bf16)

        @pl.loop(1, planes)
        def _(j):
            plane_back(stage, j).start()

    def gather_stage(stage):
        @pl.loop(1, planes)
        def _(j):
            plane_back(stage, j).wait_recv()

        @pl.loop(1, chips)
        def _(j):
            chip_back(stage, j).start()

    def last_stage(stage):
        @pl.loop(1, chips)
        def _(j):
            chip_back(stage, j).wait_recv()

        core_back(stage).start()

    def norm_tile(i):
        rows = slice(i * TILE, (i + 1) * TILE)
        grad_normed = dot_nt(grad_packed[rows, :], w_qkv[...])
        normal, inverse = norm_parts(tok[rows, :].astype(f32))
        grad_norm, grad_gain = norm_back(grad_normed, gain_attn[...], normal, inverse)
        small_own[0:1, :] += grad_gain
        grad_tokens[rows, :] = grad_residual[rows, :] + grad_norm

    small_own[...] = partial[...]
    seg_row = seg[...].astype(f32)
    seg_col[...] = jnp.transpose(jnp.broadcast_to(seg_row, (LANES, tokens)))
    slab_bias(bias, seg_col, seg_row)
    for load in loads[:3]:
        load.wait()
    normed_t[...] = jnp.transpose(normed_attn[...])
    pair_products(0)
    pl.semaphore_wait(barrier, chips + planes - 1)
    if pairs == 1:
        core_copy(0).start()
    for load in loads[3:5]:
        load.wait()
    ring[...] = (ring[...].astype(f32) + third[...].astype(f32)).astype(bf16)
    last = exchange(ring, ring_last, ring_sem.at[0], ring_sem.at[1], plane_at(1)[1])
    last.start()
    for load in loads[5:8]:
        load.wait()

    @pl.loop(1, PAIRS)
    def _(pair):
        pair_backward(pair, packed, grad_context, lse, extra, bias, grad_k, grad_v, pair_grads)
        pair_products(pair)

        @pl.when(lax.rem(pair + 1, pairs) == 0)
        def _():
            stage = pair // pairs
            core_copy(stage).start()

            @pl.when(stage > 0)
            def _():
                chip_stage(stage - 1)

            @pl.when(stage > 1)
            def _():
                plane_stage(stage - 2)

            @pl.when(stage > 2)
            def _():
                own_stage(stage - 3)

    for load in loads[8:]:
        load.wait()
    steps = (chip_stage, plane_stage, own_stage, gather_stage, last_stage)
    for late in range(len(steps)):
        if late == 0:
            norm_tile(0)
        for i, step in enumerate(steps):
            stage = stages - 1 + late - i
            if i >= late and 0 <= stage < stages:
                step(stage)
        if late == 0:
            for i in range(1, tiles):
                norm_tile(i)
            small_core_copy().start()
            store = pltpu.make_async_copy(grad_tokens, grad_tokens_out, store_sem)
            store.start()
        if late == 1:
            small_core_copy().wait_recv()
            small_chip[chip] = small_own[...] + small_core[...]

            @pl.loop(1, chips)
            def _(j):
                small_chip_copy(j).start()

        if late == 2:

            @pl.loop(1, chips)
            def _(j):
                small_chip_copy(j).wait_recv()

            total = small_chip[0]
            for c in range(1, chips):
                total = total + small_chip[c]
            small_plane[plane] = total

            @pl.loop(1, planes)
            def _(j):
                small_plane_copy(j).start()

    @pl.loop(1, planes)
    def _(j):
        small_plane_copy(j).wait_recv()

    total = small_plane[0]
    for c in range(1, planes):
        total = total + small_plane[c]
    small[...] = total
    store.wait()
    last.wait()

    @pl.loop(0, stages)
    def _(stage):
        core_back(stage).wait()
        core_copy(stage).wait_send()

        @pl.loop(1, chips)
        def _(j):
            chip_back(stage, j).wait_send()
            chip_copy(stage, j).wait_send()

        @pl.loop(1, planes)
        def _(j):
            plane_back(stage, j).wait_send()
            plane_copy(stage, j).wait_send()

    @pl.loop(1, planes)
    def _(j):
        small_plane_copy(j).wait_send()

    @pl.loop(1, chips)
    def _(j):
        small_chip_copy(j).wait_send()

    small_core_copy().wait_send()


def shared_gradients(*operands):
    partial, packed = operands[2], operands[5]
    tokens = packed.shape[0]
    chips = lax.axis_size("wide") // 2
    planes = lax.axis_size("narrow")
    stages = 16 // planes
    share = D // (2 * chips)
    rows = partial.shape[0]
    dma = pltpu.SemaphoreType.DMA
    vmem = pl.BlockSpec(memory_space=pltpu.VMEM)
    anywhere = pl.BlockSpec(memory_space=pl.ANY)
    return pl.pallas_call(
        functools.partial(shared_kernel, chips, planes),
        in_specs=[vmem] * 4 + [anywhere] * 11,
        out_specs=(vmem, vmem, anywhere, anywhere),
        out_shape=(
            jax.ShapeDtypeStruct((16, D, LANES), bf16),
            jax.ShapeDtypeStruct((rows, D), f32),
            jax.ShapeDtypeStruct((tokens, D), f32),
            jax.ShapeDtypeStruct(operands[-1].shape, bf16),
        ),
        scratch_shapes=[pltpu.VMEM(operand.shape, operand.dtype) for operand in operands[4:]]
        + [
            pltpu.VMEM((tokens, D), f32),
            pltpu.VMEM((D, tokens), bf16),
            pltpu.VMEM((tokens, LANES), f32),
            pltpu.VMEM((SLAB_AT[-1], QB), f32),
            pltpu.VMEM((tokens, PAIR), f32),
            pltpu.VMEM((tokens, PAIR), f32),
            pltpu.VMEM((tokens, 3 * D), bf16),
            pltpu.VMEM((16, D // 2, LANES), f32),
            pltpu.VMEM((16, D // 2, LANES), bf16),
            pltpu.VMEM((16, D // 2, LANES), bf16),
            pltpu.VMEM((16, D // 2, LANES), bf16),
            pltpu.VMEM((chips, 16, share, LANES), bf16),
            pltpu.VMEM((16, share, LANES), bf16),
            pltpu.VMEM((planes, stages, share, LANES), bf16),
            pltpu.VMEM((rows, D), f32),
            pltpu.VMEM((rows, D), f32),
            pltpu.VMEM((chips, rows, D), f32),
            pltpu.VMEM((planes, rows, D), f32),
            dma((11,)),
            dma,
            dma((2,)),
            dma((2, stages)),
            dma((2, stages, chips)),
            dma((2, stages, planes)),
            dma((2, stages, planes)),
            dma((2, stages, chips)),
            dma((2, stages)),
            dma((2,)),
            dma((2, chips)),
            dma((2, planes)),
        ],
        compiler_params=pltpu.CompilerParams(
            vmem_limit_bytes=VMEM_LIMIT, collective_id=2, has_side_effects=True
        ),
        cost_estimate=pl.CostEstimate(
            flops=12 * tokens * D * D, bytes_accessed=16 * MIB, transcendentals=0
        ),
        name="shared_gradients",
    )(*operands)


def finish_kernel(
    experts,
    small,
    summed_in,
    ring_in,
    own_in,
    tokens_in,
    gain_attn,
    gain_moe,
    router,
    kept,
    dropped,
    qkv_out,
    proj_out,
    in_out,
    out_out,
    tokens_out,
    summed,
    ring,
    own,
    tokens,
    qkv,
    proj,
    grad_in,
    grad_out,
    load_sem,
    store_sem,
    token_sem,
):
    loads = loading((summed_in, ring_in, own_in, tokens_in), (summed, ring, own, tokens), load_sem)
    through = pltpu.make_async_copy(tokens, tokens_out, token_sem)
    gain_attn[...] = small[0, :]
    gain_moe[...] = small[1, :]
    router[...] = small[8:, :]
    counted = small[2:4, :experts]
    kept[...] = counted[0:1].astype(jnp.int32)
    dropped[...] = (counted[1:2] - counted[0:1]).astype(jnp.int32)
    loads[0].wait()
    stores = []
    step = D // 4
    for i in range(4):
        rows = slice(i * step, (i + 1) * step)
        for n in range(16):
            pair, which = divmod(n, 4)
            lanes = slice(pair * PAIR, (pair + 1) * PAIR)
            if which < 3:
                qkv[rows, which * D + lanes.start : which * D + lanes.stop] = summed[n, rows, :].astype(f32)
            else:
                proj[rows, lanes] = summed[n, rows, :].astype(f32)
        for source, target in ((qkv, qkv_out), (proj, proj_out)):
            stores.append(pltpu.make_async_copy(source.at[rows], target.at[rows], store_sem.at[len(stores)]))
            stores[-1].start()
    for load in loads[1:]:
        load.wait()
    through.start()
    grad_in[0] = ring[:D, :].astype(f32) + own[:D, :].astype(f32)
    stores.append(pltpu.make_async_copy(grad_in, in_out, store_sem.at[len(stores)]))
    stores[-1].start()
    grad_out[0] = jnp.transpose(ring[D:, :].astype(f32) + own[D:, :].astype(f32))
    stores.append(pltpu.make_async_copy(grad_out, out_out, store_sem.at[len(stores)]))
    stores[-1].start()
    for store in stores:
        store.wait()
    through.wait()


def finish(experts, small, summed, ring, own, tokens_in):
    hidden = own.shape[1]
    vmem = pl.BlockSpec(memory_space=pltpu.VMEM)
    anywhere = pl.BlockSpec(memory_space=pl.ANY)
    large = [((D, 3 * D), f32), ((D, D), f32), ((1, D, hidden), f32), ((1, hidden, D), f32)]
    dma = pltpu.SemaphoreType.DMA
    return pl.pallas_call(
        functools.partial(finish_kernel, experts),
        in_specs=[vmem] + [anywhere] * 4,
        out_specs=[vmem] * 5 + [anywhere] * 5,
        out_shape=[
            jax.ShapeDtypeStruct((D,), f32),
            jax.ShapeDtypeStruct((D,), f32),
            jax.ShapeDtypeStruct((experts, D), f32),
            jax.ShapeDtypeStruct((1, experts), jnp.int32),
            jax.ShapeDtypeStruct((1, experts), jnp.int32),
        ]
        + [jax.ShapeDtypeStruct(*shape) for shape in large]
        + [jax.ShapeDtypeStruct(tokens_in.shape, f32)],
        scratch_shapes=like((summed, ring, own, tokens_in))
        + [pltpu.VMEM(*shape) for shape in large]
        + [dma((4,)), dma((10,)), dma],
        compiler_params=pltpu.CompilerParams(vmem_limit_bytes=VMEM_LIMIT),
        cost_estimate=pl.CostEstimate(flops=0, bytes_accessed=14 * MIB, transcendentals=0),
        name="finish",
    )(small, summed, ring, own, tokens_in)


def per_device(
    tokens,
    segment_ids,
    expert_picks,
    priority_ranks,
    gain_attn,
    w_qkv,
    w_proj,
    gain_moe,
    w_router,
    w_in,
    w_out,
    cotangent,
):
    experts = w_router.shape[1]
    capacity = (21 * TOP * TOK_DEV + 20 * experts - 1) // (20 * experts)
    padded = (capacity + 3 + 15) // 16 * 16
    gain_attn = gain_attn.reshape(1, D)
    gain_moe = gain_moe.reshape(1, D)
    seg = segment_ids.reshape(1, SEQ)
    line = lax.axis_size("narrow")
    ring_steps = [(i, (i + 1) % line) for i in range(line)]
    together = lax.optimization_barrier

    def pass_on(values):
        return lax.ppermute(values, "narrow", ring_steps)

    early = [(w_in[0], w_out[0])]
    early.append(pass_on(early[0]))
    slot_col, slot_row, counts, windows, gz_send, normed_attn, packed = route(
        expert_picks.T, priority_ranks, seg, gain_attn, cotangent, tokens, w_qkv, experts, capacity, padded
    )
    gz = lax.all_to_all(gz_send, "wide", split_axis=0, concat_axis=0, tiled=True)
    early.append(pass_on(together((early[1], slot_row))[0]))
    context, lse, residual, normed_moe, gates, gate_row = forward(
        windows, seg, gain_moe, w_router.T, packed, tokens, w_proj
    )
    returned, back, ring, own, *others = moe(slot_row, gate_row, normed_moe, gz, early, line, capacity)
    ring = pass_on(ring)
    mixed, grad_residual, extra, grad_context, grad_proj, partial, first_pair = combine(
        experts,
        windows,
        seg,
        gain_moe,
        w_router.T,
        slot_col,
        gates,
        lse,
        counts,
        returned,
        back,
        cotangent,
        residual,
        w_proj,
        normed_moe,
        context,
        packed,
    )
    for other in others[:-1]:
        ring = pass_on((ring.astype(f32) + other.astype(f32)).astype(bf16))
    summed, small, grad_tokens, ring = shared_gradients(
        seg,
        lse,
        partial,
        gain_attn,
        first_pair,
        packed,
        grad_context,
        extra,
        normed_attn,
        grad_proj,
        w_qkv,
        tokens,
        grad_residual,
        ring,
        others[-1],
    )
    grad_gain_attn, grad_gain_moe, grad_router, kept, dropped, grad_qkv, grad_proj, grad_in, grad_out, grad_tokens = finish(
        experts, small, summed, ring, own, grad_tokens
    )
    return (
        mixed,
        grad_tokens,
        grad_gain_attn,
        grad_qkv,
        grad_proj,
        grad_gain_moe,
        grad_router.T,
        grad_in,
        grad_out,
        kept.reshape(experts),
        dropped.reshape(experts),
    )


def solution(mesh):
    both = ("wide", "narrow")
    placed = (
        P(both, None),
        P(both),
        P(both, None),
        P(both, None),
        P(),
        P(),
        P(),
        P(),
        P(),
        P("wide", None, "narrow"),
        P("wide", "narrow", None),
        P(both, None),
    )
    return jax.shard_map(
        per_device,
        mesh=mesh,
        in_specs=placed,
        out_specs=(
            P(both, None),
            P(both, None),
            P(),
            P(),
            P(),
            P(),
            P(),
            P("wide", None, "narrow"),
            P("wide", "narrow", None),
            P(),
            P(),
        ),
        check_vma=False,
    )
```

```python
import functools

import jax
import jax.numpy as jnp
from jax import lax
from jax.experimental import pallas as pl
from jax.experimental.pallas import tpu as pltpu
from jax.sharding import PartitionSpec as P

D = 512
HEADS = 8
HEAD = 64
PAIRS = HEADS // 2
PAIR = 2 * HEAD
TOP = 2
SEQ = 1024
TOK_DEV = 1024
LANES = 128
QB = 128
WINDOW = 432
TILE = 256
SLABS = tuple((max(0, QB * (b - 2)), min(SEQ, QB * (b + 3))) for b in range(SEQ // QB))
MIB = 1024 * 1024
MESH = pl.DeviceIdType.MESH
VMEM_LIMIT = 62 * MIB

f32 = jnp.float32
bf16 = jnp.bfloat16
NT = (((1,), (1,)), ((), ()))
TN = (((0,), (0,)), ((), ()))


def dot(a, b):
    return jnp.dot(a, b, preferred_element_type=f32)


def dot_nt(a, b):
    return lax.dot_general(a, b, NT, preferred_element_type=f32)


def dot_tn(a, b):
    return lax.dot_general(a, b, TN, preferred_element_type=f32)


def iota(shape, dim):
    return lax.broadcasted_iota(jnp.int32, shape, dim)


def norm_parts(values_in):
    centered = values_in - jnp.mean(values_in, axis=-1, keepdims=True)
    variance = jnp.mean(centered * centered, axis=-1, keepdims=True)
    inverse = lax.rsqrt(variance + 1e-06)
    return (centered * inverse, inverse)


def norm_back(grad_normed, gain, normalized, inverse):
    grad_gain = jnp.sum(grad_normed * normalized, axis=0, keepdims=True)
    scaled = grad_normed * gain
    inner = scaled - jnp.mean(scaled, axis=-1, keepdims=True)
    inner = inner - normalized * jnp.mean(scaled * normalized, axis=-1, keepdims=True)
    return (inner * inverse, grad_gain)


def split2(values_in):
    high = values_in.astype(bf16)
    low = (values_in - high.astype(f32)).astype(bf16)
    return high, low


def row_to_col(row):
    n = row.shape[1]
    return jnp.transpose(jnp.broadcast_to(row, (LANES, n)))[:, :1]


def loading(sources, targets, sems):
    copies = [pltpu.make_async_copy(source, target, sems.at[i]) for i, (source, target) in enumerate(zip(sources, targets))]
    for copy in copies:
        copy.start()
    return copies


def like(operands):
    return [pltpu.VMEM(operand.shape, operand.dtype) for operand in operands]


def route_kernel(
    experts,
    capacity,
    picks,
    ranks,
    seg,
    gain_attn,
    cot_in,
    tok_in,
    w_qkv_in,
    slot_col,
    slot_row,
    counts,
    windows,
    gz_out,
    normed_out,
    packed_out,
    cot,
    tok,
    w_qkv,
    gz_send,
    normed_attn,
    packed,
    load_sem,
    gz_sem,
    sems,
):
    loads = loading((cot_in, tok_in, w_qkv_in), (cot, tok, w_qkv), load_sem)
    tokens = ranks.shape[1]
    padded = gz_send.shape[1]
    rank_row = ranks[...].astype(f32)
    rank_col = row_to_col(rank_row)
    lane = iota((tokens, LANES), 1)
    pick0 = row_to_col(picks[0:1, :].astype(f32)).astype(jnp.int32)
    pick1 = row_to_col(picks[1:2, :].astype(f32)).astype(jnp.int32)
    hot = jnp.where(lane == jnp.where(lane < experts, pick0, pick1 + experts), 1.0, 0.0).astype(f32)
    before = (rank_row < rank_col).astype(f32).astype(bf16)
    earlier = dot(before, hot.astype(bf16))
    total = jnp.sum(hot, axis=0, keepdims=True)
    total = jnp.broadcast_to(total, (8, LANES))
    lane8 = iota((8, LANES), 1)
    first = jnp.where(lane8 < experts, total, 0.0)
    earlier = earlier + pltpu.roll(first, experts, axis=1)[:1]
    kept = (hot > 0.5) & (earlier < float(capacity))
    slots = jnp.where(kept, earlier, -1.0)
    slot_col[...] = slots
    slots = jnp.maximum(slots, pltpu.roll(slots, LANES - experts, axis=1))
    slots = jnp.where(lane < experts, slots, -1.0)
    slot_row[...] = jnp.transpose(slots)[:experts]
    kept_lane = jnp.sum(jnp.where(slots >= 0.0, 1.0, 0.0), axis=0, keepdims=True)
    both = total + pltpu.roll(total, LANES - experts, axis=1)
    both = jnp.where(lane8 < experts, both, 0.0)
    sub8 = iota((8, LANES), 0)
    counts[...] = jnp.where(sub8 == 0, kept_lane, jnp.where(sub8 == 1, both, 0.0))

    blocks = tokens // QB
    lane_row = iota((1, LANES), 1)
    plan = jnp.where(lane_row == 3 * blocks, 1.0, 0.0)
    for b, (slab_low, slab_high) in enumerate(SLABS):
        opening = seg[:, b * QB : b * QB + 1]
        closing = seg[:, (b + 1) * QB - 1 : (b + 1) * QB]
        first = jnp.sum(jnp.where(seg[...] < opening, 1.0, 0.0), axis=1, keepdims=True)
        after = jnp.sum(jnp.where(seg[...] <= closing, 1.0, 0.0), axis=1, keepdims=True)
        low = jnp.minimum(jnp.floor(first * (1.0 / 16)) * 16.0, float(SEQ - WINDOW))
        fits = jnp.where(after - low <= float(WINDOW), 1.0, 0.0)
        inside = jnp.where(first >= float(slab_low), 1.0, 0.0) * jnp.where(after <= float(slab_high), 1.0, 0.0)
        plan = jnp.where(lane_row == b, low, plan)
        plan = jnp.where(lane_row == blocks + b, fits, plan)
        plan = jnp.where(lane_row == 2 * blocks + b, inside, plan)
        plan = jnp.where(lane_row == 3 * blocks, plan * inside, plan)
    windows[...] = plan.astype(jnp.int32)
    loads[0].wait()

    @pl.loop(0, experts)
    def _(e):
        chosen = iota((padded, tokens), 0).astype(f32) == slot_row[pl.ds(e, 1), :]
        gz_send[e] = dot(chosen.astype(f32).astype(bf16), cot[...]).astype(bf16)
        pltpu.make_async_copy(gz_send.at[e], gz_out.at[e], gz_sem.at[e]).start()

    def stores(i):
        rows = pl.ds(pl.multiple_of(i * TILE, TILE), TILE)
        return (
            pltpu.make_async_copy(normed_attn.at[rows], normed_out.at[rows], sems.at[0, i]),
            pltpu.make_async_copy(packed.at[rows], packed_out.at[rows], sems.at[1, i]),
        )

    for load in loads[1:]:
        load.wait()

    @pl.loop(0, tokens // TILE)
    def _(i):
        rows = pl.ds(pl.multiple_of(i * TILE, TILE), TILE)
        normal, unused = norm_parts(tok[rows, :].astype(f32))
        normed = (normal * gain_attn[...]).astype(bf16)
        normed_attn[rows, :] = normed
        packed[rows, :] = dot(normed, w_qkv[...]).astype(bf16)
        for store in stores(i):
            store.start()

    @pl.loop(0, experts)
    def _(e):
        pltpu.make_async_copy(gz_send.at[e], gz_out.at[e], gz_sem.at[e]).wait()

    @pl.loop(0, tokens // TILE)
    def _(i):
        for store in stores(i):
            store.wait()


def route(picks, ranks, seg, gain_attn, cot, tok, w_qkv, experts, capacity, padded):
    tokens = tok.shape[0]
    vmem = pl.BlockSpec(memory_space=pltpu.VMEM)
    anywhere = pl.BlockSpec(memory_space=pl.ANY)
    return pl.pallas_call(
        functools.partial(route_kernel, experts, capacity),
        in_specs=[vmem] * 4 + [anywhere] * 3,
        out_shape=(
            jax.ShapeDtypeStruct((tokens, LANES), f32),
            jax.ShapeDtypeStruct((experts, tokens), f32),
            jax.ShapeDtypeStruct((8, LANES), f32),
            jax.ShapeDtypeStruct((1, LANES), jnp.int32),
            jax.ShapeDtypeStruct((experts, padded, D), bf16),
            jax.ShapeDtypeStruct((tokens, D), bf16),
            jax.ShapeDtypeStruct((tokens, 3 * D), bf16),
        ),
        out_specs=(vmem, vmem, vmem, vmem, anywhere, anywhere, anywhere),
        scratch_shapes=like((cot, tok, w_qkv))
        + [
            pltpu.VMEM((experts, padded, D), bf16),
            pltpu.VMEM((tokens, D), bf16),
            pltpu.VMEM((tokens, 3 * D), bf16),
            pltpu.SemaphoreType.DMA((3,)),
            pltpu.SemaphoreType.DMA((experts,)),
            pltpu.SemaphoreType.DMA((2, tokens // TILE)),
        ],
        compiler_params=pltpu.CompilerParams(vmem_limit_bytes=VMEM_LIMIT),
        cost_estimate=pl.CostEstimate(
            flops=2 * experts * padded * tokens * D, bytes_accessed=6 * MIB, transcendentals=0
        ),
        name="route",
    )(picks, ranks, seg, gain_attn, cot, tok, w_qkv)


def stack_heads(block):
    lane = iota(block.shape, 1)
    zero = jnp.zeros_like(block)
    return jnp.concatenate(
        [jnp.where(lane < HEAD, block, zero), jnp.where(lane < HEAD, zero, block)], axis=0
    )


def unstack_cols(stacked):
    row = iota((PAIR, QB), 0)
    picked = jnp.where(row < HEAD, stacked[:, :QB], stacked[:, QB:])
    return jnp.transpose(picked)


def window_bias(seg_col, seg_row, low, width, query):
    same = seg_col[pl.ds(low, width), :] == seg_row[:, pl.ds(query, QB)]
    half = jnp.where(same, 0.0, -1e30).astype(f32)
    return jnp.concatenate([half, half], axis=1)


def by_window(windows, block, body):
    low = windows[0, block]
    fits = windows[0, block + SEQ // QB]

    @pl.when(fits == 1)
    def _():
        body(pl.multiple_of(low, 16), WINDOW)

    @pl.when(fits != 1)
    def _():
        body(0, SEQ)


def forward_kernel(
    experts,
    windows,
    seg,
    gain_moe,
    w_router,
    packed_in,
    tok_in,
    w_proj_in,
    context_out,
    lse,
    residual_out,
    normed_moe_out,
    gates_out,
    gate_row,
    packed,
    tok,
    w_proj,
    context,
    residual,
    normed_moe,
    gates,
    seg_col,
    seg_row,
    router,
    load_sem,
    sems,
):
    loads = loading((packed_in, tok_in, w_proj_in), (packed, tok, w_proj), load_sem)
    writes = [
        pltpu.make_async_copy(source, target, sems.at[i])
        for i, (source, target) in enumerate(
            (
                (context, context_out),
                (residual, residual_out),
                (normed_moe, normed_moe_out),
                (gates, gates_out),
            )
        )
    ]
    tokens = tok.shape[0]
    seg_row[...] = seg[...].astype(f32)
    seg_col[...] = jnp.transpose(jnp.broadcast_to(seg_row[...], (LANES, tokens)))
    router[...] = jnp.zeros_like(router)
    router[:experts, :] = w_router[...]
    loads[0].wait()

    @pl.loop(0, tokens // QB)
    def _(block):
        query = pl.multiple_of(block * QB, QB)

        def body(low, width):
            bias = window_bias(seg_col, seg_row, low, width, query)
            spans = [slice(pair * PAIR, (pair + 1) * PAIR) for pair in range(PAIRS)]
            scores = []
            for span in spans:
                q = stack_heads(packed[pl.ds(query, QB), span]) * HEAD ** (-0.5)
                k = packed[pl.ds(low, width), D + span.start : D + span.stop]
                scores.append(dot_nt(k, q.astype(bf16)) + bias)
            peaks = [jnp.max(score, axis=0, keepdims=True) for score in scores]
            exponents = [jnp.exp(score - peak) for score, peak in zip(scores, peaks)]
            totals = [jnp.sum(exponent, axis=0, keepdims=True) for exponent in exponents]
            probs = [(exponent * (1.0 / total)).astype(bf16) for exponent, total in zip(exponents, totals)]
            for pair, span in enumerate(spans):
                lse[pl.ds(block, 1), pair, :] = peaks[pair] + jnp.log(totals[pair])
                v = packed[pl.ds(low, width), 2 * D + span.start : 2 * D + span.stop]
                mixed = dot_tn(v, probs[pair])
                context[pl.ds(query, QB), span] = unstack_cols(mixed).astype(bf16)

        by_window(windows, block, body)

    writes[0].start()
    for load in loads[1:]:
        load.wait()

    @pl.loop(0, tokens // TILE)
    def _(i):
        rows = pl.ds(pl.multiple_of(i * TILE, TILE), TILE)
        rest = tok[rows, :].astype(f32) + dot(context[rows, :], w_proj[...])
        residual[rows, :] = rest
        normal, unused = norm_parts(rest)
        normed = (normal * gain_moe[...]).astype(bf16)
        normed_moe[rows, :] = normed
        logits = dot_nt(normed, router[...])
        logits = jnp.where(iota(logits.shape, 1) < experts, logits, -1e30)
        exponent = jnp.exp(logits - jnp.max(logits, axis=1, keepdims=True))
        gates[rows, :] = exponent / jnp.sum(exponent, axis=1, keepdims=True)

    for write in writes[1:]:
        write.start()
    gate_row[...] = jnp.transpose(gates[...])[:experts]
    for write in writes:
        write.wait()


def forward(windows, seg, gain_moe, w_router, packed, tok, w_proj):
    tokens = tok.shape[0]
    experts = w_router.shape[0]
    vmem = pl.BlockSpec(memory_space=pltpu.VMEM)
    anywhere = pl.BlockSpec(memory_space=pl.ANY)
    return pl.pallas_call(
        functools.partial(forward_kernel, experts),
        in_specs=[pl.BlockSpec(memory_space=pltpu.SMEM)] + [vmem] * 3 + [anywhere] * 3,
        out_specs=[anywhere, vmem] + [anywhere] * 3 + [vmem],
        out_shape=(
            jax.ShapeDtypeStruct((tokens, D), bf16),
            jax.ShapeDtypeStruct((tokens // QB, PAIRS, 2 * QB), f32),
            jax.ShapeDtypeStruct((tokens, D), f32),
            jax.ShapeDtypeStruct((tokens, D), bf16),
            jax.ShapeDtypeStruct((tokens, LANES), f32),
            jax.ShapeDtypeStruct((experts, tokens), f32),
        ),
        scratch_shapes=like((packed, tok, w_proj))
        + [
            pltpu.VMEM((tokens, D), bf16),
            pltpu.VMEM((tokens, D), f32),
            pltpu.VMEM((tokens, D), bf16),
            pltpu.VMEM((tokens, LANES), f32),
            pltpu.VMEM((tokens, LANES), f32),
            pltpu.VMEM((1, tokens), f32),
            pltpu.VMEM((LANES, D), bf16),
            pltpu.SemaphoreType.DMA((3,)),
            pltpu.SemaphoreType.DMA((4,)),
        ],
        compiler_params=pltpu.CompilerParams(vmem_limit_bytes=VMEM_LIMIT),
        cost_estimate=pl.CostEstimate(
            flops=64 * 1024 * MIB, bytes_accessed=16 * MIB, transcendentals=4 * MIB
        ),
        name="attention_forward",
    )(windows, seg, gain_moe, w_router, packed, tok, w_proj)


def gelu_parts(x):
    density = jnp.exp(-0.5 * (x * x))
    return 0.5 + 0.5 * lax.erf(x * 2.0**-0.5), x * density * 0.3989422804014327


def shifted(index, by, size):
    return lax.rem(index + by, size)


def paired(index, by, size):
    total = 0
    bit = 1
    while bit < size:
        total = total + bit * lax.rem(index // bit + by // bit, 2)
        bit *= 2
    return total


def exchange(src, dst, send, recv, device):
    return pltpu.make_async_remote_copy(
        src_ref=src, dst_ref=dst, send_sem=send, recv_sem=recv, device_id=device, device_id_type=MESH
    )


def greet(barrier, sources):
    me = lax.axis_index("wide")
    line = lax.axis_index("narrow")

    @pl.loop(1, sources)
    def _(j):
        pl.semaphore_signal(barrier, inc=1, device_id=(paired(me, j, sources), line), device_id_type=MESH)


EARLY = 3


def moe_kernel(
    capacity,
    sources,
    shards,
    slot_row,
    gate_row,
    normed_in,
    gz_in,
    w_in0,
    w_out0,
    w_in1,
    w_out1,
    w_in2,
    w_out2,
    returned,
    back,
    ring_a,
    ring_b,
    third_b,
    own_grads,
    *refs,
):
    others, refs = refs[: shards - 4], refs[shards - 4 :]
    moe_body(
        capacity,
        sources,
        shards,
        slot_row,
        gate_row,
        normed_in,
        gz_in,
        ((w_in0, w_out0), (w_in1, w_out1), (w_in2, w_out2)),
        returned,
        back,
        ring_a,
        ring_b,
        third_b,
        own_grads,
        others,
        *refs,
    )


def moe_body(
    capacity,
    sources,
    shards,
    slot_row,
    gate_row,
    normed_in,
    gz_in,
    early,
    returned,
    back,
    ring_a,
    ring_b,
    third_b,
    own_grads,
    others,
    normed_moe,
    w_ins,
    w_outs,
    rows_send,
    rows,
    scaled,
    gate_slot,
    rows_t,
    gz_t,
    act,
    gpre,
    out_sum,
    back_sum,
    back_low,
    ring_out,
    ring_in,
    load_sem,
    row_sem,
    out_sem,
    back_sem,
    own_sem,
    weight_sem,
    ring_sem,
):
    out_low = rows_send
    padded = rows.shape[1]
    tokens = normed_in.shape[0]
    me = lax.axis_index("wide")
    line = lax.axis_index("narrow")
    right = (me, shifted(line, 1, shards))
    left = (me, shifted(line, shards - 1, shards))
    loads = [
        pltpu.make_async_copy(normed_in, normed_moe, load_sem.at[0]),
        pltpu.make_async_copy(gz_in, scaled, load_sem.at[1]),
    ]
    for c, pair in reversed(list(enumerate(early))):
        for i, (source, target) in enumerate(zip(pair, (w_ins, w_outs))):
            loads.append(pltpu.make_async_copy(source, target.at[c], load_sem.at[2 + 2 * c + i]))
    for load in loads:
        load.start()
    barrier = pltpu.get_barrier_semaphore()
    greet(barrier, sources)
    for near in (left, right):
        pl.semaphore_signal(barrier, inc=1, device_id=near, device_id_type=MESH)
    gate_slot[...] = jnp.zeros_like(gate_slot)

    def weights_on(c):
        return [
            exchange(part.at[c - 1], part.at[c], weight_sem.at[0, i, c], weight_sem.at[1, i, c], right)
            for i, part in enumerate((w_ins, w_outs))
        ]

    def row_copy(j):
        to = paired(me, j, sources)
        return exchange(rows_send.at[to], rows.at[me], row_sem.at[0, j], row_sem.at[1, j], (to, line))

    def result_copies(j):
        to = paired(me, j, sources)
        return [
            exchange(low.at[to], target.at[me], sem.at[0, j], sem.at[1, j], (to, line))
            for low, target, sem in ((out_low, returned, out_sem), (back_low, back, back_sem))
        ]

    keep = [
        pltpu.make_async_copy(low.at[me], target.at[me], own_sem.at[i])
        for i, (low, target) in enumerate(((out_low, returned), (back_low, back)))
    ]

    for load in loads[:1] + loads[2:4]:
        load.wait()

    def partner(i):
        turn = lax.rem(i + 1, 3)
        return i + lax.rem(i // 3, 2) * (turn - 3 * (turn // 2))

    @pl.loop(0, sources)
    def _(i):
        j = partner(lax.rem(i + 2, sources))
        e = paired(me, j, sources)
        chosen = iota((padded, tokens), 0).astype(f32) == slot_row[pl.ds(e, 1), :]
        chosen = chosen.astype(f32).astype(bf16)
        rows_send[e] = dot(chosen, normed_moe[...]).astype(bf16)
        gate = gate_row[pl.ds(e, 1), :]
        high, middle = split2(gate)
        low = (gate - high.astype(f32) - middle.astype(f32)).astype(bf16)
        three = jnp.concatenate(
            [high.astype(f32), middle.astype(f32), low.astype(f32), jnp.zeros((5, tokens), f32)], axis=0
        )
        gate_slot[:, :padded] = dot_nt(three.astype(bf16), chosen)
        tail = rows_send[e, padded - 16 :, :].astype(f32)
        sub = iota(tail.shape, 0)
        for part in range(3):
            tail = jnp.where(sub == 13 + part, gate_slot[part : part + 1, :], tail)
        rows_send[e, padded - 16 :, :] = tail.astype(bf16)

        @pl.when(i == 0)
        def _():
            pl.semaphore_wait(barrier, sources + 1)
            for copy in weights_on(EARLY):
                copy.start()

        @pl.when(j != 0)
        def _():
            row_copy(j).start()

    rows[me] = rows_send[me]
    for load in loads[1:2] + loads[4:]:
        load.wait()

    def prepare(j):
        s = paired(me, j, sources)

        @pl.when(j != 0)
        def _():
            row_copy(j).wait_recv()

        tail = rows[s, padded - 16 :, :].astype(f32)
        gate = tail[13:14] + tail[14:15] + tail[15:16]
        gate = jnp.transpose(jnp.broadcast_to(gate, (LANES, D)))[:padded, :1]
        live = iota((padded, 1), 0) < capacity
        scaled[s] = (jnp.where(live, gate, 0.0) * scaled[s].astype(f32)).astype(bf16)
        live16 = iota((16, 1), 0) < 16 - (padded - capacity)
        rows[s, padded - 16 :, :] = jnp.where(live16, tail, 0.0).astype(bf16)

    def shard_results(s, c):
        span = pl.ds(pl.multiple_of(s * padded, 16), padded)
        pre = dot(rows[s], w_ins[c])
        phi, slope = gelu_parts(pre)
        act_low = (pre * phi).astype(bf16)
        act[c, span, :] = act_low
        grad_pre = (dot_nt(scaled[s], w_outs[c]) * (phi + slope)).astype(bf16)
        gpre[c, span, :] = grad_pre
        return dot(act_low, w_outs[c]), dot_nt(grad_pre, w_ins[c])

    def send(j, result, grad_rows):
        s = paired(me, j, sources)

        @pl.when(j != 0)
        def _():
            row_copy(j).wait_send()

        out_low[s] = result.astype(bf16)
        back_low[s] = grad_rows.astype(bf16)

        @pl.when(j != 0)
        def _():
            for copy in result_copies(j):
                copy.start()

        @pl.when(j == 0)
        def _():
            for copy in keep:
                copy.start()

    def run(s, order, spot, fresh, final):
        for k, c in enumerate(order):
            result, grad_rows = shard_results(s, c)
            if k > 0 or not fresh:
                result = result + out_sum[spot]
                grad_rows = grad_rows + back_sum[spot]
            if k < len(order) - 1 or not final:
                out_sum[spot] = result
                back_sum[spot] = grad_rows
        return result, grad_rows

    def weight_grads(c):
        return dot(rows_t[...], gpre[c]).astype(bf16), dot(gz_t[...], act[c]).astype(bf16)

    both = pl.ds(0, 2)
    whole_step = exchange(ring_out.at[both], ring_in.at[both], ring_sem.at[0, 0], ring_sem.at[1, 0], right)
    half_step = exchange(ring_out.at[2], ring_in.at[2], ring_sem.at[0, 1], ring_sem.at[1, 1], right)

    late = tuple(range(EARLY, shards))

    def pass_over(first, last, order, opening, closing):
        @pl.loop(first, last)
        def _(i):
            j = partner(i)
            if opening:
                prepare(j)
            results = run(paired(me, j, sources), order, i, opening, closing)
            if closing:
                send(j, *results)

    pass_over(0, 4, (1, 0, 2), True, False)
    pass_over(4, 5, (1, 0), True, False)
    for c in late:
        for copy in weights_on(c):
            copy.wait()
        if c + 1 < shards:
            for copy in weights_on(c + 1):
                copy.start()
    pass_over(2, 4, late, False, True)
    pass_over(5, sources, (1,), True, False)
    for s in range(sources):
        rows_t[:, s * padded : (s + 1) * padded] = jnp.transpose(rows[s])
        gz_t[:, s * padded : (s + 1) * padded] = jnp.transpose(scaled[s])
    ring_out[0], ring_out[1] = weight_grads(1)
    whole_step.start()
    pass_over(4, 5, (2,) + late, False, True)
    pass_over(5, sources, (0, 2) + late, False, True)
    pass_over(0, 2, late, False, True)
    second = weight_grads(2)
    third = weight_grads(3)
    whole_step.wait_recv()
    ring_out[2] = (ring_in[0].astype(f32) + second[0].astype(f32)).astype(bf16)
    half_step.start()
    ring_b[...] = (ring_in[1].astype(f32) + second[1].astype(f32)).astype(bf16)
    third_b[...] = third[1]
    own_grads[:D, :], own_grads[D:, :] = weight_grads(0)
    for c in range(4, shards):
        others[c - 4][:D, :], others[c - 4][D:, :] = weight_grads(c)
    for copy in keep:
        copy.wait()
    half_step.wait()
    ring_a[...] = (ring_in[2].astype(f32) + third[0].astype(f32)).astype(bf16)
    whole_step.wait_send()

    @pl.loop(1, sources)
    def _(j):
        for copy in result_copies(j):
            copy.wait()


def moe(slot_row, gate_row, normed_moe, gz, early, shards, capacity):
    sources, padded, unused = gz.shape
    tokens = normed_moe.shape[0]
    hidden = early[0][0].shape[1]
    total = sources * padded
    vmem = pl.BlockSpec(memory_space=pltpu.VMEM)
    anywhere = pl.BlockSpec(memory_space=pl.ANY)
    dma = pltpu.SemaphoreType.DMA
    return pl.pallas_call(
        functools.partial(moe_kernel, capacity, sources, shards),
        in_specs=[vmem] * 2 + [anywhere] * (2 + 2 * EARLY),
        out_specs=[anywhere] * 2 + [vmem] * shards,
        out_shape=[jax.ShapeDtypeStruct(gz.shape, bf16)] * 2
        + [jax.ShapeDtypeStruct((D, hidden), bf16)] * 3
        + [jax.ShapeDtypeStruct((2 * D, hidden), bf16)] * (shards - 3),
        scratch_shapes=[
            pltpu.VMEM((tokens, D), bf16),
            pltpu.VMEM((shards, D, hidden), bf16),
            pltpu.VMEM((shards, hidden, D), bf16),
            pltpu.VMEM(gz.shape, bf16),
            pltpu.VMEM(gz.shape, bf16),
            pltpu.VMEM(gz.shape, bf16),
            pltpu.VMEM((8, D), f32),
            pltpu.VMEM((D, total), bf16),
            pltpu.VMEM((D, total), bf16),
            pltpu.VMEM((shards, total, hidden), bf16),
            pltpu.VMEM((shards, total, hidden), bf16),
            pltpu.VMEM((sources, padded, D), f32),
            pltpu.VMEM((sources, padded, D), f32),
            pltpu.VMEM(gz.shape, bf16),
            pltpu.VMEM((3, D, hidden), bf16),
            pltpu.VMEM((3, D, hidden), bf16),
            dma((2 + 2 * EARLY,)),
            dma((2, sources)),
            dma((2, sources)),
            dma((2, sources)),
            dma((2,)),
            dma((2, 2, shards)),
            dma((2, 2)),
        ],
        compiler_params=pltpu.CompilerParams(
            vmem_limit_bytes=VMEM_LIMIT, collective_id=1, has_side_effects=True
        ),
        cost_estimate=pl.CostEstimate(
            flops=12 * total * D * hidden * shards, bytes_accessed=20 * MIB, transcendentals=0
        ),
        name="moe",
    )(slot_row, gate_row, normed_moe, gz, *[part for pair in early for part in pair])


def combine_kernel(
    experts,
    windows,
    seg,
    gain_moe,
    w_router,
    slot_col,
    gates,
    lse,
    counts,
    returned_in,
    back_in,
    cot_in,
    residual_in,
    w_proj_in,
    normed_moe_in,
    context_in,
    packed_in,
    mixed_out,
    grad_residual_out,
    extra_out,
    grad_context,
    grad_proj,
    small,
    pair_grads,
    returned,
    back,
    cot,
    residual,
    w_proj,
    normed_moe,
    context,
    packed,
    mixed,
    grad_residual,
    extra,
    hot,
    seg_col,
    seg_row,
    router,
    grad_attn,
    grad_logits,
    grad_k,
    grad_v,
    bias,
    pair_k,
    pair_v,
    read_sem,
    sems,
):
    tokens = cot.shape[0]
    slots_all, padded = returned.shape[0] * returned.shape[1], returned.shape[1]
    reads = loading(
        (returned_in, back_in, cot_in, residual_in, w_proj_in, normed_moe_in, context_in, packed_in),
        (returned, back, cot, residual, w_proj, normed_moe, context, packed),
        read_sem,
    )
    writes = (
        pltpu.make_async_copy(mixed, mixed_out, sems.at[0]),
        pltpu.make_async_copy(grad_residual, grad_residual_out, sems.at[1]),
        pltpu.make_async_copy(extra, extra_out, sems.at[2]),
    )
    extra[...] = jnp.zeros_like(extra)
    seg_row[...] = seg[...].astype(f32)
    seg_col[...] = jnp.transpose(jnp.broadcast_to(seg_row[...], (LANES, tokens)))
    router[...] = jnp.zeros_like(router)
    router[:experts, :] = w_router[...]
    small[...] = jnp.zeros_like(small)
    small[2:4, :LANES] = counts[:2, :]

    for read in reads[:5]:
        read.wait()

    @pl.loop(0, tokens // TILE)
    def _(i):
        rows = pl.ds(pl.multiple_of(i * TILE, TILE), TILE)
        grad_z = cot[rows, :].astype(f32)
        probs = gates[rows, :]
        slots = slot_col[rows, :]
        lane = iota((TILE, LANES), 1)
        rest = residual[rows, :]
        twice = probs + pltpu.roll(probs, experts, axis=1)
        place = jnp.where(lane < experts, lane, lane - experts).astype(f32) * float(padded)
        total = rest
        grad_gates = jnp.zeros((TILE, LANES), f32)
        spots = iota((TILE, slots_all), 1).astype(f32)
        picks = []
        for k in range(TOP):
            mine = (slots >= 0.0) & (lane >= k * experts) & (lane < (k + 1) * experts)
            spot = jnp.sum(jnp.where(mine, place + slots + 1.0, 0.0), axis=1, keepdims=True) - 1.0
            hot[k * TILE : (k + 1) * TILE, :] = (spots == spot).astype(f32).astype(bf16)
            picks.append(mine)
        back_total = dot(hot[:TILE, :] + hot[TILE:, :], back[...].reshape(slots_all, D))
        results = dot(hot[...], returned[...].reshape(slots_all, D))
        for k in range(TOP):
            result = results[k * TILE : (k + 1) * TILE]
            total = total + jnp.sum(jnp.where(picks[k], twice, 0.0), axis=1, keepdims=True) * result
            inner = jnp.sum(result * grad_z, axis=1, keepdims=True)
            grad_gates = grad_gates + jnp.where(picks[k], inner, 0.0)
        grad_gates = grad_gates + pltpu.roll(grad_gates, LANES - experts, axis=1)
        grad_gates = jnp.where(lane < experts, grad_gates, 0.0)
        mixed[rows, :] = total.astype(bf16)
        gate_inner = jnp.sum(probs * grad_gates, axis=1, keepdims=True)
        high, low = split2(probs * (grad_gates - gate_inner))
        grad_logits[rows, :LANES] = high
        grad_logits[rows, LANES:] = low
        grad_normed = back_total + dot(high, router[...]) + dot(low, router[...])
        normal, inverse = norm_parts(rest)
        grad_norm, grad_gain = norm_back(grad_normed, gain_moe[...], normal, inverse)
        small[1:2, :] += grad_gain
        grad_rest = grad_z + grad_norm
        grad_residual[rows, :] = grad_rest
        attn = grad_rest.astype(bf16)
        grad_attn[rows, :] = attn
        grad_context[rows, :] = dot_nt(attn, w_proj[...]).astype(bf16)

    for write in writes[:2]:
        write.start()
    for read in reads[5:7]:
        read.wait()
    both = dot_tn(normed_moe[...], grad_logits[...])
    both = jnp.transpose(both[:, :LANES] + both[:, LANES:])
    small[8:, :] = both[:experts]
    grad_proj[...] = dot_tn(context[...], grad_attn[...])
    blocks = tokens // QB
    reads[7].wait()

    @pl.when(windows[0, 3 * blocks] != 1)
    def _():
        grad_k[...] = jnp.zeros_like(grad_k)
        grad_v[...] = jnp.zeros_like(grad_v)

        @pl.loop(0, blocks)
        def _(block):
            query = pl.multiple_of(block * QB, QB)

            @pl.when(windows[0, 2 * blocks + block] != 1)
            def _():
                bias = window_bias(seg_col, seg_row, 0, SEQ, query)
                spans = [slice(pair * PAIR, (pair + 1) * PAIR) for pair in range(PAIRS)]
                keys = pl.ds(0, SEQ)
                queries = [
                    (stack_heads(packed[pl.ds(query, QB), span]) * HEAD ** (-0.5)).astype(bf16) for span in spans
                ]
                grads = [stack_heads(grad_context[pl.ds(query, QB), span]) for span in spans]
                probs = []
                grad_probs = []
                for pair, span in enumerate(spans):
                    k = packed[keys, D + span.start : D + span.stop]
                    v = packed[keys, 2 * D + span.start : 2 * D + span.stop]
                    probs.append(jnp.exp(dot_nt(k, queries[pair]) + bias - lse[pl.ds(block, 1), pair, :]))
                    grad_probs.append(dot_nt(v, grads[pair]))
                grad_scores = []
                for pair, span in enumerate(spans):
                    grad_v[keys, span] += dot(probs[pair].astype(bf16), grads[pair])
                    weighted = probs[pair] * grad_probs[pair]
                    inner = jnp.sum(weighted, axis=0, keepdims=True)
                    grad_scores.append((weighted - probs[pair] * inner).astype(bf16))
                for pair, span in enumerate(spans):
                    k = packed[keys, D + span.start : D + span.stop]
                    grad_k[keys, span] += dot(grad_scores[pair], queries[pair])
                    grad_q = unstack_cols(dot_tn(k, grad_scores[pair])) * HEAD ** (-0.5)
                    extra[pl.ds(query, QB), span] = grad_q.astype(bf16)
                grad_context[pl.ds(query, QB), :] = jnp.zeros((QB, D), bf16)

        extra[:, D : 2 * D] = grad_k[...].astype(bf16)
        extra[:, 2 * D :] = grad_v[...].astype(bf16)

    writes[2].start()
    slab_bias(bias, seg_col, seg_row[...])
    pair_backward(0, packed, grad_context, lse, extra, bias, pair_k, pair_v, pair_grads)
    for write in writes:
        write.wait()


def combine(experts, windows, *operands):
    returned = operands[7]
    tokens = operands[9].shape[0]
    vmem = pl.BlockSpec(memory_space=pltpu.VMEM)
    anywhere = pl.BlockSpec(memory_space=pl.ANY)
    return pl.pallas_call(
        functools.partial(combine_kernel, experts),
        in_specs=[pl.BlockSpec(memory_space=pltpu.SMEM)] + [vmem] * 7 + [anywhere] * 8,
        out_specs=[anywhere, anywhere, anywhere, vmem, vmem, vmem, vmem],
        out_shape=(
            jax.ShapeDtypeStruct((tokens, D), bf16),
            jax.ShapeDtypeStruct((tokens, D), f32),
            jax.ShapeDtypeStruct((tokens, 3 * D), bf16),
            jax.ShapeDtypeStruct((tokens, D), bf16),
            jax.ShapeDtypeStruct((D, D), f32),
            jax.ShapeDtypeStruct((8 + experts, D), f32),
            jax.ShapeDtypeStruct((tokens, 3 * PAIR), bf16),
        ),
        scratch_shapes=like(operands[7:])
        + [
            pltpu.VMEM((tokens, D), bf16),
            pltpu.VMEM((tokens, D), f32),
            pltpu.VMEM((tokens, 3 * D), bf16),
            pltpu.VMEM((TOP * TILE, returned.shape[0] * returned.shape[1]), bf16),
            pltpu.VMEM((tokens, LANES), f32),
            pltpu.VMEM((1, tokens), f32),
            pltpu.VMEM((LANES, D), bf16),
            pltpu.VMEM((tokens, D), bf16),
            pltpu.VMEM((tokens, 2 * LANES), bf16),
            pltpu.VMEM((tokens, D), f32),
            pltpu.VMEM((tokens, D), f32),
            pltpu.VMEM((SLAB_AT[-1], QB), f32),
            pltpu.VMEM((tokens, PAIR), f32),
            pltpu.VMEM((tokens, PAIR), f32),
            pltpu.SemaphoreType.DMA((8,)),
            pltpu.SemaphoreType.DMA((3,)),
        ],
        compiler_params=pltpu.CompilerParams(vmem_limit_bytes=VMEM_LIMIT),
        cost_estimate=pl.CostEstimate(
            flops=30 * 1024 * MIB, bytes_accessed=30 * MIB, transcendentals=4 * MIB
        ),
        name="combine",
    )(windows, *operands)


SLAB_AT = tuple(sum(high - low for low, high in SLABS[:b]) for b in range(len(SLABS) + 1))


def slab_bias(bias, seg_col, seg_row):
    for b, (low, high) in enumerate(SLABS):
        same = seg_col[low:high, :] == seg_row[:, b * QB : (b + 1) * QB]
        bias[SLAB_AT[b] : SLAB_AT[b + 1], :] = jnp.where(same, 0.0, -1e30)


def pair_backward(pair, packed, grad_context, lse, extra, bias, grad_k, grad_v, out):
    def span(which):
        return pl.ds(pl.multiple_of(which * D + pair * PAIR, PAIR), PAIR)

    grad_k[...] = extra[:, span(1)].astype(f32)
    grad_v[...] = extra[:, span(2)].astype(f32)
    for group in range(0, len(SLABS), 4):
        blocks = range(group, group + 4)
        queries, grads, probs, grad_probs, grad_scores = [], [], [], [], []
        for b in blocks:
            low, high = SLABS[b]
            rows = slice(b * QB, (b + 1) * QB)
            queries.append((stack_heads(packed[rows, span(0)]) * HEAD ** (-0.5)).astype(bf16))
            grads.append(stack_heads(grad_context[rows, span(0)]))
            masked = bias[SLAB_AT[b] : SLAB_AT[b + 1], :]
            scores = dot_nt(packed[low:high, span(1)], queries[-1]) + jnp.concatenate([masked, masked], axis=1)
            probs.append(jnp.exp(scores - lse[b, pl.ds(pair, 1), :]))
            grad_probs.append(dot_nt(packed[low:high, span(2)], grads[-1]))
        for i, b in enumerate(blocks):
            low, high = SLABS[b]
            grad_v[low:high, :] += dot(probs[i].astype(bf16), grads[i])
            weighted = probs[i] * grad_probs[i]
            inner = jnp.sum(weighted, axis=0, keepdims=True)
            grad_scores.append((weighted - probs[i] * inner).astype(bf16))
        for i, b in enumerate(blocks):
            low, high = SLABS[b]
            rows = slice(b * QB, (b + 1) * QB)
            grad_k[low:high, :] += dot(grad_scores[i], queries[i])
            grad_q = unstack_cols(dot_tn(packed[low:high, span(1)], grad_scores[i])) * HEAD ** (-0.5)
            out[rows, :PAIR] = (grad_q + extra[rows, span(0)].astype(f32)).astype(bf16)
    out[:, PAIR : 2 * PAIR] = grad_k[...].astype(bf16)
    out[:, 2 * PAIR :] = grad_v[...].astype(bf16)


def shared_kernel(
    chips,
    planes,
    seg,
    lse,
    partial,
    gain_attn,
    first_in,
    packed_in,
    grad_context_in,
    extra_in,
    normed_attn_in,
    grad_proj_in,
    w_qkv_in,
    tok_in,
    grad_residual_in,
    ring_in,
    last_in,
    summed,
    small,
    grad_tokens_out,
    ring_last,
    pair_grads,
    packed,
    grad_context,
    extra,
    normed_attn,
    grad_proj,
    w_qkv,
    tok,
    grad_residual,
    ring,
    last_term,
    grad_tokens,
    normed_t,
    seg_col,
    bias,
    grad_k,
    grad_v,
    grad_packed,
    half,
    core_out,
    core_in,
    chip_out,
    chip_in,
    plane_out,
    plane_in,
    small_own,
    small_core,
    small_chip,
    small_plane,
    load_sem,
    store_sem,
    ring_sem,
    core_sem,
    chip_sem,
    plane_sem,
    plane_sem2,
    chip_sem2,
    core_sem2,
    small_sem,
    small_chip_sem,
    small_plane_sem,
):
    tokens = tok.shape[0]
    stages = 16 // planes
    pairs = PAIRS // stages
    tiles = tokens // TILE
    wide = lax.axis_index("wide")
    plane = lax.axis_index("narrow")
    core = lax.rem(wide, 2)
    chip = wide // 2
    share = D // (2 * chips)
    partner = (chip * 2 + 1 - core, plane)
    mine = pl.ds(pl.multiple_of(core * (D // 2), D // 2), D // 2)
    other = pl.ds(pl.multiple_of((1 - core) * (D // 2), D // 2), D // 2)
    chunk = pl.ds(pl.multiple_of(core * (D // 2) + chip * share, share), share)
    own_chunk = pl.ds(pl.multiple_of(chip * share, share), share)

    loads = [
        pltpu.make_async_copy(source, target, load_sem.at[i])
        for i, (source, target) in enumerate(
            (
                (first_in, pair_grads),
                (normed_attn_in, normed_attn),
                (grad_proj_in, grad_proj),
                (ring_in, ring),
                (last_in, last_term),
                (packed_in, packed),
                (grad_context_in, grad_context),
                (extra_in, extra),
                (w_qkv_in, w_qkv),
                (tok_in, tok),
                (grad_residual_in, grad_residual),
            )
        )
    ]
    for load in loads:
        load.start()

    def chip_at(j):
        to = shifted(chip, j, chips)
        return to, (to * 2 + core, plane)

    def plane_at(j):
        to = shifted(plane, j, planes)
        return to, (wide, to)

    barrier = pltpu.get_barrier_semaphore()
    pl.semaphore_signal(barrier, inc=1, device_id=partner, device_id_type=MESH)

    @pl.loop(1, chips)
    def _(j):
        pl.semaphore_signal(barrier, inc=1, device_id=chip_at(j)[1], device_id_type=MESH)

    @pl.loop(1, planes)
    def _(j):
        pl.semaphore_signal(barrier, inc=1, device_id=plane_at(j)[1], device_id_type=MESH)

    def blocks(stage):
        return pl.ds(stage * planes, planes)

    def core_copy(stage):
        at = blocks(stage)
        return exchange(core_out.at[at], core_in.at[at], core_sem.at[0, stage], core_sem.at[1, stage], partner)

    def chip_copy(stage, j):
        to, device = chip_at(j)
        rows = pl.ds(pl.multiple_of(to * share, share), share)
        at = blocks(stage)
        return exchange(
            chip_out.at[at, rows], chip_in.at[j, at], chip_sem.at[0, stage, j], chip_sem.at[1, stage, j], device
        )

    def plane_copy(stage, j):
        to, device = plane_at(j)
        return exchange(
            plane_out.at[stage * planes + to],
            plane_in.at[j, stage],
            plane_sem.at[0, stage, j],
            plane_sem.at[1, stage, j],
            device,
        )

    def plane_back(stage, j):
        spot = summed.at[stage * planes + plane, chunk]
        return exchange(spot, spot, plane_sem2.at[0, stage, j], plane_sem2.at[1, stage, j], plane_at(j)[1])

    def chip_back(stage, j):
        spot = summed.at[blocks(stage), chunk]
        return exchange(spot, spot, chip_sem2.at[0, stage, j], chip_sem2.at[1, stage, j], chip_at(j)[1])

    def core_back(stage):
        spot = summed.at[blocks(stage), mine]
        return exchange(spot, spot, core_sem2.at[0, stage], core_sem2.at[1, stage], partner)

    def small_core_copy():
        return exchange(small_own, small_core, small_sem.at[0], small_sem.at[1], partner)

    def small_chip_copy(j):
        spot = small_chip.at[chip]
        return exchange(spot, spot, small_chip_sem.at[0, j], small_chip_sem.at[1, j], chip_at(j)[1])

    def small_plane_copy(j):
        spot = small_plane.at[plane]
        return exchange(spot, spot, small_plane_sem.at[0, j], small_plane_sem.at[1, j], plane_at(j)[1])

    def pair_products(pair):
        spare = dot(normed_t[other, :], pair_grads[...])
        own = dot(normed_t[mine, :], pair_grads[...])
        lanes = pl.ds(pl.multiple_of(pair * PAIR, PAIR), PAIR)
        for which in range(3):
            at = slice(which * PAIR, (which + 1) * PAIR)
            core_out[pair * 4 + which] = spare[:, at].astype(bf16)
            half[pair * 4 + which] = own[:, at]
            grad_packed[:, pl.ds(pl.multiple_of(which * D + pair * PAIR, PAIR), PAIR)] = pair_grads[:, at]
        core_out[pair * 4 + 3] = grad_proj[other, lanes].astype(bf16)
        half[pair * 4 + 3] = grad_proj[mine, lanes]

    def chip_stage(stage):
        core_copy(stage).wait_recv()
        at = blocks(stage)
        total = half[at] + core_in[at].astype(f32)
        half[at] = total
        chip_out[at] = total.astype(bf16)

        @pl.loop(1, chips)
        def _(j):
            chip_copy(stage, j).start()

    def plane_stage(stage):
        at = blocks(stage)
        total = half[at, own_chunk, :]
        for j in range(1, chips):
            chip_copy(stage, j).wait_recv()
            total = total + chip_in[j, at].astype(f32)
        half[at, own_chunk, :] = total
        plane_out[at] = total.astype(bf16)

        @pl.loop(1, planes)
        def _(j):
            plane_copy(stage, j).start()

    def own_stage(stage):
        total = half[stage * planes + plane, own_chunk, :]
        for j in range(1, planes):
            plane_copy(stage, j).wait_recv()
            total = total + plane_in[j, stage].astype(f32)
        summed[stage * planes + plane, chunk, :] = total.astype(bf16)

        @pl.loop(1, planes)
        def _(j):
            plane_back(stage, j).start()

    def gather_stage(stage):
        @pl.loop(1, planes)
        def _(j):
            plane_back(stage, j).wait_recv()

        @pl.loop(1, chips)
        def _(j):
            chip_back(stage, j).start()

    def last_stage(stage):
        @pl.loop(1, chips)
        def _(j):
            chip_back(stage, j).wait_recv()

        core_back(stage).start()

    def norm_tile(i):
        rows = slice(i * TILE, (i + 1) * TILE)
        grad_normed = dot_nt(grad_packed[rows, :], w_qkv[...])
        normal, inverse = norm_parts(tok[rows, :].astype(f32))
        grad_norm, grad_gain = norm_back(grad_normed, gain_attn[...], normal, inverse)
        small_own[0:1, :] += grad_gain
        grad_tokens[rows, :] = grad_residual[rows, :] + grad_norm

    small_own[...] = partial[...]
    seg_row = seg[...].astype(f32)
    seg_col[...] = jnp.transpose(jnp.broadcast_to(seg_row, (LANES, tokens)))
    slab_bias(bias, seg_col, seg_row)
    for load in loads[:3]:
        load.wait()
    normed_t[...] = jnp.transpose(normed_attn[...])
    pair_products(0)
    pl.semaphore_wait(barrier, chips + planes - 1)
    if pairs == 1:
        core_copy(0).start()
    for load in loads[3:5]:
        load.wait()
    ring[...] = (ring[...].astype(f32) + last_term[...].astype(f32)).astype(bf16)
    last = exchange(ring, ring_last, ring_sem.at[0], ring_sem.at[1], plane_at(1)[1])
    last.start()
    for load in loads[5:8]:
        load.wait()

    @pl.loop(1, PAIRS)
    def _(pair):
        pair_backward(pair, packed, grad_context, lse, extra, bias, grad_k, grad_v, pair_grads)
        pair_products(pair)

        @pl.when(lax.rem(pair + 1, pairs) == 0)
        def _():
            stage = pair // pairs
            core_copy(stage).start()

            @pl.when(stage > 0)
            def _():
                chip_stage(stage - 1)

            @pl.when(stage > 1)
            def _():
                plane_stage(stage - 2)

            @pl.when(stage > 2)
            def _():
                own_stage(stage - 3)

    for load in loads[8:]:
        load.wait()
    steps = (chip_stage, plane_stage, own_stage, gather_stage, last_stage)
    for late in range(len(steps)):
        if late == 0:
            norm_tile(0)
        for i, step in enumerate(steps):
            stage = stages - 1 + late - i
            if i >= late and 0 <= stage < stages:
                step(stage)
        if late == 0:
            for i in range(1, tiles):
                norm_tile(i)
            small_core_copy().start()
            store = pltpu.make_async_copy(grad_tokens, grad_tokens_out, store_sem)
            store.start()
        if late == 1:
            small_core_copy().wait_recv()
            small_chip[chip] = small_own[...] + small_core[...]

            @pl.loop(1, chips)
            def _(j):
                small_chip_copy(j).start()

        if late == 2:

            @pl.loop(1, chips)
            def _(j):
                small_chip_copy(j).wait_recv()

            total = small_chip[0]
            for c in range(1, chips):
                total = total + small_chip[c]
            small_plane[plane] = total

            @pl.loop(1, planes)
            def _(j):
                small_plane_copy(j).start()

    @pl.loop(1, planes)
    def _(j):
        small_plane_copy(j).wait_recv()

    total = small_plane[0]
    for c in range(1, planes):
        total = total + small_plane[c]
    small[...] = total
    store.wait()
    last.wait()

    @pl.loop(0, stages)
    def _(stage):
        core_back(stage).wait()
        core_copy(stage).wait_send()

        @pl.loop(1, chips)
        def _(j):
            chip_back(stage, j).wait_send()
            chip_copy(stage, j).wait_send()

        @pl.loop(1, planes)
        def _(j):
            plane_back(stage, j).wait_send()
            plane_copy(stage, j).wait_send()

    @pl.loop(1, planes)
    def _(j):
        small_plane_copy(j).wait_send()

    @pl.loop(1, chips)
    def _(j):
        small_chip_copy(j).wait_send()

    small_core_copy().wait_send()


def shared_gradients(*operands):
    partial, packed = operands[2], operands[5]
    tokens = packed.shape[0]
    chips = lax.axis_size("wide") // 2
    planes = lax.axis_size("narrow")
    stages = 16 // planes
    share = D // (2 * chips)
    rows = partial.shape[0]
    dma = pltpu.SemaphoreType.DMA
    vmem = pl.BlockSpec(memory_space=pltpu.VMEM)
    anywhere = pl.BlockSpec(memory_space=pl.ANY)
    return pl.pallas_call(
        functools.partial(shared_kernel, chips, planes),
        in_specs=[vmem] * 4 + [anywhere] * 11,
        out_specs=(vmem, vmem, anywhere, anywhere),
        out_shape=(
            jax.ShapeDtypeStruct((16, D, LANES), bf16),
            jax.ShapeDtypeStruct((rows, D), f32),
            jax.ShapeDtypeStruct((tokens, D), f32),
            jax.ShapeDtypeStruct(operands[-1].shape, bf16),
        ),
        scratch_shapes=[pltpu.VMEM(operand.shape, operand.dtype) for operand in operands[4:]]
        + [
            pltpu.VMEM((tokens, D), f32),
            pltpu.VMEM((D, tokens), bf16),
            pltpu.VMEM((tokens, LANES), f32),
            pltpu.VMEM((SLAB_AT[-1], QB), f32),
            pltpu.VMEM((tokens, PAIR), f32),
            pltpu.VMEM((tokens, PAIR), f32),
            pltpu.VMEM((tokens, 3 * D), bf16),
            pltpu.VMEM((16, D // 2, LANES), f32),
            pltpu.VMEM((16, D // 2, LANES), bf16),
            pltpu.VMEM((16, D // 2, LANES), bf16),
            pltpu.VMEM((16, D // 2, LANES), bf16),
            pltpu.VMEM((chips, 16, share, LANES), bf16),
            pltpu.VMEM((16, share, LANES), bf16),
            pltpu.VMEM((planes, stages, share, LANES), bf16),
            pltpu.VMEM((rows, D), f32),
            pltpu.VMEM((rows, D), f32),
            pltpu.VMEM((chips, rows, D), f32),
            pltpu.VMEM((planes, rows, D), f32),
            dma((11,)),
            dma,
            dma((2,)),
            dma((2, stages)),
            dma((2, stages, chips)),
            dma((2, stages, planes)),
            dma((2, stages, planes)),
            dma((2, stages, chips)),
            dma((2, stages)),
            dma((2,)),
            dma((2, chips)),
            dma((2, planes)),
        ],
        compiler_params=pltpu.CompilerParams(
            vmem_limit_bytes=VMEM_LIMIT, collective_id=2, has_side_effects=True
        ),
        cost_estimate=pl.CostEstimate(
            flops=12 * tokens * D * D, bytes_accessed=16 * MIB, transcendentals=0
        ),
        name="shared_gradients",
    )(*operands)


def finish_kernel(
    experts,
    small,
    summed_in,
    ring_a_in,
    ring_b_in,
    own_in,
    tokens_in,
    gain_attn,
    gain_moe,
    router,
    kept,
    dropped,
    qkv_out,
    proj_out,
    in_out,
    out_out,
    tokens_out,
    summed,
    ring_a,
    ring_b,
    own,
    tokens,
    qkv,
    proj,
    grad_in,
    grad_out,
    load_sem,
    store_sem,
    token_sem,
):
    loads = loading(
        (summed_in, ring_a_in, ring_b_in, own_in, tokens_in), (summed, ring_a, ring_b, own, tokens), load_sem
    )
    through = pltpu.make_async_copy(tokens, tokens_out, token_sem)
    gain_attn[...] = small[0, :]
    gain_moe[...] = small[1, :]
    router[...] = small[8:, :]
    counted = small[2:4, :experts]
    kept[...] = counted[0:1].astype(jnp.int32)
    dropped[...] = (counted[1:2] - counted[0:1]).astype(jnp.int32)
    loads[0].wait()
    stores = []
    step = D // 4
    for i in range(4):
        rows = slice(i * step, (i + 1) * step)
        for n in range(16):
            pair, which = divmod(n, 4)
            lanes = slice(pair * PAIR, (pair + 1) * PAIR)
            if which < 3:
                qkv[rows, which * D + lanes.start : which * D + lanes.stop] = summed[n, rows, :].astype(f32)
            else:
                proj[rows, lanes] = summed[n, rows, :].astype(f32)
        for source, target in ((qkv, qkv_out), (proj, proj_out)):
            stores.append(pltpu.make_async_copy(source.at[rows], target.at[rows], store_sem.at[len(stores)]))
            stores[-1].start()
    for load in loads[1:]:
        load.wait()
    through.start()
    grad_in[0] = ring_a[...].astype(f32) + own[:D, :].astype(f32)
    stores.append(pltpu.make_async_copy(grad_in, in_out, store_sem.at[len(stores)]))
    stores[-1].start()
    grad_out[0] = jnp.transpose(ring_b[...].astype(f32) + own[D:, :].astype(f32))
    stores.append(pltpu.make_async_copy(grad_out, out_out, store_sem.at[len(stores)]))
    stores[-1].start()
    for store in stores:
        store.wait()
    through.wait()


def finish(experts, small, summed, ring_a, ring_b, own, tokens_in):
    hidden = own.shape[1]
    vmem = pl.BlockSpec(memory_space=pltpu.VMEM)
    anywhere = pl.BlockSpec(memory_space=pl.ANY)
    large = [((D, 3 * D), f32), ((D, D), f32), ((1, D, hidden), f32), ((1, hidden, D), f32)]
    dma = pltpu.SemaphoreType.DMA
    return pl.pallas_call(
        functools.partial(finish_kernel, experts),
        in_specs=[vmem] + [anywhere] * 5,
        out_specs=[vmem] * 5 + [anywhere] * 5,
        out_shape=[
            jax.ShapeDtypeStruct((D,), f32),
            jax.ShapeDtypeStruct((D,), f32),
            jax.ShapeDtypeStruct((experts, D), f32),
            jax.ShapeDtypeStruct((1, experts), jnp.int32),
            jax.ShapeDtypeStruct((1, experts), jnp.int32),
        ]
        + [jax.ShapeDtypeStruct(*shape) for shape in large]
        + [jax.ShapeDtypeStruct(tokens_in.shape, f32)],
        scratch_shapes=like((summed, ring_a, ring_b, own, tokens_in))
        + [pltpu.VMEM(*shape) for shape in large]
        + [dma((5,)), dma((10,)), dma],
        compiler_params=pltpu.CompilerParams(vmem_limit_bytes=VMEM_LIMIT),
        cost_estimate=pl.CostEstimate(flops=0, bytes_accessed=14 * MIB, transcendentals=0),
        name="finish",
    )(small, summed, ring_a, ring_b, own, tokens_in)


def per_device(
    tokens,
    segment_ids,
    expert_picks,
    priority_ranks,
    gain_attn,
    w_qkv,
    w_proj,
    gain_moe,
    w_router,
    w_in,
    w_out,
    cotangent,
):
    experts = w_router.shape[1]
    capacity = (21 * TOP * TOK_DEV + 20 * experts - 1) // (20 * experts)
    padded = (capacity + 3 + 15) // 16 * 16
    gain_attn = gain_attn.reshape(1, D)
    gain_moe = gain_moe.reshape(1, D)
    seg = segment_ids.reshape(1, SEQ)
    line = lax.axis_size("narrow")
    ring_steps = [(i, (i + 1) % line) for i in range(line)]
    together = lax.optimization_barrier

    def pass_on(values):
        return lax.ppermute(values, "narrow", ring_steps)

    early = [(w_in[0], w_out[0])]
    early.append(pass_on(early[0]))
    slot_col, slot_row, counts, windows, gz_send, normed_attn, packed = route(
        expert_picks.T, priority_ranks, seg, gain_attn, cotangent, tokens, w_qkv, experts, capacity, padded
    )
    gz = lax.all_to_all(gz_send, "wide", split_axis=0, concat_axis=0, tiled=True)
    early.append(pass_on(together((early[1], slot_row))[0]))
    context, lse, residual, normed_moe, gates, gate_row = forward(
        windows, seg, gain_moe, w_router.T, packed, tokens, w_proj
    )
    returned, back, ring_a, ring_b, last_b, own, *others = moe(slot_row, gate_row, normed_moe, gz, early, line, capacity)
    ring_a, ring_b = pass_on((ring_a, ring_b))
    mixed, grad_residual, extra, grad_context, grad_proj, partial, first_pair = combine(
        experts,
        windows,
        seg,
        gain_moe,
        w_router.T,
        slot_col,
        gates,
        lse,
        counts,
        returned,
        back,
        cotangent,
        residual,
        w_proj,
        normed_moe,
        context,
        packed,
    )
    for other in others:
        ring_a = pass_on((ring_a.astype(f32) + other[:D].astype(f32)).astype(bf16))
        ring_b, last_b = pass_on((ring_b.astype(f32) + last_b.astype(f32)).astype(bf16)), other[D:]
    summed, small, grad_tokens, ring_b = shared_gradients(
        seg,
        lse,
        partial,
        gain_attn,
        first_pair,
        packed,
        grad_context,
        extra,
        normed_attn,
        grad_proj,
        w_qkv,
        tokens,
        grad_residual,
        ring_b,
        last_b,
    )
    grad_gain_attn, grad_gain_moe, grad_router, kept, dropped, grad_qkv, grad_proj, grad_in, grad_out, grad_tokens = finish(
        experts, small, summed, ring_a, ring_b, own, grad_tokens
    )
    return (
        mixed,
        grad_tokens,
        grad_gain_attn,
        grad_qkv,
        grad_proj,
        grad_gain_moe,
        grad_router.T,
        grad_in,
        grad_out,
        kept.reshape(experts),
        dropped.reshape(experts),
    )


def solution(mesh):
    both = ("wide", "narrow")
    placed = (
        P(both, None),
        P(both),
        P(both, None),
        P(both, None),
        P(),
        P(),
        P(),
        P(),
        P(),
        P("wide", None, "narrow"),
        P("wide", "narrow", None),
        P(both, None),
    )
    return jax.shard_map(
        per_device,
        mesh=mesh,
        in_specs=placed,
        out_specs=(
            P(both, None),
            P(both, None),
            P(),
            P(),
            P(),
            P(),
            P(),
            P("wide", None, "narrow"),
            P("wide", "narrow", None),
            P(),
            P(),
        ),
        check_vma=False,
    )
```

```python
import functools

import jax
import jax.numpy as jnp
from jax import lax
from jax.experimental import pallas as pl
from jax.experimental.pallas import tpu as pltpu
from jax.sharding import PartitionSpec as P

D = 512
HEADS = 8
HEAD = 64
PAIRS = HEADS // 2
PAIR = 2 * HEAD
TOP = 2
SEQ = 1024
TOK_DEV = 1024
LANES = 128
QB = 128
WINDOW = 432
TILE = 256
SLABS = tuple((max(0, QB * (b - 2)), min(SEQ, QB * (b + 3))) for b in range(SEQ // QB))
MIB = 1024 * 1024
MESH = pl.DeviceIdType.MESH
VMEM_LIMIT = 62 * MIB

f32 = jnp.float32
bf16 = jnp.bfloat16
NT = (((1,), (1,)), ((), ()))
TN = (((0,), (0,)), ((), ()))


def dot(a, b):
    return jnp.dot(a, b, preferred_element_type=f32)


def dot_nt(a, b):
    return lax.dot_general(a, b, NT, preferred_element_type=f32)


def dot_tn(a, b):
    return lax.dot_general(a, b, TN, preferred_element_type=f32)


def iota(shape, dim):
    return lax.broadcasted_iota(jnp.int32, shape, dim)


def norm_parts(values_in):
    centered = values_in - jnp.mean(values_in, axis=-1, keepdims=True)
    variance = jnp.mean(centered * centered, axis=-1, keepdims=True)
    inverse = lax.rsqrt(variance + 1e-06)
    return (centered * inverse, inverse)


def norm_back(grad_normed, gain, normalized, inverse):
    grad_gain = jnp.sum(grad_normed * normalized, axis=0, keepdims=True)
    scaled = grad_normed * gain
    inner = scaled - jnp.mean(scaled, axis=-1, keepdims=True)
    inner = inner - normalized * jnp.mean(scaled * normalized, axis=-1, keepdims=True)
    return (inner * inverse, grad_gain)


def split2(values_in):
    high = values_in.astype(bf16)
    low = (values_in - high.astype(f32)).astype(bf16)
    return high, low


def row_to_col(row):
    n = row.shape[1]
    return jnp.transpose(jnp.broadcast_to(row, (LANES, n)))[:, :1]


def loading(sources, targets, sems):
    copies = [pltpu.make_async_copy(source, target, sems.at[i]) for i, (source, target) in enumerate(zip(sources, targets))]
    for copy in copies:
        copy.start()
    return copies


def like(operands):
    return [pltpu.VMEM(operand.shape, operand.dtype) for operand in operands]


def route_kernel(
    experts,
    capacity,
    picks,
    ranks,
    seg,
    gain_attn,
    cot_in,
    tok_in,
    w_qkv_in,
    slot_col,
    slot_row,
    counts,
    windows,
    gz_out,
    normed_out,
    packed_out,
    extra_out,
    cot,
    tok,
    w_qkv,
    gz_send,
    normed_attn,
    packed,
    nothing,
    load_sem,
    gz_sem,
    sems,
    zero_sem,
):
    loads = loading((cot_in, tok_in, w_qkv_in), (cot, tok, w_qkv), load_sem)
    tokens = ranks.shape[1]
    padded = gz_send.shape[1]
    nothing[...] = jnp.zeros_like(nothing)
    zeros = [
        pltpu.make_async_copy(nothing, extra_out.at[pl.ds(i * QB, QB)], zero_sem.at[i]) for i in range(tokens // QB)
    ]
    for zero in zeros:
        zero.start()
    rank_row = ranks[...].astype(f32)
    rank_col = row_to_col(rank_row)
    lane = iota((tokens, LANES), 1)
    pick0 = row_to_col(picks[0:1, :].astype(f32)).astype(jnp.int32)
    pick1 = row_to_col(picks[1:2, :].astype(f32)).astype(jnp.int32)
    hot = jnp.where(lane == jnp.where(lane < experts, pick0, pick1 + experts), 1.0, 0.0).astype(f32)
    before = (rank_row < rank_col).astype(f32).astype(bf16)
    earlier = dot(before, hot.astype(bf16))
    total = jnp.sum(hot, axis=0, keepdims=True)
    total = jnp.broadcast_to(total, (8, LANES))
    lane8 = iota((8, LANES), 1)
    first = jnp.where(lane8 < experts, total, 0.0)
    earlier = earlier + pltpu.roll(first, experts, axis=1)[:1]
    kept = (hot > 0.5) & (earlier < float(capacity))
    slots = jnp.where(kept, earlier, -1.0)
    slot_col[...] = slots
    slots = jnp.maximum(slots, pltpu.roll(slots, LANES - experts, axis=1))
    slots = jnp.where(lane < experts, slots, -1.0)
    slot_row[...] = jnp.transpose(slots)[:experts]
    kept_lane = jnp.sum(jnp.where(slots >= 0.0, 1.0, 0.0), axis=0, keepdims=True)
    both = total + pltpu.roll(total, LANES - experts, axis=1)
    both = jnp.where(lane8 < experts, both, 0.0)
    sub8 = iota((8, LANES), 0)
    counts[...] = jnp.where(sub8 == 0, kept_lane, jnp.where(sub8 == 1, both, 0.0))

    blocks = tokens // QB
    lane_row = iota((1, LANES), 1)
    plan = jnp.where(lane_row == 3 * blocks, 1.0, 0.0)
    for b, (slab_low, slab_high) in enumerate(SLABS):
        opening = seg[:, b * QB : b * QB + 1]
        closing = seg[:, (b + 1) * QB - 1 : (b + 1) * QB]
        first = jnp.sum(jnp.where(seg[...] < opening, 1.0, 0.0), axis=1, keepdims=True)
        after = jnp.sum(jnp.where(seg[...] <= closing, 1.0, 0.0), axis=1, keepdims=True)
        low = jnp.minimum(jnp.floor(first * (1.0 / 16)) * 16.0, float(SEQ - WINDOW))
        fits = jnp.where(after - low <= float(WINDOW), 1.0, 0.0)
        inside = jnp.where(first >= float(slab_low), 1.0, 0.0) * jnp.where(after <= float(slab_high), 1.0, 0.0)
        plan = jnp.where(lane_row == b, low, plan)
        plan = jnp.where(lane_row == blocks + b, fits, plan)
        plan = jnp.where(lane_row == 2 * blocks + b, inside, plan)
        plan = jnp.where(lane_row == 3 * blocks, plan * inside, plan)
    windows[...] = plan.astype(jnp.int32)
    loads[0].wait()

    @pl.loop(0, experts)
    def _(e):
        chosen = iota((padded, tokens), 0).astype(f32) == slot_row[pl.ds(e, 1), :]
        gz_send[e] = dot(chosen.astype(f32).astype(bf16), cot[...]).astype(bf16)
        pltpu.make_async_copy(gz_send.at[e], gz_out.at[e], gz_sem.at[e]).start()

    def stores(i):
        rows = pl.ds(pl.multiple_of(i * TILE, TILE), TILE)
        return (
            pltpu.make_async_copy(normed_attn.at[rows], normed_out.at[rows], sems.at[0, i]),
            pltpu.make_async_copy(packed.at[rows], packed_out.at[rows], sems.at[1, i]),
        )

    for load in loads[1:]:
        load.wait()

    @pl.loop(0, tokens // TILE)
    def _(i):
        rows = pl.ds(pl.multiple_of(i * TILE, TILE), TILE)
        normal, unused = norm_parts(tok[rows, :].astype(f32))
        normed = (normal * gain_attn[...]).astype(bf16)
        normed_attn[rows, :] = normed
        packed[rows, :] = dot(normed, w_qkv[...]).astype(bf16)
        for store in stores(i):
            store.start()

    @pl.loop(0, experts)
    def _(e):
        pltpu.make_async_copy(gz_send.at[e], gz_out.at[e], gz_sem.at[e]).wait()

    @pl.loop(0, tokens // TILE)
    def _(i):
        for store in stores(i):
            store.wait()

    for zero in zeros:
        zero.wait()


def route(picks, ranks, seg, gain_attn, cot, tok, w_qkv, experts, capacity, padded):
    tokens = tok.shape[0]
    vmem = pl.BlockSpec(memory_space=pltpu.VMEM)
    anywhere = pl.BlockSpec(memory_space=pl.ANY)
    return pl.pallas_call(
        functools.partial(route_kernel, experts, capacity),
        in_specs=[vmem] * 4 + [anywhere] * 3,
        out_shape=(
            jax.ShapeDtypeStruct((tokens, LANES), f32),
            jax.ShapeDtypeStruct((experts, tokens), f32),
            jax.ShapeDtypeStruct((8, LANES), f32),
            jax.ShapeDtypeStruct((1, LANES), jnp.int32),
            jax.ShapeDtypeStruct((experts, padded, D), bf16),
            jax.ShapeDtypeStruct((tokens, D), bf16),
            jax.ShapeDtypeStruct((tokens, 3 * D), bf16),
            jax.ShapeDtypeStruct((tokens, 3 * D), bf16),
        ),
        out_specs=(vmem, vmem, vmem, vmem, anywhere, anywhere, anywhere, anywhere),
        scratch_shapes=like((cot, tok, w_qkv))
        + [
            pltpu.VMEM((experts, padded, D), bf16),
            pltpu.VMEM((tokens, D), bf16),
            pltpu.VMEM((tokens, 3 * D), bf16),
            pltpu.VMEM((QB, 3 * D), bf16),
            pltpu.SemaphoreType.DMA((3,)),
            pltpu.SemaphoreType.DMA((experts,)),
            pltpu.SemaphoreType.DMA((2, tokens // TILE)),
            pltpu.SemaphoreType.DMA((tokens // QB,)),
        ],
        compiler_params=pltpu.CompilerParams(vmem_limit_bytes=VMEM_LIMIT),
        cost_estimate=pl.CostEstimate(
            flops=2 * experts * padded * tokens * D, bytes_accessed=6 * MIB, transcendentals=0
        ),
        name="route",
    )(picks, ranks, seg, gain_attn, cot, tok, w_qkv)


def stack_heads(block):
    lane = iota(block.shape, 1)
    zero = jnp.zeros_like(block)
    return jnp.concatenate(
        [jnp.where(lane < HEAD, block, zero), jnp.where(lane < HEAD, zero, block)], axis=0
    )


def unstack_cols(stacked):
    row = iota((PAIR, QB), 0)
    picked = jnp.where(row < HEAD, stacked[:, :QB], stacked[:, QB:])
    return jnp.transpose(picked)


def window_bias(seg_col, seg_row, low, width, query):
    same = seg_col[pl.ds(low, width), :] == seg_row[:, pl.ds(query, QB)]
    half = jnp.where(same, 0.0, -1e30).astype(f32)
    return jnp.concatenate([half, half], axis=1)


def by_window(windows, block, body):
    low = windows[0, block]
    fits = windows[0, block + SEQ // QB]

    @pl.when(fits == 1)
    def _():
        body(pl.multiple_of(low, 16), WINDOW)

    @pl.when(fits != 1)
    def _():
        body(0, SEQ)


def forward_kernel(
    experts,
    windows,
    seg,
    gain_moe,
    w_router,
    packed_in,
    tok_in,
    w_proj_in,
    context_out,
    lse,
    residual_out,
    normed_moe_out,
    gates_out,
    gate_row,
    packed,
    tok,
    w_proj,
    context,
    residual,
    normed_moe,
    gates,
    seg_col,
    seg_row,
    router,
    load_sem,
    sems,
):
    loads = loading((packed_in, tok_in, w_proj_in), (packed, tok, w_proj), load_sem)
    writes = [
        pltpu.make_async_copy(source, target, sems.at[i])
        for i, (source, target) in enumerate(
            (
                (context, context_out),
                (residual, residual_out),
                (normed_moe, normed_moe_out),
                (gates, gates_out),
            )
        )
    ]
    tokens = tok.shape[0]
    seg_row[...] = seg[...].astype(f32)
    seg_col[...] = jnp.transpose(jnp.broadcast_to(seg_row[...], (LANES, tokens)))
    router[...] = jnp.zeros_like(router)
    router[:experts, :] = w_router[...]
    loads[0].wait()

    @pl.loop(0, tokens // QB)
    def _(block):
        query = pl.multiple_of(block * QB, QB)

        def body(low, width):
            bias = window_bias(seg_col, seg_row, low, width, query)
            spans = [slice(pair * PAIR, (pair + 1) * PAIR) for pair in range(PAIRS)]
            scores = []
            for span in spans:
                q = stack_heads(packed[pl.ds(query, QB), span]) * HEAD ** (-0.5)
                k = packed[pl.ds(low, width), D + span.start : D + span.stop]
                scores.append(dot_nt(k, q.astype(bf16)) + bias)
            peaks = [jnp.max(score, axis=0, keepdims=True) for score in scores]
            exponents = [jnp.exp(score - peak) for score, peak in zip(scores, peaks)]
            totals = [jnp.sum(exponent, axis=0, keepdims=True) for exponent in exponents]
            probs = [(exponent * (1.0 / total)).astype(bf16) for exponent, total in zip(exponents, totals)]
            for pair, span in enumerate(spans):
                lse[pl.ds(block, 1), pair, :] = peaks[pair] + jnp.log(totals[pair])
                v = packed[pl.ds(low, width), 2 * D + span.start : 2 * D + span.stop]
                mixed = dot_tn(v, probs[pair])
                context[pl.ds(query, QB), span] = unstack_cols(mixed).astype(bf16)

        by_window(windows, block, body)

    writes[0].start()
    for load in loads[1:]:
        load.wait()

    @pl.loop(0, tokens // TILE)
    def _(i):
        rows = pl.ds(pl.multiple_of(i * TILE, TILE), TILE)
        rest = tok[rows, :].astype(f32) + dot(context[rows, :], w_proj[...])
        residual[rows, :] = rest
        normal, unused = norm_parts(rest)
        normed = (normal * gain_moe[...]).astype(bf16)
        normed_moe[rows, :] = normed
        logits = dot_nt(normed, router[...])
        logits = jnp.where(iota(logits.shape, 1) < experts, logits, -1e30)
        exponent = jnp.exp(logits - jnp.max(logits, axis=1, keepdims=True))
        gates[rows, :] = exponent / jnp.sum(exponent, axis=1, keepdims=True)

    for write in writes[1:]:
        write.start()
    gate_row[...] = jnp.transpose(gates[...])[:experts]
    for write in writes:
        write.wait()


def forward(windows, seg, gain_moe, w_router, packed, tok, w_proj):
    tokens = tok.shape[0]
    experts = w_router.shape[0]
    vmem = pl.BlockSpec(memory_space=pltpu.VMEM)
    anywhere = pl.BlockSpec(memory_space=pl.ANY)
    return pl.pallas_call(
        functools.partial(forward_kernel, experts),
        in_specs=[pl.BlockSpec(memory_space=pltpu.SMEM)] + [vmem] * 3 + [anywhere] * 3,
        out_specs=[anywhere, vmem] + [anywhere] * 3 + [vmem],
        out_shape=(
            jax.ShapeDtypeStruct((tokens, D), bf16),
            jax.ShapeDtypeStruct((tokens // QB, PAIRS, 2 * QB), f32),
            jax.ShapeDtypeStruct((tokens, D), f32),
            jax.ShapeDtypeStruct((tokens, D), bf16),
            jax.ShapeDtypeStruct((tokens, LANES), f32),
            jax.ShapeDtypeStruct((experts, tokens), f32),
        ),
        scratch_shapes=like((packed, tok, w_proj))
        + [
            pltpu.VMEM((tokens, D), bf16),
            pltpu.VMEM((tokens, D), f32),
            pltpu.VMEM((tokens, D), bf16),
            pltpu.VMEM((tokens, LANES), f32),
            pltpu.VMEM((tokens, LANES), f32),
            pltpu.VMEM((1, tokens), f32),
            pltpu.VMEM((LANES, D), bf16),
            pltpu.SemaphoreType.DMA((3,)),
            pltpu.SemaphoreType.DMA((4,)),
        ],
        compiler_params=pltpu.CompilerParams(vmem_limit_bytes=VMEM_LIMIT),
        cost_estimate=pl.CostEstimate(
            flops=64 * 1024 * MIB, bytes_accessed=16 * MIB, transcendentals=4 * MIB
        ),
        name="attention_forward",
    )(windows, seg, gain_moe, w_router, packed, tok, w_proj)


def gelu_parts(x):
    density = jnp.exp(-0.5 * (x * x))
    return 0.5 + 0.5 * lax.erf(x * 2.0**-0.5), x * density * 0.3989422804014327


def shifted(index, by, size):
    return lax.rem(index + by, size)


def paired(index, by, size):
    total = 0
    bit = 1
    while bit < size:
        total = total + bit * lax.rem(index // bit + by // bit, 2)
        bit *= 2
    return total


def exchange(src, dst, send, recv, device):
    return pltpu.make_async_remote_copy(
        src_ref=src, dst_ref=dst, send_sem=send, recv_sem=recv, device_id=device, device_id_type=MESH
    )


def greet(barrier, sources):
    me = lax.axis_index("wide")
    line = lax.axis_index("narrow")

    @pl.loop(1, sources)
    def _(j):
        pl.semaphore_signal(barrier, inc=1, device_id=(paired(me, j, sources), line), device_id_type=MESH)


EARLY = 3


def moe_kernel(
    capacity,
    sources,
    shards,
    slot_row,
    gate_row,
    w_router,
    gain_moe,
    counts,
    normed_in,
    gz_in,
    slot_in,
    gates_in,
    cot_in,
    residual_in,
    context_in,
    w_proj_in,
    w_in0,
    w_out0,
    w_in1,
    w_out1,
    w_in2,
    w_out2,
    ring,
    own_grads,
    small,
    mixed_out,
    grad_residual_out,
    grad_context_out,
    grad_proj_out,
    *refs,
):
    others, refs = refs[: shards - 4], refs[shards - 4 :]
    normed_moe, slot_col, gates, w_proj, w_ins, w_outs, rows_send, rows, scaled, gate_slot, rows_t, gz_t = refs[:12]
    act, gpre, out_sum, back_sum, back_low, returned, back, ring_out, ring_in = refs[12:21]
    router, grad_gates, grad_logits = refs[21:24]
    load_sem, row_sem, out_sem, back_sem, weight_sem, ring_sem, late_sem, store_sem = refs[24:]
    out_low = rows_send
    depth = act.shape[0]
    padded = rows_send.shape[1]
    tokens = normed_in.shape[0]
    me = lax.axis_index("wide")
    line = lax.axis_index("narrow")
    right = (me, shifted(line, 1, shards))
    left = (me, shifted(line, shards - 1, shards))
    loads = [
        pltpu.make_async_copy(normed_in, normed_moe, load_sem.at[0]),
        pltpu.make_async_copy(gz_in, scaled, load_sem.at[1]),
    ]
    for c, pair in reversed(list(enumerate(((w_in0, w_out0), (w_in1, w_out1), (w_in2, w_out2))))):
        for i, (source, target) in enumerate(zip(pair, (w_ins, w_outs))):
            loads.append(pltpu.make_async_copy(source, target.at[c], load_sem.at[2 + 2 * c + i]))
    for i, (source, target) in enumerate(((slot_in, slot_col), (gates_in, gates), (w_proj_in, w_proj))):
        loads.append(pltpu.make_async_copy(source, target, load_sem.at[2 + 2 * EARLY + i]))
    for load in loads:
        load.start()
    barrier = pltpu.get_barrier_semaphore()
    greet(barrier, sources)
    for near in (left, right):
        pl.semaphore_signal(barrier, inc=1, device_id=near, device_id_type=MESH)
    gate_slot[...] = jnp.zeros_like(gate_slot)

    def block(s):
        return pl.ds(pl.multiple_of(s * padded, 16), padded)

    def weights_on(c):
        return [
            exchange(part.at[c - 1], part.at[c], weight_sem.at[0, i, c], weight_sem.at[1, i, c], right)
            for i, part in enumerate((w_ins, w_outs))
        ]

    def row_copy(j):
        to = paired(me, j, sources)
        return exchange(rows_send.at[to], rows.at[block(me)], row_sem.at[0, j], row_sem.at[1, j], (to, line))

    def result_copies(j):
        to = paired(me, j, sources)
        return [
            exchange(low.at[to], target.at[me], sem.at[0, j], sem.at[1, j], (to, line))
            for low, target, sem in ((out_low, returned, out_sem), (back_low, back, back_sem))
        ]

    for load in loads[:1] + loads[2:4]:
        load.wait()

    def partner(i):
        turn = lax.rem(i + 1, 3)
        return i + lax.rem(i // 3, 2) * (turn - 3 * (turn // 2))

    @pl.loop(0, sources)
    def _(i):
        j = partner(lax.rem(i + 2, sources))
        e = paired(me, j, sources)
        chosen = iota((padded, tokens), 0).astype(f32) == slot_row[pl.ds(e, 1), :]
        chosen = chosen.astype(f32).astype(bf16)
        rows_send[e] = dot(chosen, normed_moe[...]).astype(bf16)
        gate = gate_row[pl.ds(e, 1), :]
        high, middle = split2(gate)
        low = (gate - high.astype(f32) - middle.astype(f32)).astype(bf16)
        three = jnp.concatenate(
            [high.astype(f32), middle.astype(f32), low.astype(f32), jnp.zeros((5, tokens), f32)], axis=0
        )
        gate_slot[:, :padded] = dot_nt(three.astype(bf16), chosen)
        tail = rows_send[e, padded - 16 :, :].astype(f32)
        sub = iota(tail.shape, 0)
        for part in range(3):
            tail = jnp.where(sub == 13 + part, gate_slot[part : part + 1, :], tail)
        rows_send[e, padded - 16 :, :] = tail.astype(bf16)

        @pl.when(i == 0)
        def _():
            pl.semaphore_wait(barrier, sources + 1)
            for copy in weights_on(EARLY):
                copy.start()

        @pl.when(j != 0)
        def _():
            row_copy(j).start()

    rows[block(me), :] = rows_send[me]
    for load in loads[1:2] + loads[4:]:
        load.wait()

    def prepare(j):
        s = paired(me, j, sources)

        @pl.when(j != 0)
        def _():
            row_copy(j).wait_recv()

        end = pl.ds(pl.multiple_of(s * padded + padded - 16, 16), 16)
        tail = rows[end, :].astype(f32)
        gate = tail[13:14] + tail[14:15] + tail[15:16]
        gate = jnp.transpose(jnp.broadcast_to(gate, (LANES, D)))[:padded, :1]
        live = iota((padded, 1), 0) < capacity
        scaled[block(s), :] = (jnp.where(live, gate, 0.0) * scaled[block(s), :].astype(f32)).astype(bf16)
        live16 = iota((16, 1), 0) < 16 - (padded - capacity)
        rows[end, :] = jnp.where(live16, tail, 0.0).astype(bf16)

    def shard_results(s, c):
        pre = dot(rows[block(s), :], w_ins[c])
        phi, slope = gelu_parts(pre)
        act_low = (pre * phi).astype(bf16)
        act[c % depth, block(s), :] = act_low
        grad_pre = (dot_nt(scaled[block(s), :], w_outs[c]) * (phi + slope)).astype(bf16)
        gpre[c % depth, block(s), :] = grad_pre
        return dot(act_low, w_outs[c]), dot_nt(grad_pre, w_ins[c])

    def send(j, result, grad_rows):
        s = paired(me, j, sources)

        @pl.when(j != 0)
        def _():
            row_copy(j).wait_send()

        out_low[s] = result.astype(bf16)
        back_low[s] = grad_rows.astype(bf16)

        @pl.when(j != 0)
        def _():
            for copy in result_copies(j):
                copy.start()

    def run(s, order, fresh, final):
        for k, c in enumerate(order):
            result, grad_rows = shard_results(s, c)
            if k > 0 or not fresh:
                result = result + out_sum[block(s), :]
                grad_rows = grad_rows + back_sum[block(s), :]
            if k < len(order) - 1 or not final:
                out_sum[block(s), :] = result
                back_sum[block(s), :] = grad_rows
        return result, grad_rows

    def weight_grads(c):
        return dot(rows_t[...], gpre[c % depth]).astype(bf16), dot(gz_t[...], act[c % depth]).astype(bf16)

    first_step = exchange(ring_out, ring_in.at[0], ring_sem.at[0, 0], ring_sem.at[1, 0], right)
    second_step = exchange(ring_in.at[0], ring_in.at[1], ring_sem.at[0, 1], ring_sem.at[1, 1], right)
    late = tuple(range(EARLY, shards))

    def pass_over(first, last, order, opening, closing):
        @pl.loop(first, last)
        def _(i):
            j = partner(i)
            if opening:
                prepare(j)
            results = run(paired(me, j, sources), order, opening, closing)
            if closing:
                send(j, *results)

    def late_weights():
        for c in late:
            for copy in weights_on(c):
                copy.wait()
            if c + 1 < shards:
                for copy in weights_on(c + 1):
                    copy.start()

    def turn_rows():
        for s in range(sources):
            rows_t[:, s * padded : (s + 1) * padded] = jnp.transpose(rows[s * padded : (s + 1) * padded, :])
            gz_t[:, s * padded : (s + 1) * padded] = jnp.transpose(scaled[s * padded : (s + 1) * padded, :])

    def start_ring():
        ring_out[:D, :], ring_out[D:, :] = weight_grads(1)
        first_step.start()

    def keep_grads(c):
        target = own_grads if c == 0 else ring if c == 3 else others[c - 4]
        target[:D, :], target[D:, :] = weight_grads(c)

    if depth == shards:
        pass_over(0, 4, (1, 0, 2), True, False)
        pass_over(4, 5, (1, 0), True, False)
        late_weights()
        pass_over(2, 4, late, False, True)
        pass_over(5, sources, (1,), True, False)
        turn_rows()
        start_ring()
        pass_over(4, 5, (2,) + late, False, True)
        pass_over(5, sources, (0, 2) + late, False, True)
        pass_over(0, 2, late, False, True)
    else:
        late_weights()
        pass_over(0, sources, (1,), True, False)
        turn_rows()
        start_ring()
        for c in (0,) + late:
            pass_over(0, sources, (c,), False, False)
            keep_grads(c)
        pass_over(0, sources, (2,), False, True)

    upper = slice(tokens, 2 * tokens)
    late_loads = loading(
        (cot_in, residual_in, context_in),
        (rows.at[pl.ds(0, tokens)], out_sum.at[pl.ds(tokens, tokens)], rows.at[pl.ds(tokens, tokens)]),
        late_sem,
    )
    returned[me] = out_low[me]
    back[me] = back_low[me]
    second = weight_grads(2)
    if depth == shards:
        keep_grads(3)
    first_step.wait()
    for half in range(2):
        span = slice(half * D, half * D + D)
        ring_in[0, span, :] = (ring_in[0, span, :].astype(f32) + second[half].astype(f32)).astype(bf16)
    second_step.start()
    if depth == shards:
        keep_grads(0)

    lane = iota((TILE, LANES), 1)
    router[...] = jnp.zeros_like(router)
    router[:sources, :] = w_router[...]
    small[...] = jnp.zeros_like(small)
    small[2:4, :LANES] = counts[:2, :]
    grad_gates[...] = jnp.zeros_like(grad_gates)
    out_sum[:tokens, :] = jnp.zeros((tokens, D), f32)
    back_sum[:tokens, :] = jnp.zeros((tokens, D), f32)
    for load in late_loads:
        load.wait()

    def collect(e):
        for i in range(tokens // TILE):
            at = slice(i * TILE, (i + 1) * TILE)
            slots = slot_col[at, :]
            slot = jnp.max(
                jnp.where((lane == e) | (lane == e + sources), slots, -1.0), axis=1, keepdims=True
            )
            gate = jnp.sum(jnp.where(lane == e, gates[at, :], 0.0), axis=1, keepdims=True)
            chosen = (iota((TILE, padded), 1).astype(f32) == slot).astype(f32).astype(bf16)
            result = dot(chosen, returned[e])
            out_sum[at, :] += gate * result
            inner = jnp.sum(result * rows[at, :].astype(f32), axis=1, keepdims=True)
            grad_gates[at, :] += jnp.where(lane == e, inner, 0.0)
            back_sum[at, :] += dot(chosen, back[e])

    collect(me)

    @pl.loop(1, sources)
    def _(i):
        j = partner(lax.rem(i, sources - 1) + 1)
        for copy in result_copies(j):
            copy.wait_recv()
        collect(paired(me, j, sources))

    for i in range(tokens // TILE):
        at = slice(i * TILE, (i + 1) * TILE)
        above = slice(tokens + i * TILE, tokens + (i + 1) * TILE)
        grad_z = rows[at, :].astype(f32)
        probs = gates[at, :]
        rest = out_sum[above, :]
        scaled[at, :] = (rest + out_sum[at, :]).astype(bf16)
        gate_inner = jnp.sum(probs * grad_gates[at, :], axis=1, keepdims=True)
        high, low = split2(probs * (grad_gates[at, :] - gate_inner))
        grad_logits[at, :LANES] = high
        grad_logits[at, LANES:] = low
        grad_normed = back_sum[at, :] + dot(high, router[...]) + dot(low, router[...])
        normal, inverse = norm_parts(rest)
        grad_norm, grad_gain = norm_back(grad_normed, gain_moe[...], normal, inverse)
        small[1:2, :] += grad_gain
        grad_rest = grad_z + grad_norm
        back_sum[above, :] = grad_rest
        attn = grad_rest.astype(bf16)
        scaled[above, :] = attn
        rows[at, :] = dot_nt(attn, w_proj[...]).astype(bf16)
    stores = [
        pltpu.make_async_copy(source, target, store_sem.at[i])
        for i, (source, target) in enumerate(
            (
                (scaled.at[pl.ds(0, tokens)], mixed_out),
                (back_sum.at[pl.ds(tokens, tokens)], grad_residual_out),
                (rows.at[pl.ds(0, tokens)], grad_context_out),
                (out_sum.at[pl.ds(0, D)], grad_proj_out),
            )
        )
    ]
    for store in stores[:3]:
        store.start()
    out_sum[:D, :] = dot_tn(rows[upper, :], scaled[upper, :])
    stores[3].start()
    both = dot_tn(normed_moe[...], grad_logits[...])
    both = jnp.transpose(both[:, :LANES] + both[:, LANES:])
    small[8:, :] = both[:sources]
    second_step.wait()
    ring[...] = (ring_in[1].astype(f32) + ring[...].astype(f32)).astype(bf16)
    for store in stores:
        store.wait()

    @pl.loop(1, sources)
    def _(j):
        for copy in result_copies(j):
            copy.wait_send()


def moe(slot_row, gate_row, w_router, gain_moe, counts, *large, shards, capacity):
    normed_moe, gz = large[:2]
    sources = slot_row.shape[0]
    tokens = normed_moe.shape[0]
    hidden = large[-2].shape[1]
    total = gz.shape[0]
    blocks = (sources, total // sources, D)
    depth = shards if shards == 4 else 1
    vmem = pl.BlockSpec(memory_space=pltpu.VMEM)
    anywhere = pl.BlockSpec(memory_space=pl.ANY)
    dma = pltpu.SemaphoreType.DMA
    piece = jax.ShapeDtypeStruct((2 * D, hidden), bf16)
    return pl.pallas_call(
        functools.partial(moe_kernel, capacity, sources, shards),
        in_specs=[vmem] * 5 + [anywhere] * len(large),
        out_specs=[vmem] * 3 + [anywhere] * 4 + [vmem] * (shards - 4),
        out_shape=[
            piece,
            piece,
            jax.ShapeDtypeStruct((8 + sources, D), f32),
            jax.ShapeDtypeStruct((tokens, D), bf16),
            jax.ShapeDtypeStruct((tokens, D), f32),
            jax.ShapeDtypeStruct((tokens, D), bf16),
            jax.ShapeDtypeStruct((D, D), f32),
        ]
        + [piece] * (shards - 4),
        scratch_shapes=[
            pltpu.VMEM((tokens, D), bf16),
            pltpu.VMEM((tokens, LANES), f32),
            pltpu.VMEM((tokens, LANES), f32),
            pltpu.VMEM((D, D), bf16),
            pltpu.VMEM((shards, D, hidden), bf16),
            pltpu.VMEM((shards, hidden, D), bf16),
            pltpu.VMEM(blocks, bf16),
            pltpu.VMEM((total, D), bf16),
            pltpu.VMEM((total, D), bf16),
            pltpu.VMEM((8, D), f32),
            pltpu.VMEM((D, total), bf16),
            pltpu.VMEM((D, total), bf16),
            pltpu.VMEM((depth, total, hidden), bf16),
            pltpu.VMEM((depth, total, hidden), bf16),
            pltpu.VMEM((total, D), f32),
            pltpu.VMEM((total, D), f32),
            pltpu.VMEM(blocks, bf16),
            pltpu.VMEM(blocks, bf16),
            pltpu.VMEM(blocks, bf16),
            pltpu.VMEM((2 * D, hidden), bf16),
            pltpu.VMEM((2, 2 * D, hidden), bf16),
            pltpu.VMEM((LANES, D), bf16),
            pltpu.VMEM((tokens, LANES), f32),
            pltpu.VMEM((tokens, 2 * LANES), bf16),
            dma((5 + 2 * EARLY,)),
            dma((2, sources)),
            dma((2, sources)),
            dma((2, sources)),
            dma((2, 2, shards)),
            dma((2, 2)),
            dma((3,)),
            dma((4,)),
        ],
        compiler_params=pltpu.CompilerParams(
            vmem_limit_bytes=VMEM_LIMIT, collective_id=1, has_side_effects=True
        ),
        cost_estimate=pl.CostEstimate(
            flops=12 * total * D * hidden * shards, bytes_accessed=20 * MIB, transcendentals=0
        ),
        name="moe",
    )(slot_row, gate_row, w_router, gain_moe, counts, *large)


def repair_kernel(
    windows,
    seg,
    lse,
    packed_in,
    extra_in,
    grad_context_in,
    extra_out,
    grad_context_out,
    packed,
    extra,
    grad_context,
    seg_col,
    seg_row,
    grad_k,
    grad_v,
    sems,
):
    tokens = packed.shape[0]
    blocks = tokens // QB

    @pl.when(windows[0, 3 * blocks] != 1)
    def _():
        loads = loading((packed_in, extra_in, grad_context_in), (packed, extra, grad_context), sems)
        seg_row[...] = seg[...].astype(f32)
        seg_col[...] = jnp.transpose(jnp.broadcast_to(seg_row[...], (LANES, tokens)))
        for load in loads:
            load.wait()
        grad_k[...] = jnp.zeros_like(grad_k)
        grad_v[...] = jnp.zeros_like(grad_v)

        @pl.loop(0, blocks)
        def _(block):
            query = pl.multiple_of(block * QB, QB)

            @pl.when(windows[0, 2 * blocks + block] != 1)
            def _():
                bias = window_bias(seg_col, seg_row, 0, SEQ, query)
                spans = [slice(pair * PAIR, (pair + 1) * PAIR) for pair in range(PAIRS)]
                keys = pl.ds(0, SEQ)
                queries = [
                    (stack_heads(packed[pl.ds(query, QB), span]) * HEAD ** (-0.5)).astype(bf16) for span in spans
                ]
                grads = [stack_heads(grad_context[pl.ds(query, QB), span]) for span in spans]
                probs = []
                grad_probs = []
                for pair, span in enumerate(spans):
                    k = packed[keys, D + span.start : D + span.stop]
                    v = packed[keys, 2 * D + span.start : 2 * D + span.stop]
                    probs.append(jnp.exp(dot_nt(k, queries[pair]) + bias - lse[pl.ds(block, 1), pair, :]))
                    grad_probs.append(dot_nt(v, grads[pair]))
                grad_scores = []
                for pair, span in enumerate(spans):
                    grad_v[keys, span] += dot(probs[pair].astype(bf16), grads[pair])
                    weighted = probs[pair] * grad_probs[pair]
                    inner = jnp.sum(weighted, axis=0, keepdims=True)
                    grad_scores.append((weighted - probs[pair] * inner).astype(bf16))
                for pair, span in enumerate(spans):
                    k = packed[keys, D + span.start : D + span.stop]
                    grad_k[keys, span] += dot(grad_scores[pair], queries[pair])
                    grad_q = unstack_cols(dot_tn(k, grad_scores[pair])) * HEAD ** (-0.5)
                    extra[pl.ds(query, QB), span] = grad_q.astype(bf16)
                grad_context[pl.ds(query, QB), :] = jnp.zeros((QB, D), bf16)

        extra[:, D : 2 * D] = grad_k[...].astype(bf16)
        extra[:, 2 * D :] = grad_v[...].astype(bf16)
        for store in loading((extra, grad_context), (extra_out, grad_context_out), sems):
            store.wait()


def repair(windows, seg, lse, packed, extra, grad_context):
    tokens = packed.shape[0]
    vmem = pl.BlockSpec(memory_space=pltpu.VMEM)
    anywhere = pl.BlockSpec(memory_space=pl.ANY)
    return pl.pallas_call(
        repair_kernel,
        in_specs=[pl.BlockSpec(memory_space=pltpu.SMEM)] + [vmem] * 2 + [anywhere] * 3,
        out_specs=(anywhere, anywhere),
        out_shape=(
            jax.ShapeDtypeStruct(extra.shape, bf16),
            jax.ShapeDtypeStruct(grad_context.shape, bf16),
        ),
        input_output_aliases={4: 0, 5: 1},
        scratch_shapes=like((packed, extra, grad_context))
        + [
            pltpu.VMEM((tokens, LANES), f32),
            pltpu.VMEM((1, tokens), f32),
            pltpu.VMEM((tokens, D), f32),
            pltpu.VMEM((tokens, D), f32),
            pltpu.SemaphoreType.DMA((3,)),
        ],
        compiler_params=pltpu.CompilerParams(vmem_limit_bytes=VMEM_LIMIT),
        cost_estimate=pl.CostEstimate(flops=MIB, bytes_accessed=MIB, transcendentals=0),
        name="repair",
    )(windows, seg, lse, packed, extra, grad_context)


SLAB_AT = tuple(sum(high - low for low, high in SLABS[:b]) for b in range(len(SLABS) + 1))


def slab_bias(bias, seg_col, seg_row):
    for b, (low, high) in enumerate(SLABS):
        same = seg_col[low:high, :] == seg_row[:, b * QB : (b + 1) * QB]
        bias[SLAB_AT[b] : SLAB_AT[b + 1], :] = jnp.where(same, 0.0, -1e30)


def pair_backward(pair, packed, grad_context, lse, extra, bias, grad_k, grad_v, out):
    def span(which):
        return pl.ds(pl.multiple_of(which * D + pair * PAIR, PAIR), PAIR)

    grad_k[...] = extra[:, span(1)].astype(f32)
    grad_v[...] = extra[:, span(2)].astype(f32)
    for group in range(0, len(SLABS), 4):
        blocks = range(group, group + 4)
        queries, grads, probs, grad_probs, grad_scores = [], [], [], [], []
        for b in blocks:
            low, high = SLABS[b]
            rows = slice(b * QB, (b + 1) * QB)
            queries.append((stack_heads(packed[rows, span(0)]) * HEAD ** (-0.5)).astype(bf16))
            grads.append(stack_heads(grad_context[rows, span(0)]))
            masked = bias[SLAB_AT[b] : SLAB_AT[b + 1], :]
            scores = dot_nt(packed[low:high, span(1)], queries[-1]) + jnp.concatenate([masked, masked], axis=1)
            probs.append(jnp.exp(scores - lse[b, pl.ds(pair, 1), :]))
            grad_probs.append(dot_nt(packed[low:high, span(2)], grads[-1]))
        for i, b in enumerate(blocks):
            low, high = SLABS[b]
            grad_v[low:high, :] += dot(probs[i].astype(bf16), grads[i])
            weighted = probs[i] * grad_probs[i]
            inner = jnp.sum(weighted, axis=0, keepdims=True)
            grad_scores.append((weighted - probs[i] * inner).astype(bf16))
        for i, b in enumerate(blocks):
            low, high = SLABS[b]
            rows = slice(b * QB, (b + 1) * QB)
            grad_k[low:high, :] += dot(grad_scores[i], queries[i])
            grad_q = unstack_cols(dot_tn(packed[low:high, span(1)], grad_scores[i])) * HEAD ** (-0.5)
            out[rows, :PAIR] = (grad_q + extra[rows, span(0)].astype(f32)).astype(bf16)
    out[:, PAIR : 2 * PAIR] = grad_k[...].astype(bf16)
    out[:, 2 * PAIR :] = grad_v[...].astype(bf16)


def shared_kernel(
    chips,
    planes,
    seg,
    lse,
    partial,
    gain_attn,
    packed_in,
    grad_context_in,
    extra_in,
    normed_attn_in,
    grad_proj_in,
    w_qkv_in,
    tok_in,
    grad_residual_in,
    summed,
    small,
    grad_tokens_out,
    packed,
    grad_context,
    extra,
    normed_attn,
    grad_proj,
    w_qkv,
    tok,
    grad_residual,
    pair_grads,
    grad_tokens,
    normed_t,
    seg_col,
    bias,
    grad_k,
    grad_v,
    grad_packed,
    half,
    core_out,
    core_in,
    chip_out,
    chip_in,
    plane_out,
    plane_in,
    small_own,
    small_core,
    small_chip,
    small_plane,
    load_sem,
    store_sem,
    core_sem,
    chip_sem,
    plane_sem,
    plane_sem2,
    chip_sem2,
    core_sem2,
    small_sem,
    small_chip_sem,
    small_plane_sem,
):
    tokens = tok.shape[0]
    stages = 16 // planes
    pairs = PAIRS // stages
    tiles = tokens // TILE
    wide = lax.axis_index("wide")
    plane = lax.axis_index("narrow")
    core = lax.rem(wide, 2)
    chip = wide // 2
    share = D // (2 * chips)
    partner = (chip * 2 + 1 - core, plane)
    mine = pl.ds(pl.multiple_of(core * (D // 2), D // 2), D // 2)
    other = pl.ds(pl.multiple_of((1 - core) * (D // 2), D // 2), D // 2)
    chunk = pl.ds(pl.multiple_of(core * (D // 2) + chip * share, share), share)
    own_chunk = pl.ds(pl.multiple_of(chip * share, share), share)

    loads = [
        pltpu.make_async_copy(source, target, load_sem.at[i])
        for i, (source, target) in enumerate(
            (
                (packed_in, packed),
                (grad_context_in, grad_context),
                (extra_in, extra),
                (normed_attn_in, normed_attn),
                (grad_proj_in, grad_proj),
                (w_qkv_in, w_qkv),
                (tok_in, tok),
                (grad_residual_in, grad_residual),
            )
        )
    ]
    for load in loads:
        load.start()

    def chip_at(j):
        to = shifted(chip, j, chips)
        return to, (to * 2 + core, plane)

    def plane_at(j):
        to = shifted(plane, j, planes)
        return to, (wide, to)

    barrier = pltpu.get_barrier_semaphore()
    pl.semaphore_signal(barrier, inc=1, device_id=partner, device_id_type=MESH)

    @pl.loop(1, chips)
    def _(j):
        pl.semaphore_signal(barrier, inc=1, device_id=chip_at(j)[1], device_id_type=MESH)

    @pl.loop(1, planes)
    def _(j):
        pl.semaphore_signal(barrier, inc=1, device_id=plane_at(j)[1], device_id_type=MESH)

    def blocks(stage):
        return pl.ds(stage * planes, planes)

    def core_copy(stage):
        at = blocks(stage)
        return exchange(core_out.at[at], core_in.at[at], core_sem.at[0, stage], core_sem.at[1, stage], partner)

    def chip_copy(stage, j):
        to, device = chip_at(j)
        rows = pl.ds(pl.multiple_of(to * share, share), share)
        at = blocks(stage)
        return exchange(
            chip_out.at[at, rows], chip_in.at[j, at], chip_sem.at[0, stage, j], chip_sem.at[1, stage, j], device
        )

    def plane_copy(stage, j):
        to, device = plane_at(j)
        return exchange(
            plane_out.at[stage * planes + to],
            plane_in.at[j, stage],
            plane_sem.at[0, stage, j],
            plane_sem.at[1, stage, j],
            device,
        )

    def plane_back(stage, j):
        spot = summed.at[stage * planes + plane, chunk]
        return exchange(spot, spot, plane_sem2.at[0, stage, j], plane_sem2.at[1, stage, j], plane_at(j)[1])

    def chip_back(stage, j):
        spot = summed.at[blocks(stage), chunk]
        return exchange(spot, spot, chip_sem2.at[0, stage, j], chip_sem2.at[1, stage, j], chip_at(j)[1])

    def core_back(stage):
        spot = summed.at[blocks(stage), mine]
        return exchange(spot, spot, core_sem2.at[0, stage], core_sem2.at[1, stage], partner)

    def small_core_copy():
        return exchange(small_own, small_core, small_sem.at[0], small_sem.at[1], partner)

    def small_chip_copy(j):
        spot = small_chip.at[chip]
        return exchange(spot, spot, small_chip_sem.at[0, j], small_chip_sem.at[1, j], chip_at(j)[1])

    def small_plane_copy(j):
        spot = small_plane.at[plane]
        return exchange(spot, spot, small_plane_sem.at[0, j], small_plane_sem.at[1, j], plane_at(j)[1])

    def pair_products(pair):
        spare = dot(normed_t[other, :], pair_grads[...])
        own = dot(normed_t[mine, :], pair_grads[...])
        lanes = pl.ds(pl.multiple_of(pair * PAIR, PAIR), PAIR)
        for which in range(3):
            at = slice(which * PAIR, (which + 1) * PAIR)
            core_out[pair * 4 + which] = spare[:, at].astype(bf16)
            half[pair * 4 + which] = own[:, at]
            grad_packed[:, pl.ds(pl.multiple_of(which * D + pair * PAIR, PAIR), PAIR)] = pair_grads[:, at]
        core_out[pair * 4 + 3] = grad_proj[other, lanes].astype(bf16)
        half[pair * 4 + 3] = grad_proj[mine, lanes]

    def chip_stage(stage):
        core_copy(stage).wait_recv()
        at = blocks(stage)
        total = half[at] + core_in[at].astype(f32)
        half[at] = total
        chip_out[at] = total.astype(bf16)

        @pl.loop(1, chips)
        def _(j):
            chip_copy(stage, j).start()

    def plane_stage(stage):
        at = blocks(stage)
        total = half[at, own_chunk, :]
        for j in range(1, chips):
            chip_copy(stage, j).wait_recv()
            total = total + chip_in[j, at].astype(f32)
        half[at, own_chunk, :] = total
        plane_out[at] = total.astype(bf16)

        @pl.loop(1, planes)
        def _(j):
            plane_copy(stage, j).start()

    def own_stage(stage):
        total = half[stage * planes + plane, own_chunk, :]
        for j in range(1, planes):
            plane_copy(stage, j).wait_recv()
            total = total + plane_in[j, stage].astype(f32)
        summed[stage * planes + plane, chunk, :] = total.astype(bf16)

        @pl.loop(1, planes)
        def _(j):
            plane_back(stage, j).start()

    def gather_stage(stage):
        @pl.loop(1, planes)
        def _(j):
            plane_back(stage, j).wait_recv()

        @pl.loop(1, chips)
        def _(j):
            chip_back(stage, j).start()

    def last_stage(stage):
        @pl.loop(1, chips)
        def _(j):
            chip_back(stage, j).wait_recv()

        core_back(stage).start()

    def norm_tile(i):
        rows = slice(i * TILE, (i + 1) * TILE)
        grad_normed = dot_nt(grad_packed[rows, :], w_qkv[...])
        normal, inverse = norm_parts(tok[rows, :].astype(f32))
        grad_norm, grad_gain = norm_back(grad_normed, gain_attn[...], normal, inverse)
        small_own[0:1, :] += grad_gain
        grad_tokens[rows, :] = grad_residual[rows, :] + grad_norm

    small_own[...] = partial[...]
    seg_row = seg[...].astype(f32)
    seg_col[...] = jnp.transpose(jnp.broadcast_to(seg_row, (LANES, tokens)))
    slab_bias(bias, seg_col, seg_row)
    for load in loads[:3]:
        load.wait()

    @pl.loop(0, PAIRS)
    def _(pair):
        pair_backward(pair, packed, grad_context, lse, extra, bias, grad_k, grad_v, pair_grads)

        @pl.when(pair == 0)
        def _():
            for load in loads[3:5]:
                load.wait()
            normed_t[...] = jnp.transpose(normed_attn[...])
            pl.semaphore_wait(barrier, chips + planes - 1)

        pair_products(pair)

        @pl.when(lax.rem(pair + 1, pairs) == 0)
        def _():
            stage = pair // pairs
            core_copy(stage).start()

            @pl.when(stage > 0)
            def _():
                chip_stage(stage - 1)

            @pl.when(stage > 1)
            def _():
                plane_stage(stage - 2)

            @pl.when(stage > 2)
            def _():
                own_stage(stage - 3)

    for load in loads[5:]:
        load.wait()
    steps = (chip_stage, plane_stage, own_stage, gather_stage, last_stage)
    for late in range(len(steps)):
        if late == 0:
            norm_tile(0)
        for i, step in enumerate(steps):
            stage = stages - 1 + late - i
            if i >= late and 0 <= stage < stages:
                step(stage)
        if late == 0:
            for i in range(1, tiles):
                norm_tile(i)
            small_core_copy().start()
            store = pltpu.make_async_copy(grad_tokens, grad_tokens_out, store_sem)
            store.start()
        if late == 1:
            small_core_copy().wait_recv()
            small_chip[chip] = small_own[...] + small_core[...]

            @pl.loop(1, chips)
            def _(j):
                small_chip_copy(j).start()

        if late == 2:

            @pl.loop(1, chips)
            def _(j):
                small_chip_copy(j).wait_recv()

            total = small_chip[0]
            for c in range(1, chips):
                total = total + small_chip[c]
            small_plane[plane] = total

            @pl.loop(1, planes)
            def _(j):
                small_plane_copy(j).start()

    @pl.loop(1, planes)
    def _(j):
        small_plane_copy(j).wait_recv()

    total = small_plane[0]
    for c in range(1, planes):
        total = total + small_plane[c]
    small[...] = total
    store.wait()

    @pl.loop(0, stages)
    def _(stage):
        core_back(stage).wait()
        core_copy(stage).wait_send()

        @pl.loop(1, chips)
        def _(j):
            chip_back(stage, j).wait_send()
            chip_copy(stage, j).wait_send()

        @pl.loop(1, planes)
        def _(j):
            plane_back(stage, j).wait_send()
            plane_copy(stage, j).wait_send()

    @pl.loop(1, planes)
    def _(j):
        small_plane_copy(j).wait_send()

    @pl.loop(1, chips)
    def _(j):
        small_chip_copy(j).wait_send()

    small_core_copy().wait_send()


def shared_gradients(*operands):
    partial, packed = operands[2], operands[4]
    tokens = packed.shape[0]
    chips = lax.axis_size("wide") // 2
    planes = lax.axis_size("narrow")
    stages = 16 // planes
    share = D // (2 * chips)
    rows = partial.shape[0]
    dma = pltpu.SemaphoreType.DMA
    vmem = pl.BlockSpec(memory_space=pltpu.VMEM)
    anywhere = pl.BlockSpec(memory_space=pl.ANY)
    return pl.pallas_call(
        functools.partial(shared_kernel, chips, planes),
        in_specs=[vmem] * 4 + [anywhere] * 8,
        out_specs=(vmem, vmem, anywhere),
        out_shape=(
            jax.ShapeDtypeStruct((16, D, LANES), bf16),
            jax.ShapeDtypeStruct((rows, D), f32),
            jax.ShapeDtypeStruct((tokens, D), f32),
        ),
        scratch_shapes=[pltpu.VMEM(operand.shape, operand.dtype) for operand in operands[4:]]
        + [
            pltpu.VMEM((tokens, 3 * PAIR), bf16),
            pltpu.VMEM((tokens, D), f32),
            pltpu.VMEM((D, tokens), bf16),
            pltpu.VMEM((tokens, LANES), f32),
            pltpu.VMEM((SLAB_AT[-1], QB), f32),
            pltpu.VMEM((tokens, PAIR), f32),
            pltpu.VMEM((tokens, PAIR), f32),
            pltpu.VMEM((tokens, 3 * D), bf16),
            pltpu.VMEM((16, D // 2, LANES), f32),
            pltpu.VMEM((16, D // 2, LANES), bf16),
            pltpu.VMEM((16, D // 2, LANES), bf16),
            pltpu.VMEM((16, D // 2, LANES), bf16),
            pltpu.VMEM((chips, 16, share, LANES), bf16),
            pltpu.VMEM((16, share, LANES), bf16),
            pltpu.VMEM((planes, stages, share, LANES), bf16),
            pltpu.VMEM((rows, D), f32),
            pltpu.VMEM((rows, D), f32),
            pltpu.VMEM((chips, rows, D), f32),
            pltpu.VMEM((planes, rows, D), f32),
            dma((8,)),
            dma,
            dma((2, stages)),
            dma((2, stages, chips)),
            dma((2, stages, planes)),
            dma((2, stages, planes)),
            dma((2, stages, chips)),
            dma((2, stages)),
            dma((2,)),
            dma((2, chips)),
            dma((2, planes)),
        ],
        compiler_params=pltpu.CompilerParams(
            vmem_limit_bytes=VMEM_LIMIT, collective_id=2, has_side_effects=True
        ),
        cost_estimate=pl.CostEstimate(
            flops=12 * tokens * D * D, bytes_accessed=16 * MIB, transcendentals=0
        ),
        name="shared_gradients",
    )(*operands)


def finish_kernel(
    experts,
    small,
    summed_in,
    ring_in,
    own_in,
    tokens_in,
    gain_attn,
    gain_moe,
    router,
    kept,
    dropped,
    qkv_out,
    proj_out,
    in_out,
    out_out,
    tokens_out,
    summed,
    ring,
    own,
    tokens,
    qkv,
    proj,
    grad_in,
    grad_out,
    load_sem,
    store_sem,
    token_sem,
):
    loads = loading(
        (summed_in, ring_in, own_in, tokens_in), (summed, ring, own, tokens), load_sem
    )
    through = pltpu.make_async_copy(tokens, tokens_out, token_sem)
    gain_attn[...] = small[0, :]
    gain_moe[...] = small[1, :]
    router[...] = small[8:, :]
    counted = small[2:4, :experts]
    kept[...] = counted[0:1].astype(jnp.int32)
    dropped[...] = (counted[1:2] - counted[0:1]).astype(jnp.int32)
    loads[0].wait()
    stores = []
    step = D // 4
    for i in range(4):
        rows = slice(i * step, (i + 1) * step)
        for n in range(16):
            pair, which = divmod(n, 4)
            lanes = slice(pair * PAIR, (pair + 1) * PAIR)
            if which < 3:
                qkv[rows, which * D + lanes.start : which * D + lanes.stop] = summed[n, rows, :].astype(f32)
            else:
                proj[rows, lanes] = summed[n, rows, :].astype(f32)
        for source, target in ((qkv, qkv_out), (proj, proj_out)):
            stores.append(pltpu.make_async_copy(source.at[rows], target.at[rows], store_sem.at[len(stores)]))
            stores[-1].start()
    for load in loads[1:]:
        load.wait()
    through.start()
    grad_in[0] = ring[:D, :].astype(f32) + own[:D, :].astype(f32)
    stores.append(pltpu.make_async_copy(grad_in, in_out, store_sem.at[len(stores)]))
    stores[-1].start()
    grad_out[0] = jnp.transpose(ring[D:, :].astype(f32) + own[D:, :].astype(f32))
    stores.append(pltpu.make_async_copy(grad_out, out_out, store_sem.at[len(stores)]))
    stores[-1].start()
    for store in stores:
        store.wait()
    through.wait()


def finish(experts, small, summed, ring, own, tokens_in):
    hidden = own.shape[1]
    vmem = pl.BlockSpec(memory_space=pltpu.VMEM)
    anywhere = pl.BlockSpec(memory_space=pl.ANY)
    large = [((D, 3 * D), f32), ((D, D), f32), ((1, D, hidden), f32), ((1, hidden, D), f32)]
    dma = pltpu.SemaphoreType.DMA
    return pl.pallas_call(
        functools.partial(finish_kernel, experts),
        in_specs=[vmem] + [anywhere] * 4,
        out_specs=[vmem] * 5 + [anywhere] * 5,
        out_shape=[
            jax.ShapeDtypeStruct((D,), f32),
            jax.ShapeDtypeStruct((D,), f32),
            jax.ShapeDtypeStruct((experts, D), f32),
            jax.ShapeDtypeStruct((1, experts), jnp.int32),
            jax.ShapeDtypeStruct((1, experts), jnp.int32),
        ]
        + [jax.ShapeDtypeStruct(*shape) for shape in large]
        + [jax.ShapeDtypeStruct(tokens_in.shape, f32)],
        scratch_shapes=like((summed, ring, own, tokens_in))
        + [pltpu.VMEM(*shape) for shape in large]
        + [dma((4,)), dma((10,)), dma],
        compiler_params=pltpu.CompilerParams(vmem_limit_bytes=VMEM_LIMIT),
        cost_estimate=pl.CostEstimate(flops=0, bytes_accessed=14 * MIB, transcendentals=0),
        name="finish",
    )(small, summed, ring, own, tokens_in)


def per_device(
    tokens,
    segment_ids,
    expert_picks,
    priority_ranks,
    gain_attn,
    w_qkv,
    w_proj,
    gain_moe,
    w_router,
    w_in,
    w_out,
    cotangent,
):
    experts = w_router.shape[1]
    capacity = (21 * TOP * TOK_DEV + 20 * experts - 1) // (20 * experts)
    padded = (capacity + 3 + 15) // 16 * 16
    gain_attn = gain_attn.reshape(1, D)
    gain_moe = gain_moe.reshape(1, D)
    seg = segment_ids.reshape(1, SEQ)
    line = lax.axis_size("narrow")
    ring_steps = [(i, (i + 1) % line) for i in range(line)]
    together = lax.optimization_barrier

    def pass_on(values):
        return lax.ppermute(values, "narrow", ring_steps)

    early = [(w_in[0], w_out[0])]
    early.append(pass_on(early[0]))
    slot_col, slot_row, counts, windows, gz_send, normed_attn, packed, extra = route(
        expert_picks.T, priority_ranks, seg, gain_attn, cotangent, tokens, w_qkv, experts, capacity, padded
    )
    gz = lax.all_to_all(gz_send, "wide", split_axis=0, concat_axis=0, tiled=True)
    early.append(pass_on(together((early[1], slot_row))[0]))
    context, lse, residual, normed_moe, gates, gate_row = forward(
        windows, seg, gain_moe, w_router.T, packed, tokens, w_proj
    )
    ring, own, partial, mixed, grad_residual, grad_context, grad_proj, *others = moe(
        slot_row,
        gate_row,
        w_router.T,
        gain_moe,
        counts,
        normed_moe,
        gz.reshape(experts * padded, D),
        slot_col,
        gates,
        cotangent,
        residual,
        context,
        w_proj,
        *[part for pair in early for part in pair],
        shards=line,
        capacity=capacity,
    )
    for other in others:
        ring = (pass_on(ring).astype(f32) + other.astype(f32)).astype(bf16)
    ring = pass_on(ring)
    extra, grad_context = repair(windows, seg, lse, packed, extra, grad_context)
    summed, small, grad_tokens = shared_gradients(
        seg,
        lse,
        partial,
        gain_attn,
        packed,
        grad_context,
        extra,
        normed_attn,
        grad_proj,
        w_qkv,
        tokens,
        grad_residual,
    )
    grad_gain_attn, grad_gain_moe, grad_router, kept, dropped, grad_qkv, grad_proj, grad_in, grad_out, grad_tokens = finish(
        experts, small, summed, ring, own, grad_tokens
    )
    return (
        mixed,
        grad_tokens,
        grad_gain_attn,
        grad_qkv,
        grad_proj,
        grad_gain_moe,
        grad_router.T,
        grad_in,
        grad_out,
        kept.reshape(experts),
        dropped.reshape(experts),
    )


def solution(mesh):
    both = ("wide", "narrow")
    placed = (
        P(both, None),
        P(both),
        P(both, None),
        P(both, None),
        P(),
        P(),
        P(),
        P(),
        P(),
        P("wide", None, "narrow"),
        P("wide", "narrow", None),
        P(both, None),
    )
    return jax.shard_map(
        per_device,
        mesh=mesh,
        in_specs=placed,
        out_specs=(
            P(both, None),
            P(both, None),
            P(),
            P(),
            P(),
            P(),
            P(),
            P("wide", None, "narrow"),
            P("wide", "narrow", None),
            P(),
            P(),
        ),
        check_vma=False,
    )
```

```python
import functools

import jax
import jax.numpy as jnp
from jax import lax
from jax.experimental import pallas as pl
from jax.experimental.pallas import tpu as pltpu
from jax.sharding import PartitionSpec as P

D = 512
HEADS = 8
HEAD = 64
PAIRS = HEADS // 2
PAIR = 2 * HEAD
TOP = 2
SEQ = 1024
TOK_DEV = 1024
LANES = 128
QB = 128
WINDOW = 432
TILE = 256
SLABS = tuple((max(0, QB * (b - 2)), min(SEQ, QB * (b + 3))) for b in range(SEQ // QB))
MIB = 1024 * 1024
MESH = pl.DeviceIdType.MESH
VMEM_LIMIT = 62 * MIB

f32 = jnp.float32
bf16 = jnp.bfloat16
NT = (((1,), (1,)), ((), ()))
TN = (((0,), (0,)), ((), ()))


def dot(a, b):
    return jnp.dot(a, b, preferred_element_type=f32)


def dot_nt(a, b):
    return lax.dot_general(a, b, NT, preferred_element_type=f32)


def dot_tn(a, b):
    return lax.dot_general(a, b, TN, preferred_element_type=f32)


def iota(shape, dim):
    return lax.broadcasted_iota(jnp.int32, shape, dim)


def norm_parts(values_in):
    centered = values_in - jnp.mean(values_in, axis=-1, keepdims=True)
    variance = jnp.mean(centered * centered, axis=-1, keepdims=True)
    inverse = lax.rsqrt(variance + 1e-06)
    return (centered * inverse, inverse)


def norm_back(grad_normed, gain, normalized, inverse):
    grad_gain = jnp.sum(grad_normed * normalized, axis=0, keepdims=True)
    scaled = grad_normed * gain
    inner = scaled - jnp.mean(scaled, axis=-1, keepdims=True)
    inner = inner - normalized * jnp.mean(scaled * normalized, axis=-1, keepdims=True)
    return (inner * inverse, grad_gain)


def split2(values_in):
    high = values_in.astype(bf16)
    low = (values_in - high.astype(f32)).astype(bf16)
    return high, low


def row_to_col(row):
    n = row.shape[1]
    return jnp.transpose(jnp.broadcast_to(row, (LANES, n)))[:, :1]


def loading(sources, targets, sems):
    copies = [pltpu.make_async_copy(source, target, sems.at[i]) for i, (source, target) in enumerate(zip(sources, targets))]
    for copy in copies:
        copy.start()
    return copies


def like(operands):
    return [pltpu.VMEM(operand.shape, operand.dtype) for operand in operands]


def route_kernel(
    experts,
    capacity,
    picks,
    ranks,
    seg,
    gain_attn,
    cot_in,
    tok_in,
    w_qkv_in,
    slot_col,
    slot_row,
    counts,
    windows,
    gz_out,
    normed_out,
    packed_out,
    extra_out,
    cot,
    tok,
    w_qkv,
    gz_send,
    normed_attn,
    packed,
    nothing,
    load_sem,
    gz_sem,
    sems,
    zero_sem,
):
    loads = loading((cot_in, tok_in, w_qkv_in), (cot, tok, w_qkv), load_sem)
    tokens = ranks.shape[1]
    padded = gz_send.shape[1]
    nothing[...] = jnp.zeros_like(nothing)
    zeros = [
        pltpu.make_async_copy(nothing, extra_out.at[pl.ds(i * QB, QB)], zero_sem.at[i]) for i in range(tokens // QB)
    ]
    for zero in zeros:
        zero.start()
    rank_row = ranks[...].astype(f32)
    rank_col = row_to_col(rank_row)
    lane = iota((tokens, LANES), 1)
    pick0 = row_to_col(picks[0:1, :].astype(f32)).astype(jnp.int32)
    pick1 = row_to_col(picks[1:2, :].astype(f32)).astype(jnp.int32)
    hot = jnp.where(lane == jnp.where(lane < experts, pick0, pick1 + experts), 1.0, 0.0).astype(f32)
    before = (rank_row < rank_col).astype(f32).astype(bf16)
    earlier = dot(before, hot.astype(bf16))
    total = jnp.sum(hot, axis=0, keepdims=True)
    total = jnp.broadcast_to(total, (8, LANES))
    lane8 = iota((8, LANES), 1)
    first = jnp.where(lane8 < experts, total, 0.0)
    earlier = earlier + pltpu.roll(first, experts, axis=1)[:1]
    kept = (hot > 0.5) & (earlier < float(capacity))
    slots = jnp.where(kept, earlier, -1.0)
    slot_col[...] = slots
    slots = jnp.maximum(slots, pltpu.roll(slots, LANES - experts, axis=1))
    slots = jnp.where(lane < experts, slots, -1.0)
    slot_row[...] = jnp.transpose(slots)[:experts]
    kept_lane = jnp.sum(jnp.where(slots >= 0.0, 1.0, 0.0), axis=0, keepdims=True)
    both = total + pltpu.roll(total, LANES - experts, axis=1)
    both = jnp.where(lane8 < experts, both, 0.0)
    sub8 = iota((8, LANES), 0)
    counts[...] = jnp.where(sub8 == 0, kept_lane, jnp.where(sub8 == 1, both, 0.0))

    blocks = tokens // QB
    lane_row = iota((1, LANES), 1)
    plan = jnp.where(lane_row == 3 * blocks, 1.0, 0.0)
    for b, (slab_low, slab_high) in enumerate(SLABS):
        opening = seg[:, b * QB : b * QB + 1]
        closing = seg[:, (b + 1) * QB - 1 : (b + 1) * QB]
        first = jnp.sum(jnp.where(seg[...] < opening, 1.0, 0.0), axis=1, keepdims=True)
        after = jnp.sum(jnp.where(seg[...] <= closing, 1.0, 0.0), axis=1, keepdims=True)
        low = jnp.minimum(jnp.floor(first * (1.0 / 16)) * 16.0, float(SEQ - WINDOW))
        fits = jnp.where(after - low <= float(WINDOW), 1.0, 0.0)
        inside = jnp.where(first >= float(slab_low), 1.0, 0.0) * jnp.where(after <= float(slab_high), 1.0, 0.0)
        plan = jnp.where(lane_row == b, low, plan)
        plan = jnp.where(lane_row == blocks + b, fits, plan)
        plan = jnp.where(lane_row == 2 * blocks + b, inside, plan)
        plan = jnp.where(lane_row == 3 * blocks, plan * inside, plan)
    windows[...] = plan.astype(jnp.int32)
    loads[0].wait()

    @pl.loop(0, experts)
    def _(e):
        chosen = iota((padded, tokens), 0).astype(f32) == slot_row[pl.ds(e, 1), :]
        gz_send[e] = dot(chosen.astype(f32).astype(bf16), cot[...]).astype(bf16)
        pltpu.make_async_copy(gz_send.at[e], gz_out.at[e], gz_sem.at[e]).start()

    def stores(i):
        rows = pl.ds(pl.multiple_of(i * TILE, TILE), TILE)
        return (
            pltpu.make_async_copy(normed_attn.at[rows], normed_out.at[rows], sems.at[0, i]),
            pltpu.make_async_copy(packed.at[rows], packed_out.at[rows], sems.at[1, i]),
        )

    for load in loads[1:]:
        load.wait()

    @pl.loop(0, tokens // TILE)
    def _(i):
        rows = pl.ds(pl.multiple_of(i * TILE, TILE), TILE)
        normal, unused = norm_parts(tok[rows, :].astype(f32))
        normed = (normal * gain_attn[...]).astype(bf16)
        normed_attn[rows, :] = normed
        packed[rows, :] = dot(normed, w_qkv[...]).astype(bf16)
        for store in stores(i):
            store.start()

    @pl.loop(0, experts)
    def _(e):
        pltpu.make_async_copy(gz_send.at[e], gz_out.at[e], gz_sem.at[e]).wait()

    @pl.loop(0, tokens // TILE)
    def _(i):
        for store in stores(i):
            store.wait()

    for zero in zeros:
        zero.wait()


def route(picks, ranks, seg, gain_attn, cot, tok, w_qkv, experts, capacity, padded):
    tokens = tok.shape[0]
    vmem = pl.BlockSpec(memory_space=pltpu.VMEM)
    anywhere = pl.BlockSpec(memory_space=pl.ANY)
    return pl.pallas_call(
        functools.partial(route_kernel, experts, capacity),
        in_specs=[vmem] * 4 + [anywhere] * 3,
        out_shape=(
            jax.ShapeDtypeStruct((tokens, LANES), f32),
            jax.ShapeDtypeStruct((experts, tokens), f32),
            jax.ShapeDtypeStruct((8, LANES), f32),
            jax.ShapeDtypeStruct((1, LANES), jnp.int32),
            jax.ShapeDtypeStruct((experts, padded, D), bf16),
            jax.ShapeDtypeStruct((tokens, D), bf16),
            jax.ShapeDtypeStruct((tokens, 3 * D), bf16),
            jax.ShapeDtypeStruct((tokens, 3 * D), bf16),
        ),
        out_specs=(vmem, vmem, vmem, vmem, anywhere, anywhere, anywhere, anywhere),
        scratch_shapes=like((cot, tok, w_qkv))
        + [
            pltpu.VMEM((experts, padded, D), bf16),
            pltpu.VMEM((tokens, D), bf16),
            pltpu.VMEM((tokens, 3 * D), bf16),
            pltpu.VMEM((QB, 3 * D), bf16),
            pltpu.SemaphoreType.DMA((3,)),
            pltpu.SemaphoreType.DMA((experts,)),
            pltpu.SemaphoreType.DMA((2, tokens // TILE)),
            pltpu.SemaphoreType.DMA((tokens // QB,)),
        ],
        compiler_params=pltpu.CompilerParams(vmem_limit_bytes=VMEM_LIMIT),
        cost_estimate=pl.CostEstimate(
            flops=2 * experts * padded * tokens * D, bytes_accessed=6 * MIB, transcendentals=0
        ),
        name="route",
    )(picks, ranks, seg, gain_attn, cot, tok, w_qkv)


def stack_heads(block):
    lane = iota(block.shape, 1)
    zero = jnp.zeros_like(block)
    return jnp.concatenate(
        [jnp.where(lane < HEAD, block, zero), jnp.where(lane < HEAD, zero, block)], axis=0
    )


def unstack_cols(stacked):
    row = iota((PAIR, QB), 0)
    picked = jnp.where(row < HEAD, stacked[:, :QB], stacked[:, QB:])
    return jnp.transpose(picked)


def window_bias(seg_col, seg_row, low, width, query):
    same = seg_col[pl.ds(low, width), :] == seg_row[:, pl.ds(query, QB)]
    half = jnp.where(same, 0.0, -1e30).astype(f32)
    return jnp.concatenate([half, half], axis=1)


def by_window(windows, block, body):
    low = windows[0, block]
    fits = windows[0, block + SEQ // QB]

    @pl.when(fits == 1)
    def _():
        body(pl.multiple_of(low, 16), WINDOW)

    @pl.when(fits != 1)
    def _():
        body(0, SEQ)


def forward_kernel(
    experts,
    windows,
    seg,
    gain_moe,
    w_router,
    packed_in,
    tok_in,
    w_proj_in,
    context_out,
    lse,
    residual_out,
    normed_moe_out,
    gates_out,
    gate_row,
    packed,
    tok,
    w_proj,
    context,
    residual,
    normed_moe,
    gates,
    seg_col,
    seg_row,
    router,
    load_sem,
    sems,
):
    loads = loading((packed_in, tok_in, w_proj_in), (packed, tok, w_proj), load_sem)
    writes = [
        pltpu.make_async_copy(source, target, sems.at[i])
        for i, (source, target) in enumerate(
            (
                (context, context_out),
                (residual, residual_out),
                (normed_moe, normed_moe_out),
                (gates, gates_out),
            )
        )
    ]
    tokens = tok.shape[0]
    seg_row[...] = seg[...].astype(f32)
    seg_col[...] = jnp.transpose(jnp.broadcast_to(seg_row[...], (LANES, tokens)))
    router[...] = jnp.zeros_like(router)
    router[:experts, :] = w_router[...]
    loads[0].wait()

    @pl.loop(0, tokens // QB)
    def _(block):
        query = pl.multiple_of(block * QB, QB)

        def body(low, width):
            bias = window_bias(seg_col, seg_row, low, width, query)
            spans = [slice(pair * PAIR, (pair + 1) * PAIR) for pair in range(PAIRS)]
            scores = []
            for span in spans:
                q = stack_heads(packed[pl.ds(query, QB), span]) * HEAD ** (-0.5)
                k = packed[pl.ds(low, width), D + span.start : D + span.stop]
                scores.append(dot_nt(k, q.astype(bf16)) + bias)
            peaks = [jnp.max(score, axis=0, keepdims=True) for score in scores]
            exponents = [jnp.exp(score - peak) for score, peak in zip(scores, peaks)]
            totals = [jnp.sum(exponent, axis=0, keepdims=True) for exponent in exponents]
            probs = [(exponent * (1.0 / total)).astype(bf16) for exponent, total in zip(exponents, totals)]
            for pair, span in enumerate(spans):
                lse[pl.ds(block, 1), pair, :] = peaks[pair] + jnp.log(totals[pair])
                v = packed[pl.ds(low, width), 2 * D + span.start : 2 * D + span.stop]
                mixed = dot_tn(v, probs[pair])
                context[pl.ds(query, QB), span] = unstack_cols(mixed).astype(bf16)

        by_window(windows, block, body)

    writes[0].start()
    for load in loads[1:]:
        load.wait()

    @pl.loop(0, tokens // TILE)
    def _(i):
        rows = pl.ds(pl.multiple_of(i * TILE, TILE), TILE)
        rest = tok[rows, :].astype(f32) + dot(context[rows, :], w_proj[...])
        residual[rows, :] = rest
        normal, unused = norm_parts(rest)
        normed = (normal * gain_moe[...]).astype(bf16)
        normed_moe[rows, :] = normed
        logits = dot_nt(normed, router[...])
        logits = jnp.where(iota(logits.shape, 1) < experts, logits, -1e30)
        exponent = jnp.exp(logits - jnp.max(logits, axis=1, keepdims=True))
        gates[rows, :] = exponent / jnp.sum(exponent, axis=1, keepdims=True)

    for write in writes[1:]:
        write.start()
    gate_row[...] = jnp.transpose(gates[...])[:experts]
    for write in writes:
        write.wait()


def forward(windows, seg, gain_moe, w_router, packed, tok, w_proj):
    tokens = tok.shape[0]
    experts = w_router.shape[0]
    vmem = pl.BlockSpec(memory_space=pltpu.VMEM)
    anywhere = pl.BlockSpec(memory_space=pl.ANY)
    return pl.pallas_call(
        functools.partial(forward_kernel, experts),
        in_specs=[pl.BlockSpec(memory_space=pltpu.SMEM)] + [vmem] * 3 + [anywhere] * 3,
        out_specs=[anywhere, vmem] + [anywhere] * 3 + [vmem],
        out_shape=(
            jax.ShapeDtypeStruct((tokens, D), bf16),
            jax.ShapeDtypeStruct((tokens // QB, PAIRS, 2 * QB), f32),
            jax.ShapeDtypeStruct((tokens, D), f32),
            jax.ShapeDtypeStruct((tokens, D), bf16),
            jax.ShapeDtypeStruct((tokens, LANES), f32),
            jax.ShapeDtypeStruct((experts, tokens), f32),
        ),
        scratch_shapes=like((packed, tok, w_proj))
        + [
            pltpu.VMEM((tokens, D), bf16),
            pltpu.VMEM((tokens, D), f32),
            pltpu.VMEM((tokens, D), bf16),
            pltpu.VMEM((tokens, LANES), f32),
            pltpu.VMEM((tokens, LANES), f32),
            pltpu.VMEM((1, tokens), f32),
            pltpu.VMEM((LANES, D), bf16),
            pltpu.SemaphoreType.DMA((3,)),
            pltpu.SemaphoreType.DMA((4,)),
        ],
        compiler_params=pltpu.CompilerParams(vmem_limit_bytes=VMEM_LIMIT),
        cost_estimate=pl.CostEstimate(
            flops=64 * 1024 * MIB, bytes_accessed=16 * MIB, transcendentals=4 * MIB
        ),
        name="attention_forward",
    )(windows, seg, gain_moe, w_router, packed, tok, w_proj)


def gelu_parts(x):
    density = jnp.exp(-0.5 * (x * x))
    return 0.5 + 0.5 * lax.erf(x * 2.0**-0.5), x * density * 0.3989422804014327


def shifted(index, by, size):
    return lax.rem(index + by, size)


def paired(index, by, size):
    total = 0
    bit = 1
    while bit < size:
        total = total + bit * lax.rem(index // bit + by // bit, 2)
        bit *= 2
    return total


def exchange(src, dst, send, recv, device):
    return pltpu.make_async_remote_copy(
        src_ref=src, dst_ref=dst, send_sem=send, recv_sem=recv, device_id=device, device_id_type=MESH
    )


def greet(barrier, sources):
    me = lax.axis_index("wide")
    line = lax.axis_index("narrow")

    @pl.loop(1, sources)
    def _(j):
        pl.semaphore_signal(barrier, inc=1, device_id=(paired(me, j, sources), line), device_id_type=MESH)


EARLY = 3


def moe_kernel(
    capacity,
    sources,
    shards,
    slot_row,
    gate_row,
    w_router,
    gain_moe,
    counts,
    normed_in,
    gz_in,
    slot_in,
    gates_in,
    cot_in,
    residual_in,
    context_in,
    w_proj_in,
    w_in0,
    w_out0,
    w_in1,
    w_out1,
    w_in2,
    w_out2,
    ring,
    own_grads,
    small,
    mixed_out,
    grad_residual_out,
    grad_context_out,
    grad_proj_out,
    *refs,
):
    others, refs = refs[: shards - 4], refs[shards - 4 :]
    normed_moe, slot_col, gates, w_proj, w_ins, w_outs, rows_send, rows, scaled, gate_slot, rows_t, gz_t = refs[:12]
    act, gpre, out_sum, back_sum, back_low, returned, back, ring_out, ring_in = refs[12:21]
    router, grad_gates, grad_logits = refs[21:24]
    load_sem, row_sem, out_sem, back_sem, weight_sem, ring_sem, late_sem, store_sem = refs[24:]
    out_low = rows_send
    depth = act.shape[0]
    padded = rows_send.shape[1]
    tokens = normed_in.shape[0]
    me = lax.axis_index("wide")
    line = lax.axis_index("narrow")
    right = (me, shifted(line, 1, shards))
    left = (me, shifted(line, shards - 1, shards))
    loads = [
        pltpu.make_async_copy(normed_in, normed_moe, load_sem.at[0]),
        pltpu.make_async_copy(gz_in, scaled, load_sem.at[1]),
    ]
    for c, pair in reversed(list(enumerate(((w_in0, w_out0), (w_in1, w_out1), (w_in2, w_out2))))):
        for i, (source, target) in enumerate(zip(pair, (w_ins, w_outs))):
            loads.append(pltpu.make_async_copy(source, target.at[c], load_sem.at[2 + 2 * c + i]))
    for i, (source, target) in enumerate(((slot_in, slot_col), (gates_in, gates), (w_proj_in, w_proj))):
        loads.append(pltpu.make_async_copy(source, target, load_sem.at[2 + 2 * EARLY + i]))
    for load in loads:
        load.start()
    barrier = pltpu.get_barrier_semaphore()
    greet(barrier, sources)
    for near in (left, right):
        pl.semaphore_signal(barrier, inc=1, device_id=near, device_id_type=MESH)
    gate_slot[...] = jnp.zeros_like(gate_slot)

    def block(s):
        return pl.ds(pl.multiple_of(s * padded, 16), padded)

    def weights_on(c):
        return [
            exchange(part.at[c - 1], part.at[c], weight_sem.at[0, i, c], weight_sem.at[1, i, c], right)
            for i, part in enumerate((w_ins, w_outs))
        ]

    def row_copy(j):
        to = paired(me, j, sources)
        return exchange(rows_send.at[to], rows.at[block(me)], row_sem.at[0, j], row_sem.at[1, j], (to, line))

    def result_copies(j):
        to = paired(me, j, sources)
        return [
            exchange(low.at[to], target.at[me], sem.at[0, j], sem.at[1, j], (to, line))
            for low, target, sem in ((out_low, returned, out_sem), (back_low, back, back_sem))
        ]

    for load in loads[:1] + loads[2:4]:
        load.wait()

    def partner(i):
        turn = lax.rem(i + 1, 3)
        return i + lax.rem(i // 3, 2) * (turn - 3 * (turn // 2))

    @pl.loop(0, sources)
    def _(i):
        j = partner(lax.rem(i + 2, sources))
        e = paired(me, j, sources)
        chosen = iota((padded, tokens), 0).astype(f32) == slot_row[pl.ds(e, 1), :]
        chosen = chosen.astype(f32).astype(bf16)
        rows_send[e] = dot(chosen, normed_moe[...]).astype(bf16)
        gate = gate_row[pl.ds(e, 1), :]
        high, middle = split2(gate)
        low = (gate - high.astype(f32) - middle.astype(f32)).astype(bf16)
        three = jnp.concatenate(
            [high.astype(f32), middle.astype(f32), low.astype(f32), jnp.zeros((5, tokens), f32)], axis=0
        )
        gate_slot[:, :padded] = dot_nt(three.astype(bf16), chosen)
        tail = rows_send[e, padded - 16 :, :].astype(f32)
        sub = iota(tail.shape, 0)
        for part in range(3):
            tail = jnp.where(sub == 13 + part, gate_slot[part : part + 1, :], tail)
        rows_send[e, padded - 16 :, :] = tail.astype(bf16)

        @pl.when(i == 0)
        def _():
            pl.semaphore_wait(barrier, sources + 1)
            for copy in weights_on(EARLY):
                copy.start()

        @pl.when(j != 0)
        def _():
            row_copy(j).start()

    rows[block(me), :] = rows_send[me]
    for load in loads[1:2] + loads[4:]:
        load.wait()

    def prepare(j):
        s = paired(me, j, sources)

        @pl.when(j != 0)
        def _():
            row_copy(j).wait_recv()

        end = pl.ds(pl.multiple_of(s * padded + padded - 16, 16), 16)
        tail = rows[end, :].astype(f32)
        gate = tail[13:14] + tail[14:15] + tail[15:16]
        gate = jnp.transpose(jnp.broadcast_to(gate, (LANES, D)))[:padded, :1]
        live = iota((padded, 1), 0) < capacity
        scaled[block(s), :] = (jnp.where(live, gate, 0.0) * scaled[block(s), :].astype(f32)).astype(bf16)
        live16 = iota((16, 1), 0) < 16 - (padded - capacity)
        rows[end, :] = jnp.where(live16, tail, 0.0).astype(bf16)

    def shard_results(s, c):
        pre = dot(rows[block(s), :], w_ins[c])
        phi, slope = gelu_parts(pre)
        act_low = (pre * phi).astype(bf16)
        act[c % depth, block(s), :] = act_low
        grad_pre = (dot_nt(scaled[block(s), :], w_outs[c]) * (phi + slope)).astype(bf16)
        gpre[c % depth, block(s), :] = grad_pre
        return dot(act_low, w_outs[c]), dot_nt(grad_pre, w_ins[c])

    def send(j, result, grad_rows):
        s = paired(me, j, sources)

        @pl.when(j != 0)
        def _():
            row_copy(j).wait_send()

        out_low[s] = result.astype(bf16)
        back_low[s] = grad_rows.astype(bf16)

        @pl.when(j != 0)
        def _():
            for copy in result_copies(j):
                copy.start()

    def run(s, order, fresh, final):
        for k, c in enumerate(order):
            result, grad_rows = shard_results(s, c)
            if k > 0 or not fresh:
                result = result + out_sum[block(s), :]
                grad_rows = grad_rows + back_sum[block(s), :]
            if k < len(order) - 1 or not final:
                out_sum[block(s), :] = result
                back_sum[block(s), :] = grad_rows
        return result, grad_rows

    def weight_grads(c):
        return dot(rows_t[...], gpre[c % depth]).astype(bf16), dot(gz_t[...], act[c % depth]).astype(bf16)

    first_step = exchange(ring_out, ring_in.at[0], ring_sem.at[0, 0], ring_sem.at[1, 0], right)
    second_step = exchange(ring_in.at[0], ring_in.at[1], ring_sem.at[0, 1], ring_sem.at[1, 1], right)
    late = tuple(range(EARLY, shards))

    def pass_over(first, last, order, opening, closing):
        @pl.loop(first, last)
        def _(i):
            j = partner(i)
            if opening:
                prepare(j)
            results = run(paired(me, j, sources), order, opening, closing)
            if closing:
                send(j, *results)

    def late_weights():
        for c in late:
            for copy in weights_on(c):
                copy.wait()
            if c + 1 < shards:
                for copy in weights_on(c + 1):
                    copy.start()

    def turn_rows():
        for s in range(sources):
            rows_t[:, s * padded : (s + 1) * padded] = jnp.transpose(rows[s * padded : (s + 1) * padded, :])
            gz_t[:, s * padded : (s + 1) * padded] = jnp.transpose(scaled[s * padded : (s + 1) * padded, :])

    def start_ring():
        ring_out[:D, :], ring_out[D:, :] = weight_grads(1)
        first_step.start()

    def keep_grads(c):
        target = own_grads if c == 0 else ring if c == 3 else others[c - 4]
        target[:D, :], target[D:, :] = weight_grads(c)

    if depth == shards:
        pass_over(0, 4, (1, 0, 2), True, False)
        pass_over(4, 5, (1, 0), True, False)
        late_weights()
        pass_over(2, 4, late, False, True)
        pass_over(5, sources, (1,), True, False)
        turn_rows()
        start_ring()
        pass_over(4, 5, (2,) + late, False, True)
        pass_over(5, sources, (0, 2) + late, False, True)
        pass_over(0, 2, late, False, True)
    else:
        late_weights()
        pass_over(0, sources, (1,), True, False)
        turn_rows()
        start_ring()
        for c in (0,) + late:
            pass_over(0, sources, (c,), False, False)
            keep_grads(c)
        pass_over(0, sources, (2,), False, True)

    upper = slice(tokens, 2 * tokens)
    late_loads = loading(
        (cot_in, residual_in, context_in),
        (rows.at[pl.ds(0, tokens)], out_sum.at[pl.ds(tokens, tokens)], rows.at[pl.ds(tokens, tokens)]),
        late_sem,
    )
    returned[me] = out_low[me]
    back[me] = back_low[me]
    second = weight_grads(2)
    if depth == shards:
        keep_grads(3)
    first_step.wait()
    for half in range(2):
        span = slice(half * D, half * D + D)
        ring_in[0, span, :] = (ring_in[0, span, :].astype(f32) + second[half].astype(f32)).astype(bf16)
    second_step.start()
    if depth == shards:
        keep_grads(0)

    lane = iota((TILE, LANES), 1)
    router[...] = jnp.zeros_like(router)
    router[:sources, :] = w_router[...]
    small[...] = jnp.zeros_like(small)
    small[2:4, :LANES] = counts[:2, :]
    grad_gates[...] = jnp.zeros_like(grad_gates)
    out_sum[:tokens, :] = jnp.zeros((tokens, D), f32)
    back_sum[:tokens, :] = jnp.zeros((tokens, D), f32)
    for load in late_loads:
        load.wait()

    def collect(e):
        for i in range(tokens // TILE):
            at = slice(i * TILE, (i + 1) * TILE)
            slots = slot_col[at, :]
            slot = jnp.max(
                jnp.where((lane == e) | (lane == e + sources), slots, -1.0), axis=1, keepdims=True
            )
            gate = jnp.sum(jnp.where(lane == e, gates[at, :], 0.0), axis=1, keepdims=True)
            chosen = (iota((TILE, padded), 1).astype(f32) == slot).astype(f32).astype(bf16)
            result = dot(chosen, returned[e])
            out_sum[at, :] += gate * result
            inner = jnp.sum(result * rows[at, :].astype(f32), axis=1, keepdims=True)
            grad_gates[at, :] += jnp.where(lane == e, inner, 0.0)
            back_sum[at, :] += dot(chosen, back[e])

    collect(me)

    @pl.loop(1, sources)
    def _(i):
        j = partner(i)
        for copy in result_copies(j):
            copy.wait_recv()
        collect(paired(me, j, sources))

    stores = []
    for i in range(tokens // TILE):
        at = slice(i * TILE, (i + 1) * TILE)
        above = slice(tokens + i * TILE, tokens + (i + 1) * TILE)
        grad_z = rows[at, :].astype(f32)
        probs = gates[at, :]
        rest = out_sum[above, :]
        scaled[at, :] = (rest + out_sum[at, :]).astype(bf16)
        gate_inner = jnp.sum(probs * grad_gates[at, :], axis=1, keepdims=True)
        high, low = split2(probs * (grad_gates[at, :] - gate_inner))
        grad_logits[at, :LANES] = high
        grad_logits[at, LANES:] = low
        grad_normed = back_sum[at, :] + dot(high, router[...]) + dot(low, router[...])
        normal, inverse = norm_parts(rest)
        grad_norm, grad_gain = norm_back(grad_normed, gain_moe[...], normal, inverse)
        small[1:2, :] += grad_gain
        grad_rest = grad_z + grad_norm
        back_sum[above, :] = grad_rest
        attn = grad_rest.astype(bf16)
        scaled[above, :] = attn
        rows[at, :] = dot_nt(attn, w_proj[...]).astype(bf16)
        here = pl.ds(i * TILE, TILE)
        for k, (source, target) in enumerate(
            (
                (scaled.at[here], mixed_out),
                (back_sum.at[pl.ds(tokens + i * TILE, TILE)], grad_residual_out),
                (rows.at[here], grad_context_out),
            )
        ):
            stores.append(pltpu.make_async_copy(source, target.at[here], store_sem.at[k, i]))
            stores[-1].start()
    out_sum[:D, :] = dot_tn(rows[upper, :], scaled[upper, :])
    stores.append(pltpu.make_async_copy(out_sum.at[pl.ds(0, D)], grad_proj_out, store_sem.at[3, 0]))
    stores[-1].start()
    both = dot_tn(normed_moe[...], grad_logits[...])
    both = jnp.transpose(both[:, :LANES] + both[:, LANES:])
    small[8:, :] = both[:sources]
    second_step.wait()
    ring[...] = (ring_in[1].astype(f32) + ring[...].astype(f32)).astype(bf16)
    for store in stores:
        store.wait()

    @pl.loop(1, sources)
    def _(j):
        for copy in result_copies(j):
            copy.wait_send()


def moe(slot_row, gate_row, w_router, gain_moe, counts, *large, shards, capacity):
    normed_moe, gz = large[:2]
    sources = slot_row.shape[0]
    tokens = normed_moe.shape[0]
    hidden = large[-2].shape[1]
    total = gz.shape[0]
    blocks = (sources, total // sources, D)
    depth = shards if shards == 4 else 1
    vmem = pl.BlockSpec(memory_space=pltpu.VMEM)
    anywhere = pl.BlockSpec(memory_space=pl.ANY)
    dma = pltpu.SemaphoreType.DMA
    piece = jax.ShapeDtypeStruct((2 * D, hidden), bf16)
    return pl.pallas_call(
        functools.partial(moe_kernel, capacity, sources, shards),
        in_specs=[vmem] * 5 + [anywhere] * len(large),
        out_specs=[vmem] * 3 + [anywhere] * 4 + [vmem] * (shards - 4),
        out_shape=[
            piece,
            piece,
            jax.ShapeDtypeStruct((8 + sources, D), f32),
            jax.ShapeDtypeStruct((tokens, D), bf16),
            jax.ShapeDtypeStruct((tokens, D), f32),
            jax.ShapeDtypeStruct((tokens, D), bf16),
            jax.ShapeDtypeStruct((D, D), f32),
        ]
        + [piece] * (shards - 4),
        scratch_shapes=[
            pltpu.VMEM((tokens, D), bf16),
            pltpu.VMEM((tokens, LANES), f32),
            pltpu.VMEM((tokens, LANES), f32),
            pltpu.VMEM((D, D), bf16),
            pltpu.VMEM((shards, D, hidden), bf16),
            pltpu.VMEM((shards, hidden, D), bf16),
            pltpu.VMEM(blocks, bf16),
            pltpu.VMEM((total, D), bf16),
            pltpu.VMEM((total, D), bf16),
            pltpu.VMEM((8, D), f32),
            pltpu.VMEM((D, total), bf16),
            pltpu.VMEM((D, total), bf16),
            pltpu.VMEM((depth, total, hidden), bf16),
            pltpu.VMEM((depth, total, hidden), bf16),
            pltpu.VMEM((total, D), f32),
            pltpu.VMEM((total, D), f32),
            pltpu.VMEM(blocks, bf16),
            pltpu.VMEM(blocks, bf16),
            pltpu.VMEM(blocks, bf16),
            pltpu.VMEM((2 * D, hidden), bf16),
            pltpu.VMEM((2, 2 * D, hidden), bf16),
            pltpu.VMEM((LANES, D), bf16),
            pltpu.VMEM((tokens, LANES), f32),
            pltpu.VMEM((tokens, 2 * LANES), bf16),
            dma((5 + 2 * EARLY,)),
            dma((2, sources)),
            dma((2, sources)),
            dma((2, sources)),
            dma((2, 2, shards)),
            dma((2, 2)),
            dma((3,)),
            dma((4, tokens // TILE)),
        ],
        compiler_params=pltpu.CompilerParams(
            vmem_limit_bytes=VMEM_LIMIT, collective_id=1, has_side_effects=True
        ),
        cost_estimate=pl.CostEstimate(
            flops=12 * total * D * hidden * shards, bytes_accessed=20 * MIB, transcendentals=0
        ),
        name="moe",
    )(slot_row, gate_row, w_router, gain_moe, counts, *large)


def repair_kernel(
    windows,
    seg,
    lse,
    packed_in,
    extra_in,
    grad_context_in,
    extra_out,
    grad_context_out,
    packed,
    extra,
    grad_context,
    seg_col,
    seg_row,
    grad_k,
    grad_v,
    sems,
):
    tokens = packed.shape[0]
    blocks = tokens // QB

    @pl.when(windows[0, 3 * blocks] != 1)
    def _():
        loads = loading((packed_in, extra_in, grad_context_in), (packed, extra, grad_context), sems)
        seg_row[...] = seg[...].astype(f32)
        seg_col[...] = jnp.transpose(jnp.broadcast_to(seg_row[...], (LANES, tokens)))
        for load in loads:
            load.wait()
        grad_k[...] = jnp.zeros_like(grad_k)
        grad_v[...] = jnp.zeros_like(grad_v)

        @pl.loop(0, blocks)
        def _(block):
            query = pl.multiple_of(block * QB, QB)

            @pl.when(windows[0, 2 * blocks + block] != 1)
            def _():
                bias = window_bias(seg_col, seg_row, 0, SEQ, query)
                spans = [slice(pair * PAIR, (pair + 1) * PAIR) for pair in range(PAIRS)]
                keys = pl.ds(0, SEQ)
                queries = [
                    (stack_heads(packed[pl.ds(query, QB), span]) * HEAD ** (-0.5)).astype(bf16) for span in spans
                ]
                grads = [stack_heads(grad_context[pl.ds(query, QB), span]) for span in spans]
                probs = []
                grad_probs = []
                for pair, span in enumerate(spans):
                    k = packed[keys, D + span.start : D + span.stop]
                    v = packed[keys, 2 * D + span.start : 2 * D + span.stop]
                    probs.append(jnp.exp(dot_nt(k, queries[pair]) + bias - lse[pl.ds(block, 1), pair, :]))
                    grad_probs.append(dot_nt(v, grads[pair]))
                grad_scores = []
                for pair, span in enumerate(spans):
                    grad_v[keys, span] += dot(probs[pair].astype(bf16), grads[pair])
                    weighted = probs[pair] * grad_probs[pair]
                    inner = jnp.sum(weighted, axis=0, keepdims=True)
                    grad_scores.append((weighted - probs[pair] * inner).astype(bf16))
                for pair, span in enumerate(spans):
                    k = packed[keys, D + span.start : D + span.stop]
                    grad_k[keys, span] += dot(grad_scores[pair], queries[pair])
                    grad_q = unstack_cols(dot_tn(k, grad_scores[pair])) * HEAD ** (-0.5)
                    extra[pl.ds(query, QB), span] = grad_q.astype(bf16)
                grad_context[pl.ds(query, QB), :] = jnp.zeros((QB, D), bf16)

        extra[:, D : 2 * D] = grad_k[...].astype(bf16)
        extra[:, 2 * D :] = grad_v[...].astype(bf16)
        for store in loading((extra, grad_context), (extra_out, grad_context_out), sems):
            store.wait()


def repair(windows, seg, lse, packed, extra, grad_context):
    tokens = packed.shape[0]
    vmem = pl.BlockSpec(memory_space=pltpu.VMEM)
    anywhere = pl.BlockSpec(memory_space=pl.ANY)
    return pl.pallas_call(
        repair_kernel,
        in_specs=[pl.BlockSpec(memory_space=pltpu.SMEM)] + [vmem] * 2 + [anywhere] * 3,
        out_specs=(anywhere, anywhere),
        out_shape=(
            jax.ShapeDtypeStruct(extra.shape, bf16),
            jax.ShapeDtypeStruct(grad_context.shape, bf16),
        ),
        input_output_aliases={4: 0, 5: 1},
        scratch_shapes=like((packed, extra, grad_context))
        + [
            pltpu.VMEM((tokens, LANES), f32),
            pltpu.VMEM((1, tokens), f32),
            pltpu.VMEM((tokens, D), f32),
            pltpu.VMEM((tokens, D), f32),
            pltpu.SemaphoreType.DMA((3,)),
        ],
        compiler_params=pltpu.CompilerParams(vmem_limit_bytes=VMEM_LIMIT),
        cost_estimate=pl.CostEstimate(flops=MIB, bytes_accessed=MIB, transcendentals=0),
        name="repair",
    )(windows, seg, lse, packed, extra, grad_context)


SLAB_AT = tuple(sum(high - low for low, high in SLABS[:b]) for b in range(len(SLABS) + 1))


def slab_bias(bias, seg_col, seg_row):
    for b, (low, high) in enumerate(SLABS):
        same = seg_col[low:high, :] == seg_row[:, b * QB : (b + 1) * QB]
        bias[SLAB_AT[b] : SLAB_AT[b + 1], :] = jnp.where(same, 0.0, -1e30)


def pair_backward(pair, packed, grad_context, lse, extra, bias, grad_k, grad_v, out):
    def span(which):
        return pl.ds(pl.multiple_of(which * D + pair * PAIR, PAIR), PAIR)

    grad_k[...] = extra[:, span(1)].astype(f32)
    grad_v[...] = extra[:, span(2)].astype(f32)
    for group in range(0, len(SLABS), 4):
        blocks = range(group, group + 4)
        queries, grads, probs, grad_probs, grad_scores = [], [], [], [], []
        for b in blocks:
            low, high = SLABS[b]
            rows = slice(b * QB, (b + 1) * QB)
            queries.append((stack_heads(packed[rows, span(0)]) * HEAD ** (-0.5)).astype(bf16))
            grads.append(stack_heads(grad_context[rows, span(0)]))
            masked = bias[SLAB_AT[b] : SLAB_AT[b + 1], :]
            scores = dot_nt(packed[low:high, span(1)], queries[-1]) + jnp.concatenate([masked, masked], axis=1)
            probs.append(jnp.exp(scores - lse[b, pl.ds(pair, 1), :]))
            grad_probs.append(dot_nt(packed[low:high, span(2)], grads[-1]))
        for i, b in enumerate(blocks):
            low, high = SLABS[b]
            grad_v[low:high, :] += dot(probs[i].astype(bf16), grads[i])
            weighted = probs[i] * grad_probs[i]
            inner = jnp.sum(weighted, axis=0, keepdims=True)
            grad_scores.append((weighted - probs[i] * inner).astype(bf16))
        for i, b in enumerate(blocks):
            low, high = SLABS[b]
            rows = slice(b * QB, (b + 1) * QB)
            grad_k[low:high, :] += dot(grad_scores[i], queries[i])
            grad_q = unstack_cols(dot_tn(packed[low:high, span(1)], grad_scores[i])) * HEAD ** (-0.5)
            out[rows, :PAIR] = (grad_q + extra[rows, span(0)].astype(f32)).astype(bf16)
    out[:, PAIR : 2 * PAIR] = grad_k[...].astype(bf16)
    out[:, 2 * PAIR :] = grad_v[...].astype(bf16)


def shared_kernel(
    chips,
    planes,
    seg,
    lse,
    partial,
    gain_attn,
    packed_in,
    grad_context_in,
    extra_in,
    normed_attn_in,
    grad_proj_in,
    w_qkv_in,
    tok_in,
    grad_residual_in,
    summed,
    small,
    grad_tokens_out,
    packed,
    grad_context,
    extra,
    normed_attn,
    grad_proj,
    w_qkv,
    tok,
    grad_residual,
    pair_grads,
    grad_tokens,
    normed_t,
    seg_col,
    bias,
    grad_k,
    grad_v,
    grad_packed,
    half,
    core_out,
    core_in,
    chip_out,
    chip_in,
    plane_out,
    plane_in,
    small_own,
    small_core,
    small_chip,
    small_plane,
    pair_sem,
    load_sem,
    store_sem,
    core_sem,
    chip_sem,
    plane_sem,
    plane_sem2,
    chip_sem2,
    core_sem2,
    small_sem,
    small_chip_sem,
    small_plane_sem,
):
    tokens = tok.shape[0]
    stages = 16 // planes
    pairs = PAIRS // stages
    tiles = tokens // TILE
    wide = lax.axis_index("wide")
    plane = lax.axis_index("narrow")
    core = lax.rem(wide, 2)
    chip = wide // 2
    share = D // (2 * chips)
    partner = (chip * 2 + 1 - core, plane)
    mine = pl.ds(pl.multiple_of(core * (D // 2), D // 2), D // 2)
    other = pl.ds(pl.multiple_of((1 - core) * (D // 2), D // 2), D // 2)
    chunk = pl.ds(pl.multiple_of(core * (D // 2) + chip * share, share), share)
    own_chunk = pl.ds(pl.multiple_of(chip * share, share), share)

    loads = [
        pltpu.make_async_copy(source, target, load_sem.at[i])
        for i, (source, target) in enumerate(
            (
                (normed_attn_in, normed_attn),
                (grad_proj_in, grad_proj),
                (w_qkv_in, w_qkv),
                (tok_in, tok),
                (grad_residual_in, grad_residual),
            )
        )
    ]

    def pair_loads(pair):
        copies = []
        for source, target, parts in ((packed_in, packed, 3), (grad_context_in, grad_context, 1), (extra_in, extra, 3)):
            for which in range(parts):
                lanes = pl.ds(pl.multiple_of(which * D + pair * PAIR, PAIR), PAIR)
                copies.append(
                    pltpu.make_async_copy(source.at[:, lanes], target.at[:, lanes], pair_sem.at[pair, len(copies)])
                )
        return copies

    for pair in range(PAIRS):
        for load in pair_loads(pair):
            load.start()
    for load in loads:
        load.start()

    def chip_at(j):
        to = shifted(chip, j, chips)
        return to, (to * 2 + core, plane)

    def plane_at(j):
        to = shifted(plane, j, planes)
        return to, (wide, to)

    barrier = pltpu.get_barrier_semaphore()
    pl.semaphore_signal(barrier, inc=1, device_id=partner, device_id_type=MESH)

    @pl.loop(1, chips)
    def _(j):
        pl.semaphore_signal(barrier, inc=1, device_id=chip_at(j)[1], device_id_type=MESH)

    @pl.loop(1, planes)
    def _(j):
        pl.semaphore_signal(barrier, inc=1, device_id=plane_at(j)[1], device_id_type=MESH)

    def blocks(stage):
        return pl.ds(stage * planes, planes)

    def core_copy(stage):
        at = blocks(stage)
        return exchange(core_out.at[at], core_in.at[at], core_sem.at[0, stage], core_sem.at[1, stage], partner)

    def chip_copy(stage, j):
        to, device = chip_at(j)
        rows = pl.ds(pl.multiple_of(to * share, share), share)
        at = blocks(stage)
        return exchange(
            chip_out.at[at, rows], chip_in.at[j, at], chip_sem.at[0, stage, j], chip_sem.at[1, stage, j], device
        )

    def plane_copy(stage, j):
        to, device = plane_at(j)
        return exchange(
            plane_out.at[stage * planes + to],
            plane_in.at[j, stage],
            plane_sem.at[0, stage, j],
            plane_sem.at[1, stage, j],
            device,
        )

    def plane_back(stage, j):
        spot = summed.at[stage * planes + plane, chunk]
        return exchange(spot, spot, plane_sem2.at[0, stage, j], plane_sem2.at[1, stage, j], plane_at(j)[1])

    def chip_back(stage, j):
        spot = summed.at[blocks(stage), chunk]
        return exchange(spot, spot, chip_sem2.at[0, stage, j], chip_sem2.at[1, stage, j], chip_at(j)[1])

    def core_back(stage):
        spot = summed.at[blocks(stage), mine]
        return exchange(spot, spot, core_sem2.at[0, stage], core_sem2.at[1, stage], partner)

    def small_core_copy():
        return exchange(small_own, small_core, small_sem.at[0], small_sem.at[1], partner)

    def small_chip_copy(j):
        spot = small_chip.at[chip]
        return exchange(spot, spot, small_chip_sem.at[0, j], small_chip_sem.at[1, j], chip_at(j)[1])

    def small_plane_copy(j):
        spot = small_plane.at[plane]
        return exchange(spot, spot, small_plane_sem.at[0, j], small_plane_sem.at[1, j], plane_at(j)[1])

    def pair_products(pair):
        spare = dot(normed_t[other, :], pair_grads[...])
        own = dot(normed_t[mine, :], pair_grads[...])
        lanes = pl.ds(pl.multiple_of(pair * PAIR, PAIR), PAIR)
        for which in range(3):
            at = slice(which * PAIR, (which + 1) * PAIR)
            core_out[pair * 4 + which] = spare[:, at].astype(bf16)
            half[pair * 4 + which] = own[:, at]
            grad_packed[:, pl.ds(pl.multiple_of(which * D + pair * PAIR, PAIR), PAIR)] = pair_grads[:, at]
        core_out[pair * 4 + 3] = grad_proj[other, lanes].astype(bf16)
        half[pair * 4 + 3] = grad_proj[mine, lanes]

    def chip_stage(stage):
        core_copy(stage).wait_recv()
        at = blocks(stage)
        total = half[at] + core_in[at].astype(f32)
        half[at] = total
        chip_out[at] = total.astype(bf16)

        @pl.loop(1, chips)
        def _(j):
            chip_copy(stage, j).start()

    def plane_stage(stage):
        at = blocks(stage)
        total = half[at, own_chunk, :]
        for j in range(1, chips):
            chip_copy(stage, j).wait_recv()
            total = total + chip_in[j, at].astype(f32)
        half[at, own_chunk, :] = total
        plane_out[at] = total.astype(bf16)

        @pl.loop(1, planes)
        def _(j):
            plane_copy(stage, j).start()

    def own_stage(stage):
        total = half[stage * planes + plane, own_chunk, :]
        for j in range(1, planes):
            plane_copy(stage, j).wait_recv()
            total = total + plane_in[j, stage].astype(f32)
        summed[stage * planes + plane, chunk, :] = total.astype(bf16)

        @pl.loop(1, planes)
        def _(j):
            plane_back(stage, j).start()

    def gather_stage(stage):
        @pl.loop(1, planes)
        def _(j):
            plane_back(stage, j).wait_recv()

        @pl.loop(1, chips)
        def _(j):
            chip_back(stage, j).start()

    def last_stage(stage):
        @pl.loop(1, chips)
        def _(j):
            chip_back(stage, j).wait_recv()

        core_back(stage).start()

    def norm_tile(i):
        rows = slice(i * TILE, (i + 1) * TILE)
        grad_normed = dot_nt(grad_packed[rows, :], w_qkv[...])
        normal, inverse = norm_parts(tok[rows, :].astype(f32))
        grad_norm, grad_gain = norm_back(grad_normed, gain_attn[...], normal, inverse)
        small_own[0:1, :] += grad_gain
        grad_tokens[rows, :] = grad_residual[rows, :] + grad_norm

    small_own[...] = partial[...]
    seg_row = seg[...].astype(f32)
    seg_col[...] = jnp.transpose(jnp.broadcast_to(seg_row, (LANES, tokens)))
    slab_bias(bias, seg_col, seg_row)

    @pl.loop(0, PAIRS)
    def _(pair):
        for load in pair_loads(pair):
            load.wait()
        pair_backward(pair, packed, grad_context, lse, extra, bias, grad_k, grad_v, pair_grads)

        @pl.when(pair == 0)
        def _():
            for load in loads[:2]:
                load.wait()
            normed_t[...] = jnp.transpose(normed_attn[...])
            pl.semaphore_wait(barrier, chips + planes - 1)

        pair_products(pair)

        @pl.when(lax.rem(pair + 1, pairs) == 0)
        def _():
            stage = pair // pairs
            core_copy(stage).start()

            @pl.when(stage > 0)
            def _():
                chip_stage(stage - 1)

            @pl.when(stage > 1)
            def _():
                plane_stage(stage - 2)

            @pl.when(stage > 2)
            def _():
                own_stage(stage - 3)

    for load in loads[2:]:
        load.wait()
    steps = (chip_stage, plane_stage, own_stage, gather_stage, last_stage)
    for late in range(len(steps)):
        if late == 0:
            norm_tile(0)
        for i, step in enumerate(steps):
            stage = stages - 1 + late - i
            if i >= late and 0 <= stage < stages:
                step(stage)
        if late == 0:
            for i in range(1, tiles):
                norm_tile(i)
            small_core_copy().start()
            store = pltpu.make_async_copy(grad_tokens, grad_tokens_out, store_sem)
            store.start()
        if late == 1:
            small_core_copy().wait_recv()
            small_chip[chip] = small_own[...] + small_core[...]

            @pl.loop(1, chips)
            def _(j):
                small_chip_copy(j).start()

        if late == 2:

            @pl.loop(1, chips)
            def _(j):
                small_chip_copy(j).wait_recv()

            total = small_chip[0]
            for c in range(1, chips):
                total = total + small_chip[c]
            small_plane[plane] = total

            @pl.loop(1, planes)
            def _(j):
                small_plane_copy(j).start()

    @pl.loop(1, planes)
    def _(j):
        small_plane_copy(j).wait_recv()

    total = small_plane[0]
    for c in range(1, planes):
        total = total + small_plane[c]
    small[...] = total
    store.wait()

    @pl.loop(0, stages)
    def _(stage):
        core_back(stage).wait()
        core_copy(stage).wait_send()

        @pl.loop(1, chips)
        def _(j):
            chip_back(stage, j).wait_send()
            chip_copy(stage, j).wait_send()

        @pl.loop(1, planes)
        def _(j):
            plane_back(stage, j).wait_send()
            plane_copy(stage, j).wait_send()

    @pl.loop(1, planes)
    def _(j):
        small_plane_copy(j).wait_send()

    @pl.loop(1, chips)
    def _(j):
        small_chip_copy(j).wait_send()

    small_core_copy().wait_send()


def shared_gradients(*operands):
    partial, packed = operands[2], operands[4]
    tokens = packed.shape[0]
    chips = lax.axis_size("wide") // 2
    planes = lax.axis_size("narrow")
    stages = 16 // planes
    share = D // (2 * chips)
    rows = partial.shape[0]
    dma = pltpu.SemaphoreType.DMA
    vmem = pl.BlockSpec(memory_space=pltpu.VMEM)
    anywhere = pl.BlockSpec(memory_space=pl.ANY)
    return pl.pallas_call(
        functools.partial(shared_kernel, chips, planes),
        in_specs=[vmem] * 4 + [anywhere] * 8,
        out_specs=(vmem, vmem, anywhere),
        out_shape=(
            jax.ShapeDtypeStruct((16, D, LANES), bf16),
            jax.ShapeDtypeStruct((rows, D), f32),
            jax.ShapeDtypeStruct((tokens, D), f32),
        ),
        scratch_shapes=[pltpu.VMEM(operand.shape, operand.dtype) for operand in operands[4:]]
        + [
            pltpu.VMEM((tokens, 3 * PAIR), bf16),
            pltpu.VMEM((tokens, D), f32),
            pltpu.VMEM((D, tokens), bf16),
            pltpu.VMEM((tokens, LANES), f32),
            pltpu.VMEM((SLAB_AT[-1], QB), f32),
            pltpu.VMEM((tokens, PAIR), f32),
            pltpu.VMEM((tokens, PAIR), f32),
            pltpu.VMEM((tokens, 3 * D), bf16),
            pltpu.VMEM((16, D // 2, LANES), f32),
            pltpu.VMEM((16, D // 2, LANES), bf16),
            pltpu.VMEM((16, D // 2, LANES), bf16),
            pltpu.VMEM((16, D // 2, LANES), bf16),
            pltpu.VMEM((chips, 16, share, LANES), bf16),
            pltpu.VMEM((16, share, LANES), bf16),
            pltpu.VMEM((planes, stages, share, LANES), bf16),
            pltpu.VMEM((rows, D), f32),
            pltpu.VMEM((rows, D), f32),
            pltpu.VMEM((chips, rows, D), f32),
            pltpu.VMEM((planes, rows, D), f32),
            dma((PAIRS, 7)),
            dma((5,)),
            dma,
            dma((2, stages)),
            dma((2, stages, chips)),
            dma((2, stages, planes)),
            dma((2, stages, planes)),
            dma((2, stages, chips)),
            dma((2, stages)),
            dma((2,)),
            dma((2, chips)),
            dma((2, planes)),
        ],
        compiler_params=pltpu.CompilerParams(
            vmem_limit_bytes=VMEM_LIMIT, collective_id=2, has_side_effects=True
        ),
        cost_estimate=pl.CostEstimate(
            flops=12 * tokens * D * D, bytes_accessed=16 * MIB, transcendentals=0
        ),
        name="shared_gradients",
    )(*operands)


def finish_kernel(
    experts,
    small,
    summed_in,
    ring_in,
    own_in,
    tokens_in,
    gain_attn,
    gain_moe,
    router,
    kept,
    dropped,
    qkv_out,
    proj_out,
    in_out,
    out_out,
    tokens_out,
    summed,
    ring,
    own,
    tokens,
    qkv,
    proj,
    grad_in,
    grad_out,
    load_sem,
    store_sem,
    token_sem,
):
    loads = loading(
        (summed_in, ring_in, own_in, tokens_in), (summed, ring, own, tokens), load_sem
    )
    through = pltpu.make_async_copy(tokens, tokens_out, token_sem)
    gain_attn[...] = small[0, :]
    gain_moe[...] = small[1, :]
    router[...] = small[8:, :]
    counted = small[2:4, :experts]
    kept[...] = counted[0:1].astype(jnp.int32)
    dropped[...] = (counted[1:2] - counted[0:1]).astype(jnp.int32)
    loads[0].wait()
    stores = []
    step = D // 4
    for i in range(4):
        rows = slice(i * step, (i + 1) * step)
        for n in range(16):
            pair, which = divmod(n, 4)
            lanes = slice(pair * PAIR, (pair + 1) * PAIR)
            if which < 3:
                qkv[rows, which * D + lanes.start : which * D + lanes.stop] = summed[n, rows, :].astype(f32)
            else:
                proj[rows, lanes] = summed[n, rows, :].astype(f32)
        for source, target in ((qkv, qkv_out), (proj, proj_out)):
            stores.append(pltpu.make_async_copy(source.at[rows], target.at[rows], store_sem.at[len(stores)]))
            stores[-1].start()
    for load in loads[1:]:
        load.wait()
    through.start()
    grad_in[0] = ring[:D, :].astype(f32) + own[:D, :].astype(f32)
    stores.append(pltpu.make_async_copy(grad_in, in_out, store_sem.at[len(stores)]))
    stores[-1].start()
    grad_out[0] = jnp.transpose(ring[D:, :].astype(f32) + own[D:, :].astype(f32))
    stores.append(pltpu.make_async_copy(grad_out, out_out, store_sem.at[len(stores)]))
    stores[-1].start()
    for store in stores:
        store.wait()
    through.wait()


def finish(experts, small, summed, ring, own, tokens_in):
    hidden = own.shape[1]
    vmem = pl.BlockSpec(memory_space=pltpu.VMEM)
    anywhere = pl.BlockSpec(memory_space=pl.ANY)
    large = [((D, 3 * D), f32), ((D, D), f32), ((1, D, hidden), f32), ((1, hidden, D), f32)]
    dma = pltpu.SemaphoreType.DMA
    return pl.pallas_call(
        functools.partial(finish_kernel, experts),
        in_specs=[vmem] + [anywhere] * 4,
        out_specs=[vmem] * 5 + [anywhere] * 5,
        out_shape=[
            jax.ShapeDtypeStruct((D,), f32),
            jax.ShapeDtypeStruct((D,), f32),
            jax.ShapeDtypeStruct((experts, D), f32),
            jax.ShapeDtypeStruct((1, experts), jnp.int32),
            jax.ShapeDtypeStruct((1, experts), jnp.int32),
        ]
        + [jax.ShapeDtypeStruct(*shape) for shape in large]
        + [jax.ShapeDtypeStruct(tokens_in.shape, f32)],
        scratch_shapes=like((summed, ring, own, tokens_in))
        + [pltpu.VMEM(*shape) for shape in large]
        + [dma((4,)), dma((10,)), dma],
        compiler_params=pltpu.CompilerParams(vmem_limit_bytes=VMEM_LIMIT),
        cost_estimate=pl.CostEstimate(flops=0, bytes_accessed=14 * MIB, transcendentals=0),
        name="finish",
    )(small, summed, ring, own, tokens_in)


def per_device(
    tokens,
    segment_ids,
    expert_picks,
    priority_ranks,
    gain_attn,
    w_qkv,
    w_proj,
    gain_moe,
    w_router,
    w_in,
    w_out,
    cotangent,
):
    experts = w_router.shape[1]
    capacity = (21 * TOP * TOK_DEV + 20 * experts - 1) // (20 * experts)
    padded = (capacity + 3 + 15) // 16 * 16
    gain_attn = gain_attn.reshape(1, D)
    gain_moe = gain_moe.reshape(1, D)
    seg = segment_ids.reshape(1, SEQ)
    line = lax.axis_size("narrow")
    ring_steps = [(i, (i + 1) % line) for i in range(line)]
    together = lax.optimization_barrier

    def pass_on(values):
        return lax.ppermute(values, "narrow", ring_steps)

    early = [(w_in[0], w_out[0])]
    early.append(pass_on(early[0]))
    slot_col, slot_row, counts, windows, gz_send, normed_attn, packed, extra = route(
        expert_picks.T, priority_ranks, seg, gain_attn, cotangent, tokens, w_qkv, experts, capacity, padded
    )
    gz = lax.all_to_all(gz_send, "wide", split_axis=0, concat_axis=0, tiled=True)
    early.append(pass_on(together((early[1], slot_row))[0]))
    context, lse, residual, normed_moe, gates, gate_row = forward(
        windows, seg, gain_moe, w_router.T, packed, tokens, w_proj
    )
    ring, own, partial, mixed, grad_residual, grad_context, grad_proj, *others = moe(
        slot_row,
        gate_row,
        w_router.T,
        gain_moe,
        counts,
        normed_moe,
        gz.reshape(experts * padded, D),
        slot_col,
        gates,
        cotangent,
        residual,
        context,
        w_proj,
        *[part for pair in early for part in pair],
        shards=line,
        capacity=capacity,
    )
    for other in others:
        ring = (pass_on(ring).astype(f32) + other.astype(f32)).astype(bf16)
    ring = pass_on(ring)
    extra, grad_context = repair(windows, seg, lse, packed, extra, grad_context)
    summed, small, grad_tokens = shared_gradients(
        seg,
        lse,
        partial,
        gain_attn,
        packed,
        grad_context,
        extra,
        normed_attn,
        grad_proj,
        w_qkv,
        tokens,
        grad_residual,
    )
    grad_gain_attn, grad_gain_moe, grad_router, kept, dropped, grad_qkv, grad_proj, grad_in, grad_out, grad_tokens = finish(
        experts, small, summed, ring, own, grad_tokens
    )
    return (
        mixed,
        grad_tokens,
        grad_gain_attn,
        grad_qkv,
        grad_proj,
        grad_gain_moe,
        grad_router.T,
        grad_in,
        grad_out,
        kept.reshape(experts),
        dropped.reshape(experts),
    )


def solution(mesh):
    both = ("wide", "narrow")
    placed = (
        P(both, None),
        P(both),
        P(both, None),
        P(both, None),
        P(),
        P(),
        P(),
        P(),
        P(),
        P("wide", None, "narrow"),
        P("wide", "narrow", None),
        P(both, None),
    )
    return jax.shard_map(
        per_device,
        mesh=mesh,
        in_specs=placed,
        out_specs=(
            P(both, None),
            P(both, None),
            P(),
            P(),
            P(),
            P(),
            P(),
            P("wide", None, "narrow"),
            P("wide", "narrow", None),
            P(),
            P(),
        ),
        check_vma=False,
    )
```

```python
import functools

import jax
import jax.numpy as jnp
from jax import lax
from jax.experimental import pallas as pl
from jax.experimental.pallas import tpu as pltpu
from jax.sharding import PartitionSpec as P

D = 512
HEADS = 8
HEAD = 64
PAIRS = HEADS // 2
PAIR = 2 * HEAD
TOP = 2
SEQ = 1024
TOK_DEV = 1024
LANES = 128
QB = 128
WINDOW = 432
TILE = 256
SLABS = tuple((max(0, QB * (b - 2)), min(SEQ, QB * (b + 3))) for b in range(SEQ // QB))
MIB = 1024 * 1024
MESH = pl.DeviceIdType.MESH
VMEM_LIMIT = 62 * MIB

f32 = jnp.float32
bf16 = jnp.bfloat16
NT = (((1,), (1,)), ((), ()))
TN = (((0,), (0,)), ((), ()))


def dot(a, b):
    return jnp.dot(a, b, preferred_element_type=f32)


def dot_nt(a, b):
    return lax.dot_general(a, b, NT, preferred_element_type=f32)


def dot_tn(a, b):
    return lax.dot_general(a, b, TN, preferred_element_type=f32)


def iota(shape, dim):
    return lax.broadcasted_iota(jnp.int32, shape, dim)


def norm_parts(values_in):
    centered = values_in - jnp.mean(values_in, axis=-1, keepdims=True)
    variance = jnp.mean(centered * centered, axis=-1, keepdims=True)
    inverse = lax.rsqrt(variance + 1e-06)
    return (centered * inverse, inverse)


def norm_back(grad_normed, gain, normalized, inverse):
    grad_gain = jnp.sum(grad_normed * normalized, axis=0, keepdims=True)
    scaled = grad_normed * gain
    inner = scaled - jnp.mean(scaled, axis=-1, keepdims=True)
    inner = inner - normalized * jnp.mean(scaled * normalized, axis=-1, keepdims=True)
    return (inner * inverse, grad_gain)


def split2(values_in):
    high = values_in.astype(bf16)
    low = (values_in - high.astype(f32)).astype(bf16)
    return high, low


def row_to_col(row):
    n = row.shape[1]
    return jnp.transpose(jnp.broadcast_to(row, (LANES, n)))[:, :1]


def loading(sources, targets, sems):
    copies = [pltpu.make_async_copy(source, target, sems.at[i]) for i, (source, target) in enumerate(zip(sources, targets))]
    for copy in copies:
        copy.start()
    return copies


def like(operands):
    return [pltpu.VMEM(operand.shape, operand.dtype) for operand in operands]


def route_kernel(
    experts,
    capacity,
    picks,
    ranks,
    seg,
    gain_attn,
    cot_in,
    tok_in,
    w_qkv_in,
    slot_col,
    slot_row,
    counts,
    windows,
    gz_out,
    normed_out,
    packed_out,
    extra_out,
    cot,
    tok,
    w_qkv,
    gz_send,
    normed_attn,
    packed,
    nothing,
    load_sem,
    gz_sem,
    sems,
    zero_sem,
):
    loads = loading((cot_in, tok_in, w_qkv_in), (cot, tok, w_qkv), load_sem)
    tokens = ranks.shape[1]
    padded = gz_send.shape[1]
    nothing[...] = jnp.zeros_like(nothing)
    zeros = [
        pltpu.make_async_copy(nothing, extra_out.at[pl.ds(i * QB, QB)], zero_sem.at[i]) for i in range(tokens // QB)
    ]
    for zero in zeros:
        zero.start()
    rank_row = ranks[...].astype(f32)
    rank_col = row_to_col(rank_row)
    lane = iota((tokens, LANES), 1)
    pick0 = row_to_col(picks[0:1, :].astype(f32)).astype(jnp.int32)
    pick1 = row_to_col(picks[1:2, :].astype(f32)).astype(jnp.int32)
    hot = jnp.where(lane == jnp.where(lane < experts, pick0, pick1 + experts), 1.0, 0.0).astype(f32)
    before = (rank_row < rank_col).astype(f32).astype(bf16)
    earlier = dot(before, hot.astype(bf16))
    total = jnp.sum(hot, axis=0, keepdims=True)
    total = jnp.broadcast_to(total, (8, LANES))
    lane8 = iota((8, LANES), 1)
    first = jnp.where(lane8 < experts, total, 0.0)
    earlier = earlier + pltpu.roll(first, experts, axis=1)[:1]
    kept = (hot > 0.5) & (earlier < float(capacity))
    slots = jnp.where(kept, earlier, -1.0)
    slot_col[...] = slots
    slots = jnp.maximum(slots, pltpu.roll(slots, LANES - experts, axis=1))
    slots = jnp.where(lane < experts, slots, -1.0)
    slot_row[...] = jnp.transpose(slots)[:experts]
    kept_lane = jnp.sum(jnp.where(slots >= 0.0, 1.0, 0.0), axis=0, keepdims=True)
    both = total + pltpu.roll(total, LANES - experts, axis=1)
    both = jnp.where(lane8 < experts, both, 0.0)
    sub8 = iota((8, LANES), 0)
    counts[...] = jnp.where(sub8 == 0, kept_lane, jnp.where(sub8 == 1, both, 0.0))

    blocks = tokens // QB
    lane_row = iota((1, LANES), 1)
    plan = jnp.where(lane_row == 3 * blocks, 1.0, 0.0)
    for b, (slab_low, slab_high) in enumerate(SLABS):
        opening = seg[:, b * QB : b * QB + 1]
        closing = seg[:, (b + 1) * QB - 1 : (b + 1) * QB]
        first = jnp.sum(jnp.where(seg[...] < opening, 1.0, 0.0), axis=1, keepdims=True)
        after = jnp.sum(jnp.where(seg[...] <= closing, 1.0, 0.0), axis=1, keepdims=True)
        low = jnp.minimum(jnp.floor(first * (1.0 / 16)) * 16.0, float(SEQ - WINDOW))
        fits = jnp.where(after - low <= float(WINDOW), 1.0, 0.0)
        inside = jnp.where(first >= float(slab_low), 1.0, 0.0) * jnp.where(after <= float(slab_high), 1.0, 0.0)
        plan = jnp.where(lane_row == b, low, plan)
        plan = jnp.where(lane_row == blocks + b, fits, plan)
        plan = jnp.where(lane_row == 2 * blocks + b, inside, plan)
        plan = jnp.where(lane_row == 3 * blocks, plan * inside, plan)
    windows[...] = plan.astype(jnp.int32)
    loads[0].wait()

    @pl.loop(0, experts)
    def _(e):
        chosen = iota((padded, tokens), 0).astype(f32) == slot_row[pl.ds(e, 1), :]
        gz_send[e] = dot(chosen.astype(f32).astype(bf16), cot[...]).astype(bf16)
        pltpu.make_async_copy(gz_send.at[e], gz_out.at[e], gz_sem.at[e]).start()

    def stores(i):
        rows = pl.ds(pl.multiple_of(i * TILE, TILE), TILE)
        return (
            pltpu.make_async_copy(normed_attn.at[rows], normed_out.at[rows], sems.at[0, i]),
            pltpu.make_async_copy(packed.at[rows], packed_out.at[rows], sems.at[1, i]),
        )

    for load in loads[1:]:
        load.wait()

    @pl.loop(0, tokens // TILE)
    def _(i):
        rows = pl.ds(pl.multiple_of(i * TILE, TILE), TILE)
        normal, unused = norm_parts(tok[rows, :].astype(f32))
        normed = (normal * gain_attn[...]).astype(bf16)
        normed_attn[rows, :] = normed
        packed[rows, :] = dot(normed, w_qkv[...]).astype(bf16)
        for store in stores(i):
            store.start()

    @pl.loop(0, experts)
    def _(e):
        pltpu.make_async_copy(gz_send.at[e], gz_out.at[e], gz_sem.at[e]).wait()

    @pl.loop(0, tokens // TILE)
    def _(i):
        for store in stores(i):
            store.wait()

    for zero in zeros:
        zero.wait()


def route(picks, ranks, seg, gain_attn, cot, tok, w_qkv, experts, capacity, padded):
    tokens = tok.shape[0]
    vmem = pl.BlockSpec(memory_space=pltpu.VMEM)
    anywhere = pl.BlockSpec(memory_space=pl.ANY)
    return pl.pallas_call(
        functools.partial(route_kernel, experts, capacity),
        in_specs=[vmem] * 4 + [anywhere] * 3,
        out_shape=(
            jax.ShapeDtypeStruct((tokens, LANES), f32),
            jax.ShapeDtypeStruct((experts, tokens), f32),
            jax.ShapeDtypeStruct((8, LANES), f32),
            jax.ShapeDtypeStruct((1, LANES), jnp.int32),
            jax.ShapeDtypeStruct((experts, padded, D), bf16),
            jax.ShapeDtypeStruct((tokens, D), bf16),
            jax.ShapeDtypeStruct((tokens, 3 * D), bf16),
            jax.ShapeDtypeStruct((tokens, 3 * D), bf16),
        ),
        out_specs=(vmem, vmem, vmem, vmem, anywhere, anywhere, anywhere, anywhere),
        scratch_shapes=like((cot, tok, w_qkv))
        + [
            pltpu.VMEM((experts, padded, D), bf16),
            pltpu.VMEM((tokens, D), bf16),
            pltpu.VMEM((tokens, 3 * D), bf16),
            pltpu.VMEM((QB, 3 * D), bf16),
            pltpu.SemaphoreType.DMA((3,)),
            pltpu.SemaphoreType.DMA((experts,)),
            pltpu.SemaphoreType.DMA((2, tokens // TILE)),
            pltpu.SemaphoreType.DMA((tokens // QB,)),
        ],
        compiler_params=pltpu.CompilerParams(vmem_limit_bytes=VMEM_LIMIT),
        cost_estimate=pl.CostEstimate(
            flops=2 * experts * padded * tokens * D, bytes_accessed=6 * MIB, transcendentals=0
        ),
        name="route",
    )(picks, ranks, seg, gain_attn, cot, tok, w_qkv)


def stack_heads(block):
    lane = iota(block.shape, 1)
    zero = jnp.zeros_like(block)
    return jnp.concatenate(
        [jnp.where(lane < HEAD, block, zero), jnp.where(lane < HEAD, zero, block)], axis=0
    )


def unstack_cols(stacked):
    row = iota((PAIR, QB), 0)
    picked = jnp.where(row < HEAD, stacked[:, :QB], stacked[:, QB:])
    return jnp.transpose(picked)


def window_bias(seg_col, seg_row, low, width, query):
    same = seg_col[pl.ds(low, width), :] == seg_row[:, pl.ds(query, QB)]
    half = jnp.where(same, 0.0, -1e30).astype(f32)
    return jnp.concatenate([half, half], axis=1)


def by_window(windows, block, body):
    low = windows[0, block]
    fits = windows[0, block + SEQ // QB]

    @pl.when(fits == 1)
    def _():
        body(pl.multiple_of(low, 16), WINDOW)

    @pl.when(fits != 1)
    def _():
        body(0, SEQ)


def forward_kernel(
    experts,
    windows,
    seg,
    gain_moe,
    w_router,
    packed_in,
    tok_in,
    w_proj_in,
    context_out,
    lse,
    residual_out,
    normed_moe_out,
    gates_out,
    gate_row,
    packed,
    tok,
    w_proj,
    context,
    residual,
    normed_moe,
    gates,
    seg_col,
    seg_row,
    router,
    load_sem,
    sems,
):
    loads = loading((packed_in, tok_in, w_proj_in), (packed, tok, w_proj), load_sem)
    writes = [
        pltpu.make_async_copy(source, target, sems.at[i])
        for i, (source, target) in enumerate(
            (
                (context, context_out),
                (residual, residual_out),
                (normed_moe, normed_moe_out),
                (gates, gates_out),
            )
        )
    ]
    tokens = tok.shape[0]
    seg_row[...] = seg[...].astype(f32)
    seg_col[...] = jnp.transpose(jnp.broadcast_to(seg_row[...], (LANES, tokens)))
    router[...] = jnp.zeros_like(router)
    router[:experts, :] = w_router[...]
    loads[0].wait()

    @pl.loop(0, tokens // QB)
    def _(block):
        query = pl.multiple_of(block * QB, QB)

        def body(low, width):
            bias = window_bias(seg_col, seg_row, low, width, query)
            spans = [slice(pair * PAIR, (pair + 1) * PAIR) for pair in range(PAIRS)]
            scores = []
            for span in spans:
                q = stack_heads(packed[pl.ds(query, QB), span]) * HEAD ** (-0.5)
                k = packed[pl.ds(low, width), D + span.start : D + span.stop]
                scores.append(dot_nt(k, q.astype(bf16)) + bias)
            peaks = [jnp.max(score, axis=0, keepdims=True) for score in scores]
            exponents = [jnp.exp(score - peak) for score, peak in zip(scores, peaks)]
            totals = [jnp.sum(exponent, axis=0, keepdims=True) for exponent in exponents]
            probs = [(exponent * (1.0 / total)).astype(bf16) for exponent, total in zip(exponents, totals)]
            for pair, span in enumerate(spans):
                lse[pl.ds(block, 1), pair, :] = peaks[pair] + jnp.log(totals[pair])
                v = packed[pl.ds(low, width), 2 * D + span.start : 2 * D + span.stop]
                mixed = dot_tn(v, probs[pair])
                context[pl.ds(query, QB), span] = unstack_cols(mixed).astype(bf16)

        by_window(windows, block, body)

    writes[0].start()
    for load in loads[1:]:
        load.wait()

    @pl.loop(0, tokens // TILE)
    def _(i):
        rows = pl.ds(pl.multiple_of(i * TILE, TILE), TILE)
        rest = tok[rows, :].astype(f32) + dot(context[rows, :], w_proj[...])
        residual[rows, :] = rest
        normal, unused = norm_parts(rest)
        normed = (normal * gain_moe[...]).astype(bf16)
        normed_moe[rows, :] = normed
        logits = dot_nt(normed, router[...])
        logits = jnp.where(iota(logits.shape, 1) < experts, logits, -1e30)
        exponent = jnp.exp(logits - jnp.max(logits, axis=1, keepdims=True))
        gates[rows, :] = exponent / jnp.sum(exponent, axis=1, keepdims=True)

    for write in writes[1:]:
        write.start()
    gate_row[...] = jnp.transpose(gates[...])[:experts]
    for write in writes:
        write.wait()


def forward(windows, seg, gain_moe, w_router, packed, tok, w_proj):
    tokens = tok.shape[0]
    experts = w_router.shape[0]
    vmem = pl.BlockSpec(memory_space=pltpu.VMEM)
    anywhere = pl.BlockSpec(memory_space=pl.ANY)
    return pl.pallas_call(
        functools.partial(forward_kernel, experts),
        in_specs=[pl.BlockSpec(memory_space=pltpu.SMEM)] + [vmem] * 3 + [anywhere] * 3,
        out_specs=[anywhere, vmem] + [anywhere] * 3 + [vmem],
        out_shape=(
            jax.ShapeDtypeStruct((tokens, D), bf16),
            jax.ShapeDtypeStruct((tokens // QB, PAIRS, 2 * QB), f32),
            jax.ShapeDtypeStruct((tokens, D), f32),
            jax.ShapeDtypeStruct((tokens, D), bf16),
            jax.ShapeDtypeStruct((tokens, LANES), f32),
            jax.ShapeDtypeStruct((experts, tokens), f32),
        ),
        scratch_shapes=like((packed, tok, w_proj))
        + [
            pltpu.VMEM((tokens, D), bf16),
            pltpu.VMEM((tokens, D), f32),
            pltpu.VMEM((tokens, D), bf16),
            pltpu.VMEM((tokens, LANES), f32),
            pltpu.VMEM((tokens, LANES), f32),
            pltpu.VMEM((1, tokens), f32),
            pltpu.VMEM((LANES, D), bf16),
            pltpu.SemaphoreType.DMA((3,)),
            pltpu.SemaphoreType.DMA((4,)),
        ],
        compiler_params=pltpu.CompilerParams(vmem_limit_bytes=48 * MIB),
        cost_estimate=pl.CostEstimate(
            flops=64 * 1024 * MIB, bytes_accessed=16 * MIB, transcendentals=4 * MIB
        ),
        name="attention_forward",
    )(windows, seg, gain_moe, w_router, packed, tok, w_proj)


def gelu_parts(x):
    density = jnp.exp(-0.5 * (x * x))
    return 0.5 + 0.5 * lax.erf(x * 2.0**-0.5), x * density * 0.3989422804014327


def shifted(index, by, size):
    return lax.rem(index + by, size)


def paired(index, by, size):
    total = 0
    bit = 1
    while bit < size:
        total = total + bit * lax.rem(index // bit + by // bit, 2)
        bit *= 2
    return total


def exchange(src, dst, send, recv, device):
    return pltpu.make_async_remote_copy(
        src_ref=src, dst_ref=dst, send_sem=send, recv_sem=recv, device_id=device, device_id_type=MESH
    )


def greet(barrier, sources):
    me = lax.axis_index("wide")
    line = lax.axis_index("narrow")

    @pl.loop(1, sources)
    def _(j):
        pl.semaphore_signal(barrier, inc=1, device_id=(paired(me, j, sources), line), device_id_type=MESH)


EARLY = 3


def moe_kernel(
    capacity,
    sources,
    shards,
    slot_row,
    gate_row,
    w_router,
    gain_moe,
    counts,
    normed_in,
    gz_in,
    slot_in,
    gates_in,
    cot_in,
    residual_in,
    context_in,
    w_proj_in,
    w_in0,
    w_out0,
    w_in1,
    w_out1,
    w_in2,
    w_out2,
    ring,
    own_grads,
    small,
    mixed_out,
    grad_residual_out,
    grad_context_out,
    grad_proj_out,
    *refs,
):
    others, refs = refs[: shards - 4], refs[shards - 4 :]
    normed_moe, slot_col, gates, w_proj, w_ins, w_outs, rows_send, rows, scaled, gate_slot, rows_t, gz_t = refs[:12]
    act, gpre, out_sum, back_sum, back_low, returned, back, ring_out, ring_in = refs[12:21]
    router, grad_gates, grad_logits = refs[21:24]
    load_sem, row_sem, out_sem, back_sem, weight_sem, ring_sem, late_sem, store_sem = refs[24:]
    out_low = rows_send
    depth = act.shape[0]
    padded = rows_send.shape[1]
    tokens = normed_in.shape[0]
    me = lax.axis_index("wide")
    line = lax.axis_index("narrow")
    right = (me, shifted(line, 1, shards))
    left = (me, shifted(line, shards - 1, shards))
    loads = [
        pltpu.make_async_copy(normed_in, normed_moe, load_sem.at[0]),
        pltpu.make_async_copy(gz_in, scaled, load_sem.at[1]),
    ]
    for c, pair in reversed(list(enumerate(((w_in0, w_out0), (w_in1, w_out1), (w_in2, w_out2))))):
        for i, (source, target) in enumerate(zip(pair, (w_ins, w_outs))):
            loads.append(pltpu.make_async_copy(source, target.at[c], load_sem.at[2 + 2 * c + i]))
    for i, (source, target) in enumerate(((slot_in, slot_col), (gates_in, gates), (w_proj_in, w_proj))):
        loads.append(pltpu.make_async_copy(source, target, load_sem.at[2 + 2 * EARLY + i]))
    for load in loads:
        load.start()
    barrier = pltpu.get_barrier_semaphore()
    greet(barrier, sources)
    for near in (left, right):
        pl.semaphore_signal(barrier, inc=1, device_id=near, device_id_type=MESH)
    gate_slot[...] = jnp.zeros_like(gate_slot)

    def block(s):
        return pl.ds(pl.multiple_of(s * padded, 16), padded)

    def weights_on(c):
        return [
            exchange(part.at[c - 1], part.at[c], weight_sem.at[0, i, c], weight_sem.at[1, i, c], right)
            for i, part in enumerate((w_ins, w_outs))
        ]

    def row_copy(j):
        to = paired(me, j, sources)
        return exchange(rows_send.at[to], rows.at[block(me)], row_sem.at[0, j], row_sem.at[1, j], (to, line))

    def result_copies(j):
        to = paired(me, j, sources)
        return [
            exchange(low.at[to], target.at[me], sem.at[0, j], sem.at[1, j], (to, line))
            for low, target, sem in ((out_low, returned, out_sem), (back_low, back, back_sem))
        ]

    for load in loads[:1] + loads[2:4]:
        load.wait()

    def partner(i):
        turn = lax.rem(i + 1, 3)
        return i + lax.rem(i // 3, 2) * (turn - 3 * (turn // 2))

    @pl.loop(0, sources)
    def _(i):
        j = partner(lax.rem(i + 2, sources))
        e = paired(me, j, sources)
        chosen = iota((padded, tokens), 0).astype(f32) == slot_row[pl.ds(e, 1), :]
        chosen = chosen.astype(f32).astype(bf16)
        rows_send[e] = dot(chosen, normed_moe[...]).astype(bf16)
        gate = gate_row[pl.ds(e, 1), :]
        high, middle = split2(gate)
        low = (gate - high.astype(f32) - middle.astype(f32)).astype(bf16)
        three = jnp.concatenate(
            [high.astype(f32), middle.astype(f32), low.astype(f32), jnp.zeros((5, tokens), f32)], axis=0
        )
        gate_slot[:, :padded] = dot_nt(three.astype(bf16), chosen)
        tail = rows_send[e, padded - 16 :, :].astype(f32)
        sub = iota(tail.shape, 0)
        for part in range(3):
            tail = jnp.where(sub == 13 + part, gate_slot[part : part + 1, :], tail)
        rows_send[e, padded - 16 :, :] = tail.astype(bf16)

        @pl.when(i == 0)
        def _():
            pl.semaphore_wait(barrier, sources + 1)
            for copy in weights_on(EARLY):
                copy.start()

        @pl.when(j != 0)
        def _():
            row_copy(j).start()

    rows[block(me), :] = rows_send[me]
    for load in loads[1:2] + loads[4:]:
        load.wait()

    def prepare(j):
        s = paired(me, j, sources)

        @pl.when(j != 0)
        def _():
            row_copy(j).wait_recv()

        end = pl.ds(pl.multiple_of(s * padded + padded - 16, 16), 16)
        tail = rows[end, :].astype(f32)
        gate = tail[13:14] + tail[14:15] + tail[15:16]
        gate = jnp.transpose(jnp.broadcast_to(gate, (LANES, D)))[:padded, :1]
        live = iota((padded, 1), 0) < capacity
        scaled[block(s), :] = (jnp.where(live, gate, 0.0) * scaled[block(s), :].astype(f32)).astype(bf16)
        live16 = iota((16, 1), 0) < 16 - (padded - capacity)
        rows[end, :] = jnp.where(live16, tail, 0.0).astype(bf16)

    def shard_results(s, c):
        pre = dot(rows[block(s), :], w_ins[c])
        phi, slope = gelu_parts(pre)
        act_low = (pre * phi).astype(bf16)
        act[c % depth, block(s), :] = act_low
        grad_pre = (dot_nt(scaled[block(s), :], w_outs[c]) * (phi + slope)).astype(bf16)
        gpre[c % depth, block(s), :] = grad_pre
        return dot(act_low, w_outs[c]), dot_nt(grad_pre, w_ins[c])

    def send(j, result, grad_rows):
        s = paired(me, j, sources)

        @pl.when(j != 0)
        def _():
            row_copy(j).wait_send()

        out_low[s] = result.astype(bf16)
        back_low[s] = grad_rows.astype(bf16)

        @pl.when(j != 0)
        def _():
            for copy in result_copies(j):
                copy.start()

    def run(s, order, fresh, final):
        for k, c in enumerate(order):
            result, grad_rows = shard_results(s, c)
            if k > 0 or not fresh:
                result = result + out_sum[block(s), :]
                grad_rows = grad_rows + back_sum[block(s), :]
            if k < len(order) - 1 or not final:
                out_sum[block(s), :] = result
                back_sum[block(s), :] = grad_rows
        return result, grad_rows

    def weight_grads(c):
        return dot(rows_t[...], gpre[c % depth]).astype(bf16), dot(gz_t[...], act[c % depth]).astype(bf16)

    first_step = exchange(ring_out, ring_in.at[0], ring_sem.at[0, 0], ring_sem.at[1, 0], right)
    second_step = exchange(ring_in.at[0], ring_in.at[1], ring_sem.at[0, 1], ring_sem.at[1, 1], right)
    late = tuple(range(EARLY, shards))

    def pass_over(first, last, order, opening, closing):
        @pl.loop(first, last)
        def _(i):
            j = partner(i)
            if opening:
                prepare(j)
            results = run(paired(me, j, sources), order, opening, closing)
            if closing:
                send(j, *results)

    def late_weights():
        for c in late:
            for copy in weights_on(c):
                copy.wait()
            if c + 1 < shards:
                for copy in weights_on(c + 1):
                    copy.start()

    def turn_rows():
        for s in range(sources):
            rows_t[:, s * padded : (s + 1) * padded] = jnp.transpose(rows[s * padded : (s + 1) * padded, :])
            gz_t[:, s * padded : (s + 1) * padded] = jnp.transpose(scaled[s * padded : (s + 1) * padded, :])

    def start_ring():
        ring_out[:D, :], ring_out[D:, :] = weight_grads(1)
        first_step.start()

    def keep_grads(c):
        target = own_grads if c == 0 else ring if c == 3 else others[c - 4]
        target[:D, :], target[D:, :] = weight_grads(c)

    if depth == shards:
        pass_over(0, 4, (1, 0, 2), True, False)
        pass_over(4, 5, (1, 0), True, False)
        late_weights()
        pass_over(2, 4, late, False, True)
        pass_over(5, sources, (1,), True, False)
        turn_rows()
        start_ring()
        pass_over(4, 5, (2,) + late, False, True)
        pass_over(5, sources, (0, 2) + late, False, True)
        pass_over(0, 2, late, False, True)
    else:
        late_weights()
        pass_over(0, sources, (1,), True, False)
        turn_rows()
        start_ring()
        for c in (0,) + late:
            pass_over(0, sources, (c,), False, False)
            keep_grads(c)
        pass_over(0, sources, (2,), False, True)

    upper = slice(tokens, 2 * tokens)
    late_loads = loading(
        (cot_in, residual_in, context_in),
        (rows.at[pl.ds(0, tokens)], out_sum.at[pl.ds(tokens, tokens)], rows.at[pl.ds(tokens, tokens)]),
        late_sem,
    )
    returned[me] = out_low[me]
    back[me] = back_low[me]
    second = weight_grads(2)
    if depth == shards:
        keep_grads(3)
    first_step.wait()
    for half in range(2):
        span = slice(half * D, half * D + D)
        ring_in[0, span, :] = (ring_in[0, span, :].astype(f32) + second[half].astype(f32)).astype(bf16)
    second_step.start()
    if depth == shards:
        keep_grads(0)

    lane = iota((TILE, LANES), 1)
    router[...] = jnp.zeros_like(router)
    router[:sources, :] = w_router[...]
    small[...] = jnp.zeros_like(small)
    small[2:4, :LANES] = counts[:2, :]
    grad_gates[...] = jnp.zeros_like(grad_gates)
    out_sum[:tokens, :] = jnp.zeros((tokens, D), f32)
    back_sum[:tokens, :] = jnp.zeros((tokens, D), f32)
    for load in late_loads:
        load.wait()

    def collect(e):
        for i in range(tokens // TILE):
            at = slice(i * TILE, (i + 1) * TILE)
            slots = slot_col[at, :]
            slot = jnp.max(
                jnp.where((lane == e) | (lane == e + sources), slots, -1.0), axis=1, keepdims=True
            )
            gate = jnp.sum(jnp.where(lane == e, gates[at, :], 0.0), axis=1, keepdims=True)
            chosen = (iota((TILE, padded), 1).astype(f32) == slot).astype(f32).astype(bf16)
            result = dot(chosen, returned[e])
            out_sum[at, :] += gate * result
            inner = jnp.sum(result * rows[at, :].astype(f32), axis=1, keepdims=True)
            grad_gates[at, :] += jnp.where(lane == e, inner, 0.0)
            back_sum[at, :] += dot(chosen, back[e])

    collect(me)

    @pl.loop(1, sources)
    def _(i):
        j = partner(i)
        for copy in result_copies(j):
            copy.wait_recv()
        collect(paired(me, j, sources))

    stores = []
    for i in range(tokens // TILE):
        at = slice(i * TILE, (i + 1) * TILE)
        above = slice(tokens + i * TILE, tokens + (i + 1) * TILE)
        grad_z = rows[at, :].astype(f32)
        probs = gates[at, :]
        rest = out_sum[above, :]
        scaled[at, :] = (rest + out_sum[at, :]).astype(bf16)
        gate_inner = jnp.sum(probs * grad_gates[at, :], axis=1, keepdims=True)
        high, low = split2(probs * (grad_gates[at, :] - gate_inner))
        grad_logits[at, :LANES] = high
        grad_logits[at, LANES:] = low
        grad_normed = back_sum[at, :] + dot(high, router[...]) + dot(low, router[...])
        normal, inverse = norm_parts(rest)
        grad_norm, grad_gain = norm_back(grad_normed, gain_moe[...], normal, inverse)
        small[1:2, :] += grad_gain
        grad_rest = grad_z + grad_norm
        back_sum[above, :] = grad_rest
        attn = grad_rest.astype(bf16)
        scaled[above, :] = attn
        rows[at, :] = dot_nt(attn, w_proj[...]).astype(bf16)
        here = pl.ds(i * TILE, TILE)
        for k, (source, target) in enumerate(
            (
                (scaled.at[here], mixed_out),
                (back_sum.at[pl.ds(tokens + i * TILE, TILE)], grad_residual_out),
                (rows.at[here], grad_context_out),
            )
        ):
            stores.append(pltpu.make_async_copy(source, target.at[here], store_sem.at[k, i]))
            stores[-1].start()
    out_sum[:D, :] = dot_tn(rows[upper, :], scaled[upper, :])
    stores.append(pltpu.make_async_copy(out_sum.at[pl.ds(0, D)], grad_proj_out, store_sem.at[3, 0]))
    stores[-1].start()
    both = dot_tn(normed_moe[...], grad_logits[...])
    both = jnp.transpose(both[:, :LANES] + both[:, LANES:])
    small[8:, :] = both[:sources]
    second_step.wait()
    ring[...] = (ring_in[1].astype(f32) + ring[...].astype(f32)).astype(bf16)
    for store in stores:
        store.wait()

    @pl.loop(1, sources)
    def _(j):
        for copy in result_copies(j):
            copy.wait_send()


def moe(slot_row, gate_row, w_router, gain_moe, counts, *large, shards, capacity):
    normed_moe, gz = large[:2]
    sources = slot_row.shape[0]
    tokens = normed_moe.shape[0]
    hidden = large[-2].shape[1]
    total = gz.shape[0]
    blocks = (sources, total // sources, D)
    depth = shards if shards == 4 else 1
    vmem = pl.BlockSpec(memory_space=pltpu.VMEM)
    anywhere = pl.BlockSpec(memory_space=pl.ANY)
    dma = pltpu.SemaphoreType.DMA
    piece = jax.ShapeDtypeStruct((2 * D, hidden), bf16)
    return pl.pallas_call(
        functools.partial(moe_kernel, capacity, sources, shards),
        in_specs=[vmem] * 5 + [anywhere] * len(large),
        out_specs=[vmem] * 3 + [anywhere] * 4 + [vmem] * (shards - 4),
        out_shape=[
            piece,
            piece,
            jax.ShapeDtypeStruct((8 + sources, D), f32),
            jax.ShapeDtypeStruct((tokens, D), bf16),
            jax.ShapeDtypeStruct((tokens, D), f32),
            jax.ShapeDtypeStruct((tokens, D), bf16),
            jax.ShapeDtypeStruct((D, D), f32),
        ]
        + [piece] * (shards - 4),
        scratch_shapes=[
            pltpu.VMEM((tokens, D), bf16),
            pltpu.VMEM((tokens, LANES), f32),
            pltpu.VMEM((tokens, LANES), f32),
            pltpu.VMEM((D, D), bf16),
            pltpu.VMEM((shards, D, hidden), bf16),
            pltpu.VMEM((shards, hidden, D), bf16),
            pltpu.VMEM(blocks, bf16),
            pltpu.VMEM((total, D), bf16),
            pltpu.VMEM((total, D), bf16),
            pltpu.VMEM((8, D), f32),
            pltpu.VMEM((D, total), bf16),
            pltpu.VMEM((D, total), bf16),
            pltpu.VMEM((depth, total, hidden), bf16),
            pltpu.VMEM((depth, total, hidden), bf16),
            pltpu.VMEM((total, D), f32),
            pltpu.VMEM((total, D), f32),
            pltpu.VMEM(blocks, bf16),
            pltpu.VMEM(blocks, bf16),
            pltpu.VMEM(blocks, bf16),
            pltpu.VMEM((2 * D, hidden), bf16),
            pltpu.VMEM((2, 2 * D, hidden), bf16),
            pltpu.VMEM((LANES, D), bf16),
            pltpu.VMEM((tokens, LANES), f32),
            pltpu.VMEM((tokens, 2 * LANES), bf16),
            dma((5 + 2 * EARLY,)),
            dma((2, sources)),
            dma((2, sources)),
            dma((2, sources)),
            dma((2, 2, shards)),
            dma((2, 2)),
            dma((3,)),
            dma((4, tokens // TILE)),
        ],
        compiler_params=pltpu.CompilerParams(
            vmem_limit_bytes=VMEM_LIMIT, collective_id=1, has_side_effects=True
        ),
        cost_estimate=pl.CostEstimate(
            flops=12 * total * D * hidden * shards, bytes_accessed=20 * MIB, transcendentals=0
        ),
        name="moe",
    )(slot_row, gate_row, w_router, gain_moe, counts, *large)


def repair_kernel(
    windows,
    seg,
    lse,
    packed_in,
    extra_in,
    grad_context_in,
    extra_out,
    grad_context_out,
    packed,
    extra,
    grad_context,
    seg_col,
    seg_row,
    grad_k,
    grad_v,
    sems,
):
    tokens = packed.shape[0]
    blocks = tokens // QB

    @pl.when(windows[0, 3 * blocks] != 1)
    def _():
        loads = loading((packed_in, extra_in, grad_context_in), (packed, extra, grad_context), sems)
        seg_row[...] = seg[...].astype(f32)
        seg_col[...] = jnp.transpose(jnp.broadcast_to(seg_row[...], (LANES, tokens)))
        for load in loads:
            load.wait()
        grad_k[...] = jnp.zeros_like(grad_k)
        grad_v[...] = jnp.zeros_like(grad_v)

        @pl.loop(0, blocks)
        def _(block):
            query = pl.multiple_of(block * QB, QB)

            @pl.when(windows[0, 2 * blocks + block] != 1)
            def _():
                bias = window_bias(seg_col, seg_row, 0, SEQ, query)
                spans = [slice(pair * PAIR, (pair + 1) * PAIR) for pair in range(PAIRS)]
                keys = pl.ds(0, SEQ)
                queries = [
                    (stack_heads(packed[pl.ds(query, QB), span]) * HEAD ** (-0.5)).astype(bf16) for span in spans
                ]
                grads = [stack_heads(grad_context[pl.ds(query, QB), span]) for span in spans]
                probs = []
                grad_probs = []
                for pair, span in enumerate(spans):
                    k = packed[keys, D + span.start : D + span.stop]
                    v = packed[keys, 2 * D + span.start : 2 * D + span.stop]
                    probs.append(jnp.exp(dot_nt(k, queries[pair]) + bias - lse[pl.ds(block, 1), pair, :]))
                    grad_probs.append(dot_nt(v, grads[pair]))
                grad_scores = []
                for pair, span in enumerate(spans):
                    grad_v[keys, span] += dot(probs[pair].astype(bf16), grads[pair])
                    weighted = probs[pair] * grad_probs[pair]
                    inner = jnp.sum(weighted, axis=0, keepdims=True)
                    grad_scores.append((weighted - probs[pair] * inner).astype(bf16))
                for pair, span in enumerate(spans):
                    k = packed[keys, D + span.start : D + span.stop]
                    grad_k[keys, span] += dot(grad_scores[pair], queries[pair])
                    grad_q = unstack_cols(dot_tn(k, grad_scores[pair])) * HEAD ** (-0.5)
                    extra[pl.ds(query, QB), span] = grad_q.astype(bf16)
                grad_context[pl.ds(query, QB), :] = jnp.zeros((QB, D), bf16)

        extra[:, D : 2 * D] = grad_k[...].astype(bf16)
        extra[:, 2 * D :] = grad_v[...].astype(bf16)
        for store in loading((extra, grad_context), (extra_out, grad_context_out), sems):
            store.wait()


def repair(windows, seg, lse, packed, extra, grad_context):
    tokens = packed.shape[0]
    vmem = pl.BlockSpec(memory_space=pltpu.VMEM)
    anywhere = pl.BlockSpec(memory_space=pl.ANY)
    return pl.pallas_call(
        repair_kernel,
        in_specs=[pl.BlockSpec(memory_space=pltpu.SMEM)] + [vmem] * 2 + [anywhere] * 3,
        out_specs=(anywhere, anywhere),
        out_shape=(
            jax.ShapeDtypeStruct(extra.shape, bf16),
            jax.ShapeDtypeStruct(grad_context.shape, bf16),
        ),
        input_output_aliases={4: 0, 5: 1},
        scratch_shapes=like((packed, extra, grad_context))
        + [
            pltpu.VMEM((tokens, LANES), f32),
            pltpu.VMEM((1, tokens), f32),
            pltpu.VMEM((tokens, D), f32),
            pltpu.VMEM((tokens, D), f32),
            pltpu.SemaphoreType.DMA((3,)),
        ],
        compiler_params=pltpu.CompilerParams(vmem_limit_bytes=VMEM_LIMIT),
        cost_estimate=pl.CostEstimate(flops=MIB, bytes_accessed=MIB, transcendentals=0),
        name="repair",
    )(windows, seg, lse, packed, extra, grad_context)


SLAB_AT = tuple(sum(high - low for low, high in SLABS[:b]) for b in range(len(SLABS) + 1))


def slab_bias(bias, seg_col, seg_row):
    for b, (low, high) in enumerate(SLABS):
        same = seg_col[low:high, :] == seg_row[:, b * QB : (b + 1) * QB]
        bias[SLAB_AT[b] : SLAB_AT[b + 1], :] = jnp.where(same, 0.0, -1e30)


def pair_backward(pair, packed, grad_context, lse, extra, bias, grad_k, grad_v, out):
    def span(which):
        return pl.ds(pl.multiple_of(which * D + pair * PAIR, PAIR), PAIR)

    grad_k[...] = extra[:, span(1)].astype(f32)
    grad_v[...] = extra[:, span(2)].astype(f32)
    for group in range(0, len(SLABS), 4):
        blocks = range(group, group + 4)
        queries, grads, probs, grad_probs, grad_scores = [], [], [], [], []
        for b in blocks:
            low, high = SLABS[b]
            rows = slice(b * QB, (b + 1) * QB)
            queries.append((stack_heads(packed[rows, span(0)]) * HEAD ** (-0.5)).astype(bf16))
            grads.append(stack_heads(grad_context[rows, span(0)]))
            masked = bias[SLAB_AT[b] : SLAB_AT[b + 1], :]
            scores = dot_nt(packed[low:high, span(1)], queries[-1]) + jnp.concatenate([masked, masked], axis=1)
            probs.append(jnp.exp(scores - lse[b, pl.ds(pair, 1), :]))
            grad_probs.append(dot_nt(packed[low:high, span(2)], grads[-1]))
        for i, b in enumerate(blocks):
            low, high = SLABS[b]
            grad_v[low:high, :] += dot(probs[i].astype(bf16), grads[i])
            weighted = probs[i] * grad_probs[i]
            inner = jnp.sum(weighted, axis=0, keepdims=True)
            grad_scores.append((weighted - probs[i] * inner).astype(bf16))
        for i, b in enumerate(blocks):
            low, high = SLABS[b]
            rows = slice(b * QB, (b + 1) * QB)
            grad_k[low:high, :] += dot(grad_scores[i], queries[i])
            grad_q = unstack_cols(dot_tn(packed[low:high, span(1)], grad_scores[i])) * HEAD ** (-0.5)
            out[rows, :PAIR] = (grad_q + extra[rows, span(0)].astype(f32)).astype(bf16)
    out[:, PAIR : 2 * PAIR] = grad_k[...].astype(bf16)
    out[:, 2 * PAIR :] = grad_v[...].astype(bf16)


def shared_kernel(
    chips,
    planes,
    seg,
    lse,
    partial,
    gain_attn,
    packed_in,
    grad_context_in,
    extra_in,
    normed_attn_in,
    grad_proj_in,
    w_qkv_in,
    tok_in,
    grad_residual_in,
    summed,
    small,
    grad_tokens_out,
    packed,
    grad_context,
    extra,
    normed_attn,
    grad_proj,
    w_qkv,
    tok,
    grad_residual,
    pair_grads,
    grad_tokens,
    normed_t,
    seg_col,
    bias,
    grad_k,
    grad_v,
    grad_packed,
    half,
    core_out,
    core_in,
    chip_out,
    chip_in,
    plane_out,
    plane_in,
    small_own,
    small_core,
    small_chip,
    small_plane,
    pair_sem,
    load_sem,
    store_sem,
    core_sem,
    chip_sem,
    plane_sem,
    plane_sem2,
    chip_sem2,
    core_sem2,
    small_sem,
    small_chip_sem,
    small_plane_sem,
):
    tokens = tok.shape[0]
    stages = 16 // planes
    pairs = PAIRS // stages
    tiles = tokens // TILE
    wide = lax.axis_index("wide")
    plane = lax.axis_index("narrow")
    core = lax.rem(wide, 2)
    chip = wide // 2
    share = D // (2 * chips)
    partner = (chip * 2 + 1 - core, plane)
    mine = pl.ds(pl.multiple_of(core * (D // 2), D // 2), D // 2)
    other = pl.ds(pl.multiple_of((1 - core) * (D // 2), D // 2), D // 2)
    chunk = pl.ds(pl.multiple_of(core * (D // 2) + chip * share, share), share)
    own_chunk = pl.ds(pl.multiple_of(chip * share, share), share)

    loads = [
        pltpu.make_async_copy(source, target, load_sem.at[i])
        for i, (source, target) in enumerate(
            (
                (normed_attn_in, normed_attn),
                (grad_proj_in, grad_proj),
                (w_qkv_in, w_qkv),
                (tok_in, tok),
                (grad_residual_in, grad_residual),
            )
        )
    ]

    def pair_loads(pair):
        copies = []
        for source, target, parts in ((packed_in, packed, 3), (grad_context_in, grad_context, 1), (extra_in, extra, 3)):
            for which in range(parts):
                lanes = pl.ds(pl.multiple_of(which * D + pair * PAIR, PAIR), PAIR)
                copies.append(
                    pltpu.make_async_copy(source.at[:, lanes], target.at[:, lanes], pair_sem.at[pair, len(copies)])
                )
        return copies

    for pair in range(PAIRS):
        for load in pair_loads(pair):
            load.start()
    for load in loads:
        load.start()

    def chip_at(j):
        to = shifted(chip, j, chips)
        return to, (to * 2 + core, plane)

    def plane_at(j):
        to = shifted(plane, j, planes)
        return to, (wide, to)

    barrier = pltpu.get_barrier_semaphore()
    pl.semaphore_signal(barrier, inc=1, device_id=partner, device_id_type=MESH)

    @pl.loop(1, chips)
    def _(j):
        pl.semaphore_signal(barrier, inc=1, device_id=chip_at(j)[1], device_id_type=MESH)

    @pl.loop(1, planes)
    def _(j):
        pl.semaphore_signal(barrier, inc=1, device_id=plane_at(j)[1], device_id_type=MESH)

    def blocks(stage):
        return pl.ds(stage * planes, planes)

    def core_copy(stage):
        at = blocks(stage)
        return exchange(core_out.at[at], core_in.at[at], core_sem.at[0, stage], core_sem.at[1, stage], partner)

    def chip_copy(stage, j):
        to, device = chip_at(j)
        rows = pl.ds(pl.multiple_of(to * share, share), share)
        at = blocks(stage)
        return exchange(
            chip_out.at[at, rows], chip_in.at[j, at], chip_sem.at[0, stage, j], chip_sem.at[1, stage, j], device
        )

    def plane_copy(stage, j):
        to, device = plane_at(j)
        return exchange(
            plane_out.at[stage * planes + to],
            plane_in.at[j, stage],
            plane_sem.at[0, stage, j],
            plane_sem.at[1, stage, j],
            device,
        )

    def plane_back(stage, j):
        spot = summed.at[stage * planes + plane, chunk]
        return exchange(spot, spot, plane_sem2.at[0, stage, j], plane_sem2.at[1, stage, j], plane_at(j)[1])

    def chip_back(stage, j):
        spot = summed.at[blocks(stage), chunk]
        return exchange(spot, spot, chip_sem2.at[0, stage, j], chip_sem2.at[1, stage, j], chip_at(j)[1])

    def core_back(stage):
        spot = summed.at[blocks(stage), mine]
        return exchange(spot, spot, core_sem2.at[0, stage], core_sem2.at[1, stage], partner)

    def small_core_copy():
        return exchange(small_own, small_core, small_sem.at[0], small_sem.at[1], partner)

    def small_chip_copy(j):
        spot = small_chip.at[chip]
        return exchange(spot, spot, small_chip_sem.at[0, j], small_chip_sem.at[1, j], chip_at(j)[1])

    def small_plane_copy(j):
        spot = small_plane.at[plane]
        return exchange(spot, spot, small_plane_sem.at[0, j], small_plane_sem.at[1, j], plane_at(j)[1])

    def pair_products(pair):
        spare = dot(normed_t[other, :], pair_grads[...])
        own = dot(normed_t[mine, :], pair_grads[...])
        lanes = pl.ds(pl.multiple_of(pair * PAIR, PAIR), PAIR)
        for which in range(3):
            at = slice(which * PAIR, (which + 1) * PAIR)
            core_out[pair * 4 + which] = spare[:, at].astype(bf16)
            half[pair * 4 + which] = own[:, at]
            grad_packed[:, pl.ds(pl.multiple_of(which * D + pair * PAIR, PAIR), PAIR)] = pair_grads[:, at]
        core_out[pair * 4 + 3] = grad_proj[other, lanes].astype(bf16)
        half[pair * 4 + 3] = grad_proj[mine, lanes]

    def chip_stage(stage):
        core_copy(stage).wait_recv()
        at = blocks(stage)
        total = half[at] + core_in[at].astype(f32)
        half[at] = total
        chip_out[at] = total.astype(bf16)

        @pl.loop(1, chips)
        def _(j):
            chip_copy(stage, j).start()

    def plane_stage(stage):
        at = blocks(stage)
        total = half[at, own_chunk, :]
        for j in range(1, chips):
            chip_copy(stage, j).wait_recv()
            total = total + chip_in[j, at].astype(f32)
        half[at, own_chunk, :] = total
        plane_out[at] = total.astype(bf16)

        @pl.loop(1, planes)
        def _(j):
            plane_copy(stage, j).start()

    def own_stage(stage):
        total = half[stage * planes + plane, own_chunk, :]
        for j in range(1, planes):
            plane_copy(stage, j).wait_recv()
            total = total + plane_in[j, stage].astype(f32)
        summed[stage * planes + plane, chunk, :] = total.astype(bf16)

        @pl.loop(1, planes)
        def _(j):
            plane_back(stage, j).start()

    def gather_stage(stage):
        @pl.loop(1, planes)
        def _(j):
            plane_back(stage, j).wait_recv()

        @pl.loop(1, chips)
        def _(j):
            chip_back(stage, j).start()

    def last_stage(stage):
        @pl.loop(1, chips)
        def _(j):
            chip_back(stage, j).wait_recv()

        core_back(stage).start()

    def norm_tile(i):
        rows = slice(i * TILE, (i + 1) * TILE)
        grad_normed = dot_nt(grad_packed[rows, :], w_qkv[...])
        normal, inverse = norm_parts(tok[rows, :].astype(f32))
        grad_norm, grad_gain = norm_back(grad_normed, gain_attn[...], normal, inverse)
        small_own[0:1, :] += grad_gain
        grad_tokens[rows, :] = grad_residual[rows, :] + grad_norm

    small_own[...] = partial[...]
    seg_row = seg[...].astype(f32)
    seg_col[...] = jnp.transpose(jnp.broadcast_to(seg_row, (LANES, tokens)))
    slab_bias(bias, seg_col, seg_row)

    @pl.loop(0, PAIRS)
    def _(pair):
        for load in pair_loads(pair):
            load.wait()
        pair_backward(pair, packed, grad_context, lse, extra, bias, grad_k, grad_v, pair_grads)

        @pl.when(pair == 0)
        def _():
            for load in loads[:2]:
                load.wait()
            normed_t[...] = jnp.transpose(normed_attn[...])
            pl.semaphore_wait(barrier, chips + planes - 1)

        pair_products(pair)

        @pl.when(lax.rem(pair + 1, pairs) == 0)
        def _():
            stage = pair // pairs
            core_copy(stage).start()

            @pl.when(stage > 0)
            def _():
                chip_stage(stage - 1)

            @pl.when(stage > 1)
            def _():
                plane_stage(stage - 2)

            @pl.when(stage > 2)
            def _():
                own_stage(stage - 3)

    for load in loads[2:]:
        load.wait()
    steps = (chip_stage, plane_stage, own_stage, gather_stage, last_stage)
    for late in range(len(steps)):
        if late == 0:
            norm_tile(0)
        for i, step in enumerate(steps):
            stage = stages - 1 + late - i
            if i >= late and 0 <= stage < stages:
                step(stage)
        if late == 0:
            for i in range(1, tiles):
                norm_tile(i)
            small_core_copy().start()
            store = pltpu.make_async_copy(grad_tokens, grad_tokens_out, store_sem)
            store.start()
        if late == 1:
            small_core_copy().wait_recv()
            small_chip[chip] = small_own[...] + small_core[...]

            @pl.loop(1, chips)
            def _(j):
                small_chip_copy(j).start()

        if late == 2:

            @pl.loop(1, chips)
            def _(j):
                small_chip_copy(j).wait_recv()

            total = small_chip[0]
            for c in range(1, chips):
                total = total + small_chip[c]
            small_plane[plane] = total

            @pl.loop(1, planes)
            def _(j):
                small_plane_copy(j).start()

    @pl.loop(1, planes)
    def _(j):
        small_plane_copy(j).wait_recv()

    total = small_plane[0]
    for c in range(1, planes):
        total = total + small_plane[c]
    small[...] = total
    store.wait()

    @pl.loop(0, stages)
    def _(stage):
        core_back(stage).wait()
        core_copy(stage).wait_send()

        @pl.loop(1, chips)
        def _(j):
            chip_back(stage, j).wait_send()
            chip_copy(stage, j).wait_send()

        @pl.loop(1, planes)
        def _(j):
            plane_back(stage, j).wait_send()
            plane_copy(stage, j).wait_send()

    @pl.loop(1, planes)
    def _(j):
        small_plane_copy(j).wait_send()

    @pl.loop(1, chips)
    def _(j):
        small_chip_copy(j).wait_send()

    small_core_copy().wait_send()


def shared_gradients(*operands):
    partial, packed = operands[2], operands[4]
    tokens = packed.shape[0]
    chips = lax.axis_size("wide") // 2
    planes = lax.axis_size("narrow")
    stages = 16 // planes
    share = D // (2 * chips)
    rows = partial.shape[0]
    dma = pltpu.SemaphoreType.DMA
    vmem = pl.BlockSpec(memory_space=pltpu.VMEM)
    anywhere = pl.BlockSpec(memory_space=pl.ANY)
    return pl.pallas_call(
        functools.partial(shared_kernel, chips, planes),
        in_specs=[vmem] * 4 + [anywhere] * 8,
        out_specs=(vmem, vmem, anywhere),
        out_shape=(
            jax.ShapeDtypeStruct((16, D, LANES), bf16),
            jax.ShapeDtypeStruct((rows, D), f32),
            jax.ShapeDtypeStruct((tokens, D), f32),
        ),
        scratch_shapes=[pltpu.VMEM(operand.shape, operand.dtype) for operand in operands[4:]]
        + [
            pltpu.VMEM((tokens, 3 * PAIR), bf16),
            pltpu.VMEM((tokens, D), f32),
            pltpu.VMEM((D, tokens), bf16),
            pltpu.VMEM((tokens, LANES), f32),
            pltpu.VMEM((SLAB_AT[-1], QB), f32),
            pltpu.VMEM((tokens, PAIR), f32),
            pltpu.VMEM((tokens, PAIR), f32),
            pltpu.VMEM((tokens, 3 * D), bf16),
            pltpu.VMEM((16, D // 2, LANES), f32),
            pltpu.VMEM((16, D // 2, LANES), bf16),
            pltpu.VMEM((16, D // 2, LANES), bf16),
            pltpu.VMEM((16, D // 2, LANES), bf16),
            pltpu.VMEM((chips, 16, share, LANES), bf16),
            pltpu.VMEM((16, share, LANES), bf16),
            pltpu.VMEM((planes, stages, share, LANES), bf16),
            pltpu.VMEM((rows, D), f32),
            pltpu.VMEM((rows, D), f32),
            pltpu.VMEM((chips, rows, D), f32),
            pltpu.VMEM((planes, rows, D), f32),
            dma((PAIRS, 7)),
            dma((5,)),
            dma,
            dma((2, stages)),
            dma((2, stages, chips)),
            dma((2, stages, planes)),
            dma((2, stages, planes)),
            dma((2, stages, chips)),
            dma((2, stages)),
            dma((2,)),
            dma((2, chips)),
            dma((2, planes)),
        ],
        compiler_params=pltpu.CompilerParams(
            vmem_limit_bytes=VMEM_LIMIT, collective_id=2, has_side_effects=True
        ),
        cost_estimate=pl.CostEstimate(
            flops=12 * tokens * D * D, bytes_accessed=16 * MIB, transcendentals=0
        ),
        name="shared_gradients",
    )(*operands)


def finish_kernel(
    experts,
    small,
    summed_in,
    ring_in,
    own_in,
    tokens_in,
    gain_attn,
    gain_moe,
    router,
    kept,
    dropped,
    qkv_out,
    proj_out,
    in_out,
    out_out,
    tokens_out,
    summed,
    ring,
    own,
    tokens,
    qkv,
    proj,
    grad_in,
    grad_out,
    load_sem,
    store_sem,
    token_sem,
):
    loads = loading(
        (summed_in, ring_in, own_in, tokens_in), (summed, ring, own, tokens), load_sem
    )
    through = pltpu.make_async_copy(tokens, tokens_out, token_sem)
    gain_attn[...] = small[0, :]
    gain_moe[...] = small[1, :]
    router[...] = small[8:, :]
    counted = small[2:4, :experts]
    kept[...] = counted[0:1].astype(jnp.int32)
    dropped[...] = (counted[1:2] - counted[0:1]).astype(jnp.int32)
    loads[0].wait()
    stores = []
    step = D // 4
    for i in range(4):
        rows = slice(i * step, (i + 1) * step)
        for n in range(16):
            pair, which = divmod(n, 4)
            lanes = slice(pair * PAIR, (pair + 1) * PAIR)
            if which < 3:
                qkv[rows, which * D + lanes.start : which * D + lanes.stop] = summed[n, rows, :].astype(f32)
            else:
                proj[rows, lanes] = summed[n, rows, :].astype(f32)
        for source, target in ((qkv, qkv_out), (proj, proj_out)):
            stores.append(pltpu.make_async_copy(source.at[rows], target.at[rows], store_sem.at[len(stores)]))
            stores[-1].start()
    for load in loads[1:]:
        load.wait()
    through.start()
    grad_in[0] = ring[:D, :].astype(f32) + own[:D, :].astype(f32)
    stores.append(pltpu.make_async_copy(grad_in, in_out, store_sem.at[len(stores)]))
    stores[-1].start()
    grad_out[0] = jnp.transpose(ring[D:, :].astype(f32) + own[D:, :].astype(f32))
    stores.append(pltpu.make_async_copy(grad_out, out_out, store_sem.at[len(stores)]))
    stores[-1].start()
    for store in stores:
        store.wait()
    through.wait()


def finish(experts, small, summed, ring, own, tokens_in):
    hidden = own.shape[1]
    vmem = pl.BlockSpec(memory_space=pltpu.VMEM)
    anywhere = pl.BlockSpec(memory_space=pl.ANY)
    large = [((D, 3 * D), f32), ((D, D), f32), ((1, D, hidden), f32), ((1, hidden, D), f32)]
    dma = pltpu.SemaphoreType.DMA
    return pl.pallas_call(
        functools.partial(finish_kernel, experts),
        in_specs=[vmem] + [anywhere] * 4,
        out_specs=[vmem] * 5 + [anywhere] * 5,
        out_shape=[
            jax.ShapeDtypeStruct((D,), f32),
            jax.ShapeDtypeStruct((D,), f32),
            jax.ShapeDtypeStruct((experts, D), f32),
            jax.ShapeDtypeStruct((1, experts), jnp.int32),
            jax.ShapeDtypeStruct((1, experts), jnp.int32),
        ]
        + [jax.ShapeDtypeStruct(*shape) for shape in large]
        + [jax.ShapeDtypeStruct(tokens_in.shape, f32)],
        scratch_shapes=like((summed, ring, own, tokens_in))
        + [pltpu.VMEM(*shape) for shape in large]
        + [dma((4,)), dma((10,)), dma],
        compiler_params=pltpu.CompilerParams(vmem_limit_bytes=VMEM_LIMIT),
        cost_estimate=pl.CostEstimate(flops=0, bytes_accessed=14 * MIB, transcendentals=0),
        name="finish",
    )(small, summed, ring, own, tokens_in)


def per_device(
    tokens,
    segment_ids,
    expert_picks,
    priority_ranks,
    gain_attn,
    w_qkv,
    w_proj,
    gain_moe,
    w_router,
    w_in,
    w_out,
    cotangent,
):
    experts = w_router.shape[1]
    capacity = (21 * TOP * TOK_DEV + 20 * experts - 1) // (20 * experts)
    padded = (capacity + 3 + 15) // 16 * 16
    gain_attn = gain_attn.reshape(1, D)
    gain_moe = gain_moe.reshape(1, D)
    seg = segment_ids.reshape(1, SEQ)
    line = lax.axis_size("narrow")
    ring_steps = [(i, (i + 1) % line) for i in range(line)]
    together = lax.optimization_barrier

    def pass_on(values):
        return lax.ppermute(values, "narrow", ring_steps)

    early = [(w_in[0], w_out[0])]
    early.append(pass_on(early[0]))
    slot_col, slot_row, counts, windows, gz_send, normed_attn, packed, extra = route(
        expert_picks.T, priority_ranks, seg, gain_attn, cotangent, tokens, w_qkv, experts, capacity, padded
    )
    gz = lax.all_to_all(gz_send, "wide", split_axis=0, concat_axis=0, tiled=True)
    early.append(pass_on(together((early[1], slot_row))[0]))
    context, lse, residual, normed_moe, gates, gate_row = forward(
        windows, seg, gain_moe, w_router.T, packed, tokens, w_proj
    )
    ring, own, partial, mixed, grad_residual, grad_context, grad_proj, *others = moe(
        slot_row,
        gate_row,
        w_router.T,
        gain_moe,
        counts,
        normed_moe,
        gz.reshape(experts * padded, D),
        slot_col,
        gates,
        cotangent,
        residual,
        context,
        w_proj,
        *[part for pair in early for part in pair],
        shards=line,
        capacity=capacity,
    )
    for other in others:
        ring = (pass_on(ring).astype(f32) + other.astype(f32)).astype(bf16)
    ring = pass_on(ring)
    extra, grad_context = repair(windows, seg, lse, packed, extra, grad_context)
    summed, small, grad_tokens = shared_gradients(
        seg,
        lse,
        partial,
        gain_attn,
        packed,
        grad_context,
        extra,
        normed_attn,
        grad_proj,
        w_qkv,
        tokens,
        grad_residual,
    )
    grad_gain_attn, grad_gain_moe, grad_router, kept, dropped, grad_qkv, grad_proj, grad_in, grad_out, grad_tokens = finish(
        experts, small, summed, ring, own, grad_tokens
    )
    return (
        mixed,
        grad_tokens,
        grad_gain_attn,
        grad_qkv,
        grad_proj,
        grad_gain_moe,
        grad_router.T,
        grad_in,
        grad_out,
        kept.reshape(experts),
        dropped.reshape(experts),
    )


def solution(mesh):
    both = ("wide", "narrow")
    placed = (
        P(both, None),
        P(both),
        P(both, None),
        P(both, None),
        P(),
        P(),
        P(),
        P(),
        P(),
        P("wide", None, "narrow"),
        P("wide", "narrow", None),
        P(both, None),
    )
    return jax.shard_map(
        per_device,
        mesh=mesh,
        in_specs=placed,
        out_specs=(
            P(both, None),
            P(both, None),
            P(),
            P(),
            P(),
            P(),
            P(),
            P("wide", None, "narrow"),
            P("wide", "narrow", None),
            P(),
            P(),
        ),
        check_vma=False,
    )
```
